32 devices in a mesh: groups: 2 (over x), heads: 16 (over z, y, core).
Axes of the slice: x: 2, y: 2, z: 4, core: 2. Of those that a mesh axis runs over, the one named last changes fastest.
Arguments:
- tokens: bfloat16 [64, 4, 2304], P('groups'), parts along dimension 0, may hold values from -6 to 6
- qkv_weight: bfloat16 [4608, 12288], P(('groups', 'heads')), parts along dimension 0, may hold values from -0.125 to 0.125
- gate_weight: bfloat16 [4608, 64], P(('groups', 'heads')), parts along dimension 0, may hold values from -0.125 to 0.125
- conv_weight: bfloat16 [8, 12288], P('groups', 'heads'), parts along dimension 0, may hold values from -3 to 3
- delta_state: float32 [64, 32, 128, 128], P(('groups', 'heads')), parts along dimension 0, may hold values from -0.8 to 0.8
- conv_state: float32 [64, 3, 12288], P(('groups', 'heads')), parts along dimension 0, may hold values from -6 to 6
- old_heads: int32 [32], replicated, may hold values from 0 to 31, each once
- new_units: int32 [64], replicated, may hold values from 0 to 63, each once
- slot_of: int32 [64], P('groups'), parts along dimension 0, may hold values from 0 to 31, each once
- lengths: int32 [64], P('groups'), parts along dimension 0, may hold values from 1 to 4, as said below
Outputs:
- readout: bfloat16 [64, 4, 4096], P('groups', None, 'heads'), parts along dimension 0
The draws below stay inside these ranges and needn't reach their ends.
There are 2 independent parts, one for each index of `groups`. The reference program is written for one: setup_inputs(seed, part) draws one part's arguments, and reference() takes and returns one part's arrays. A program takes and returns all parts, laid end to end along the dimension named above; an argument that names none is the same for every part. Nothing has to cross between parts.
Inputs may be any that keep to these rules, and one draw needn't show every extreme that they name: `old_heads`: a permutation of the heads; old column slot p holds head old_heads[p]. `new_units`: a permutation of the head units; unit u is the half u % 2 of the values of head u // 2. `slot_of`: a permutation of the rows. `lengths`: some row decodes all 4 steps and some row only one.
All inputs are finite; a program needn't handle non-finite values.
Results may differ from the reference program's by a relative error of at most 0.001.
Values may be sent and summed in bfloat16 or wider, within the bound.
No kernel may reach another device: no remote copies, remote signals or barrier semaphores. Data moves between devices by JAX's collectives and lax.ppermute only.
A program may use at most 128 MiB of HBM per device.

```python
import jax
import jax.numpy as jnp
from jax import lax

D = 2304
H = 32
DK = 128
TAPS = 4
STEPS = 4
ROLLOUTS = 32
HALF = 64
UNITS = 64


def draw_lengths(key, part):
    first_key, second_key = jax.random.split(key)
    values = jax.random.randint(first_key, (ROLLOUTS,), 1, STEPS + 1)
    spots = jax.random.permutation(second_key, ROLLOUTS)
    values = values.at[spots[0]].set(STEPS)
    values = values.at[spots[1]].set(1)
    return values.astype(jnp.int32)


def steps_of(rng, dims, shards, least, top_value):
    gain = 1.0
    for axis_at, shards_of in shards:
        heights = jax.random.uniform(jax.random.fold_in(jax.random.fold_in(rng, 6), axis_at), (shards_of,), jnp.float32, least / len(shards), top_value / len(shards))
        gain = gain * jnp.repeat(jnp.exp(heights), dims[axis_at] // shards_of).reshape((-1,) + (1,) * (len(dims) - 1 - axis_at))
    return gain


def bell_draw(own_key, shape, scale, bound, pieces=(), held_as=jnp.bfloat16):
    drawn = scale * jax.random.normal(own_key, shape, jnp.float32)
    if pieces:
        drawn = drawn * steps_of(own_key, shape, pieces, -0.22, 0.18)
    return jnp.clip(drawn, -bound, bound).astype(held_as)


def setup_inputs(seed: int = 0, part: int = 0) -> dict:
    streams_of = jax.random.split(jax.random.key(seed), 11)
    part_keys = jax.random.split(jax.random.fold_in(streams_of[10], part), 11)
    return {
        "tokens": bell_draw(part_keys[0], (ROLLOUTS, STEPS, D), 1.0, 6.0),
        "qkv_weight": bell_draw(part_keys[1], (D, 3 * H * DK), D ** -0.5, 0.125, ((0, 16),)),
        "gate_weight": bell_draw(part_keys[2], (D, 2 * H), D ** -0.5, 0.125, ((0, 16),)),
        "conv_weight": bell_draw(part_keys[3], (TAPS, 3 * H * DK), TAPS ** -0.5, 3.0, ((1, 16),)),
        "delta_state": bell_draw(part_keys[4], (ROLLOUTS, H, DK, DK), 0.1, 0.8, ((0, 16),), jnp.float32),
        "conv_state": bell_draw(part_keys[5], (ROLLOUTS, TAPS - 1, 3 * H * DK), 1.0, 6.0, ((0, 16),), jnp.float32),
        "old_heads": jax.random.permutation(streams_of[6], H).astype(jnp.int32),
        "new_units": jax.random.permutation(streams_of[7], UNITS).astype(jnp.int32),
        "slot_of": jax.random.permutation(part_keys[8], ROLLOUTS).astype(jnp.int32),
        "lengths": draw_lengths(jax.random.fold_in(jax.random.fold_in(streams_of[10], part), 71), part),
    }


norm_eps = 1e-06

def unit_tables(old_heads, new_units):
    positions = jnp.arange(H, dtype=jnp.int32)
    inverse = lax.optimization_barrier(jnp.sum(jnp.where(old_heads[None, :] == positions[:, None], positions[None, :], 0), axis=1)).astype(jnp.int32)
    heads_of = (new_units // 2).astype(jnp.int32)
    halves = (new_units % 2).astype(jnp.int32)
    old_slots = lax.optimization_barrier(jnp.sum(jnp.where(heads_of[:, None] == positions[None, :], inverse[None, :], 0), axis=1)).astype(jnp.int32)
    return (old_slots, halves)

def normalize(values):
    return values * jax.lax.rsqrt(lax.optimization_barrier(jnp.sum(values * values, axis=-1, keepdims=True)) + norm_eps)

def reference(tokens, qkv_weight, gate_weight, conv_weight, delta_state, conv_state, old_heads, new_units, slot_of, lengths):
    row_count = tokens.shape[0]
    flattened = tokens.reshape(row_count * STEPS, D)
    projected = jnp.dot(flattened, qkv_weight, preferred_element_type=jnp.float32).reshape(row_count, STEPS, 3 * H * DK)
    gate_logits = jnp.dot(flattened, gate_weight, preferred_element_type=jnp.float32).reshape(row_count, STEPS, 2, H)
    history = conv_state[slot_of]
    sequence = jnp.concatenate([history, projected], axis=1)
    tap_weights = conv_weight.astype(jnp.float32)
    convolved = tap_weights[0][None, None, :] * sequence[:, 0:STEPS]
    for tap_index in range(1, TAPS):
        convolved = convolved + tap_weights[tap_index][None, None, :] * sequence[:, tap_index:tap_index + STEPS]
    activated = jax.nn.silu(convolved).reshape(row_count, STEPS, 3, H, DK)
    queries = normalize(activated[:, :, 0])
    keys_all = normalize(activated[:, :, 1])
    values_all = activated[:, :, 2]
    beta = jax.nn.sigmoid(gate_logits[:, :, 0])
    decay = jnp.exp(-jax.nn.softplus(gate_logits[:, :, 1]))
    carried = delta_state[slot_of]
    readouts = []
    for step_index in range(STEPS):
        is_live = (step_index < lengths)[:, None, None, None]
        faded = decay[:, step_index, :, None, None] * carried
        predicted = lax.optimization_barrier(jnp.sum(keys_all[:, step_index, :, :, None] * faded, axis=2))
        updated = faded + beta[:, step_index, :, None, None] * keys_all[:, step_index, :, :, None] * (values_all[:, step_index] - predicted)[:, :, None, :]
        heads_now = lax.optimization_barrier(jnp.sum(queries[:, step_index, :, :, None] * updated, axis=2))
        carried = jnp.where(is_live, updated, carried)
        readouts.append(jnp.where(is_live[..., 0], heads_now, jnp.zeros_like(heads_now)))
    heads_out = jnp.stack(readouts, axis=1)
    old_slots, halves = unit_tables(old_heads, new_units)
    split_heads = heads_out.reshape(row_count, STEPS, H, 2, HALF)[:, :, old_slots]
    chosen = jnp.where((halves == 0)[None, None, :, None], split_heads[:, :, :, 0], split_heads[:, :, :, 1])
    return chosen.reshape(row_count, STEPS, UNITS * HALF).astype(jnp.bfloat16)
```

```python
import functools

import jax
import jax.numpy as jnp
from jax import lax
from jax.experimental import pallas as pl
from jax.experimental.pallas import tpu as pltpu
from jax.sharding import PartitionSpec as P

D = 2304
H = 32
DK = 128
TAPS = 4
STEPS = 4
HALF = 64
UNITS = 64
LOCAL = 2
ROWS = LOCAL * STEPS
HEADS_WIDTH = H * DK

norm_eps = 1e-06


def unit_tables(old_heads, new_units):
    positions = jnp.arange(H, dtype=jnp.int32)
    inverse = jnp.sum(
        jnp.where(old_heads[None, :] == positions[:, None], positions[None, :], 0), axis=1
    )
    heads_of = new_units // 2
    halves = new_units % 2
    old_slots = jnp.sum(
        jnp.where(heads_of[:, None] == positions[None, :], inverse[None, :], 0), axis=1
    )
    return (old_slots, halves)


def shift_rows(value, lag, row_step):
    if lag == 0:
        return value
    moved = pltpu.roll(value, lag, 0)
    return jnp.where(row_step >= lag, moved, 0.0)


def delta_kernel(
    slots_ref, halves_ref, lengths_ref, queries_ref, keys_ref, values_ref, gates_ref,
    early_ref, taps_ref, state_ref, out_ref, heads_ref,
):
    row = lax.broadcasted_iota(jnp.int32, (ROWS, DK), 0)
    row_step = row % STEPS
    lane = lax.broadcasted_iota(jnp.int32, (ROWS, DK), 1)
    row_length = jnp.where(row < STEPS, lengths_ref[0], lengths_ref[1])
    live = row_step < row_length

    def activate(source_ref, part, head):
        columns = pl.ds(part * HEADS_WIDTH + head * DK, DK)
        fresh = source_ref[:, pl.ds(head * DK, DK)]
        total = early_ref[:, columns]
        for lag in range(TAPS):
            tap = taps_ref[TAPS - 1 - lag : TAPS - lag, columns].astype(jnp.float32)
            total = total + tap * shift_rows(fresh, lag, row_step)
        return total / (1.0 + jnp.exp(-total))

    def lane_sum(value):
        return jnp.sum(value, axis=-1, keepdims=True)

    def unit_length(value):
        return value * lax.rsqrt(lane_sum(value * value) + norm_eps)

    for head in range(H):
        query = unit_length(activate(queries_ref, 0, head))
        key = unit_length(activate(keys_ref, 1, head))
        value = activate(values_ref, 2, head)
        beta_logit = jnp.broadcast_to(gates_ref[:, head : head + 1], (ROWS, DK))
        decay_logit = jnp.broadcast_to(gates_ref[:, H + head : H + head + 1], (ROWS, DK))
        beta = 1.0 / (1.0 + jnp.exp(-beta_logit))
        decay = 1.0 / (1.0 + jnp.exp(decay_logit))
        fades = [jnp.ones_like(decay)]
        for lag in range(1, STEPS + 1):
            fades.append(
                jnp.where(
                    row_step >= lag - 1,
                    fades[-1] * (pltpu.roll(decay, lag - 1, 0) if lag > 1 else decay),
                    fades[-1],
                )
            )
        both = jnp.concatenate([key, query], axis=0)
        seen = [
            jnp.dot(both, state_ref[r, head], precision=lax.Precision.HIGHEST,
                    preferred_element_type=jnp.float32)
            for r in range(LOCAL)
        ]
        key_seen = jnp.where(row < STEPS, seen[0][:ROWS], seen[1][:ROWS])
        query_seen = jnp.where(row < STEPS, seen[0][ROWS:], seen[1][ROWS:])
        base = beta * (value - fades[STEPS] * key_seen)
        pulls = [None] + [
            beta * fades[lag] * lane_sum(key * shift_rows(key, lag, row_step))
            for lag in range(1, STEPS)
        ]
        solved = base
        for _ in range(STEPS - 1):
            following = base
            for lag in range(1, STEPS):
                following = following - pulls[lag] * shift_rows(solved, lag, row_step)
            solved = following
        out = fades[STEPS] * query_seen
        for lag in range(STEPS):
            moved_key = shift_rows(key, lag, row_step)
            weight = fades[lag] * lane_sum(query * moved_key)
            out = out + weight * shift_rows(solved, lag, row_step)
        heads_ref[head] = jnp.where(live, out, 0.0)

    for pair in range(UNITS // 2):
        first = heads_ref[slots_ref[2 * pair]]
        second = heads_ref[slots_ref[2 * pair + 1]]
        first = jnp.where(halves_ref[2 * pair] == 0, first, pltpu.roll(first, HALF, 1))
        second = jnp.where(halves_ref[2 * pair + 1] == 0, pltpu.roll(second, HALF, 1), second)
        joined = jnp.where(lane < HALF, first, second)
        heads_ref[H + pair] = joined
    for quad in range(UNITS // 4):
        out_ref[quad] = jnp.concatenate(
            [heads_ref[H + 2 * quad], heads_ref[H + 2 * quad + 1]], axis=0
        ).astype(jnp.bfloat16)


def run_delta(slots, halves, lengths, queries, keys, values, gates, early, taps, state):
    smem = pl.BlockSpec(memory_space=pltpu.SMEM)
    vmem = pl.BlockSpec(memory_space=pltpu.VMEM)
    return pl.pallas_call(
        delta_kernel,
        out_shape=jax.ShapeDtypeStruct((UNITS // 4, 2 * ROWS, DK), jnp.bfloat16),
        in_specs=[smem] * 3 + [vmem] * 7,
        out_specs=vmem,
        scratch_shapes=[pltpu.VMEM((2 * H, ROWS, DK), jnp.float32)],
        compiler_params=pltpu.CompilerParams(vmem_limit_bytes=32 * 1024 * 1024),
        cost_estimate=pl.CostEstimate(flops=40_000_000, bytes_accessed=5_000_000, transcendentals=0),
        name="delta_rule",
    )(slots, halves, lengths, queries, keys, values, gates, early, taps, state)


def swap(value, bit, devices):
    return lax.ppermute(value, "heads", [(i, i ^ bit) for i in range(devices)])


def on_device(
    tokens,
    qkv_weight,
    gate_weight,
    conv_weight,
    delta_state,
    conv_state,
    old_heads,
    new_units,
    slot_of,
    lengths,
):
    devices = lax.axis_size("heads")
    me = lax.axis_index("heads")
    per_device = UNITS // devices
    depth = qkv_weight.shape[0]
    row_count = tokens.shape[0]
    chips = devices // 2

    old_slots, halves = unit_tables(old_heads, new_units)
    bits = [1 << b for b in range(1, devices.bit_length() - 1)]
    order = []
    for place in range(chips):
        offset = 0
        for at, bit in enumerate(bits):
            if place & (chips >> (at + 1)):
                offset |= bit
        order.append(offset)
    holders = jnp.bitwise_xor(jnp.asarray(order, jnp.int32), me)
    old_rows = (holders[:, None] * LOCAL + jnp.arange(LOCAL, dtype=jnp.int32)[None, :]).reshape(-1)
    flat_tokens = tokens.reshape(row_count * STEPS, D)
    steps = jnp.arange(STEPS, dtype=jnp.int32)
    wanted = (old_rows[:, None] * STEPS + steps[None, :]).reshape(-1)
    offered = (slot_of[:, None] * STEPS + steps[None, :]).reshape(-1)
    picker = (wanted[:, None] == offered[None, :]).astype(jnp.bfloat16)

    def token_part(owner):
        columns = lax.dynamic_slice_in_dim(flat_tokens, owner * depth, depth, 1)
        return jnp.dot(picker, columns, preferred_element_type=jnp.float32).astype(jnp.bfloat16)

    mine, theirs = token_part(me), token_part(jnp.bitwise_xor(me, 1))
    half_rows = chips * ROWS // 2

    chunks = []
    for part in (1, 0, 2):
        block = qkv_weight[:, part * HEADS_WIDTH : (part + 1) * HEADS_WIDTH]
        if part == 1:
            block = jnp.concatenate([block, gate_weight], axis=1)
        chunks.append(block)
    others = [swap(block, 1, devices) for block in chunks]

    def product(rows, block, other):
        return jnp.dot(mine[rows], block, preferred_element_type=jnp.float32) + jnp.dot(
            theirs[rows], other, preferred_element_type=jnp.float32
        )

    sums = []
    for block, other in zip(chunks, others):
        sent = swap(product(slice(half_rows, None), block, other), bits[0], devices)
        kept = product(slice(0, half_rows), block, other)
        total = kept + sent
        for bit in bits[1:]:
            half = total.shape[0] // 2
            total = total[:half] + swap(total[half:], bit, devices)
        sums.append(total)

    taps = lax.all_gather(conv_weight, "heads", axis=1, tiled=True)
    taps_f = taps.astype(jnp.float32)
    early = []
    for step in range(STEPS):
        term = jnp.zeros_like(conv_state[:, 0])
        for tap in range(TAPS - 1 - step):
            term = term + taps_f[tap][None] * conv_state[:, step + tap]
        early.append(term)
    early = jnp.stack(early, axis=1).reshape(ROWS, 3 * HEADS_WIDTH)

    my_rows = me * LOCAL + jnp.arange(LOCAL, dtype=jnp.int32)
    my_lengths = jnp.sum(
        jnp.where(slot_of[None, :] == my_rows[:, None], lengths[None, :], 0), axis=1
    )
    keys, gates = sums[0][:, :HEADS_WIDTH], sums[0][:, HEADS_WIDTH:]
    local_out = run_delta(
        old_slots, halves, my_lengths, sums[1], keys, sums[2], gates, early, taps, delta_state
    )

    placer = (offered[:, None] == jnp.arange(row_count * STEPS, dtype=jnp.int32)[None, :]).astype(
        jnp.bfloat16
    )
    if per_device % 2 == 0:
        pairs = per_device // 2
        sending = local_out.reshape(devices, pairs * ROWS, DK)
        got = lax.all_to_all(sending, "heads", split_axis=0, concat_axis=0, tiled=True)
        got = got.reshape(devices, pairs, ROWS, DK)
        got = jnp.concatenate([got[:, pair] for pair in range(pairs)], axis=-1)
        got = got.reshape(devices * ROWS, pairs * DK)
    else:
        units = local_out.reshape(UNITS // 2, ROWS, 2, HALF).transpose(0, 2, 1, 3)
        sending = units.reshape(devices, per_device * ROWS, HALF)
        got = lax.all_to_all(sending, "heads", split_axis=0, concat_axis=0, tiled=True)
        got = got.reshape(devices, per_device, ROWS, HALF).transpose(0, 2, 1, 3)
        got = got.reshape(devices * ROWS, per_device * HALF)
    outputs = jnp.dot(placer, got, preferred_element_type=jnp.float32).astype(jnp.bfloat16)
    return outputs.reshape(row_count, STEPS, per_device * HALF)


def solution(mesh):
    in_specs = (
        P("groups", None, None),
        P(("groups", "heads"), None),
        P(("groups", "heads"), None),
        P("groups", "heads"),
        P(("groups", "heads"), None, None, None),
        P(("groups", "heads"), None, None),
        P(),
        P(),
        P("groups"),
        P("groups"),
    )
    out_specs = P("groups", None, "heads")
    return jax.shard_map(
        on_device, mesh=mesh, in_specs=in_specs, out_specs=out_specs, check_vma=False
    )
```

```python
import functools

import jax
import jax.numpy as jnp
from jax import lax
from jax.experimental import pallas as pl
from jax.experimental.pallas import tpu as pltpu
from jax.sharding import PartitionSpec as P

D = 2304
H = 32
DK = 128
TAPS = 4
STEPS = 4
HALF = 64
UNITS = 64
LOCAL = 2
ROWS = LOCAL * STEPS
HEADS_WIDTH = H * DK
PIECES = 2

norm_eps = 1e-06


def unit_tables(old_heads, new_units):
    positions = jnp.arange(H, dtype=jnp.int32)
    inverse = jnp.sum(
        jnp.where(old_heads[None, :] == positions[:, None], positions[None, :], 0), axis=1
    )
    heads_of = new_units // 2
    halves = new_units % 2
    old_slots = jnp.sum(
        jnp.where(heads_of[:, None] == positions[None, :], inverse[None, :], 0), axis=1
    )
    return (old_slots, halves)


def shift_rows(value, lag, row_step):
    if lag == 0:
        return value
    moved = pltpu.roll(value, lag, 0)
    return jnp.where(row_step >= lag, moved, 0.0)


def lane_sum(value):
    return jnp.sum(value, axis=-1, keepdims=True)


def unit_length(value):
    return value * lax.rsqrt(lane_sum(value * value) + norm_eps)


def activate(pieces, part, head, early_ref, taps_ref, row_step):
    per_piece = H // len(pieces)
    kept_ref, sent_ref = pieces[head // per_piece]
    inner = pl.ds(head % per_piece * DK, DK)
    fresh = kept_ref[:ROWS, inner] + sent_ref[:, inner]
    columns = pl.ds(part * HEADS_WIDTH + head * DK, DK)
    total = early_ref[:, columns]
    for lag in range(TAPS):
        tap = taps_ref[TAPS - 1 - lag : TAPS - lag, columns].astype(jnp.float32)
        total = total + tap * shift_rows(fresh, lag, row_step)
    return total / (1.0 + jnp.exp(-total))


def keys_kernel(*refs):
    ins, outs = refs[: 4 * PIECES + 3], refs[4 * PIECES + 3 :]
    key_refs = [(ins[2 * i], ins[2 * i + 1]) for i in range(PIECES)]
    query_refs = [(ins[2 * i], ins[2 * i + 1]) for i in range(PIECES, 2 * PIECES)]
    early_ref, taps_ref, state_ref = ins[4 * PIECES :]
    beta_ref, key_seen_ref, query_seen_ref, pulls_ref, weights_ref = outs
    row = lax.broadcasted_iota(jnp.int32, (ROWS, DK), 0)
    row_step = row % STEPS
    kept_ref, sent_ref = key_refs[0]
    width = HEADS_WIDTH // PIECES
    gates = kept_ref[:ROWS, width : width + 2 * H] + sent_ref[:, width : width + 2 * H]
    for head in range(H):
        key = unit_length(activate(key_refs, 1, head, early_ref, taps_ref, row_step))
        query = unit_length(activate(query_refs, 0, head, early_ref, taps_ref, row_step))
        beta_logit = jnp.broadcast_to(gates[:, head : head + 1], (ROWS, DK))
        decay_logit = jnp.broadcast_to(gates[:, H + head : H + head + 1], (ROWS, DK))
        beta = 1.0 / (1.0 + jnp.exp(-beta_logit))
        decay = 1.0 / (1.0 + jnp.exp(decay_logit))
        fades = [jnp.ones_like(decay), decay]
        for lag in range(2, STEPS + 1):
            earlier = pltpu.roll(decay, lag - 1, 0)
            fades.append(jnp.where(row_step >= lag - 1, fades[-1] * earlier, fades[-1]))
        both = jnp.concatenate([key, query], axis=0)
        seen = [
            jnp.dot(both, state_ref[r, head], precision=lax.Precision.HIGHEST,
                    preferred_element_type=jnp.float32)
            for r in range(LOCAL)
        ]
        beta_ref[head] = beta
        key_seen_ref[head] = beta * fades[STEPS] * jnp.where(
            row < STEPS, seen[0][:ROWS], seen[1][:ROWS]
        )
        query_seen_ref[head] = fades[STEPS] * jnp.where(
            row < STEPS, seen[0][ROWS:], seen[1][ROWS:]
        )
        for lag in range(STEPS):
            moved_key = shift_rows(key, lag, row_step)
            if lag:
                pulls_ref[lag - 1, head] = beta * fades[lag] * lane_sum(key * moved_key)
            weights_ref[lag, head] = fades[lag] * lane_sum(query * moved_key)


def values_kernel(slots_ref, halves_ref, lengths_ref, *refs):
    value_refs = [(refs[2 * i], refs[2 * i + 1]) for i in range(PIECES)]
    early_ref, taps_ref, beta_ref, key_seen_ref, query_seen_ref, pulls_ref, weights_ref = refs[
        2 * PIECES : 2 * PIECES + 7
    ]
    out_ref, heads_ref = refs[2 * PIECES + 7 :]
    row = lax.broadcasted_iota(jnp.int32, (ROWS, DK), 0)
    row_step = row % STEPS
    lane = lax.broadcasted_iota(jnp.int32, (ROWS, DK), 1)
    row_length = jnp.where(row < STEPS, lengths_ref[0], lengths_ref[1])
    live = row_step < row_length
    for head in range(H):
        value = activate(value_refs, 2, head, early_ref, taps_ref, row_step)
        base = beta_ref[head] * value - key_seen_ref[head]
        solved = base
        for _ in range(STEPS - 1):
            following = base
            for lag in range(1, STEPS):
                following = following - pulls_ref[lag - 1, head] * shift_rows(
                    solved, lag, row_step
                )
            solved = following
        out = query_seen_ref[head]
        for lag in range(STEPS):
            out = out + weights_ref[lag, head] * shift_rows(solved, lag, row_step)
        heads_ref[head] = jnp.where(live, out, 0.0)
    for quad in range(UNITS // 4):
        joined = []
        for pair in (2 * quad, 2 * quad + 1):
            first = heads_ref[slots_ref[2 * pair]]
            second = heads_ref[slots_ref[2 * pair + 1]]
            first = jnp.where(halves_ref[2 * pair] == 0, first, pltpu.roll(first, HALF, 1))
            second = jnp.where(halves_ref[2 * pair + 1] == 0, pltpu.roll(second, HALF, 1), second)
            joined.append(jnp.where(lane < HALF, first, second))
        out_ref[quad] = jnp.concatenate(joined, axis=0).astype(jnp.bfloat16)


def run_delta(slots, halves, lengths, keys, queries, values, early, taps, state):
    smem = pl.BlockSpec(memory_space=pltpu.SMEM)
    vmem = pl.BlockSpec(memory_space=pltpu.VMEM)
    params = pltpu.CompilerParams(vmem_limit_bytes=32 * 1024 * 1024)
    per_head = jax.ShapeDtypeStruct((H, ROWS, DK), jnp.float32)
    lags = [
        jax.ShapeDtypeStruct((count, H, ROWS, DK), jnp.float32) for count in (STEPS - 1, STEPS)
    ]
    flat = lambda pieces: [ref for piece in pieces for ref in piece]
    prepared = pl.pallas_call(
        keys_kernel,
        out_shape=[per_head] * 3 + lags,
        in_specs=[vmem] * (4 * PIECES + 3),
        out_specs=[vmem] * 5,
        compiler_params=params,
        cost_estimate=pl.CostEstimate(flops=40_000_000, bytes_accessed=9_000_000, transcendentals=0),
        name="keys_part",
    )(*flat(keys), *flat(queries), early, taps, state)
    return pl.pallas_call(
        values_kernel,
        out_shape=jax.ShapeDtypeStruct((UNITS // 4, 2 * ROWS, DK), jnp.bfloat16),
        in_specs=[smem] * 3 + [vmem] * (2 * PIECES + 7),
        out_specs=vmem,
        scratch_shapes=[pltpu.VMEM((H, ROWS, DK), jnp.float32)],
        compiler_params=params,
        cost_estimate=pl.CostEstimate(flops=4_000_000, bytes_accessed=2_000_000, transcendentals=0),
        name="values_part",
    )(slots, halves, lengths, *flat(values), early, taps, *prepared)


def swap(value, bit, devices):
    return lax.ppermute(value, "heads", [(i, i ^ bit) for i in range(devices)])


def on_device(
    tokens,
    qkv_weight,
    gate_weight,
    conv_weight,
    delta_state,
    conv_state,
    old_heads,
    new_units,
    slot_of,
    lengths,
):
    devices = lax.axis_size("heads")
    me = lax.axis_index("heads")
    per_device = UNITS // devices
    depth = qkv_weight.shape[0]
    row_count = tokens.shape[0]
    chips = devices // 2

    old_slots, halves = unit_tables(old_heads, new_units)
    bits = [1 << b for b in range(1, devices.bit_length() - 1)]
    order = []
    for place in range(chips):
        offset = 0
        for at, bit in enumerate(bits):
            if place & (chips >> (at + 1)):
                offset |= bit
        order.append(offset)
    holders = jnp.bitwise_xor(jnp.asarray(order, jnp.int32), me)
    old_rows = (holders[:, None] * LOCAL + jnp.arange(LOCAL, dtype=jnp.int32)[None, :]).reshape(-1)
    flat_tokens = tokens.reshape(row_count * STEPS, D)
    steps = jnp.arange(STEPS, dtype=jnp.int32)
    wanted = (old_rows[:, None] * STEPS + steps[None, :]).reshape(-1)
    offered = (slot_of[:, None] * STEPS + steps[None, :]).reshape(-1)
    picker = (wanted[:, None] == offered[None, :]).astype(jnp.bfloat16)

    def token_part(owner):
        columns = lax.dynamic_slice_in_dim(flat_tokens, owner * depth, depth, 1)
        return jnp.dot(picker, columns, preferred_element_type=jnp.float32).astype(jnp.bfloat16)

    mine, theirs = token_part(me), token_part(jnp.bitwise_xor(me, 1))
    half_rows = chips * ROWS // 2

    width = HEADS_WIDTH // PIECES
    chunks, others = [], []
    weight = qkv_weight
    for part in (1, 0, 2):
        for piece in range(PIECES):
            begin = part * HEADS_WIDTH + piece * width
            block = weight[:, begin : begin + width]
            if not chunks:
                block = jnp.concatenate([block, gate_weight], axis=1)
            block, weight = lax.optimization_barrier((block, weight))
            chunks.append(block)
            others.append(swap(block, 1, devices))

    pieces = []
    for block, other in zip(chunks, others):
        total = jnp.dot(mine, block, preferred_element_type=jnp.float32)
        total = total + jnp.dot(theirs, other, preferred_element_type=jnp.float32)
        for bit in bits[:-1]:
            half = total.shape[0] // 2
            total = total[:half] + swap(total[half:], bit, devices)
        pieces.append((total, swap(total[ROWS:], bits[-1], devices)))
    keys, queries, values = (pieces[i * PIECES : (i + 1) * PIECES] for i in range(3))

    gathered = conv_weight[None]
    for b in range(devices.bit_length() - 1):
        gathered = jnp.concatenate([gathered, swap(gathered, 1 << b, devices)], axis=0)
    places = jnp.arange(devices, dtype=jnp.int32)
    sorter = (jnp.bitwise_xor(places, me)[:, None] == places[None, :]).astype(jnp.bfloat16)
    taps = jnp.einsum("aj,jtc->tac", sorter, gathered, preferred_element_type=jnp.float32)
    taps = taps.astype(jnp.bfloat16).reshape(TAPS, 3 * HEADS_WIDTH)
    taps_f = taps.astype(jnp.float32)
    early = []
    for step in range(STEPS):
        term = jnp.zeros_like(conv_state[:, 0])
        for tap in range(TAPS - 1 - step):
            term = term + taps_f[tap][None] * conv_state[:, step + tap]
        early.append(term)
    early = jnp.stack(early, axis=1).reshape(ROWS, 3 * HEADS_WIDTH)

    my_rows = me * LOCAL + jnp.arange(LOCAL, dtype=jnp.int32)
    my_lengths = jnp.sum(
        jnp.where(slot_of[None, :] == my_rows[:, None], lengths[None, :], 0), axis=1
    )
    local_out = run_delta(
        old_slots, halves, my_lengths, keys, queries, values, early, taps, delta_state
    )

    placer = (offered[:, None] == jnp.arange(row_count * STEPS, dtype=jnp.int32)[None, :]).astype(
        jnp.bfloat16
    )
    if per_device % 2 == 0:
        pairs = per_device // 2
        sending = local_out.reshape(devices, pairs * ROWS, DK)
        got = lax.all_to_all(sending, "heads", split_axis=0, concat_axis=0, tiled=True)
        got = got.reshape(devices, pairs, ROWS, DK)
        got = jnp.concatenate([got[:, pair] for pair in range(pairs)], axis=-1)
        got = got.reshape(devices * ROWS, pairs * DK)
    else:
        units = local_out.reshape(UNITS // 2, ROWS, 2, HALF).transpose(0, 2, 1, 3)
        sending = units.reshape(devices, per_device * ROWS, HALF)
        got = lax.all_to_all(sending, "heads", split_axis=0, concat_axis=0, tiled=True)
        got = got.reshape(devices, per_device, ROWS, HALF).transpose(0, 2, 1, 3)
        got = got.reshape(devices * ROWS, per_device * HALF)
    outputs = jnp.dot(placer, got, preferred_element_type=jnp.float32).astype(jnp.bfloat16)
    return outputs.reshape(row_count, STEPS, per_device * HALF)


def solution(mesh):
    in_specs = (
        P("groups", None, None),
        P(("groups", "heads"), None),
        P(("groups", "heads"), None),
        P("groups", "heads"),
        P(("groups", "heads"), None, None, None),
        P(("groups", "heads"), None, None),
        P(),
        P(),
        P("groups"),
        P("groups"),
    )
    out_specs = P("groups", None, "heads")
    return jax.shard_map(
        on_device, mesh=mesh, in_specs=in_specs, out_specs=out_specs, check_vma=False
    )
```

```python
import functools

import jax
import jax.numpy as jnp
from jax import lax
from jax.experimental import pallas as pl
from jax.experimental.pallas import tpu as pltpu
from jax.sharding import PartitionSpec as P

D = 2304
H = 32
DK = 128
TAPS = 4
STEPS = 4
HALF = 64
UNITS = 64
LOCAL = 2
ROWS = LOCAL * STEPS
HEADS_WIDTH = H * DK
KEY_WIDTHS = (1024, 3072)
QUERY_WIDTHS = (4096,)
VALUE_WIDTHS = (3072, 1024)

norm_eps = 1e-06


def unit_tables(old_heads, new_units):
    positions = jnp.arange(H, dtype=jnp.int32)
    inverse = jnp.sum(
        jnp.where(old_heads[None, :] == positions[:, None], positions[None, :], 0), axis=1
    )
    heads_of = new_units // 2
    halves = new_units % 2
    old_slots = jnp.sum(
        jnp.where(heads_of[:, None] == positions[None, :], inverse[None, :], 0), axis=1
    )
    return (old_slots, halves)


def shift_rows(value, lag, row_step):
    if lag == 0:
        return value
    moved = pltpu.roll(value, lag, 0)
    return jnp.where(row_step >= lag, moved, 0.0)


def lane_sum(value):
    return jnp.sum(value, axis=-1, keepdims=True)


def unit_length(value):
    return value * lax.rsqrt(lane_sum(value * value) + norm_eps)


def activate(pieces, part, head, early_ref, taps_ref, row_step):
    begin = head * DK
    for kept_ref, sent_ref, width in pieces:
        if begin < width:
            break
        begin -= width
    inner = pl.ds(begin, DK)
    fresh = kept_ref[:ROWS, inner] + sent_ref[:, inner]
    columns = pl.ds(part * HEADS_WIDTH + head * DK, DK)
    total = early_ref[:, columns]
    for lag in range(TAPS):
        tap = taps_ref[TAPS - 1 - lag : TAPS - lag, columns].astype(jnp.float32)
        total = total + tap * shift_rows(fresh, lag, row_step)
    return total / (1.0 + jnp.exp(-total))


def paired(refs, widths):
    return [(refs[2 * i], refs[2 * i + 1], width) for i, width in enumerate(widths)]


def keys_kernel(*refs):
    key_refs = paired(refs, KEY_WIDTHS)
    query_refs = paired(refs[2 * len(KEY_WIDTHS) :], QUERY_WIDTHS)
    rest = refs[2 * len(KEY_WIDTHS + QUERY_WIDTHS) :]
    (early_ref, taps_ref, state_ref), outs = rest[:3], rest[3:]
    beta_ref, key_seen_ref, query_seen_ref, pulls_ref, weights_ref = outs
    row = lax.broadcasted_iota(jnp.int32, (ROWS, DK), 0)
    row_step = row % STEPS
    kept_ref, sent_ref, width = key_refs[0]
    gates = kept_ref[:ROWS, width : width + 2 * H] + sent_ref[:, width : width + 2 * H]
    for head in range(H):
        key = unit_length(activate(key_refs, 1, head, early_ref, taps_ref, row_step))
        query = unit_length(activate(query_refs, 0, head, early_ref, taps_ref, row_step))
        beta_logit = jnp.broadcast_to(gates[:, head : head + 1], (ROWS, DK))
        decay_logit = jnp.broadcast_to(gates[:, H + head : H + head + 1], (ROWS, DK))
        beta = 1.0 / (1.0 + jnp.exp(-beta_logit))
        decay = 1.0 / (1.0 + jnp.exp(decay_logit))
        fades = [jnp.ones_like(decay), decay]
        for lag in range(2, STEPS + 1):
            earlier = pltpu.roll(decay, lag - 1, 0)
            fades.append(jnp.where(row_step >= lag - 1, fades[-1] * earlier, fades[-1]))
        both = jnp.concatenate([key, query], axis=0)
        seen = [
            jnp.dot(both, state_ref[r, head], precision=lax.Precision.HIGHEST,
                    preferred_element_type=jnp.float32)
            for r in range(LOCAL)
        ]
        beta_ref[head] = beta
        key_seen_ref[head] = beta * fades[STEPS] * jnp.where(
            row < STEPS, seen[0][:ROWS], seen[1][:ROWS]
        )
        query_seen_ref[head] = fades[STEPS] * jnp.where(
            row < STEPS, seen[0][ROWS:], seen[1][ROWS:]
        )
        for lag in range(STEPS):
            moved_key = shift_rows(key, lag, row_step)
            if lag:
                pulls_ref[lag - 1, head] = beta * fades[lag] * lane_sum(key * moved_key)
            weights_ref[lag, head] = fades[lag] * lane_sum(query * moved_key)


def values_kernel(slots_ref, halves_ref, lengths_ref, *refs):
    value_refs = paired(refs, VALUE_WIDTHS)
    rest = refs[2 * len(VALUE_WIDTHS) :]
    early_ref, taps_ref, beta_ref, key_seen_ref, query_seen_ref, pulls_ref, weights_ref = rest[:7]
    out_ref, heads_ref = rest[7:]
    row = lax.broadcasted_iota(jnp.int32, (ROWS, DK), 0)
    row_step = row % STEPS
    lane = lax.broadcasted_iota(jnp.int32, (ROWS, DK), 1)
    row_length = jnp.where(row < STEPS, lengths_ref[0], lengths_ref[1])
    live = row_step < row_length
    for head in range(H):
        value = activate(value_refs, 2, head, early_ref, taps_ref, row_step)
        base = beta_ref[head] * value - key_seen_ref[head]
        solved = base
        for _ in range(STEPS - 1):
            following = base
            for lag in range(1, STEPS):
                following = following - pulls_ref[lag - 1, head] * shift_rows(
                    solved, lag, row_step
                )
            solved = following
        out = query_seen_ref[head]
        for lag in range(STEPS):
            out = out + weights_ref[lag, head] * shift_rows(solved, lag, row_step)
        heads_ref[head] = jnp.where(live, out, 0.0)
    for quad in range(UNITS // 4):
        joined = []
        for pair in (2 * quad, 2 * quad + 1):
            first = heads_ref[slots_ref[2 * pair]]
            second = heads_ref[slots_ref[2 * pair + 1]]
            first = jnp.where(halves_ref[2 * pair] == 0, first, pltpu.roll(first, HALF, 1))
            second = jnp.where(halves_ref[2 * pair + 1] == 0, pltpu.roll(second, HALF, 1), second)
            joined.append(jnp.where(lane < HALF, first, second))
        out_ref[quad] = jnp.concatenate(joined, axis=0).astype(jnp.bfloat16)


def run_delta(slots, halves, lengths, keys, queries, values, early, taps, state):
    smem = pl.BlockSpec(memory_space=pltpu.SMEM)
    vmem = pl.BlockSpec(memory_space=pltpu.VMEM)
    params = pltpu.CompilerParams(vmem_limit_bytes=32 * 1024 * 1024)
    per_head = jax.ShapeDtypeStruct((H, ROWS, DK), jnp.float32)
    lags = [
        jax.ShapeDtypeStruct((count, H, ROWS, DK), jnp.float32) for count in (STEPS - 1, STEPS)
    ]
    flat = lambda pieces: [ref for piece in pieces for ref in piece]
    prepared = pl.pallas_call(
        keys_kernel,
        out_shape=[per_head] * 3 + lags,
        in_specs=[vmem] * (2 * len(KEY_WIDTHS + QUERY_WIDTHS) + 3),
        out_specs=[vmem] * 5,
        compiler_params=params,
        cost_estimate=pl.CostEstimate(flops=40_000_000, bytes_accessed=9_000_000, transcendentals=0),
        name="keys_part",
    )(*flat(keys), *flat(queries), early, taps, state)
    return pl.pallas_call(
        values_kernel,
        out_shape=jax.ShapeDtypeStruct((UNITS // 4, 2 * ROWS, DK), jnp.bfloat16),
        in_specs=[smem] * 3 + [vmem] * (2 * len(VALUE_WIDTHS) + 7),
        out_specs=vmem,
        scratch_shapes=[pltpu.VMEM((H, ROWS, DK), jnp.float32)],
        compiler_params=params,
        cost_estimate=pl.CostEstimate(flops=4_000_000, bytes_accessed=2_000_000, transcendentals=0),
        name="values_part",
    )(slots, halves, lengths, *flat(values), early, taps, *prepared)


def swap(value, bit, devices):
    return lax.ppermute(value, "heads", [(i, i ^ bit) for i in range(devices)])


def on_device(
    tokens,
    qkv_weight,
    gate_weight,
    conv_weight,
    delta_state,
    conv_state,
    old_heads,
    new_units,
    slot_of,
    lengths,
):
    devices = lax.axis_size("heads")
    me = lax.axis_index("heads")
    per_device = UNITS // devices
    depth = qkv_weight.shape[0]
    row_count = tokens.shape[0]
    chips = devices // 2

    old_slots, halves = unit_tables(old_heads, new_units)
    bits = [1 << b for b in range(1, devices.bit_length() - 1)]
    order = []
    for place in range(chips):
        offset = 0
        for at, bit in enumerate(bits):
            if place & (chips >> (at + 1)):
                offset |= bit
        order.append(offset)
    holders = jnp.bitwise_xor(jnp.asarray(order, jnp.int32), me)
    old_rows = (holders[:, None] * LOCAL + jnp.arange(LOCAL, dtype=jnp.int32)[None, :]).reshape(-1)
    steps = jnp.arange(STEPS, dtype=jnp.int32)
    wanted = (old_rows[:, None] * STEPS + steps[None, :]).reshape(-1)
    offered = (slot_of[:, None] * STEPS + steps[None, :]).reshape(-1)
    picker = (wanted[:, None] == offered[None, :]).astype(jnp.bfloat16)

    def token_part(owner):
        columns = lax.dynamic_slice_in_dim(tokens, owner * depth, depth, 2)
        columns = columns.reshape(row_count * STEPS, depth)
        return jnp.dot(picker, columns, preferred_element_type=jnp.float32).astype(jnp.bfloat16)

    mine, theirs = token_part(me), token_part(jnp.bitwise_xor(me, 1))

    blocks, others = [], []
    weight = qkv_weight
    for part, widths in ((1, KEY_WIDTHS), (0, QUERY_WIDTHS), (2, VALUE_WIDTHS)):
        begin = part * HEADS_WIDTH
        for width in widths:
            block = weight[:, begin : begin + width]
            if not blocks:
                block = jnp.concatenate([block, gate_weight], axis=1)
            block, weight = lax.optimization_barrier((block, weight))
            blocks.append(block)
            others.append(swap(block, 1, devices))
            begin += width

    products = []
    for block, other in zip(blocks, others):
        total = jnp.dot(mine, block, preferred_element_type=jnp.float32)
        total = total + jnp.dot(theirs, other, preferred_element_type=jnp.float32)
        total, mine, theirs = lax.optimization_barrier((total, mine, theirs))
        products.append(total)
    first_tap, _ = lax.optimization_barrier((conv_weight, products[-1]))
    pieces = []
    for total in products:
        for bit in bits[:-1]:
            half = total.shape[0] // 2
            total = total[:half] + swap(total[half:], bit, devices)
        pieces.append((total, swap(total[ROWS:], bits[-1], devices)))
    keys, pieces = pieces[: len(KEY_WIDTHS)], pieces[len(KEY_WIDTHS) :]
    queries, values = pieces[: len(QUERY_WIDTHS)], pieces[len(QUERY_WIDTHS) :]

    gathered = first_tap[None]
    for b in range(devices.bit_length() - 1):
        gathered = jnp.concatenate([gathered, swap(gathered, 1 << b, devices)], axis=0)
    places = jnp.arange(devices, dtype=jnp.int32)
    sorter = (jnp.bitwise_xor(places, me)[:, None] == places[None, :]).astype(jnp.bfloat16)
    taps = jnp.einsum("aj,jtc->tac", sorter, gathered, preferred_element_type=jnp.float32)
    taps = taps.astype(jnp.bfloat16).reshape(TAPS, 3 * HEADS_WIDTH)
    taps_f = taps.astype(jnp.float32)
    early = []
    for step in range(STEPS):
        term = jnp.zeros_like(conv_state[:, 0])
        for tap in range(TAPS - 1 - step):
            term = term + taps_f[tap][None] * conv_state[:, step + tap]
        early.append(term)
    early = jnp.stack(early, axis=1).reshape(ROWS, 3 * HEADS_WIDTH)

    my_rows = me * LOCAL + jnp.arange(LOCAL, dtype=jnp.int32)
    my_lengths = jnp.sum(
        jnp.where(slot_of[None, :] == my_rows[:, None], lengths[None, :], 0), axis=1
    )
    local_out = run_delta(
        old_slots, halves, my_lengths, keys, queries, values, early, taps, delta_state
    )

    placer = (offered[:, None] == jnp.arange(row_count * STEPS, dtype=jnp.int32)[None, :]).astype(
        jnp.bfloat16
    )
    if per_device % 2 == 0:
        pairs = per_device // 2
        sending = local_out.reshape(devices, pairs * ROWS, DK)
        got = lax.all_to_all(sending, "heads", split_axis=0, concat_axis=0, tiled=True)
        got = got.reshape(devices, pairs, ROWS, DK)
        got = jnp.concatenate([got[:, pair] for pair in range(pairs)], axis=-1)
        got = got.reshape(devices * ROWS, pairs * DK)
    else:
        units = local_out.reshape(UNITS // 2, ROWS, 2, HALF).transpose(0, 2, 1, 3)
        sending = units.reshape(devices, per_device * ROWS, HALF)
        got = lax.all_to_all(sending, "heads", split_axis=0, concat_axis=0, tiled=True)
        got = got.reshape(devices, per_device, ROWS, HALF).transpose(0, 2, 1, 3)
        got = got.reshape(devices * ROWS, per_device * HALF)
    outputs = jnp.dot(placer, got, preferred_element_type=jnp.float32).astype(jnp.bfloat16)
    return outputs.reshape(row_count, STEPS, per_device * HALF)


def solution(mesh):
    in_specs = (
        P("groups", None, None),
        P(("groups", "heads"), None),
        P(("groups", "heads"), None),
        P("groups", "heads"),
        P(("groups", "heads"), None, None, None),
        P(("groups", "heads"), None, None),
        P(),
        P(),
        P("groups"),
        P("groups"),
    )
    out_specs = P("groups", None, "heads")
    return jax.shard_map(
        on_device, mesh=mesh, in_specs=in_specs, out_specs=out_specs, check_vma=False
    )
```

```python
import functools

import jax
import jax.numpy as jnp
from jax import lax
from jax.experimental import pallas as pl
from jax.experimental.pallas import tpu as pltpu
from jax.sharding import PartitionSpec as P

D = 2304
H = 32
DK = 128
TAPS = 4
STEPS = 4
HALF = 64
UNITS = 64
LOCAL = 2
ROWS = LOCAL * STEPS
HEADS_WIDTH = H * DK
QUERY_WIDTHS = (4096,)
KEY_WIDTHS = (4096,)
VALUE_WIDTHS = (3072, 1024)
FIRST_RANGES = (((0, 4096),),)
SECOND_RANGES = (((0, 4096), (8192, 64)), ((4096, 3072),), ((7168, 1024),))

norm_eps = 1e-06


def unit_tables(old_heads, new_units):
    positions = jnp.arange(H, dtype=jnp.int32)
    inverse = jnp.sum(
        jnp.where(old_heads[None, :] == positions[:, None], positions[None, :], 0), axis=1
    )
    heads_of = new_units // 2
    halves = new_units % 2
    old_slots = jnp.sum(
        jnp.where(heads_of[:, None] == positions[None, :], inverse[None, :], 0), axis=1
    )
    return (old_slots, halves)


def shift_rows(value, lag, row_step):
    if lag == 0:
        return value
    moved = pltpu.roll(value, lag, 0)
    return jnp.where(row_step >= lag, moved, 0.0)


def lane_sum(value):
    return jnp.sum(value, axis=-1, keepdims=True)


def unit_length(value):
    return value * lax.rsqrt(lane_sum(value * value) + norm_eps)


def activate(pieces, part, head, early_ref, taps_ref, row_step):
    begin = head * DK
    for kept_ref, sent_ref, width in pieces:
        if begin < width:
            break
        begin -= width
    inner = pl.ds(begin, DK)
    fresh = kept_ref[:ROWS, inner] + sent_ref[:, inner]
    columns = pl.ds(part * HEADS_WIDTH + head * DK, DK)
    total = early_ref[:, columns]
    for lag in range(TAPS):
        tap = taps_ref[TAPS - 1 - lag : TAPS - lag, columns].astype(jnp.float32)
        total = total + tap * shift_rows(fresh, lag, row_step)
    return total / (1.0 + jnp.exp(-total))


def paired(refs, widths):
    return [(refs[2 * i], refs[2 * i + 1], width) for i, width in enumerate(widths)]


def keys_kernel(*refs):
    key_refs = paired(refs, KEY_WIDTHS)
    query_refs = paired(refs[2 * len(KEY_WIDTHS) :], QUERY_WIDTHS)
    rest = refs[2 * len(KEY_WIDTHS + QUERY_WIDTHS) :]
    (early_ref, taps_ref, state_ref), outs = rest[:3], rest[3:]
    beta_ref, key_seen_ref, query_seen_ref, pulls_ref, weights_ref = outs
    row = lax.broadcasted_iota(jnp.int32, (ROWS, DK), 0)
    row_step = row % STEPS
    kept_ref, sent_ref, width = key_refs[0]
    gates = kept_ref[:ROWS, width : width + 2 * H] + sent_ref[:, width : width + 2 * H]
    for head in range(H):
        key = unit_length(activate(key_refs, 1, head, early_ref, taps_ref, row_step))
        query = unit_length(activate(query_refs, 0, head, early_ref, taps_ref, row_step))
        beta_logit = jnp.broadcast_to(gates[:, head : head + 1], (ROWS, DK))
        decay_logit = jnp.broadcast_to(gates[:, H + head : H + head + 1], (ROWS, DK))
        beta = 1.0 / (1.0 + jnp.exp(-beta_logit))
        decay = 1.0 / (1.0 + jnp.exp(decay_logit))
        fades = [jnp.ones_like(decay), decay]
        for lag in range(2, STEPS + 1):
            earlier = pltpu.roll(decay, lag - 1, 0)
            fades.append(jnp.where(row_step >= lag - 1, fades[-1] * earlier, fades[-1]))
        both = jnp.concatenate([key, query], axis=0)
        seen = [
            jnp.dot(both, state_ref[r, head], precision=lax.Precision.HIGHEST,
                    preferred_element_type=jnp.float32)
            for r in range(LOCAL)
        ]
        beta_ref[head] = beta
        key_seen_ref[head] = beta * fades[STEPS] * jnp.where(
            row < STEPS, seen[0][:ROWS], seen[1][:ROWS]
        )
        query_seen_ref[head] = fades[STEPS] * jnp.where(
            row < STEPS, seen[0][ROWS:], seen[1][ROWS:]
        )
        for lag in range(STEPS):
            moved_key = shift_rows(key, lag, row_step)
            if lag:
                pulls_ref[lag - 1, head] = beta * fades[lag] * lane_sum(key * moved_key)
            weights_ref[lag, head] = fades[lag] * lane_sum(query * moved_key)


def values_kernel(slots_ref, halves_ref, lengths_ref, *refs):
    value_refs = paired(refs, VALUE_WIDTHS)
    rest = refs[2 * len(VALUE_WIDTHS) :]
    early_ref, taps_ref, beta_ref, key_seen_ref, query_seen_ref, pulls_ref, weights_ref = rest[:7]
    out_ref, heads_ref = rest[7:]
    row = lax.broadcasted_iota(jnp.int32, (ROWS, DK), 0)
    row_step = row % STEPS
    lane = lax.broadcasted_iota(jnp.int32, (ROWS, DK), 1)
    row_length = jnp.where(row < STEPS, lengths_ref[0], lengths_ref[1])
    live = row_step < row_length
    for head in range(H):
        value = activate(value_refs, 2, head, early_ref, taps_ref, row_step)
        base = beta_ref[head] * value - key_seen_ref[head]
        solved = base
        for _ in range(STEPS - 1):
            following = base
            for lag in range(1, STEPS):
                following = following - pulls_ref[lag - 1, head] * shift_rows(
                    solved, lag, row_step
                )
            solved = following
        out = query_seen_ref[head]
        for lag in range(STEPS):
            out = out + weights_ref[lag, head] * shift_rows(solved, lag, row_step)
        heads_ref[head] = jnp.where(live, out, 0.0)
    for quad in range(UNITS // 4):
        joined = []
        for pair in (2 * quad, 2 * quad + 1):
            first = heads_ref[slots_ref[2 * pair]]
            second = heads_ref[slots_ref[2 * pair + 1]]
            first = jnp.where(halves_ref[2 * pair] == 0, first, pltpu.roll(first, HALF, 1))
            second = jnp.where(halves_ref[2 * pair + 1] == 0, pltpu.roll(second, HALF, 1), second)
            joined.append(jnp.where(lane < HALF, first, second))
        out_ref[quad] = jnp.concatenate(joined, axis=0).astype(jnp.bfloat16)


def run_delta(slots, halves, lengths, keys, queries, values, early, taps, state):
    smem = pl.BlockSpec(memory_space=pltpu.SMEM)
    vmem = pl.BlockSpec(memory_space=pltpu.VMEM)
    params = pltpu.CompilerParams(vmem_limit_bytes=32 * 1024 * 1024)
    per_head = jax.ShapeDtypeStruct((H, ROWS, DK), jnp.float32)
    lags = [
        jax.ShapeDtypeStruct((count, H, ROWS, DK), jnp.float32) for count in (STEPS - 1, STEPS)
    ]
    flat = lambda pieces: [ref for piece in pieces for ref in piece]
    prepared = pl.pallas_call(
        keys_kernel,
        out_shape=[per_head] * 3 + lags,
        in_specs=[vmem] * (2 * len(KEY_WIDTHS + QUERY_WIDTHS) + 3),
        out_specs=[vmem] * 5,
        compiler_params=params,
        cost_estimate=pl.CostEstimate(flops=0, bytes_accessed=0, transcendentals=0),
        name="keys_part",
    )(*flat(keys), *flat(queries), early, taps, state)
    return pl.pallas_call(
        values_kernel,
        out_shape=jax.ShapeDtypeStruct((UNITS // 4, 2 * ROWS, DK), jnp.bfloat16),
        in_specs=[smem] * 3 + [vmem] * (2 * len(VALUE_WIDTHS) + 7),
        out_specs=vmem,
        scratch_shapes=[pltpu.VMEM((H, ROWS, DK), jnp.float32)],
        compiler_params=params,
        cost_estimate=pl.CostEstimate(flops=4_000_000, bytes_accessed=2_000_000, transcendentals=0),
        name="values_part",
    )(slots, halves, lengths, *flat(values), early, taps, *prepared)


def product_kernel(ranges, mine_ref, theirs_ref, block_ref, other_ref, *out_refs):
    half = mine_ref.shape[0] // 2
    for at, parts in enumerate(ranges):
        place = 0
        for begin, width in parts:
            columns, target = pl.ds(begin, width), pl.ds(place, width)
            total = jnp.dot(
                mine_ref[...], block_ref[:, columns], preferred_element_type=jnp.float32
            )
            total = total + jnp.dot(
                theirs_ref[...], other_ref[:, columns], preferred_element_type=jnp.float32
            )
            out_refs[2 * at][:, target] = total[:half]
            out_refs[2 * at + 1][:, target] = total[half:]
            place += width


def run_product(mine, theirs, block, other, ranges):
    vmem = pl.BlockSpec(memory_space=pltpu.VMEM)
    half = mine.shape[0] // 2
    widths = [sum(width for _, width in parts) for parts in ranges]
    outs = pl.pallas_call(
        functools.partial(product_kernel, ranges),
        out_shape=[
            jax.ShapeDtypeStruct((half, width), jnp.float32) for width in widths for _ in range(2)
        ],
        in_specs=[vmem] * 4,
        out_specs=[vmem] * (2 * len(widths)),
        compiler_params=pltpu.CompilerParams(vmem_limit_bytes=32 * 1024 * 1024),
        cost_estimate=pl.CostEstimate(flops=0, bytes_accessed=0, transcendentals=0),
        name="partial_product",
    )(mine, theirs, block, other)
    return [(outs[2 * at], outs[2 * at + 1]) for at in range(len(widths))]


def swap(value, bit, devices):
    return lax.ppermute(value, "heads", [(i, i ^ bit) for i in range(devices)])


def on_device(
    tokens,
    qkv_weight,
    gate_weight,
    conv_weight,
    delta_state,
    conv_state,
    old_heads,
    new_units,
    slot_of,
    lengths,
):
    devices = lax.axis_size("heads")
    me = lax.axis_index("heads")
    per_device = UNITS // devices
    depth = qkv_weight.shape[0]
    row_count = tokens.shape[0]
    chips = devices // 2

    old_slots, halves = unit_tables(old_heads, new_units)
    bits = [1 << b for b in range(1, devices.bit_length() - 1)]
    order = []
    for place in range(chips):
        offset = 0
        for at, bit in enumerate(bits):
            if place & (chips >> (at + 1)):
                offset |= bit
        order.append(offset)
    holders = jnp.bitwise_xor(jnp.asarray(order, jnp.int32), me)
    old_rows = (holders[:, None] * LOCAL + jnp.arange(LOCAL, dtype=jnp.int32)[None, :]).reshape(-1)
    steps = jnp.arange(STEPS, dtype=jnp.int32)
    wanted = (old_rows[:, None] * STEPS + steps[None, :]).reshape(-1)
    offered = (slot_of[:, None] * STEPS + steps[None, :]).reshape(-1)
    picker = (wanted[:, None] == offered[None, :]).astype(jnp.bfloat16)

    def token_part(owner):
        columns = lax.dynamic_slice_in_dim(tokens, owner * depth, depth, 2)
        columns = columns.reshape(row_count * STEPS, depth)
        return jnp.dot(picker, columns, preferred_element_type=jnp.float32).astype(jnp.bfloat16)

    mine, theirs = token_part(me), token_part(jnp.bitwise_xor(me, 1))

    def widen(gathered, beside, bit):
        other, beside = lax.optimization_barrier((swap(gathered, bit, devices), beside))
        return jnp.concatenate([gathered, other], axis=0), beside

    tap_bits = [1 << b for b in range(devices.bit_length() - 1)]
    gathered = conv_weight[None]
    first = qkv_weight[:, :HEADS_WIDTH]
    first, weight = lax.optimization_barrier((first, qkv_weight))
    first_other = swap(first, 1, devices)
    for bit in tap_bits[:-3]:
        gathered, weight = widen(gathered, weight, bit)
    gathered, weight = widen(gathered, weight, tap_bits[-3])
    second = jnp.concatenate([weight[:, HEADS_WIDTH:], gate_weight], axis=1)
    second_other = swap(second, 1, devices)
    gathered, (mine, theirs) = widen(gathered, (mine, theirs), tap_bits[-2])

    products = run_product(mine, theirs, first, first_other, FIRST_RANGES)
    products, mine, theirs = lax.optimization_barrier((products, mine, theirs))
    more = run_product(mine, theirs, second, second_other, SECOND_RANGES)
    gathered, more = widen(gathered, more, tap_bits[-1])
    (kept, sent), more = lax.optimization_barrier((products[0], more))
    products = [(kept, products[0][1])] + more
    pieces = []
    done = [[] for _ in bits]
    for kept, sent in products:
        for level, bit in enumerate(bits):
            window = 2 if level == 0 else 1
            if len(done[level]) >= window:
                sent, _ = lax.optimization_barrier((sent, done[level][-window]))
            got = swap(sent, bit, devices)
            done[level].append(got)
            if bit != bits[-1]:
                added = kept + got
                half = added.shape[0] // 2
                kept, sent = added[:half], added[half:]
        pieces.append((kept, got))
    queries, keys, values = pieces[:1], pieces[1:2], pieces[2:]

    places = jnp.arange(devices, dtype=jnp.int32)
    sorter = (jnp.bitwise_xor(places, me)[:, None] == places[None, :]).astype(jnp.bfloat16)
    taps = jnp.einsum("aj,jtc->tac", sorter, gathered, preferred_element_type=jnp.float32)
    taps = taps.astype(jnp.bfloat16).reshape(TAPS, 3 * HEADS_WIDTH)
    taps_f = taps.astype(jnp.float32)
    early = []
    for step in range(STEPS):
        term = jnp.zeros_like(conv_state[:, 0])
        for tap in range(TAPS - 1 - step):
            term = term + taps_f[tap][None] * conv_state[:, step + tap]
        early.append(term)
    early = jnp.stack(early, axis=1).reshape(ROWS, 3 * HEADS_WIDTH)

    my_rows = me * LOCAL + jnp.arange(LOCAL, dtype=jnp.int32)
    my_lengths = jnp.sum(
        jnp.where(slot_of[None, :] == my_rows[:, None], lengths[None, :], 0), axis=1
    )
    local_out = run_delta(
        old_slots, halves, my_lengths, keys, queries, values, early, taps, delta_state
    )

    placer = (offered[:, None] == jnp.arange(row_count * STEPS, dtype=jnp.int32)[None, :]).astype(
        jnp.bfloat16
    )
    if per_device % 2 == 0:
        pairs = per_device // 2
        sending = local_out.reshape(devices, pairs * ROWS, DK)
        got = lax.all_to_all(sending, "heads", split_axis=0, concat_axis=0, tiled=True)
        got = got.reshape(devices, pairs, ROWS, DK)
        got = jnp.concatenate([got[:, pair] for pair in range(pairs)], axis=-1)
        got = got.reshape(devices * ROWS, pairs * DK)
    else:
        units = local_out.reshape(UNITS // 2, ROWS, 2, HALF).transpose(0, 2, 1, 3)
        sending = units.reshape(devices, per_device * ROWS, HALF)
        got = lax.all_to_all(sending, "heads", split_axis=0, concat_axis=0, tiled=True)
        got = got.reshape(devices, per_device, ROWS, HALF).transpose(0, 2, 1, 3)
        got = got.reshape(devices * ROWS, per_device * HALF)
    outputs = jnp.dot(placer, got, preferred_element_type=jnp.float32).astype(jnp.bfloat16)
    return outputs.reshape(row_count, STEPS, per_device * HALF)


def solution(mesh):
    in_specs = (
        P("groups", None, None),
        P(("groups", "heads"), None),
        P(("groups", "heads"), None),
        P("groups", "heads"),
        P(("groups", "heads"), None, None, None),
        P(("groups", "heads"), None, None),
        P(),
        P(),
        P("groups"),
        P("groups"),
    )
    out_specs = P("groups", None, "heads")
    return jax.shard_map(
        on_device, mesh=mesh, in_specs=in_specs, out_specs=out_specs, check_vma=False
    )
```

```python
import functools

import jax
import jax.numpy as jnp
from jax import lax
from jax.experimental import pallas as pl
from jax.experimental.pallas import tpu as pltpu
from jax.sharding import PartitionSpec as P

D = 2304
H = 32
DK = 128
TAPS = 4
STEPS = 4
HALF = 64
UNITS = 64
LOCAL = 2
ROWS = LOCAL * STEPS
HEADS_WIDTH = H * DK
LEVELS = 32767.0
SCALE_LANES = 128
EXPONENT_AT = 64
BLOCKS = HEADS_WIDTH // DK
STATE_COPIES = 4


norm_eps = 1e-06


def unit_tables(old_heads, new_units):
    positions = jnp.arange(H, dtype=jnp.int32)
    inverse = jnp.sum(
        jnp.where(old_heads[None, :] == positions[:, None], positions[None, :], 0), axis=1
    )
    heads_of = new_units // 2
    halves = new_units % 2
    old_slots = jnp.sum(
        jnp.where(heads_of[:, None] == positions[None, :], inverse[None, :], 0), axis=1
    )
    return (old_slots, halves)


def shift_rows(value, lag, row_step):
    if lag == 0:
        return value
    moved = pltpu.roll(value, lag, 0)
    return jnp.where(row_step >= lag, moved, 0.0)


def lane_sum(value):
    return jnp.sum(value, axis=-1, keepdims=True)


def unit_length(value):
    return value * lax.rsqrt(lane_sum(value * value) + norm_eps)


def pack_rows(total, packed_ref):
    rows, width = total.shape
    blocks = width // DK
    lane = lax.broadcasted_iota(jnp.int32, (rows, SCALE_LANES), 1)
    scales = jnp.zeros((rows, SCALE_LANES), jnp.float32)
    for block in range(blocks):
        part = total[:, block * DK : (block + 1) * DK]
        top = jnp.max(jnp.abs(part), axis=-1, keepdims=True) + 1e-30
        exponent = jnp.ceil(jnp.log2(top))
        mantissa = jnp.ceil(jnp.minimum(top * jnp.exp2(-exponent) * LEVELS, LEVELS))
        factor = LEVELS * LEVELS * jnp.exp2(-exponent) / mantissa
        coded = jnp.clip(jnp.floor(part * factor + 0.5), -LEVELS, LEVELS)
        packed_ref[:, block * DK : (block + 1) * DK] = coded.astype(jnp.int32).astype(jnp.int16)
        scales = jnp.where(lane == block, mantissa, scales)
        scales = jnp.where(lane == EXPONENT_AT + block, exponent, scales)
    packed_ref[:, width:] = scales.astype(jnp.int32).astype(jnp.int16)


def to_float(coded):
    return coded.astype(jnp.int32).astype(jnp.float32)


def steps_of(packed_ref):
    scales = to_float(packed_ref[:, packed_ref.shape[1] - SCALE_LANES :])
    exponents = pltpu.roll(scales, EXPONENT_AT, 1)
    return scales * jnp.exp2(exponents) * (1.0 / (LEVELS * LEVELS))


def unpack_block(packed_ref, steps, block):
    return to_float(packed_ref[:, block * DK : (block + 1) * DK]) * steps[:, block : block + 1]


def fold_rows(value):
    half = value.shape[1] // 2
    return jnp.concatenate([value[:, :half], value[:, half:]], axis=0)


def received(kept_ref, got_ref, steps, block):
    half = kept_ref.shape[1] // DK // 2
    rows = unpack_block(got_ref, steps, block % half)
    rows = rows[:ROWS] if block < half else rows[ROWS:]
    return kept_ref[:, block * DK : (block + 1) * DK] + rows


def activate(kept_ref, got_ref, steps, part, head, early_ref, taps_ref, row_step):
    fresh = received(kept_ref, got_ref, steps, head)
    columns = pl.ds(part * HEADS_WIDTH + head * DK, DK)
    total = early_ref[:, columns]
    for lag in range(TAPS):
        tap = taps_ref[TAPS - 1 - lag : TAPS - lag, columns].astype(jnp.float32)
        total = total + tap * shift_rows(fresh, lag, row_step)
    return total / (1.0 + jnp.exp(-total))


def keys_kernel(
    query_ref, query_got_ref, key_ref, key_got_ref, early_ref, taps_ref, state_hbm,
    beta_ref, key_seen_ref, query_seen_ref, pulls_ref, weights_ref, state_ref, sems,
):
    per_copy = H // STATE_COPIES
    copies = []
    for at in range(STATE_COPIES):
        some = pl.ds(at * per_copy, per_copy)
        copies.append(
            pltpu.make_async_copy(state_hbm.at[:, some], state_ref.at[:, some], sems.at[at])
        )
        copies[-1].start()
    row = lax.broadcasted_iota(jnp.int32, (ROWS, DK), 0)
    row_step = row % STEPS
    query_steps, key_steps = steps_of(query_got_ref), steps_of(key_got_ref)
    gates = received(key_ref, key_got_ref, key_steps, BLOCKS)
    for head in range(H):
        key = unit_length(
            activate(key_ref, key_got_ref, key_steps, 1, head, early_ref, taps_ref, row_step)
        )
        query = unit_length(
            activate(query_ref, query_got_ref, query_steps, 0, head, early_ref, taps_ref, row_step)
        )
        beta_logit = jnp.broadcast_to(gates[:, head : head + 1], (ROWS, DK))
        decay_logit = jnp.broadcast_to(gates[:, H + head : H + head + 1], (ROWS, DK))
        beta = 1.0 / (1.0 + jnp.exp(-beta_logit))
        decay = 1.0 / (1.0 + jnp.exp(decay_logit))
        fades = [jnp.ones_like(decay), decay]
        for lag in range(2, STEPS + 1):
            earlier = pltpu.roll(decay, lag - 1, 0)
            fades.append(jnp.where(row_step >= lag - 1, fades[-1] * earlier, fades[-1]))
        both = jnp.concatenate([key, query], axis=0)
        if head % per_copy == 0:
            copies[head // per_copy].wait()
        seen = [
            jnp.dot(both, state_ref[r, head], precision=lax.Precision.HIGHEST,
                    preferred_element_type=jnp.float32)
            for r in range(LOCAL)
        ]
        beta_ref[head] = beta
        key_seen_ref[head] = beta * fades[STEPS] * jnp.where(
            row < STEPS, seen[0][:ROWS], seen[1][:ROWS]
        )
        query_seen_ref[head] = fades[STEPS] * jnp.where(
            row < STEPS, seen[0][ROWS:], seen[1][ROWS:]
        )
        for lag in range(STEPS):
            moved_key = shift_rows(key, lag, row_step)
            if lag:
                pulls_ref[lag - 1, head] = beta * fades[lag] * lane_sum(key * moved_key)
            weights_ref[lag, head] = fades[lag] * lane_sum(query * moved_key)


def values_kernel(
    slots_ref, halves_ref, lengths_ref, value_ref, value_got_ref, early_ref, taps_ref,
    beta_ref, key_seen_ref, query_seen_ref, pulls_ref, weights_ref, out_ref, heads_ref,
):
    row = lax.broadcasted_iota(jnp.int32, (ROWS, DK), 0)
    row_step = row % STEPS
    lane = lax.broadcasted_iota(jnp.int32, (ROWS, DK), 1)
    row_length = jnp.where(row < STEPS, lengths_ref[0], lengths_ref[1])
    live = row_step < row_length
    value_steps = steps_of(value_got_ref)
    for head in range(H):
        value = activate(
            value_ref, value_got_ref, value_steps, 2, head, early_ref, taps_ref, row_step
        )
        base = beta_ref[head] * value - key_seen_ref[head]
        solved = base
        for _ in range(STEPS - 1):
            following = base
            for lag in range(1, STEPS):
                following = following - pulls_ref[lag - 1, head] * shift_rows(
                    solved, lag, row_step
                )
            solved = following
        out = query_seen_ref[head]
        for lag in range(STEPS):
            out = out + weights_ref[lag, head] * shift_rows(solved, lag, row_step)
        heads_ref[head] = jnp.where(live, out, 0.0)
    for quad in range(UNITS // 4):
        joined = []
        for pair in (2 * quad, 2 * quad + 1):
            first = heads_ref[slots_ref[2 * pair]]
            second = heads_ref[slots_ref[2 * pair + 1]]
            first = jnp.where(halves_ref[2 * pair] == 0, first, pltpu.roll(first, HALF, 1))
            second = jnp.where(halves_ref[2 * pair + 1] == 0, pltpu.roll(second, HALF, 1), second)
            joined.append(jnp.where(lane < HALF, first, second))
        out_ref[quad] = jnp.concatenate(joined, axis=0).astype(jnp.bfloat16)


def run_delta(slots, halves, lengths, queries, keys, values, early, taps, state):
    smem = pl.BlockSpec(memory_space=pltpu.SMEM)
    vmem = pl.BlockSpec(memory_space=pltpu.VMEM)
    params = pltpu.CompilerParams(vmem_limit_bytes=32 * 1024 * 1024)
    per_head = jax.ShapeDtypeStruct((H, ROWS, DK), jnp.float32)
    lags = [
        jax.ShapeDtypeStruct((count, H, ROWS, DK), jnp.float32) for count in (STEPS - 1, STEPS)
    ]
    prepared = pl.pallas_call(
        keys_kernel,
        out_shape=[per_head] * 3 + lags,
        in_specs=[vmem] * 6 + [pl.BlockSpec(memory_space=pl.ANY)],
        out_specs=[vmem] * 5,
        scratch_shapes=[
            pltpu.VMEM(state.shape, jnp.float32),
            pltpu.SemaphoreType.DMA((STATE_COPIES,)),
        ],
        compiler_params=params,
        cost_estimate=pl.CostEstimate(flops=40_000_000, bytes_accessed=9_000_000, transcendentals=0),
        name="keys_part",
    )(*queries, *keys, early, taps, state)
    return pl.pallas_call(
        values_kernel,
        out_shape=jax.ShapeDtypeStruct((UNITS // 4, 2 * ROWS, DK), jnp.bfloat16),
        in_specs=[smem] * 3 + [vmem] * 9,
        out_specs=vmem,
        scratch_shapes=[pltpu.VMEM((H, ROWS, DK), jnp.float32)],
        compiler_params=params,
        cost_estimate=pl.CostEstimate(flops=4_000_000, bytes_accessed=2_000_000, transcendentals=0),
        name="values_part",
    )(slots, halves, lengths, *values, early, taps, *prepared)


def product_kernel(mine_ref, theirs_ref, block_ref, other_ref, *refs):
    gate_refs, (kept_ref, packed_ref) = refs[:-2], refs[-2:]
    half = mine_ref.shape[0] // 2

    def product(own, other):
        total = jnp.dot(mine_ref[...], own, preferred_element_type=jnp.float32)
        return total + jnp.dot(theirs_ref[...], other, preferred_element_type=jnp.float32)

    total = product(block_ref[...], other_ref[...])
    if gate_refs:
        gates = product(gate_refs[0][...], gate_refs[1][...])
        zeros = jnp.zeros((gates.shape[0], 2 * DK - gates.shape[1]), jnp.float32)
        total = jnp.concatenate([total, gates, zeros], axis=1)
    kept_ref[...] = total[:half]
    pack_rows(total[half:], packed_ref)


def run_product(mine, theirs, weights, part, gates=()):
    vmem = pl.BlockSpec(memory_space=pltpu.VMEM)
    block = pl.BlockSpec((mine.shape[1], HEADS_WIDTH), lambda i: (0, part))
    half = mine.shape[0] // 2
    width = HEADS_WIDTH + len(gates) * DK
    return pl.pallas_call(
        product_kernel,
        grid=(1,),
        out_shape=[
            jax.ShapeDtypeStruct((half, width), jnp.float32),
            jax.ShapeDtypeStruct((half, width + SCALE_LANES), jnp.int16),
        ],
        in_specs=[vmem, vmem, block, block] + [vmem] * len(gates),
        out_specs=[vmem] * 2,
        compiler_params=pltpu.CompilerParams(vmem_limit_bytes=32 * 1024 * 1024),
        cost_estimate=pl.CostEstimate(flops=0, bytes_accessed=0, transcendentals=0),
        name="partial_product",
    )(mine, theirs, *weights, *gates)


def combine_kernel(kept_ref, got_ref, still_ref, packed_ref):
    half = still_ref.shape[0]
    steps = steps_of(got_ref)
    sent = []
    for block in range(kept_ref.shape[1] // DK):
        columns = pl.ds(block * DK, DK)
        total = kept_ref[:, columns] + unpack_block(got_ref, steps, block)
        still_ref[:, columns] = total[:half]
        sent.append(total[half:])
    sent = jnp.concatenate(sent, axis=1)
    pack_rows(fold_rows(sent) if half == ROWS else sent, packed_ref)


def run_combine(kept, got):
    vmem = pl.BlockSpec(memory_space=pltpu.VMEM)
    half, width = kept.shape[0] // 2, kept.shape[1]
    packed = (2 * ROWS, width // 2 + SCALE_LANES) if half == ROWS else (half, width + SCALE_LANES)
    return pl.pallas_call(
        combine_kernel,
        out_shape=[
            jax.ShapeDtypeStruct((half, width), jnp.float32),
            jax.ShapeDtypeStruct(packed, jnp.int16),
        ],
        in_specs=[vmem] * 2,
        out_specs=[vmem] * 2,
        compiler_params=pltpu.CompilerParams(vmem_limit_bytes=32 * 1024 * 1024),
        cost_estimate=pl.CostEstimate(flops=0, bytes_accessed=0, transcendentals=0),
        name="combine",
    )(kept, got)


def swap(value, bit, devices):
    return lax.ppermute(value, "heads", [(i, i ^ bit) for i in range(devices)])


def on_device(
    tokens,
    qkv_weight,
    gate_weight,
    conv_weight,
    delta_state,
    conv_state,
    old_heads,
    new_units,
    slot_of,
    lengths,
):
    devices = lax.axis_size("heads")
    me = lax.axis_index("heads")
    per_device = UNITS // devices
    depth = qkv_weight.shape[0]
    row_count = tokens.shape[0]
    chips = devices // 2

    old_slots, halves = unit_tables(old_heads, new_units)
    bits = [1 << b for b in range(1, devices.bit_length() - 1)]
    order = []
    for place in range(chips):
        offset = 0
        for at, bit in enumerate(bits):
            if place & (chips >> (at + 1)):
                offset |= bit
        order.append(offset)
    holders = jnp.bitwise_xor(jnp.asarray(order, jnp.int32), me)
    old_rows = (holders[:, None] * LOCAL + jnp.arange(LOCAL, dtype=jnp.int32)[None, :]).reshape(-1)
    steps = jnp.arange(STEPS, dtype=jnp.int32)
    wanted = (old_rows[:, None] * STEPS + steps[None, :]).reshape(-1)
    offered = (slot_of[:, None] * STEPS + steps[None, :]).reshape(-1)
    picker = (wanted[:, None] == offered[None, :]).astype(jnp.bfloat16)

    def token_part(owner):
        columns = lax.dynamic_slice_in_dim(tokens, owner * depth, depth, 2)
        columns = columns.reshape(row_count * STEPS, depth)
        return jnp.dot(picker, columns, preferred_element_type=jnp.float32).astype(jnp.bfloat16)

    mine, theirs = token_part(me), token_part(jnp.bitwise_xor(me, 1))

    weights = (qkv_weight, swap(qkv_weight, 1, devices))
    gates = (gate_weight, swap(gate_weight, 1, devices))

    def in_order(value, *earlier):
        return lax.optimization_barrier((value,) + earlier)[0]

    def widen(gathered, unit, count):
        others = [swap(gathered, unit * i, devices) for i in range(1, count)]
        return jnp.concatenate([gathered] + others, axis=0)

    near = widen(conv_weight[None], 1, 4)
    gathered = widen(near, 4, devices // 4)
    mine = in_order(mine, near)
    query = run_product(mine, theirs, weights, 0)
    query = (query[0], in_order(query[1], gathered))
    mine = in_order(mine, *query)
    key = run_product(mine, theirs, weights, 1, gates)
    mine = in_order(mine, *key)
    value = run_product(mine, theirs, weights, 2)

    chunks = [query, key, value]
    got = [swap(packed, bits[0], devices) for _, packed in chunks]
    got[0] = in_order(got[0], *value)
    for level, bit in enumerate(bits[1:]):
        for at in range(len(chunks)):
            arrived = in_order(got[at], *chunks[at - 1]) if at else got[at]
            chunks[at] = run_combine(chunks[at][0], arrived)
            got[at] = swap(chunks[at][1], bit, devices)
    queries, keys, values = [(kept, came) for (kept, _), came in zip(chunks, got)]

    places = jnp.arange(devices, dtype=jnp.int32)
    sorter = (jnp.bitwise_xor(places, me)[:, None] == places[None, :]).astype(jnp.bfloat16)
    taps = jnp.einsum("aj,jtc->tac", sorter, gathered, preferred_element_type=jnp.float32)
    taps = taps.astype(jnp.bfloat16).reshape(TAPS, 3 * HEADS_WIDTH)
    taps_f = taps.astype(jnp.float32)
    early = []
    for step in range(STEPS):
        term = jnp.zeros_like(conv_state[:, 0])
        for tap in range(TAPS - 1 - step):
            term = term + taps_f[tap][None] * conv_state[:, step + tap]
        early.append(term)
    early = jnp.stack(early, axis=1).reshape(ROWS, 3 * HEADS_WIDTH)

    my_rows = me * LOCAL + jnp.arange(LOCAL, dtype=jnp.int32)
    my_lengths = jnp.sum(
        jnp.where(slot_of[None, :] == my_rows[:, None], lengths[None, :], 0), axis=1
    )
    local_out = run_delta(
        old_slots, halves, my_lengths, queries, keys, values, early, taps, delta_state
    )

    placer = (offered[:, None] == jnp.arange(row_count * STEPS, dtype=jnp.int32)[None, :]).astype(
        jnp.bfloat16
    )
    if per_device % 2 == 0:
        pairs = per_device // 2
        sending = local_out.reshape(devices, pairs * ROWS, DK)
        got = lax.all_to_all(sending, "heads", split_axis=0, concat_axis=0, tiled=True)
        got = got.reshape(devices, pairs, ROWS, DK)
        got = jnp.concatenate([got[:, pair] for pair in range(pairs)], axis=-1)
        got = got.reshape(devices * ROWS, pairs * DK)
    else:
        units = local_out.reshape(UNITS // 2, ROWS, 2, HALF).transpose(0, 2, 1, 3)
        sending = units.reshape(devices, per_device * ROWS, HALF)
        got = lax.all_to_all(sending, "heads", split_axis=0, concat_axis=0, tiled=True)
        got = got.reshape(devices, per_device, ROWS, HALF).transpose(0, 2, 1, 3)
        got = got.reshape(devices * ROWS, per_device * HALF)
    outputs = jnp.dot(placer, got, preferred_element_type=jnp.float32).astype(jnp.bfloat16)
    return outputs.reshape(row_count, STEPS, per_device * HALF)


def solution(mesh):
    in_specs = (
        P("groups", None, None),
        P(("groups", "heads"), None),
        P(("groups", "heads"), None),
        P("groups", "heads"),
        P(("groups", "heads"), None, None, None),
        P(("groups", "heads"), None, None),
        P(),
        P(),
        P("groups"),
        P("groups"),
    )
    out_specs = P("groups", None, "heads")
    return jax.shard_map(
        on_device, mesh=mesh, in_specs=in_specs, out_specs=out_specs, check_vma=False
    )
```

```python
import functools

import jax
import jax.numpy as jnp
from jax import lax
from jax.experimental import pallas as pl
from jax.experimental.pallas import tpu as pltpu
from jax.sharding import PartitionSpec as P

D = 2304
H = 32
DK = 128
TAPS = 4
STEPS = 4
HALF = 64
UNITS = 64
LOCAL = 2
ROWS = LOCAL * STEPS
HEADS_WIDTH = H * DK
LEVELS = 32767.0
SCALE_LANES = 128
EXPONENT_AT = 64
BLOCKS = HEADS_WIDTH // DK
WEIGHT_COPIES = 2


norm_eps = 1e-06


def unit_tables(old_heads, new_units):
    positions = jnp.arange(H, dtype=jnp.int32)
    inverse = jnp.sum(
        jnp.where(old_heads[None, :] == positions[:, None], positions[None, :], 0), axis=1
    )
    heads_of = new_units // 2
    halves = new_units % 2
    old_slots = jnp.sum(
        jnp.where(heads_of[:, None] == positions[None, :], inverse[None, :], 0), axis=1
    )
    return (old_slots, halves)


def shift_rows(value, lag, row_step):
    if lag == 0:
        return value
    moved = pltpu.roll(value, lag, 0)
    return jnp.where(row_step >= lag, moved, 0.0)


def lane_sum(value):
    return jnp.sum(value, axis=-1, keepdims=True)


def unit_length(value):
    return value * lax.rsqrt(lane_sum(value * value) + norm_eps)


def pack_rows(total, packed_ref):
    rows, width = total.shape
    blocks = width // DK
    lane = lax.broadcasted_iota(jnp.int32, (rows, SCALE_LANES), 1)
    scales = jnp.zeros((rows, SCALE_LANES), jnp.float32)
    for block in range(blocks):
        part = total[:, block * DK : (block + 1) * DK]
        top = jnp.max(jnp.abs(part), axis=-1, keepdims=True) + 1e-30
        exponent = jnp.ceil(jnp.log2(top))
        mantissa = jnp.ceil(jnp.minimum(top * jnp.exp2(-exponent) * LEVELS, LEVELS))
        factor = LEVELS * LEVELS * jnp.exp2(-exponent) / mantissa
        coded = jnp.clip(jnp.floor(part * factor + 0.5), -LEVELS, LEVELS)
        packed_ref[:, block * DK : (block + 1) * DK] = coded.astype(jnp.int32).astype(jnp.int16)
        scales = jnp.where(lane == block, mantissa, scales)
        scales = jnp.where(lane == EXPONENT_AT + block, exponent, scales)
    packed_ref[:, width:] = scales.astype(jnp.int32).astype(jnp.int16)


def to_float(coded):
    return coded.astype(jnp.int32).astype(jnp.float32)


def steps_of(packed_ref):
    scales = to_float(packed_ref[:, packed_ref.shape[1] - SCALE_LANES :])
    exponents = pltpu.roll(scales, EXPONENT_AT, 1)
    return scales * jnp.exp2(exponents) * (1.0 / (LEVELS * LEVELS))


def unpack_block(packed_ref, steps, block):
    return to_float(packed_ref[:, block * DK : (block + 1) * DK]) * steps[:, block : block + 1]


def fold_rows(value):
    half = value.shape[1] // 2
    return jnp.concatenate([value[:, :half], value[:, half:]], axis=0)


def received(kept_ref, got_ref, steps, block):
    half = kept_ref.shape[1] // DK // 2
    rows = unpack_block(got_ref, steps, block % half)
    rows = rows[:ROWS] if block < half else rows[ROWS:]
    return kept_ref[:, block * DK : (block + 1) * DK] + rows


def activate(kept_ref, got_ref, steps, part, head, early_ref, taps_ref, row_step):
    fresh = received(kept_ref, got_ref, steps, head)
    columns = pl.ds(part * HEADS_WIDTH + head * DK, DK)
    total = early_ref[:, columns]
    for lag in range(TAPS):
        tap = taps_ref[TAPS - 1 - lag : TAPS - lag, columns].astype(jnp.float32)
        total = total + tap * shift_rows(fresh, lag, row_step)
    return total / (1.0 + jnp.exp(-total))


def state_kernel(state_ref, high_ref, low_ref):
    for r in range(LOCAL):
        for at in range(state_ref.shape[1]):
            value = state_ref[r, at]
            high = value.astype(jnp.bfloat16)
            high_ref[at, :, r * DK : (r + 1) * DK] = high
            low = (value - high.astype(jnp.float32)).astype(jnp.bfloat16)
            low_ref[at, :, r * DK : (r + 1) * DK] = low


def run_state(state):
    heads = H // 4
    out = jax.ShapeDtypeStruct((H, DK, LOCAL * DK), jnp.bfloat16)
    spec = pl.BlockSpec((heads, DK, LOCAL * DK), lambda i: (i, 0, 0))
    return pl.pallas_call(
        state_kernel,
        grid=(4,),
        out_shape=[out, out],
        in_specs=[pl.BlockSpec((LOCAL, heads, DK, DK), lambda i: (0, i, 0, 0))],
        out_specs=[spec, spec],
        compiler_params=pltpu.CompilerParams(vmem_limit_bytes=32 * 1024 * 1024),
        cost_estimate=pl.CostEstimate(flops=0, bytes_accessed=0, transcendentals=0),
        name="state_parts",
    )(state)


def keys_kernel(
    query_ref, query_got_ref, key_ref, key_got_ref, early_ref, taps_ref, high_ref, low_ref,
    beta_ref, key_seen_ref, query_seen_ref, pulls_ref, weights_ref,
):
    row = lax.broadcasted_iota(jnp.int32, (ROWS, DK), 0)
    row_step = row % STEPS
    query_steps, key_steps = steps_of(query_got_ref), steps_of(key_got_ref)
    gates = received(key_ref, key_got_ref, key_steps, BLOCKS)
    for head in range(H):
        key = unit_length(
            activate(key_ref, key_got_ref, key_steps, 1, head, early_ref, taps_ref, row_step)
        )
        query = unit_length(
            activate(query_ref, query_got_ref, query_steps, 0, head, early_ref, taps_ref, row_step)
        )
        beta_logit = jnp.broadcast_to(gates[:, head : head + 1], (ROWS, DK))
        decay_logit = jnp.broadcast_to(gates[:, H + head : H + head + 1], (ROWS, DK))
        beta = 1.0 / (1.0 + jnp.exp(-beta_logit))
        decay = 1.0 / (1.0 + jnp.exp(decay_logit))
        fades = [jnp.ones_like(decay), decay]
        for lag in range(2, STEPS + 1):
            earlier = pltpu.roll(decay, lag - 1, 0)
            fades.append(jnp.where(row_step >= lag - 1, fades[-1] * earlier, fades[-1]))
        both = jnp.concatenate([key, query], axis=0)
        both_high = both.astype(jnp.bfloat16)
        both_low = (both - both_high.astype(jnp.float32)).astype(jnp.bfloat16)
        stacked = jnp.concatenate([both_high, both_low], axis=0)
        main = jnp.dot(stacked, high_ref[head], preferred_element_type=jnp.float32)
        rest = jnp.dot(both_high, low_ref[head], preferred_element_type=jnp.float32)
        seen = main[: 2 * ROWS] + main[2 * ROWS :] + rest
        seen = [seen[:, r * DK : (r + 1) * DK] for r in range(LOCAL)]
        beta_ref[head] = beta
        key_seen_ref[head] = beta * fades[STEPS] * jnp.where(
            row < STEPS, seen[0][:ROWS], seen[1][:ROWS]
        )
        query_seen_ref[head] = fades[STEPS] * jnp.where(
            row < STEPS, seen[0][ROWS:], seen[1][ROWS:]
        )
        for lag in range(STEPS):
            moved_key = shift_rows(key, lag, row_step)
            if lag:
                pulls_ref[lag - 1, head] = beta * fades[lag] * lane_sum(key * moved_key)
            weights_ref[lag, head] = fades[lag] * lane_sum(query * moved_key)


def values_kernel(
    slots_ref, halves_ref, lengths_ref, value_ref, value_got_ref, early_ref, taps_ref,
    beta_ref, key_seen_ref, query_seen_ref, pulls_ref, weights_ref, out_ref, heads_ref,
):
    row = lax.broadcasted_iota(jnp.int32, (ROWS, DK), 0)
    row_step = row % STEPS
    lane = lax.broadcasted_iota(jnp.int32, (ROWS, DK), 1)
    row_length = jnp.where(row < STEPS, lengths_ref[0], lengths_ref[1])
    live = row_step < row_length
    value_steps = steps_of(value_got_ref)
    for head in range(H):
        value = activate(
            value_ref, value_got_ref, value_steps, 2, head, early_ref, taps_ref, row_step
        )
        base = beta_ref[head] * value - key_seen_ref[head]
        solved = base
        for _ in range(STEPS - 1):
            following = base
            for lag in range(1, STEPS):
                following = following - pulls_ref[lag - 1, head] * shift_rows(
                    solved, lag, row_step
                )
            solved = following
        out = query_seen_ref[head]
        for lag in range(STEPS):
            out = out + weights_ref[lag, head] * shift_rows(solved, lag, row_step)
        heads_ref[head] = jnp.where(live, out, 0.0)
    for quad in range(UNITS // 4):
        joined = []
        for pair in (2 * quad, 2 * quad + 1):
            first = heads_ref[slots_ref[2 * pair]]
            second = heads_ref[slots_ref[2 * pair + 1]]
            first = jnp.where(halves_ref[2 * pair] == 0, first, pltpu.roll(first, HALF, 1))
            second = jnp.where(halves_ref[2 * pair + 1] == 0, pltpu.roll(second, HALF, 1), second)
            joined.append(jnp.where(lane < HALF, first, second))
        out_ref[quad] = jnp.concatenate(joined, axis=0).astype(jnp.bfloat16)


def run_delta(slots, halves, lengths, queries, keys, values, early, taps, state):
    smem = pl.BlockSpec(memory_space=pltpu.SMEM)
    vmem = pl.BlockSpec(memory_space=pltpu.VMEM)
    params = pltpu.CompilerParams(vmem_limit_bytes=32 * 1024 * 1024)
    per_head = jax.ShapeDtypeStruct((H, ROWS, DK), jnp.float32)
    lags = [
        jax.ShapeDtypeStruct((count, H, ROWS, DK), jnp.float32) for count in (STEPS - 1, STEPS)
    ]
    prepared = pl.pallas_call(
        keys_kernel,
        out_shape=[per_head] * 3 + lags,
        in_specs=[vmem] * 8,
        out_specs=[vmem] * 5,
        compiler_params=params,
        cost_estimate=pl.CostEstimate(flops=40_000_000, bytes_accessed=9_000_000, transcendentals=0),
        name="keys_part",
    )(*queries, *keys, early, taps, *state)
    return pl.pallas_call(
        values_kernel,
        out_shape=jax.ShapeDtypeStruct((UNITS // 4, 2 * ROWS, DK), jnp.bfloat16),
        in_specs=[smem] * 3 + [vmem] * 9,
        out_specs=vmem,
        scratch_shapes=[pltpu.VMEM((H, ROWS, DK), jnp.float32)],
        compiler_params=params,
        cost_estimate=pl.CostEstimate(flops=4_000_000, bytes_accessed=2_000_000, transcendentals=0),
        name="values_part",
    )(slots, halves, lengths, *values, early, taps, *prepared)


def rows_kernel(
    depth, me_ref, slot_of_ref, tokens_hbm, mine_ref, theirs_ref, window_ref, sem
):
    me = me_ref[0]
    width = window_ref.shape[2]
    offset = me // 2 * (2 * depth)
    start = jnp.minimum(offset // DK * DK, D - width)
    columns = pl.ds(pl.multiple_of(start, DK), width)
    copy = pltpu.make_async_copy(tokens_hbm.at[:, :, columns], window_ref, sem)
    copy.start()
    shape = (mine_ref.shape[0], slot_of_ref.shape[1])
    row = lax.broadcasted_iota(jnp.int32, shape, 0)
    place = row // ROWS
    count = (shape[0] // ROWS).bit_length() - 1
    holder = jnp.zeros(shape, jnp.int32)
    for at in range(count):
        holder = holder + ((place >> (count - 1 - at)) & 1) * (2 << at)
    holder = jnp.bitwise_xor(holder, me)
    match = holder * LOCAL + row % ROWS // STEPS == slot_of_ref[...]
    copy.wait()
    window = window_ref[...].astype(jnp.float32)
    total = jnp.zeros((shape[0], width), jnp.float32)
    for step in range(STEPS):
        picker = jnp.where(match & (row % STEPS == step), 1.0, 0.0).astype(jnp.bfloat16)
        here = window[:, step, :].astype(jnp.bfloat16)
        total = total + jnp.dot(picker, here, preferred_element_type=jnp.float32)
    total = pltpu.roll(total, lax.rem(width - (offset - start), width), 1)
    low, high = total[:, :depth], total[:, depth : 2 * depth]
    first_core = me % 2 == 0
    mine_ref[...] = jnp.where(first_core, low, high).astype(jnp.bfloat16)
    theirs_ref[...] = jnp.where(first_core, high, low).astype(jnp.bfloat16)


def run_rows(me, slot_of, tokens, depth, chips):
    width = -(-(2 * depth + DK - 1) // DK) * DK
    out = jax.ShapeDtypeStruct((chips * ROWS, depth), jnp.bfloat16)
    vmem = pl.BlockSpec(memory_space=pltpu.VMEM)
    return pl.pallas_call(
        functools.partial(rows_kernel, depth),
        out_shape=[out, out],
        in_specs=[
            pl.BlockSpec(memory_space=pltpu.SMEM), vmem, pl.BlockSpec(memory_space=pltpu.HBM)
        ],
        out_specs=[vmem, vmem],
        scratch_shapes=[
            pltpu.VMEM((tokens.shape[0], STEPS, width), jnp.bfloat16),
            pltpu.SemaphoreType.DMA,
        ],
        compiler_params=pltpu.CompilerParams(vmem_limit_bytes=32 * 1024 * 1024),
        cost_estimate=pl.CostEstimate(flops=0, bytes_accessed=0, transcendentals=0),
        name="token_rows",
    )(me.reshape(1), slot_of.reshape(1, -1), tokens)


def product_kernel(part, mine_ref, theirs_ref, own_hbm, other_hbm, *refs):
    gate_refs, (kept_ref, packed_ref, own_ref, other_ref, sems) = refs[:-5], refs[-5:]
    half = mine_ref.shape[0] // 2
    step = HEADS_WIDTH // WEIGHT_COPIES
    copies = []
    for at in range(WEIGHT_COPIES):
        source, target = pl.ds(part * HEADS_WIDTH + at * step, step), pl.ds(at * step, step)
        pair = [
            pltpu.make_async_copy(hbm.at[:, source], ref.at[:, target], sems.at[side, at])
            for side, (hbm, ref) in enumerate(((own_hbm, own_ref), (other_hbm, other_ref)))
        ]
        for copy in pair:
            copy.start()
        copies.append(pair)

    def product(own, other):
        total = jnp.dot(mine_ref[...], own, preferred_element_type=jnp.float32)
        return total + jnp.dot(theirs_ref[...], other, preferred_element_type=jnp.float32)

    totals = []
    for at in range(WEIGHT_COPIES):
        for copy in copies[at]:
            copy.wait()
        columns = pl.ds(at * step, step)
        totals.append(product(own_ref[:, columns], other_ref[:, columns]))
    if gate_refs:
        gates = product(gate_refs[0][...], gate_refs[1][...])
        totals += [gates, jnp.zeros((gates.shape[0], 2 * DK - gates.shape[1]), jnp.float32)]
    total = jnp.concatenate(totals, axis=1)
    kept_ref[...] = total[:half]
    pack_rows(total[half:], packed_ref)


def run_product(mine, theirs, weights, part, gates=()):
    vmem, hbm = pl.BlockSpec(memory_space=pltpu.VMEM), pl.BlockSpec(memory_space=pltpu.HBM)
    half = mine.shape[0] // 2
    width = HEADS_WIDTH + len(gates) * DK
    return pl.pallas_call(
        functools.partial(product_kernel, part),
        out_shape=[
            jax.ShapeDtypeStruct((half, width), jnp.float32),
            jax.ShapeDtypeStruct((half, width + SCALE_LANES), jnp.int16),
        ],
        in_specs=[vmem, vmem, hbm, hbm] + [vmem] * len(gates),
        out_specs=[vmem] * 2,
        scratch_shapes=[pltpu.VMEM((mine.shape[1], HEADS_WIDTH), jnp.bfloat16)] * 2
        + [pltpu.SemaphoreType.DMA((2, WEIGHT_COPIES))],
        compiler_params=pltpu.CompilerParams(vmem_limit_bytes=32 * 1024 * 1024),
        cost_estimate=pl.CostEstimate(flops=0, bytes_accessed=0, transcendentals=0),
        name="partial_product",
    )(mine, theirs, *weights, *gates)


def combine_kernel(kept_ref, got_ref, still_ref, packed_ref):
    half = still_ref.shape[0]
    steps = steps_of(got_ref)
    sent = []
    for block in range(kept_ref.shape[1] // DK):
        columns = pl.ds(block * DK, DK)
        total = kept_ref[:, columns] + unpack_block(got_ref, steps, block)
        still_ref[:, columns] = total[:half]
        sent.append(total[half:])
    sent = jnp.concatenate(sent, axis=1)
    pack_rows(fold_rows(sent) if half == ROWS else sent, packed_ref)


def run_combine(kept, got):
    vmem = pl.BlockSpec(memory_space=pltpu.VMEM)
    half, width = kept.shape[0] // 2, kept.shape[1]
    packed = (2 * ROWS, width // 2 + SCALE_LANES) if half == ROWS else (half, width + SCALE_LANES)
    return pl.pallas_call(
        combine_kernel,
        out_shape=[
            jax.ShapeDtypeStruct((half, width), jnp.float32),
            jax.ShapeDtypeStruct(packed, jnp.int16),
        ],
        in_specs=[vmem] * 2,
        out_specs=[vmem] * 2,
        compiler_params=pltpu.CompilerParams(vmem_limit_bytes=32 * 1024 * 1024),
        cost_estimate=pl.CostEstimate(flops=0, bytes_accessed=0, transcendentals=0),
        name="combine",
    )(kept, got)


def swap(value, bit, devices):
    return lax.ppermute(value, "heads", [(i, i ^ bit) for i in range(devices)])


def on_device(
    tokens,
    qkv_weight,
    gate_weight,
    conv_weight,
    delta_state,
    conv_state,
    old_heads,
    new_units,
    slot_of,
    lengths,
):
    devices = lax.axis_size("heads")
    me = lax.axis_index("heads")
    per_device = UNITS // devices
    depth = qkv_weight.shape[0]
    row_count = tokens.shape[0]
    chips = devices // 2

    old_slots, halves = unit_tables(old_heads, new_units)
    bits = [1 << b for b in range(1, devices.bit_length() - 1)]
    steps = jnp.arange(STEPS, dtype=jnp.int32)
    offered = (slot_of[:, None] * STEPS + steps[None, :]).reshape(-1)

    mine, theirs = run_rows(me, slot_of, tokens, depth, chips)

    weights = (qkv_weight, swap(qkv_weight, 1, devices))
    gates = (gate_weight, swap(gate_weight, 1, devices))

    def in_order(value, *earlier):
        return lax.optimization_barrier((value,) + earlier)[0]

    query = run_product(mine, theirs, weights, 0)
    mine = in_order(mine, *query)
    key = run_product(mine, theirs, weights, 1, gates)
    mine = in_order(mine, *key)
    value = run_product(mine, theirs, weights, 2)

    state = run_state(in_order(delta_state, *value))
    taps = in_order(lax.all_gather(conv_weight, "heads", axis=0), *state)
    taps = taps.transpose(1, 0, 2).reshape(TAPS, 3 * HEADS_WIDTH)
    taps_f = taps.astype(jnp.float32)
    early = []
    for step in range(STEPS):
        term = jnp.zeros_like(conv_state[:, 0])
        for tap in range(TAPS - 1 - step):
            term = term + taps_f[tap][None] * conv_state[:, step + tap]
        early.append(term)
    early = jnp.stack(early, axis=1).reshape(ROWS, 3 * HEADS_WIDTH)

    chunks = [query, key, value]
    got = [swap(packed, bits[0], devices) for _, packed in chunks]
    got[0] = in_order(got[0], *value, *state)
    got[1] = in_order(got[1], early)
    for level, bit in enumerate(bits[1:]):
        for at in range(len(chunks)):
            arrived = in_order(got[at], *chunks[at - 1]) if at else got[at]
            chunks[at] = run_combine(chunks[at][0], arrived)
            got[at] = swap(chunks[at][1], bit, devices)
    queries, keys, values = [(kept, came) for (kept, _), came in zip(chunks, got)]

    my_rows = me * LOCAL + jnp.arange(LOCAL, dtype=jnp.int32)
    my_lengths = jnp.sum(
        jnp.where(slot_of[None, :] == my_rows[:, None], lengths[None, :], 0), axis=1
    )
    local_out = run_delta(
        old_slots, halves, my_lengths, queries, keys, values, early, taps, state
    )

    placer = (offered[:, None] == jnp.arange(row_count * STEPS, dtype=jnp.int32)[None, :]).astype(
        jnp.bfloat16
    )
    if per_device % 2 == 0:
        pairs = per_device // 2
        sending = local_out.reshape(devices, pairs * ROWS, DK)
        got = lax.all_to_all(sending, "heads", split_axis=0, concat_axis=0, tiled=True)
        got = got.reshape(devices, pairs, ROWS, DK)
        got = jnp.concatenate([got[:, pair] for pair in range(pairs)], axis=-1)
        got = got.reshape(devices * ROWS, pairs * DK)
    else:
        units = local_out.reshape(UNITS // 2, ROWS, 2, HALF).transpose(0, 2, 1, 3)
        sending = units.reshape(devices, per_device * ROWS, HALF)
        got = lax.all_to_all(sending, "heads", split_axis=0, concat_axis=0, tiled=True)
        got = got.reshape(devices, per_device, ROWS, HALF).transpose(0, 2, 1, 3)
        got = got.reshape(devices * ROWS, per_device * HALF)
    outputs = jnp.dot(placer, got, preferred_element_type=jnp.float32).astype(jnp.bfloat16)
    return outputs.reshape(row_count, STEPS, per_device * HALF)


def solution(mesh):
    in_specs = (
        P("groups", None, None),
        P(("groups", "heads"), None),
        P(("groups", "heads"), None),
        P("groups", "heads"),
        P(("groups", "heads"), None, None, None),
        P(("groups", "heads"), None, None),
        P(),
        P(),
        P("groups"),
        P("groups"),
    )
    out_specs = P("groups", None, "heads")
    return jax.shard_map(
        on_device, mesh=mesh, in_specs=in_specs, out_specs=out_specs, check_vma=False
    )
```

```python
import functools

import jax
import jax.numpy as jnp
from jax import lax
from jax.experimental import pallas as pl
from jax.experimental.pallas import tpu as pltpu
from jax.sharding import PartitionSpec as P

D = 2304
H = 32
DK = 128
TAPS = 4
STEPS = 4
HALF = 64
UNITS = 64
LOCAL = 2
ROWS = LOCAL * STEPS
HEADS_WIDTH = H * DK
LEVELS = 32767.0
SCALE_LANES = 128
EXPONENT_AT = 64
BLOCKS = HEADS_WIDTH // DK
TAP_WIDTH = 384
TAP_BLOCKS = 3 * HEADS_WIDTH // TAP_WIDTH


norm_eps = 1e-06


def unit_tables(old_heads, new_units):
    positions = jnp.arange(H, dtype=jnp.int32)
    inverse = jnp.sum(
        jnp.where(old_heads[None, :] == positions[:, None], positions[None, :], 0), axis=1
    )
    heads_of = new_units // 2
    halves = new_units % 2
    old_slots = jnp.sum(
        jnp.where(heads_of[:, None] == positions[None, :], inverse[None, :], 0), axis=1
    )
    return (old_slots, halves)


def shift_rows(value, lag, row_step):
    if lag == 0:
        return value
    moved = pltpu.roll(value, lag, 0)
    return jnp.where(row_step >= lag, moved, 0.0)


def lane_sum(value):
    return jnp.sum(value, axis=-1, keepdims=True)


def unit_length(value):
    return value * lax.rsqrt(lane_sum(value * value) + norm_eps)


def pack_rows(total, packed_ref):
    rows, width = total.shape
    blocks = width // DK
    lane = lax.broadcasted_iota(jnp.int32, (rows, SCALE_LANES), 1)
    scales = jnp.zeros((rows, SCALE_LANES), jnp.float32)
    for block in range(blocks):
        part = total[:, block * DK : (block + 1) * DK]
        top = jnp.max(jnp.abs(part), axis=-1, keepdims=True) + 1e-30
        exponent = jnp.ceil(jnp.log2(top))
        mantissa = jnp.ceil(jnp.minimum(top * jnp.exp2(-exponent) * LEVELS, LEVELS))
        factor = LEVELS * LEVELS * jnp.exp2(-exponent) / mantissa
        coded = jnp.clip(jnp.floor(part * factor + 0.5), -LEVELS, LEVELS)
        packed_ref[:, block * DK : (block + 1) * DK] = coded.astype(jnp.int32).astype(jnp.int16)
        scales = jnp.where(lane == block, mantissa, scales)
        scales = jnp.where(lane == EXPONENT_AT + block, exponent, scales)
    packed_ref[:, width:] = scales.astype(jnp.int32).astype(jnp.int16)


def to_float(coded):
    return coded.astype(jnp.int32).astype(jnp.float32)


def steps_of(packed_ref):
    scales = to_float(packed_ref[:, packed_ref.shape[1] - SCALE_LANES :])
    exponents = pltpu.roll(scales, EXPONENT_AT, 1)
    return scales * jnp.exp2(exponents) * (1.0 / (LEVELS * LEVELS))


def unpack_block(packed_ref, steps, block):
    return to_float(packed_ref[:, block * DK : (block + 1) * DK]) * steps[:, block : block + 1]


def fold_rows(value):
    half = value.shape[1] // 2
    return jnp.concatenate([value[:, :half], value[:, half:]], axis=0)


def received(kept_ref, got_ref, steps, block):
    half = kept_ref.shape[1] // DK // 2
    rows = unpack_block(got_ref, steps, block % half)
    rows = rows[:ROWS] if block < half else rows[ROWS:]
    return kept_ref[:, block * DK : (block + 1) * DK] + rows


def activate(kept_ref, got_ref, steps, part, head, history_ref, taps_ref, twist, row_step):
    fresh = received(kept_ref, got_ref, steps, head)
    column = part * HEADS_WIDTH + head * DK
    carried = history_ref[:, column : column + DK]
    taps = taps_ref[jnp.bitwise_xor(column // TAP_WIDTH, twist)]
    inner = column % TAP_WIDTH
    total = taps[TAPS - 1 :, inner : inner + DK] * fresh
    for lag in range(1, TAPS):
        source = jnp.where(row_step >= STEPS - lag, carried, fresh)
        tap = taps[TAPS - 1 - lag : TAPS - lag, inner : inner + DK]
        total = total + tap * pltpu.roll(source, lag, 0)
    return total / (1.0 + jnp.exp(-total))


def state_kernel(state_ref, high_ref, low_ref):
    for r in range(LOCAL):
        for at in range(state_ref.shape[1]):
            value = state_ref[r, at]
            high = value.astype(jnp.bfloat16)
            high_ref[at, :, r * DK : (r + 1) * DK] = high
            low = (value - high.astype(jnp.float32)).astype(jnp.bfloat16)
            low_ref[at, :, r * DK : (r + 1) * DK] = low


def run_state(state):
    heads = H // 4
    out = jax.ShapeDtypeStruct((H, DK, LOCAL * DK), jnp.bfloat16)
    spec = pl.BlockSpec((heads, DK, LOCAL * DK), lambda i: (i, 0, 0))
    return pl.pallas_call(
        state_kernel,
        grid=(4,),
        out_shape=[out, out],
        in_specs=[pl.BlockSpec((LOCAL, heads, DK, DK), lambda i: (0, i, 0, 0))],
        out_specs=[spec, spec],
        compiler_params=pltpu.CompilerParams(vmem_limit_bytes=16 * 1024 * 1024),
        cost_estimate=pl.CostEstimate(flops=0, bytes_accessed=0, transcendentals=0),
        name="state_parts",
    )(state)


def keys_kernel(
    twist_ref, query_ref, query_got_ref, key_ref, key_got_ref, history_ref, near_ref, far_ref,
    high_ref, low_ref, beta_ref, key_seen_ref, query_seen_ref, pulls_ref, weights_ref, taps_ref,
):
    twist = twist_ref[0]
    half = TAP_BLOCKS // 2
    for at in range(TAP_BLOCKS):
        source = near_ref if at < half else far_ref
        if at % 4 == 0:
            some = source[at % half * TAPS : (at % half + 4) * TAPS, :].astype(jnp.float32)
        taps_ref[at] = some[at % 4 * TAPS : (at % 4 + 1) * TAPS]
    row = lax.broadcasted_iota(jnp.int32, (ROWS, DK), 0)
    row_step = row % STEPS
    query_steps, key_steps = steps_of(query_got_ref), steps_of(key_got_ref)
    gates = received(key_ref, key_got_ref, key_steps, BLOCKS)
    for head in range(H):
        key = unit_length(
            activate(
                key_ref, key_got_ref, key_steps, 1, head, history_ref, taps_ref, twist, row_step
            )
        )
        query = unit_length(
            activate(
                query_ref, query_got_ref, query_steps, 0, head, history_ref, taps_ref, twist,
                row_step,
            )
        )
        beta_logit = jnp.broadcast_to(gates[:, head : head + 1], (ROWS, DK))
        decay_logit = jnp.broadcast_to(gates[:, H + head : H + head + 1], (ROWS, DK))
        beta = 1.0 / (1.0 + jnp.exp(-beta_logit))
        decay = 1.0 / (1.0 + jnp.exp(decay_logit))
        fades = [jnp.ones_like(decay), decay]
        for lag in range(2, STEPS + 1):
            earlier = pltpu.roll(decay, lag - 1, 0)
            fades.append(jnp.where(row_step >= lag - 1, fades[-1] * earlier, fades[-1]))
        both = jnp.concatenate([key, query], axis=0)
        both_high = both.astype(jnp.bfloat16)
        both_low = (both - both_high.astype(jnp.float32)).astype(jnp.bfloat16)
        stacked = jnp.concatenate([both_high, both_low], axis=0)
        main = jnp.dot(stacked, high_ref[head], preferred_element_type=jnp.float32)
        rest = jnp.dot(both_high, low_ref[head], preferred_element_type=jnp.float32)
        seen = main[: 2 * ROWS] + main[2 * ROWS :] + rest
        seen = [seen[:, r * DK : (r + 1) * DK] for r in range(LOCAL)]
        beta_ref[head] = beta
        key_seen_ref[head] = beta * fades[STEPS] * jnp.where(
            row < STEPS, seen[0][:ROWS], seen[1][:ROWS]
        )
        query_seen_ref[head] = fades[STEPS] * jnp.where(
            row < STEPS, seen[0][ROWS:], seen[1][ROWS:]
        )
        for lag in range(STEPS):
            moved_key = shift_rows(key, lag, row_step)
            if lag:
                pulls_ref[lag - 1, head] = beta * fades[lag] * lane_sum(key * moved_key)
            weights_ref[lag, head] = fades[lag] * lane_sum(query * moved_key)


def values_kernel(
    slots_ref, halves_ref, lengths_ref, twist_ref, value_ref, value_got_ref, history_ref,
    beta_ref, key_seen_ref, query_seen_ref, pulls_ref, weights_ref, taps_ref, out_ref, heads_ref,
):
    twist = twist_ref[0]
    row = lax.broadcasted_iota(jnp.int32, (ROWS, DK), 0)
    row_step = row % STEPS
    lane = lax.broadcasted_iota(jnp.int32, (ROWS, DK), 1)
    row_length = jnp.where(row < STEPS, lengths_ref[0], lengths_ref[1])
    live = row_step < row_length
    value_steps = steps_of(value_got_ref)
    for head in range(H):
        value = activate(
            value_ref, value_got_ref, value_steps, 2, head, history_ref, taps_ref, twist, row_step
        )
        base = beta_ref[head] * value - key_seen_ref[head]
        solved = base
        for _ in range(STEPS - 1):
            following = base
            for lag in range(1, STEPS):
                following = following - pulls_ref[lag - 1, head] * shift_rows(
                    solved, lag, row_step
                )
            solved = following
        out = query_seen_ref[head]
        for lag in range(STEPS):
            out = out + weights_ref[lag, head] * shift_rows(solved, lag, row_step)
        heads_ref[head] = jnp.where(live, out, 0.0)
    for quad in range(UNITS // 4):
        joined = []
        for pair in (2 * quad, 2 * quad + 1):
            first = heads_ref[slots_ref[2 * pair]]
            second = heads_ref[slots_ref[2 * pair + 1]]
            first = jnp.where(halves_ref[2 * pair] == 0, first, pltpu.roll(first, HALF, 1))
            second = jnp.where(halves_ref[2 * pair + 1] == 0, pltpu.roll(second, HALF, 1), second)
            joined.append(jnp.where(lane < HALF, first, second))
        out_ref[quad] = jnp.concatenate(joined, axis=0).astype(jnp.bfloat16)


def run_delta(slots, halves, lengths, queries, keys, values, history, twist, taps, state):
    smem = pl.BlockSpec(memory_space=pltpu.SMEM)
    vmem = pl.BlockSpec(memory_space=pltpu.VMEM)
    params = pltpu.CompilerParams(vmem_limit_bytes=16 * 1024 * 1024)
    per_head = jax.ShapeDtypeStruct((H, ROWS, DK), jnp.float32)
    lags = [
        jax.ShapeDtypeStruct((count, H, ROWS, DK), jnp.float32) for count in (STEPS - 1, STEPS)
    ]
    tap_blocks = jax.ShapeDtypeStruct((TAP_BLOCKS, TAPS, TAP_WIDTH), jnp.float32)
    prepared = pl.pallas_call(
        keys_kernel,
        out_shape=[per_head] * 3 + lags + [tap_blocks],
        in_specs=[smem] + [vmem] * 9,
        out_specs=[vmem] * 6,
        compiler_params=params,
        cost_estimate=pl.CostEstimate(flops=40_000_000, bytes_accessed=9_000_000, transcendentals=0),
        name="keys_part",
    )(twist, *queries, *keys, history, *taps, *state)
    return pl.pallas_call(
        values_kernel,
        out_shape=jax.ShapeDtypeStruct((UNITS // 4, 2 * ROWS, DK), jnp.bfloat16),
        in_specs=[smem] * 4 + [vmem] * 9,
        out_specs=vmem,
        scratch_shapes=[pltpu.VMEM((H, ROWS, DK), jnp.float32)],
        compiler_params=params,
        cost_estimate=pl.CostEstimate(flops=4_000_000, bytes_accessed=2_000_000, transcendentals=0),
        name="values_part",
    )(slots, halves, lengths, twist, *values, history, *prepared)


def rows_kernel(
    depth, me_ref, slot_of_ref, tokens_hbm, mine_ref, theirs_ref, window_ref, sem
):
    me = me_ref[0]
    width = window_ref.shape[2]
    offset = me // 2 * (2 * depth)
    start = jnp.minimum(offset // DK * DK, D - width)
    columns = pl.ds(pl.multiple_of(start, DK), width)
    copy = pltpu.make_async_copy(tokens_hbm.at[:, :, columns], window_ref, sem)
    copy.start()
    shape = (mine_ref.shape[0], slot_of_ref.shape[1])
    row = lax.broadcasted_iota(jnp.int32, shape, 0)
    place = row // ROWS
    count = (shape[0] // ROWS).bit_length() - 1
    holder = jnp.zeros(shape, jnp.int32)
    for at in range(count):
        holder = holder + ((place >> (count - 1 - at)) & 1) * (2 << at)
    holder = jnp.bitwise_xor(holder, me)
    match = holder * LOCAL + row % ROWS // STEPS == slot_of_ref[...]
    copy.wait()
    window = window_ref[...].astype(jnp.float32)
    total = jnp.zeros((shape[0], width), jnp.float32)
    for step in range(STEPS):
        picker = jnp.where(match & (row % STEPS == step), 1.0, 0.0).astype(jnp.bfloat16)
        here = window[:, step, :].astype(jnp.bfloat16)
        total = total + jnp.dot(picker, here, preferred_element_type=jnp.float32)
    total = pltpu.roll(total, lax.rem(width - (offset - start), width), 1)
    low, high = total[:, :depth], total[:, depth : 2 * depth]
    first_core = me % 2 == 0
    mine_ref[...] = jnp.where(first_core, low, high).astype(jnp.bfloat16)
    theirs_ref[...] = jnp.where(first_core, high, low).astype(jnp.bfloat16)


def run_rows(me, slot_of, tokens, depth, chips):
    width = -(-(2 * depth + DK - 1) // DK) * DK
    out = jax.ShapeDtypeStruct((chips * ROWS, depth), jnp.bfloat16)
    vmem = pl.BlockSpec(memory_space=pltpu.VMEM)
    return pl.pallas_call(
        functools.partial(rows_kernel, depth),
        out_shape=[out, out],
        in_specs=[
            pl.BlockSpec(memory_space=pltpu.SMEM), vmem, pl.BlockSpec(memory_space=pltpu.HBM)
        ],
        out_specs=[vmem, vmem],
        scratch_shapes=[
            pltpu.VMEM((tokens.shape[0], STEPS, width), jnp.bfloat16),
            pltpu.SemaphoreType.DMA,
        ],
        compiler_params=pltpu.CompilerParams(vmem_limit_bytes=16 * 1024 * 1024),
        cost_estimate=pl.CostEstimate(flops=0, bytes_accessed=0, transcendentals=0),
        name="token_rows",
    )(me.reshape(1), slot_of.reshape(1, -1), tokens)


def product_kernel(mine_ref, theirs_ref, block_ref, other_ref, *refs):
    gate_refs, (kept_ref, packed_ref) = refs[:-2], refs[-2:]
    half = mine_ref.shape[0] // 2

    def product(own, other):
        total = jnp.dot(mine_ref[...], own, preferred_element_type=jnp.float32)
        return total + jnp.dot(theirs_ref[...], other, preferred_element_type=jnp.float32)

    total = product(block_ref[...], other_ref[...])
    if gate_refs:
        gates = product(gate_refs[0][...], gate_refs[1][...])
        zeros = jnp.zeros((gates.shape[0], 2 * DK - gates.shape[1]), jnp.float32)
        total = jnp.concatenate([total, gates, zeros], axis=1)
    kept_ref[...] = total[:half]
    pack_rows(total[half:], packed_ref)


def run_product(mine, theirs, weights, part, gates=()):
    vmem = pl.BlockSpec(memory_space=pltpu.VMEM)
    block = pl.BlockSpec((mine.shape[1], HEADS_WIDTH), lambda i: (0, part))
    half = mine.shape[0] // 2
    width = HEADS_WIDTH + len(gates) * DK
    return pl.pallas_call(
        product_kernel,
        grid=(1,),
        out_shape=[
            jax.ShapeDtypeStruct((half, width), jnp.float32),
            jax.ShapeDtypeStruct((half, width + SCALE_LANES), jnp.int16),
        ],
        in_specs=[vmem, vmem, block, block] + [vmem] * len(gates),
        out_specs=[vmem] * 2,
        compiler_params=pltpu.CompilerParams(vmem_limit_bytes=16 * 1024 * 1024),
        cost_estimate=pl.CostEstimate(flops=0, bytes_accessed=0, transcendentals=0),
        name="partial_product",
    )(mine, theirs, *weights, *gates)


def combine_kernel(kept_ref, got_ref, still_ref, packed_ref):
    half = still_ref.shape[0]
    steps = steps_of(got_ref)
    sent = []
    for block in range(kept_ref.shape[1] // DK):
        columns = pl.ds(block * DK, DK)
        total = kept_ref[:, columns] + unpack_block(got_ref, steps, block)
        still_ref[:, columns] = total[:half]
        sent.append(total[half:])
    sent = jnp.concatenate(sent, axis=1)
    pack_rows(fold_rows(sent) if half == ROWS else sent, packed_ref)


def run_combine(kept, got):
    vmem = pl.BlockSpec(memory_space=pltpu.VMEM)
    half, width = kept.shape[0] // 2, kept.shape[1]
    packed = (2 * ROWS, width // 2 + SCALE_LANES) if half == ROWS else (half, width + SCALE_LANES)
    return pl.pallas_call(
        combine_kernel,
        out_shape=[
            jax.ShapeDtypeStruct((half, width), jnp.float32),
            jax.ShapeDtypeStruct(packed, jnp.int16),
        ],
        in_specs=[vmem] * 2,
        out_specs=[vmem] * 2,
        compiler_params=pltpu.CompilerParams(vmem_limit_bytes=16 * 1024 * 1024),
        cost_estimate=pl.CostEstimate(flops=0, bytes_accessed=0, transcendentals=0),
        name="combine",
    )(kept, got)


def swap(value, bit, devices):
    return lax.ppermute(value, "heads", [(i, i ^ bit) for i in range(devices)])


def on_device(
    tokens,
    qkv_weight,
    gate_weight,
    conv_weight,
    delta_state,
    conv_state,
    old_heads,
    new_units,
    slot_of,
    lengths,
):
    devices = lax.axis_size("heads")
    me = lax.axis_index("heads")
    per_device = UNITS // devices
    depth = qkv_weight.shape[0]
    row_count = tokens.shape[0]
    chips = devices // 2

    old_slots, halves = unit_tables(old_heads, new_units)
    bits = [1 << b for b in range(1, devices.bit_length() - 1)]
    steps = jnp.arange(STEPS, dtype=jnp.int32)
    offered = (slot_of[:, None] * STEPS + steps[None, :]).reshape(-1)

    mine, theirs = run_rows(me, slot_of, tokens, depth, chips)

    weights = (qkv_weight, swap(qkv_weight, 1, devices))
    gates = (gate_weight, swap(gate_weight, 1, devices))

    def in_order(value, *earlier):
        return lax.optimization_barrier((value,) + earlier)[0]

    ride = conv_weight.shape[1] == 2 * TAP_WIDTH and len(bits) == 3
    taps = conv_weight
    if ride:
        taps = jnp.concatenate([taps, swap(taps, 1, devices)], axis=1)
    else:
        taps = lax.all_gather(taps, "heads", axis=1, tiled=True)
    blocks = range(0, taps.shape[1], TAP_WIDTH)
    taps = jnp.concatenate([taps[:, at : at + TAP_WIDTH] for at in blocks], axis=0)
    mine = in_order(mine, taps)
    query = run_product(mine, theirs, weights, 0)
    mine = in_order(mine, *query)
    key = run_product(mine, theirs, weights, 1, gates)
    mine = in_order(mine, *key)
    value = run_product(mine, theirs, weights, 2)

    state = run_state(in_order(delta_state, *value))
    history = jnp.pad(in_order(conv_state, *value)[::-1], ((0, 0), (1, 0), (0, 0)))
    history = history.reshape(ROWS, 3 * HEADS_WIDTH)

    chunks = [query, key, value]
    got = [swap(packed, bits[0], devices) for _, packed in chunks]
    got[0] = in_order(got[0], *value, *state, history)
    far = swap(taps, bits[0], devices) if ride else taps
    for level, bit in enumerate(bits[1:]):
        for at in range(len(chunks)):
            arrived = in_order(got[at], *chunks[at - 1]) if at else got[at]
            if ride and level == 0 and at != 1:
                arrived, far = lax.optimization_barrier((arrived, far))
                taps = jnp.concatenate([taps, far], axis=0)
                far = swap(taps, bits[1 + at // 2], devices)
            chunks[at] = run_combine(chunks[at][0], arrived)
            got[at] = swap(chunks[at][1], bit, devices)
    queries, keys, values = [(kept, came) for (kept, _), came in zip(chunks, got)]
    if ride:
        twist, taps = (2 * me).reshape(1), (taps, far)
    else:
        half = TAP_BLOCKS // 2 * TAPS
        twist, taps = jnp.zeros(1, jnp.int32), (taps[:half], taps[half:])

    my_rows = me * LOCAL + jnp.arange(LOCAL, dtype=jnp.int32)
    my_lengths = jnp.sum(
        jnp.where(slot_of[None, :] == my_rows[:, None], lengths[None, :], 0), axis=1
    )
    local_out = run_delta(
        old_slots, halves, my_lengths, queries, keys, values, history, twist, taps, state
    )

    placer = (offered[:, None] == jnp.arange(row_count * STEPS, dtype=jnp.int32)[None, :]).astype(
        jnp.bfloat16
    )
    if per_device % 2 == 0:
        pairs = per_device // 2
        sending = local_out.reshape(devices, pairs * ROWS, DK)
        got = lax.all_to_all(sending, "heads", split_axis=0, concat_axis=0, tiled=True)
        got = got.reshape(devices, pairs, ROWS, DK)
        got = jnp.concatenate([got[:, pair] for pair in range(pairs)], axis=-1)
        got = got.reshape(devices * ROWS, pairs * DK)
    else:
        units = local_out.reshape(UNITS // 2, ROWS, 2, HALF).transpose(0, 2, 1, 3)
        sending = units.reshape(devices, per_device * ROWS, HALF)
        got = lax.all_to_all(sending, "heads", split_axis=0, concat_axis=0, tiled=True)
        got = got.reshape(devices, per_device, ROWS, HALF).transpose(0, 2, 1, 3)
        got = got.reshape(devices * ROWS, per_device * HALF)
    outputs = jnp.dot(placer, got, preferred_element_type=jnp.float32).astype(jnp.bfloat16)
    return outputs.reshape(row_count, STEPS, per_device * HALF)


def solution(mesh):
    in_specs = (
        P("groups", None, None),
        P(("groups", "heads"), None),
        P(("groups", "heads"), None),
        P("groups", "heads"),
        P(("groups", "heads"), None, None, None),
        P(("groups", "heads"), None, None),
        P(),
        P(),
        P("groups"),
        P("groups"),
    )
    out_specs = P("groups", None, "heads")
    return jax.shard_map(
        on_device, mesh=mesh, in_specs=in_specs, out_specs=out_specs, check_vma=False
    )
```

```python
import functools

import jax
import jax.numpy as jnp
from jax import lax
from jax.experimental import pallas as pl
from jax.experimental.pallas import tpu as pltpu
from jax.sharding import PartitionSpec as P

D = 2304
H = 32
DK = 128
TAPS = 4
STEPS = 4
HALF = 64
UNITS = 64
LOCAL = 2
ROWS = LOCAL * STEPS
HEADS_WIDTH = H * DK
LEVELS = 32767.0
SCALE_LANES = 128
EXPONENT_AT = 64
BLOCKS = HEADS_WIDTH // DK
STATE_COPIES = 4
TAP_WIDTH = 384
TAP_BLOCKS = 3 * HEADS_WIDTH // TAP_WIDTH


norm_eps = 1e-06


def unit_tables(old_heads, new_units):
    positions = jnp.arange(H, dtype=jnp.int32)
    inverse = jnp.sum(
        jnp.where(old_heads[None, :] == positions[:, None], positions[None, :], 0), axis=1
    )
    heads_of = new_units // 2
    halves = new_units % 2
    old_slots = jnp.sum(
        jnp.where(heads_of[:, None] == positions[None, :], inverse[None, :], 0), axis=1
    )
    return (old_slots, halves)


def shift_rows(value, lag, row_step):
    if lag == 0:
        return value
    moved = pltpu.roll(value, lag, 0)
    return jnp.where(row_step >= lag, moved, 0.0)


def lane_sum(value):
    return jnp.sum(value, axis=-1, keepdims=True)


def unit_length(value):
    return value * lax.rsqrt(lane_sum(value * value) + norm_eps)


def pack_rows(total, packed_ref):
    rows, width = total.shape
    blocks = width // DK
    lane = lax.broadcasted_iota(jnp.int32, (rows, SCALE_LANES), 1)
    scales = jnp.zeros((rows, SCALE_LANES), jnp.float32)
    for block in range(blocks):
        part = total[:, block * DK : (block + 1) * DK]
        top = jnp.max(jnp.abs(part), axis=-1, keepdims=True) + 1e-30
        exponent = jnp.ceil(jnp.log2(top))
        mantissa = jnp.ceil(jnp.minimum(top * jnp.exp2(-exponent) * LEVELS, LEVELS))
        factor = LEVELS * LEVELS * jnp.exp2(-exponent) / mantissa
        coded = jnp.clip(jnp.floor(part * factor + 0.5), -LEVELS, LEVELS)
        packed_ref[:, block * DK : (block + 1) * DK] = coded.astype(jnp.int32).astype(jnp.int16)
        scales = jnp.where(lane == block, mantissa, scales)
        scales = jnp.where(lane == EXPONENT_AT + block, exponent, scales)
    packed_ref[:, width:] = scales.astype(jnp.int32).astype(jnp.int16)


def to_float(coded):
    return coded.astype(jnp.int32).astype(jnp.float32)


def steps_of(packed_ref):
    scales = to_float(packed_ref[:, packed_ref.shape[1] - SCALE_LANES :])
    exponents = pltpu.roll(scales, EXPONENT_AT, 1)
    return scales * jnp.exp2(exponents) * (1.0 / (LEVELS * LEVELS))


def unpack_block(packed_ref, steps, block):
    return to_float(packed_ref[:, block * DK : (block + 1) * DK]) * steps[:, block : block + 1]


def fold_rows(value):
    half = value.shape[1] // 2
    return jnp.concatenate([value[:, :half], value[:, half:]], axis=0)


def received(kept_ref, got_ref, steps, block):
    half = kept_ref.shape[1] // DK // 2
    rows = unpack_block(got_ref, steps, block % half)
    rows = rows[:ROWS] if block < half else rows[ROWS:]
    return kept_ref[:, block * DK : (block + 1) * DK] + rows


def activate(kept_ref, got_ref, steps, part, head, history_ref, taps_ref, twist, row_step):
    fresh = received(kept_ref, got_ref, steps, head)
    column = part * HEADS_WIDTH + head * DK
    carried = history_ref[:, column : column + DK]
    taps = taps_ref[jnp.bitwise_xor(column // TAP_WIDTH, twist)]
    inner = column % TAP_WIDTH
    total = taps[TAPS - 1 :, inner : inner + DK] * fresh
    for lag in range(1, TAPS):
        source = jnp.where(row_step >= STEPS - lag, carried, fresh)
        tap = taps[TAPS - 1 - lag : TAPS - lag, inner : inner + DK]
        total = total + tap * pltpu.roll(source, lag, 0)
    return total / (1.0 + jnp.exp(-total))


def keys_kernel(
    twist_ref, query_ref, query_got_ref, key_ref, key_got_ref, history_ref, near_ref, far_ref,
    state_hbm, beta_ref, key_seen_ref, query_seen_ref, pulls_ref, weights_ref, taps_ref,
    state_ref, sems,
):
    per_copy = H // STATE_COPIES
    copies = []
    for at in range(STATE_COPIES):
        some = pl.ds(at * per_copy, per_copy)
        copies.append(
            pltpu.make_async_copy(state_hbm.at[:, some], state_ref.at[:, some], sems.at[at])
        )
        copies[-1].start()
    twist = twist_ref[0]
    half = TAP_BLOCKS // 2
    for at in range(TAP_BLOCKS):
        source = near_ref if at < half else far_ref
        if at % 4 == 0:
            some = source[at % half * TAPS : (at % half + 4) * TAPS, :].astype(jnp.float32)
        taps_ref[at] = some[at % 4 * TAPS : (at % 4 + 1) * TAPS]
    row = lax.broadcasted_iota(jnp.int32, (ROWS, DK), 0)
    row_step = row % STEPS
    query_steps, key_steps = steps_of(query_got_ref), steps_of(key_got_ref)
    gates = received(key_ref, key_got_ref, key_steps, BLOCKS)
    for head in range(H):
        key = unit_length(
            activate(
                key_ref, key_got_ref, key_steps, 1, head, history_ref, taps_ref, twist, row_step
            )
        )
        query = unit_length(
            activate(
                query_ref, query_got_ref, query_steps, 0, head, history_ref, taps_ref, twist,
                row_step,
            )
        )
        beta_logit = jnp.broadcast_to(gates[:, head : head + 1], (ROWS, DK))
        decay_logit = jnp.broadcast_to(gates[:, H + head : H + head + 1], (ROWS, DK))
        beta = 1.0 / (1.0 + jnp.exp(-beta_logit))
        decay = 1.0 / (1.0 + jnp.exp(decay_logit))
        fades = [jnp.ones_like(decay), decay]
        for lag in range(2, STEPS + 1):
            earlier = pltpu.roll(decay, lag - 1, 0)
            fades.append(jnp.where(row_step >= lag - 1, fades[-1] * earlier, fades[-1]))
        both = jnp.concatenate([key, query], axis=0)
        if head % per_copy == 0:
            copies[head // per_copy].wait()
        both_high = both.astype(jnp.bfloat16)
        both_low = (both - both_high.astype(jnp.float32)).astype(jnp.bfloat16)
        stacked = jnp.concatenate([both_high, both_low], axis=0)
        seen = []
        for r in range(LOCAL):
            state = state_ref[r, head]
            high = state.astype(jnp.bfloat16)
            low = (state - high.astype(jnp.float32)).astype(jnp.bfloat16)
            main = jnp.dot(stacked, high, preferred_element_type=jnp.float32)
            rest = jnp.dot(both_high, low, preferred_element_type=jnp.float32)
            seen.append(main[: 2 * ROWS] + main[2 * ROWS :] + rest)
        beta_ref[head] = beta
        key_seen_ref[head] = beta * fades[STEPS] * jnp.where(
            row < STEPS, seen[0][:ROWS], seen[1][:ROWS]
        )
        query_seen_ref[head] = fades[STEPS] * jnp.where(
            row < STEPS, seen[0][ROWS:], seen[1][ROWS:]
        )
        for lag in range(STEPS):
            moved_key = shift_rows(key, lag, row_step)
            if lag:
                pulls_ref[lag - 1, head] = beta * fades[lag] * lane_sum(key * moved_key)
            weights_ref[lag, head] = fades[lag] * lane_sum(query * moved_key)


def values_kernel(
    slots_ref, halves_ref, lengths_ref, twist_ref, value_ref, value_got_ref, history_ref,
    beta_ref, key_seen_ref, query_seen_ref, pulls_ref, weights_ref, taps_ref, out_ref, heads_ref,
):
    twist = twist_ref[0]
    row = lax.broadcasted_iota(jnp.int32, (ROWS, DK), 0)
    row_step = row % STEPS
    lane = lax.broadcasted_iota(jnp.int32, (ROWS, DK), 1)
    row_length = jnp.where(row < STEPS, lengths_ref[0], lengths_ref[1])
    live = row_step < row_length
    value_steps = steps_of(value_got_ref)
    for head in range(H):
        value = activate(
            value_ref, value_got_ref, value_steps, 2, head, history_ref, taps_ref, twist, row_step
        )
        base = beta_ref[head] * value - key_seen_ref[head]
        solved = base
        for _ in range(STEPS - 1):
            following = base
            for lag in range(1, STEPS):
                following = following - pulls_ref[lag - 1, head] * shift_rows(
                    solved, lag, row_step
                )
            solved = following
        out = query_seen_ref[head]
        for lag in range(STEPS):
            out = out + weights_ref[lag, head] * shift_rows(solved, lag, row_step)
        heads_ref[head] = jnp.where(live, out, 0.0)
    for quad in range(UNITS // 4):
        joined = []
        for pair in (2 * quad, 2 * quad + 1):
            first = heads_ref[slots_ref[2 * pair]]
            second = heads_ref[slots_ref[2 * pair + 1]]
            first = jnp.where(halves_ref[2 * pair] == 0, first, pltpu.roll(first, HALF, 1))
            second = jnp.where(halves_ref[2 * pair + 1] == 0, pltpu.roll(second, HALF, 1), second)
            joined.append(jnp.where(lane < HALF, first, second))
        out_ref[quad] = jnp.concatenate(joined, axis=0).astype(jnp.bfloat16)


def run_delta(slots, halves, lengths, queries, keys, values, history, twist, taps, state):
    smem = pl.BlockSpec(memory_space=pltpu.SMEM)
    vmem = pl.BlockSpec(memory_space=pltpu.VMEM)
    params = pltpu.CompilerParams(vmem_limit_bytes=32 * 1024 * 1024)
    per_head = jax.ShapeDtypeStruct((H, ROWS, DK), jnp.float32)
    lags = [
        jax.ShapeDtypeStruct((count, H, ROWS, DK), jnp.float32) for count in (STEPS - 1, STEPS)
    ]
    tap_blocks = jax.ShapeDtypeStruct((TAP_BLOCKS, TAPS, TAP_WIDTH), jnp.float32)
    prepared = pl.pallas_call(
        keys_kernel,
        out_shape=[per_head] * 3 + lags + [tap_blocks],
        in_specs=[smem] + [vmem] * 7 + [pl.BlockSpec(memory_space=pl.ANY)],
        out_specs=[vmem] * 6,
        scratch_shapes=[
            pltpu.VMEM(state.shape, jnp.float32),
            pltpu.SemaphoreType.DMA((STATE_COPIES,)),
        ],
        compiler_params=params,
        cost_estimate=pl.CostEstimate(flops=40_000_000, bytes_accessed=9_000_000, transcendentals=0),
        name="keys_part",
    )(twist, *queries, *keys, history, *taps, state)
    return pl.pallas_call(
        values_kernel,
        out_shape=jax.ShapeDtypeStruct((UNITS // 4, 2 * ROWS, DK), jnp.bfloat16),
        in_specs=[smem] * 4 + [vmem] * 9,
        out_specs=vmem,
        scratch_shapes=[pltpu.VMEM((H, ROWS, DK), jnp.float32)],
        compiler_params=params,
        cost_estimate=pl.CostEstimate(flops=4_000_000, bytes_accessed=2_000_000, transcendentals=0),
        name="values_part",
    )(slots, halves, lengths, twist, *values, history, *prepared)


def rows_kernel(
    depth, me_ref, slot_of_ref, tokens_hbm, mine_ref, theirs_ref, window_ref, sem
):
    me = me_ref[0]
    width = window_ref.shape[2]
    offset = me // 2 * (2 * depth)
    start = jnp.minimum(offset // DK * DK, D - width)
    columns = pl.ds(pl.multiple_of(start, DK), width)
    copy = pltpu.make_async_copy(tokens_hbm.at[:, :, columns], window_ref, sem)
    copy.start()
    shape = (mine_ref.shape[0], slot_of_ref.shape[1])
    row = lax.broadcasted_iota(jnp.int32, shape, 0)
    place = row // ROWS
    count = (shape[0] // ROWS).bit_length() - 1
    holder = jnp.zeros(shape, jnp.int32)
    for at in range(count):
        holder = holder + ((place >> (count - 1 - at)) & 1) * (2 << at)
    holder = jnp.bitwise_xor(holder, me)
    match = holder * LOCAL + row % ROWS // STEPS == slot_of_ref[...]
    copy.wait()
    window = window_ref[...].astype(jnp.float32)
    total = jnp.zeros((shape[0], width), jnp.float32)
    for step in range(STEPS):
        picker = jnp.where(match & (row % STEPS == step), 1.0, 0.0).astype(jnp.bfloat16)
        here = window[:, step, :].astype(jnp.bfloat16)
        total = total + jnp.dot(picker, here, preferred_element_type=jnp.float32)
    total = pltpu.roll(total, lax.rem(width - (offset - start), width), 1)
    low, high = total[:, :depth], total[:, depth : 2 * depth]
    first_core = me % 2 == 0
    mine_ref[...] = jnp.where(first_core, low, high).astype(jnp.bfloat16)
    theirs_ref[...] = jnp.where(first_core, high, low).astype(jnp.bfloat16)


def run_rows(me, slot_of, tokens, depth, chips):
    width = -(-(2 * depth + DK - 1) // DK) * DK
    out = jax.ShapeDtypeStruct((chips * ROWS, depth), jnp.bfloat16)
    vmem = pl.BlockSpec(memory_space=pltpu.VMEM)
    return pl.pallas_call(
        functools.partial(rows_kernel, depth),
        out_shape=[out, out],
        in_specs=[
            pl.BlockSpec(memory_space=pltpu.SMEM), vmem, pl.BlockSpec(memory_space=pltpu.HBM)
        ],
        out_specs=[vmem, vmem],
        scratch_shapes=[
            pltpu.VMEM((tokens.shape[0], STEPS, width), jnp.bfloat16),
            pltpu.SemaphoreType.DMA,
        ],
        compiler_params=pltpu.CompilerParams(vmem_limit_bytes=32 * 1024 * 1024),
        cost_estimate=pl.CostEstimate(flops=0, bytes_accessed=0, transcendentals=0),
        name="token_rows",
    )(me.reshape(1), slot_of.reshape(1, -1), tokens)


def product_kernel(mine_ref, theirs_ref, block_ref, other_ref, *refs):
    gate_refs, (kept_ref, packed_ref) = refs[:-2], refs[-2:]
    half = mine_ref.shape[0] // 2

    def product(own, other):
        total = jnp.dot(mine_ref[...], own, preferred_element_type=jnp.float32)
        return total + jnp.dot(theirs_ref[...], other, preferred_element_type=jnp.float32)

    total = product(block_ref[...], other_ref[...])
    if gate_refs:
        gates = product(gate_refs[0][...], gate_refs[1][...])
        zeros = jnp.zeros((gates.shape[0], 2 * DK - gates.shape[1]), jnp.float32)
        total = jnp.concatenate([total, gates, zeros], axis=1)
    kept_ref[...] = total[:half]
    pack_rows(total[half:], packed_ref)


def run_product(mine, theirs, weights, part, gates=()):
    vmem = pl.BlockSpec(memory_space=pltpu.VMEM)
    block = pl.BlockSpec((mine.shape[1], HEADS_WIDTH), lambda i: (0, part))
    half = mine.shape[0] // 2
    width = HEADS_WIDTH + len(gates) * DK
    return pl.pallas_call(
        product_kernel,
        grid=(1,),
        out_shape=[
            jax.ShapeDtypeStruct((half, width), jnp.float32),
            jax.ShapeDtypeStruct((half, width + SCALE_LANES), jnp.int16),
        ],
        in_specs=[vmem, vmem, block, block] + [vmem] * len(gates),
        out_specs=[vmem] * 2,
        compiler_params=pltpu.CompilerParams(vmem_limit_bytes=32 * 1024 * 1024),
        cost_estimate=pl.CostEstimate(flops=0, bytes_accessed=0, transcendentals=0),
        name="partial_product",
    )(mine, theirs, *weights, *gates)


def combine_kernel(kept_ref, got_ref, *refs):
    tap_refs, (still_ref, packed_ref), wide_refs = refs[:-2], refs[-2:], ()
    if tap_refs:
        tap_refs, wide_refs = refs[:2], refs[2:3]
        still_ref, packed_ref = refs[3:]
    half = still_ref.shape[0]
    steps = steps_of(got_ref)
    sent = []
    for block in range(kept_ref.shape[1] // DK):
        columns = pl.ds(block * DK, DK)
        total = kept_ref[:, columns] + unpack_block(got_ref, steps, block)
        still_ref[:, columns] = total[:half]
        sent.append(total[half:])
    sent = jnp.concatenate(sent, axis=1)
    pack_rows(fold_rows(sent) if half == ROWS else sent, packed_ref)
    for wide_ref in wide_refs:
        rows = tap_refs[0].shape[0]
        wide_ref[:rows] = tap_refs[0][...]
        wide_ref[rows:] = tap_refs[1][...]


def run_combine(kept, got, taps=()):
    vmem = pl.BlockSpec(memory_space=pltpu.VMEM)
    half, width = kept.shape[0] // 2, kept.shape[1]
    packed = (2 * ROWS, width // 2 + SCALE_LANES) if half == ROWS else (half, width + SCALE_LANES)
    wide = [jax.ShapeDtypeStruct((2 * taps[0].shape[0], TAP_WIDTH), jnp.bfloat16)] if taps else []
    return pl.pallas_call(
        combine_kernel,
        out_shape=wide
        + [
            jax.ShapeDtypeStruct((half, width), jnp.float32),
            jax.ShapeDtypeStruct(packed, jnp.int16),
        ],
        in_specs=[vmem] * (2 + len(taps)),
        out_specs=[vmem] * (2 + len(wide)),
        compiler_params=pltpu.CompilerParams(vmem_limit_bytes=32 * 1024 * 1024),
        cost_estimate=pl.CostEstimate(flops=0, bytes_accessed=0, transcendentals=0),
        name="combine",
    )(kept, got, *taps)


def swap(value, bit, devices):
    return lax.ppermute(value, "heads", [(i, i ^ bit) for i in range(devices)])


def on_device(
    tokens,
    qkv_weight,
    gate_weight,
    conv_weight,
    delta_state,
    conv_state,
    old_heads,
    new_units,
    slot_of,
    lengths,
):
    devices = lax.axis_size("heads")
    me = lax.axis_index("heads")
    per_device = UNITS // devices
    depth = qkv_weight.shape[0]
    row_count = tokens.shape[0]
    chips = devices // 2

    old_slots, halves = unit_tables(old_heads, new_units)
    bits = [1 << b for b in range(1, devices.bit_length() - 1)]
    steps = jnp.arange(STEPS, dtype=jnp.int32)
    offered = (slot_of[:, None] * STEPS + steps[None, :]).reshape(-1)

    mine, theirs = run_rows(me, slot_of, tokens, depth, chips)

    weights = (qkv_weight, swap(qkv_weight, 1, devices))
    gates = (gate_weight, swap(gate_weight, 1, devices))

    def in_order(value, *earlier):
        return lax.optimization_barrier((value,) + earlier)[0]

    ride = conv_weight.shape[1] == 2 * TAP_WIDTH and len(bits) == 3
    taps = conv_weight
    if ride:
        taps = jnp.concatenate([taps, swap(taps, 1, devices)], axis=1)
    else:
        taps = lax.all_gather(taps, "heads", axis=1, tiled=True)
    blocks = range(0, taps.shape[1], TAP_WIDTH)
    taps = jnp.concatenate([taps[:, at : at + TAP_WIDTH] for at in blocks], axis=0)
    my_rows = me * LOCAL + jnp.arange(LOCAL, dtype=jnp.int32)
    my_lengths = jnp.sum(
        jnp.where(slot_of[None, :] == my_rows[:, None], lengths[None, :], 0), axis=1
    )
    carried = conv_state.reshape(LOCAL, TAPS - 1, -1)
    blank = jnp.zeros((1, carried.shape[2]), jnp.float32)
    history = jnp.concatenate([blank, carried[1], blank, carried[0]], axis=0)
    mine = in_order(mine, taps, history, my_lengths, old_slots, halves)
    query = run_product(mine, theirs, weights, 0)
    mine = in_order(mine, *query)
    key = run_product(mine, theirs, weights, 1, gates)
    mine = in_order(mine, *key)
    value = run_product(mine, theirs, weights, 2)

    chunks = [query, key, value]
    got = [swap(packed, bits[0], devices) for _, packed in chunks]
    got[0] = in_order(got[0], *value)
    far = swap(taps, bits[0], devices) if ride else taps
    for level, bit in enumerate(bits[1:]):
        for at in range(len(chunks)):
            arrived = in_order(got[at], *chunks[at - 1]) if at else got[at]
            if ride and level == 0 and at != 1:
                taps, *chunks[at] = run_combine(chunks[at][0], arrived, (taps, far))
                far = swap(taps, bits[1 + at // 2], devices)
            else:
                chunks[at] = run_combine(chunks[at][0], arrived)
            got[at] = swap(chunks[at][1], bit, devices)
    queries, keys, values = [(kept, came) for (kept, _), came in zip(chunks, got)]
    if ride:
        twist, taps = (2 * me).reshape(1), (taps, far)
    else:
        half = TAP_BLOCKS // 2 * TAPS
        twist, taps = jnp.zeros(1, jnp.int32), (taps[:half], taps[half:])

    local_out = run_delta(
        old_slots, halves, my_lengths, queries, keys, values, history, twist, taps, delta_state
    )

    placer = (offered[:, None] == jnp.arange(row_count * STEPS, dtype=jnp.int32)[None, :]).astype(
        jnp.bfloat16
    )
    if per_device % 2 == 0:
        pairs = per_device // 2
        sending = local_out.reshape(devices, pairs * ROWS, DK)
        got = lax.all_to_all(sending, "heads", split_axis=0, concat_axis=0, tiled=True)
        got = got.reshape(devices, pairs, ROWS, DK)
        got = jnp.concatenate([got[:, pair] for pair in range(pairs)], axis=-1)
        got = got.reshape(devices * ROWS, pairs * DK)
    else:
        units = local_out.reshape(UNITS // 2, ROWS, 2, HALF).transpose(0, 2, 1, 3)
        sending = units.reshape(devices, per_device * ROWS, HALF)
        got = lax.all_to_all(sending, "heads", split_axis=0, concat_axis=0, tiled=True)
        got = got.reshape(devices, per_device, ROWS, HALF).transpose(0, 2, 1, 3)
        got = got.reshape(devices * ROWS, per_device * HALF)
    outputs = jnp.dot(placer, got, preferred_element_type=jnp.float32).astype(jnp.bfloat16)
    return outputs.reshape(row_count, STEPS, per_device * HALF)


def solution(mesh):
    in_specs = (
        P("groups", None, None),
        P(("groups", "heads"), None),
        P(("groups", "heads"), None),
        P("groups", "heads"),
        P(("groups", "heads"), None, None, None),
        P(("groups", "heads"), None, None),
        P(),
        P(),
        P("groups"),
        P("groups"),
    )
    out_specs = P("groups", None, "heads")
    return jax.shard_map(
        on_device, mesh=mesh, in_specs=in_specs, out_specs=out_specs, check_vma=False
    )
```

```python
import functools

import jax
import jax.numpy as jnp
from jax import lax
from jax.experimental import pallas as pl
from jax.experimental.pallas import tpu as pltpu
from jax.sharding import PartitionSpec as P

D = 2304
H = 32
DK = 128
TAPS = 4
STEPS = 4
HALF = 64
UNITS = 64
LOCAL = 2
ROWS = LOCAL * STEPS
HEADS_WIDTH = H * DK
LEVELS = 32767.0
STATE_COPIES = 4
TAP_WIDTH = 384
TAP_BLOCKS = 3 * HEADS_WIDTH // TAP_WIDTH


norm_eps = 1e-06


def unit_tables(old_heads, new_units):
    positions = jnp.arange(H, dtype=jnp.int32)
    inverse = jnp.sum(
        jnp.where(old_heads[None, :] == positions[:, None], positions[None, :], 0), axis=1
    )
    heads_of = new_units // 2
    halves = new_units % 2
    old_slots = jnp.sum(
        jnp.where(heads_of[:, None] == positions[None, :], inverse[None, :], 0), axis=1
    )
    return (old_slots, halves)


def shift_rows(value, lag, row_step):
    if lag == 0:
        return value
    moved = pltpu.roll(value, lag, 0)
    return jnp.where(row_step >= lag, moved, 0.0)


def lane_sum(value):
    return jnp.sum(value, axis=-1, keepdims=True)


def unit_length(value):
    return value * lax.rsqrt(lane_sum(value * value) + norm_eps)


def scale_lanes(blocks):
    return -(-blocks // HALF) * DK


def pack_rows(total, packed_ref):
    rows, width = total.shape
    blocks = width // DK
    lanes = scale_lanes(blocks)
    lane = lax.broadcasted_iota(jnp.int32, (rows, lanes), 1)
    scales = jnp.zeros((rows, lanes), jnp.float32)
    for block in range(blocks):
        part = total[:, block * DK : (block + 1) * DK]
        top = jnp.max(jnp.abs(part), axis=-1, keepdims=True) + 1e-30
        exponent = jnp.ceil(jnp.log2(top))
        mantissa = jnp.ceil(jnp.minimum(top * jnp.exp2(-exponent) * LEVELS, LEVELS))
        factor = LEVELS * LEVELS * jnp.exp2(-exponent) / mantissa
        coded = jnp.clip(jnp.floor(part * factor + 0.5), -LEVELS, LEVELS)
        packed_ref[:, block * DK : (block + 1) * DK] = coded.astype(jnp.int32).astype(jnp.int16)
        scales = jnp.where(lane == block, mantissa, scales)
        scales = jnp.where(lane == lanes // 2 + block, exponent, scales)
    packed_ref[:, width:] = scales.astype(jnp.int32).astype(jnp.int16)


def to_float(coded):
    return coded.astype(jnp.int32).astype(jnp.float32)


def steps_of(packed_ref):
    lanes = DK if packed_ref.shape[1] <= (HALF + 1) * DK else 2 * DK
    scales = to_float(packed_ref[:, packed_ref.shape[1] - lanes :])
    exponents = pltpu.roll(scales, lanes // 2, 1)
    return scales * jnp.exp2(exponents) * (1.0 / (LEVELS * LEVELS))


def unpack_block(packed_ref, steps, block):
    return to_float(packed_ref[:, block * DK : (block + 1) * DK]) * steps[:, block : block + 1]


def fold_rows(value):
    half = value.shape[1] // 2
    return jnp.concatenate([value[:, :half], value[:, half:]], axis=0)


def received(kept_ref, got_ref, steps, block):
    half = kept_ref.shape[1] // DK // 2
    rows = unpack_block(got_ref, steps, block % half)
    rows = rows[:ROWS] if block < half else rows[ROWS:]
    return kept_ref[:, block * DK : (block + 1) * DK] + rows


def activate(kept_ref, got_ref, steps, at, part, head, history_ref, taps_ref, twist, row_step):
    fresh = received(kept_ref, got_ref, steps, at * H + head)
    column = part * HEADS_WIDTH + head * DK
    carried = history_ref[:, column : column + DK]
    taps = taps_ref[jnp.bitwise_xor(column // TAP_WIDTH, twist)]
    inner = column % TAP_WIDTH
    total = taps[TAPS - 1 :, inner : inner + DK] * fresh
    for lag in range(1, TAPS):
        source = jnp.where(row_step >= STEPS - lag, carried, fresh)
        tap = taps[TAPS - 1 - lag : TAPS - lag, inner : inner + DK]
        total = total + tap * pltpu.roll(source, lag, 0)
    return total / (1.0 + jnp.exp(-total))


def keys_kernel(
    twist_ref, kept_ref, got_ref, history_ref, near_ref, far_ref,
    state_hbm, beta_ref, key_seen_ref, query_seen_ref, pulls_ref, weights_ref, taps_ref,
    state_ref, sems,
):
    per_copy = H // STATE_COPIES
    copies = []
    for at in range(STATE_COPIES):
        some = pl.ds(at * per_copy, per_copy)
        copies.append(
            pltpu.make_async_copy(state_hbm.at[:, some], state_ref.at[:, some], sems.at[at])
        )
        copies[-1].start()
    twist = twist_ref[0]
    half = TAP_BLOCKS // 2
    for at in range(TAP_BLOCKS):
        source = near_ref if at < half else far_ref
        if at % 4 == 0:
            some = source[at % half * TAPS : (at % half + 4) * TAPS, :].astype(jnp.float32)
        taps_ref[at] = some[at % 4 * TAPS : (at % 4 + 1) * TAPS]
    row = lax.broadcasted_iota(jnp.int32, (ROWS, DK), 0)
    row_step = row % STEPS
    steps = steps_of(got_ref)
    gates = received(kept_ref, got_ref, steps, 2 * H)
    for head in range(H):
        key = unit_length(
            activate(
                kept_ref, got_ref, steps, 1, 1, head, history_ref, taps_ref, twist, row_step
            )
        )
        query = unit_length(
            activate(
                kept_ref, got_ref, steps, 0, 0, head, history_ref, taps_ref, twist, row_step
            )
        )
        beta_logit = jnp.broadcast_to(gates[:, head : head + 1], (ROWS, DK))
        decay_logit = jnp.broadcast_to(gates[:, H + head : H + head + 1], (ROWS, DK))
        beta = 1.0 / (1.0 + jnp.exp(-beta_logit))
        decay = 1.0 / (1.0 + jnp.exp(decay_logit))
        fades = [jnp.ones_like(decay), decay]
        for lag in range(2, STEPS + 1):
            earlier = pltpu.roll(decay, lag - 1, 0)
            fades.append(jnp.where(row_step >= lag - 1, fades[-1] * earlier, fades[-1]))
        both = jnp.concatenate([key, query], axis=0)
        if head % per_copy == 0:
            copies[head // per_copy].wait()
        both_high = both.astype(jnp.bfloat16)
        both_low = (both - both_high.astype(jnp.float32)).astype(jnp.bfloat16)
        stacked = jnp.concatenate([both_high, both_low], axis=0)
        seen = []
        for r in range(LOCAL):
            state = state_ref[r, head]
            high = state.astype(jnp.bfloat16)
            low = (state - high.astype(jnp.float32)).astype(jnp.bfloat16)
            main = jnp.dot(stacked, high, preferred_element_type=jnp.float32)
            rest = jnp.dot(both_high, low, preferred_element_type=jnp.float32)
            seen.append(main[: 2 * ROWS] + main[2 * ROWS :] + rest)
        beta_ref[head] = beta
        key_seen_ref[head] = beta * fades[STEPS] * jnp.where(
            row < STEPS, seen[0][:ROWS], seen[1][:ROWS]
        )
        query_seen_ref[head] = fades[STEPS] * jnp.where(
            row < STEPS, seen[0][ROWS:], seen[1][ROWS:]
        )
        for lag in range(STEPS):
            moved_key = shift_rows(key, lag, row_step)
            if lag:
                pulls_ref[lag - 1, head] = beta * fades[lag] * lane_sum(key * moved_key)
            weights_ref[lag, head] = fades[lag] * lane_sum(query * moved_key)


def values_kernel(
    slots_ref, halves_ref, lengths_ref, twist_ref, value_ref, value_got_ref, history_ref,
    beta_ref, key_seen_ref, query_seen_ref, pulls_ref, weights_ref, taps_ref, out_ref, heads_ref,
):
    twist = twist_ref[0]
    row = lax.broadcasted_iota(jnp.int32, (ROWS, DK), 0)
    row_step = row % STEPS
    lane = lax.broadcasted_iota(jnp.int32, (ROWS, DK), 1)
    row_length = jnp.where(row < STEPS, lengths_ref[0], lengths_ref[1])
    live = row_step < row_length
    value_steps = steps_of(value_got_ref)
    for head in range(H):
        value = activate(
            value_ref, value_got_ref, value_steps, 0, 2, head, history_ref, taps_ref, twist, row_step
        )
        base = beta_ref[head] * value - key_seen_ref[head]
        solved = base
        for _ in range(STEPS - 1):
            following = base
            for lag in range(1, STEPS):
                following = following - pulls_ref[lag - 1, head] * shift_rows(
                    solved, lag, row_step
                )
            solved = following
        out = query_seen_ref[head]
        for lag in range(STEPS):
            out = out + weights_ref[lag, head] * shift_rows(solved, lag, row_step)
        heads_ref[head] = jnp.where(live, out, 0.0)
    for quad in range(UNITS // 4):
        joined = []
        for pair in (2 * quad, 2 * quad + 1):
            first = heads_ref[slots_ref[2 * pair]]
            second = heads_ref[slots_ref[2 * pair + 1]]
            first = jnp.where(halves_ref[2 * pair] == 0, first, pltpu.roll(first, HALF, 1))
            second = jnp.where(halves_ref[2 * pair + 1] == 0, pltpu.roll(second, HALF, 1), second)
            joined.append(jnp.where(lane < HALF, first, second))
        out_ref[quad] = jnp.concatenate(joined, axis=0).astype(jnp.bfloat16)


def run_delta(slots, halves, lengths, keys, values, history, twist, taps, state):
    smem = pl.BlockSpec(memory_space=pltpu.SMEM)
    vmem = pl.BlockSpec(memory_space=pltpu.VMEM)
    params = pltpu.CompilerParams(vmem_limit_bytes=32 * 1024 * 1024)
    per_head = jax.ShapeDtypeStruct((H, ROWS, DK), jnp.float32)
    lags = [
        jax.ShapeDtypeStruct((count, H, ROWS, DK), jnp.float32) for count in (STEPS - 1, STEPS)
    ]
    tap_blocks = jax.ShapeDtypeStruct((TAP_BLOCKS, TAPS, TAP_WIDTH), jnp.float32)
    prepared = pl.pallas_call(
        keys_kernel,
        out_shape=[per_head] * 3 + lags + [tap_blocks],
        in_specs=[smem] + [vmem] * 5 + [pl.BlockSpec(memory_space=pl.ANY)],
        out_specs=[vmem] * 6,
        scratch_shapes=[
            pltpu.VMEM(state.shape, jnp.float32),
            pltpu.SemaphoreType.DMA((STATE_COPIES,)),
        ],
        compiler_params=params,
        cost_estimate=pl.CostEstimate(flops=40_000_000, bytes_accessed=9_000_000, transcendentals=0),
        name="keys_part",
    )(twist, *keys, history, *taps, state)
    return pl.pallas_call(
        values_kernel,
        out_shape=jax.ShapeDtypeStruct((UNITS // 4, 2 * ROWS, DK), jnp.bfloat16),
        in_specs=[smem] * 4 + [vmem] * 9,
        out_specs=vmem,
        scratch_shapes=[pltpu.VMEM((H, ROWS, DK), jnp.float32)],
        compiler_params=params,
        cost_estimate=pl.CostEstimate(flops=4_000_000, bytes_accessed=2_000_000, transcendentals=0),
        name="values_part",
    )(slots, halves, lengths, twist, *values, history, *prepared)


def rows_kernel(
    depth, me_ref, slot_of_ref, tokens_hbm, mine_ref, theirs_ref, window_ref, sem
):
    me = me_ref[0]
    width = window_ref.shape[2]
    offset = me // 2 * (2 * depth)
    start = jnp.minimum(offset // DK * DK, D - width)
    columns = pl.ds(pl.multiple_of(start, DK), width)
    copy = pltpu.make_async_copy(tokens_hbm.at[:, :, columns], window_ref, sem)
    copy.start()
    shape = (mine_ref.shape[0], slot_of_ref.shape[1])
    row = lax.broadcasted_iota(jnp.int32, shape, 0)
    place = row // ROWS
    count = (shape[0] // ROWS).bit_length() - 1
    holder = jnp.zeros(shape, jnp.int32)
    for at in range(count):
        holder = holder + ((place >> (count - 1 - at)) & 1) * (2 << at)
    holder = jnp.bitwise_xor(holder, me)
    match = holder * LOCAL + row % ROWS // STEPS == slot_of_ref[...]
    copy.wait()
    window = window_ref[...].astype(jnp.float32)
    total = jnp.zeros((shape[0], width), jnp.float32)
    for step in range(STEPS):
        picker = jnp.where(match & (row % STEPS == step), 1.0, 0.0).astype(jnp.bfloat16)
        here = window[:, step, :].astype(jnp.bfloat16)
        total = total + jnp.dot(picker, here, preferred_element_type=jnp.float32)
    total = pltpu.roll(total, lax.rem(width - (offset - start), width), 1)
    low, high = total[:, :depth], total[:, depth : 2 * depth]
    first_core = me % 2 == 0
    mine_ref[...] = jnp.where(first_core, low, high).astype(jnp.bfloat16)
    theirs_ref[...] = jnp.where(first_core, high, low).astype(jnp.bfloat16)


def run_rows(me, slot_of, tokens, depth, chips):
    width = -(-(2 * depth + DK - 1) // DK) * DK
    out = jax.ShapeDtypeStruct((chips * ROWS, depth), jnp.bfloat16)
    vmem = pl.BlockSpec(memory_space=pltpu.VMEM)
    return pl.pallas_call(
        functools.partial(rows_kernel, depth),
        out_shape=[out, out],
        in_specs=[
            pl.BlockSpec(memory_space=pltpu.SMEM), vmem, pl.BlockSpec(memory_space=pltpu.HBM)
        ],
        out_specs=[vmem, vmem],
        scratch_shapes=[
            pltpu.VMEM((tokens.shape[0], STEPS, width), jnp.bfloat16),
            pltpu.SemaphoreType.DMA,
        ],
        compiler_params=pltpu.CompilerParams(vmem_limit_bytes=32 * 1024 * 1024),
        cost_estimate=pl.CostEstimate(flops=0, bytes_accessed=0, transcendentals=0),
        name="token_rows",
    )(me.reshape(1), slot_of.reshape(1, -1), tokens)


def product_kernel(mine_ref, theirs_ref, block_ref, other_ref, *refs):
    gate_refs, (kept_ref, packed_ref) = refs[:-2], refs[-2:]
    half = mine_ref.shape[0] // 2

    def product(own, other):
        total = jnp.dot(mine_ref[...], own, preferred_element_type=jnp.float32)
        return total + jnp.dot(theirs_ref[...], other, preferred_element_type=jnp.float32)

    total = product(block_ref[...], other_ref[...])
    if gate_refs:
        gates = product(gate_refs[0][...], gate_refs[1][...])
        zeros = jnp.zeros((gates.shape[0], 2 * DK - gates.shape[1]), jnp.float32)
        total = jnp.concatenate([total, gates, zeros], axis=1)
    kept_ref[...] = total[:half]
    pack_rows(total[half:], packed_ref)


def run_product(mine, theirs, weights, first, parts, gates=()):
    vmem = pl.BlockSpec(memory_space=pltpu.VMEM)
    block = pl.BlockSpec((mine.shape[1], parts * HEADS_WIDTH), lambda i: (0, first // parts))
    half = mine.shape[0] // 2
    width = parts * HEADS_WIDTH + len(gates) * DK
    return pl.pallas_call(
        product_kernel,
        grid=(1,),
        out_shape=[
            jax.ShapeDtypeStruct((half, width), jnp.float32),
            jax.ShapeDtypeStruct((half, width + scale_lanes(width // DK)), jnp.int16),
        ],
        in_specs=[vmem, vmem, block, block] + [vmem] * len(gates),
        out_specs=[vmem] * 2,
        compiler_params=pltpu.CompilerParams(vmem_limit_bytes=32 * 1024 * 1024),
        cost_estimate=pl.CostEstimate(flops=0, bytes_accessed=0, transcendentals=0),
        name="partial_product",
    )(mine, theirs, *weights, *gates)


def combine_kernel(kept_ref, got_ref, still_ref, packed_ref):
    half = still_ref.shape[0]
    steps = steps_of(got_ref)
    sent = []
    for block in range(kept_ref.shape[1] // DK):
        columns = pl.ds(block * DK, DK)
        total = kept_ref[:, columns] + unpack_block(got_ref, steps, block)
        still_ref[:, columns] = total[:half]
        sent.append(total[half:])
    sent = jnp.concatenate(sent, axis=1)
    pack_rows(fold_rows(sent) if half == ROWS else sent, packed_ref)


def run_combine(kept, got):
    vmem = pl.BlockSpec(memory_space=pltpu.VMEM)
    half, width = kept.shape[0] // 2, kept.shape[1]
    rows, packed = (2 * ROWS, width // 2) if half == ROWS else (half, width)
    packed = (rows, packed + scale_lanes(packed // DK))
    return pl.pallas_call(
        combine_kernel,
        out_shape=[
            jax.ShapeDtypeStruct((half, width), jnp.float32),
            jax.ShapeDtypeStruct(packed, jnp.int16),
        ],
        in_specs=[vmem] * 2,
        out_specs=[vmem] * 2,
        compiler_params=pltpu.CompilerParams(vmem_limit_bytes=32 * 1024 * 1024),
        cost_estimate=pl.CostEstimate(flops=0, bytes_accessed=0, transcendentals=0),
        name="combine",
    )(kept, got)


def swap(value, bit, devices):
    return lax.ppermute(value, "heads", [(i, i ^ bit) for i in range(devices)])


def on_device(
    tokens,
    qkv_weight,
    gate_weight,
    conv_weight,
    delta_state,
    conv_state,
    old_heads,
    new_units,
    slot_of,
    lengths,
):
    devices = lax.axis_size("heads")
    me = lax.axis_index("heads")
    per_device = UNITS // devices
    depth = qkv_weight.shape[0]
    row_count = tokens.shape[0]
    chips = devices // 2

    bits = [1 << b for b in range(1, devices.bit_length() - 1)]
    steps = jnp.arange(STEPS, dtype=jnp.int32)
    offered = (slot_of[:, None] * STEPS + steps[None, :]).reshape(-1)

    mine, theirs = run_rows(me, slot_of, tokens, depth, chips)

    weights = (qkv_weight, swap(qkv_weight, 1, devices))
    gates = (gate_weight, swap(gate_weight, 1, devices))

    def in_order(value, *earlier):
        return lax.optimization_barrier((value,) + earlier)[0]

    ride = conv_weight.shape[1] == 2 * TAP_WIDTH and len(bits) == 3
    taps = conv_weight
    if ride:
        taps = jnp.concatenate([taps[:, :TAP_WIDTH], taps[:, TAP_WIDTH:]], axis=0)
        for bit in (1, 2):
            taps = jnp.concatenate([taps, swap(taps, bit, devices)], axis=0)
    else:
        taps = lax.all_gather(taps, "heads", axis=1, tiled=True)
        blocks = range(0, taps.shape[1], TAP_WIDTH)
        taps = jnp.concatenate([taps[:, at : at + TAP_WIDTH] for at in blocks], axis=0)
    mine = in_order(mine, taps)
    keys = run_product(mine, theirs, weights, 0, 2, gates)
    mine = in_order(mine, *keys)
    values = run_product(mine, theirs, weights, 2, 1)

    slot_of, lengths, old_heads, new_units, carried = lax.optimization_barrier(
        (slot_of, lengths, old_heads, new_units, conv_state, *values)
    )[:5]
    old_slots, halves = unit_tables(old_heads, new_units)
    my_rows = me * LOCAL + jnp.arange(LOCAL, dtype=jnp.int32)
    my_lengths = jnp.sum(
        jnp.where(slot_of[None, :] == my_rows[:, None], lengths[None, :], 0), axis=1
    )
    blank = jnp.zeros((1, carried.shape[2]), jnp.float32)
    history = jnp.concatenate([blank, carried[1], blank, carried[0]], axis=0)
    if ride:
        taps = in_order(taps, *values)
        taps = jnp.concatenate([taps, swap(taps, 4, devices)], axis=0)
        far = swap(taps, 8, devices)
        twist, taps = (2 * me).reshape(1), (taps, far)
    else:
        half = TAP_BLOCKS // 2 * TAPS
        twist, taps = jnp.zeros(1, jnp.int32), (taps[:half], taps[half:])

    chunks = [keys, values]
    got = [swap(packed, bits[0], devices) for _, packed in chunks]
    got[0] = in_order(got[0], *taps, history, my_lengths, old_slots, halves)
    for level, bit in enumerate(bits[1:]):
        for at in range(len(chunks)):
            arrived = in_order(got[at], *chunks[at - 1]) if at else got[at]
            chunks[at] = run_combine(chunks[at][0], arrived)
            got[at] = swap(chunks[at][1], bit, devices)
    keys, values = [(kept, came) for (kept, _), came in zip(chunks, got)]

    local_out = run_delta(
        old_slots, halves, my_lengths, keys, values, history, twist, taps, delta_state
    )

    placer = (offered[:, None] == jnp.arange(row_count * STEPS, dtype=jnp.int32)[None, :]).astype(
        jnp.bfloat16
    )
    if per_device % 2 == 0:
        pairs = per_device // 2
        sending = local_out.reshape(devices, pairs * ROWS, DK)
        got = lax.all_to_all(sending, "heads", split_axis=0, concat_axis=0, tiled=True)
        got = got.reshape(devices, pairs, ROWS, DK)
        got = jnp.concatenate([got[:, pair] for pair in range(pairs)], axis=-1)
        got = got.reshape(devices * ROWS, pairs * DK)
    else:
        units = local_out.reshape(UNITS // 2, ROWS, 2, HALF).transpose(0, 2, 1, 3)
        sending = units.reshape(devices, per_device * ROWS, HALF)
        got = lax.all_to_all(sending, "heads", split_axis=0, concat_axis=0, tiled=True)
        got = got.reshape(devices, per_device, ROWS, HALF).transpose(0, 2, 1, 3)
        got = got.reshape(devices * ROWS, per_device * HALF)
    outputs = jnp.dot(placer, got, preferred_element_type=jnp.float32).astype(jnp.bfloat16)
    return outputs.reshape(row_count, STEPS, per_device * HALF)


def solution(mesh):
    in_specs = (
        P("groups", None, None),
        P(("groups", "heads"), None),
        P(("groups", "heads"), None),
        P("groups", "heads"),
        P(("groups", "heads"), None, None, None),
        P(("groups", "heads"), None, None),
        P(),
        P(),
        P("groups"),
        P("groups"),
    )
    out_specs = P("groups", None, "heads")
    return jax.shard_map(
        on_device, mesh=mesh, in_specs=in_specs, out_specs=out_specs, check_vma=False
    )
```

```python
import functools

import jax
import jax.numpy as jnp
from jax import lax
from jax.experimental import pallas as pl
from jax.experimental.pallas import tpu as pltpu
from jax.sharding import PartitionSpec as P

D = 2304
H = 32
DK = 128
TAPS = 4
STEPS = 4
HALF = 64
UNITS = 64
LOCAL = 2
ROWS = LOCAL * STEPS
HEADS_WIDTH = H * DK
LEVELS = 32767.0
STATE_COPIES = 4
WEIGHT_COPIES = 2
TAP_WIDTH = 384
TAP_BLOCKS = 3 * HEADS_WIDTH // TAP_WIDTH


norm_eps = 1e-06


def unit_tables(old_heads, new_units):
    positions = jnp.arange(H, dtype=jnp.int32)
    inverse = jnp.sum(
        jnp.where(old_heads[None, :] == positions[:, None], positions[None, :], 0), axis=1
    )
    heads_of = new_units // 2
    halves = new_units % 2
    old_slots = jnp.sum(
        jnp.where(heads_of[:, None] == positions[None, :], inverse[None, :], 0), axis=1
    )
    return (old_slots, halves)


def shift_rows(value, lag, row_step):
    if lag == 0:
        return value
    moved = pltpu.roll(value, lag, 0)
    return jnp.where(row_step >= lag, moved, 0.0)


def lane_sum(value):
    return jnp.sum(value, axis=-1, keepdims=True)


def unit_length(value):
    return value * lax.rsqrt(lane_sum(value * value) + norm_eps)


def scale_lanes(blocks):
    return -(-blocks // HALF) * DK


def pack_rows(total, packed_ref):
    rows, width = total.shape
    blocks = width // DK
    lanes = scale_lanes(blocks)
    lane = lax.broadcasted_iota(jnp.int32, (rows, lanes), 1)
    scales = jnp.zeros((rows, lanes), jnp.float32)
    for block in range(blocks):
        part = total[:, block * DK : (block + 1) * DK]
        top = jnp.max(jnp.abs(part), axis=-1, keepdims=True) + 1e-30
        exponent = jnp.ceil(jnp.log2(top))
        mantissa = jnp.ceil(jnp.minimum(top * jnp.exp2(-exponent) * LEVELS, LEVELS))
        factor = LEVELS * LEVELS * jnp.exp2(-exponent) / mantissa
        coded = jnp.clip(jnp.floor(part * factor + 0.5), -LEVELS, LEVELS)
        packed_ref[:, block * DK : (block + 1) * DK] = coded.astype(jnp.int32).astype(jnp.int16)
        scales = jnp.where(lane == block, mantissa, scales)
        scales = jnp.where(lane == lanes // 2 + block, exponent, scales)
    packed_ref[:, width:] = scales.astype(jnp.int32).astype(jnp.int16)


def to_float(coded):
    return coded.astype(jnp.int32).astype(jnp.float32)


def steps_of(packed_ref):
    lanes = DK if packed_ref.shape[1] <= (HALF + 1) * DK else 2 * DK
    scales = to_float(packed_ref[:, packed_ref.shape[1] - lanes :])
    exponents = pltpu.roll(scales, lanes // 2, 1)
    return scales * jnp.exp2(exponents) * (1.0 / (LEVELS * LEVELS))


def unpack_block(packed_ref, steps, block):
    return to_float(packed_ref[:, block * DK : (block + 1) * DK]) * steps[:, block : block + 1]


def fold_rows(value):
    half = value.shape[1] // 2
    return jnp.concatenate([value[:, :half], value[:, half:]], axis=0)


def received(kept_ref, got_ref, steps, block):
    half = kept_ref.shape[1] // DK // 2
    rows = unpack_block(got_ref, steps, block % half)
    rows = rows[:ROWS] if block < half else rows[ROWS:]
    return kept_ref[:, block * DK : (block + 1) * DK] + rows


def tap_block(block, me):
    other = jnp.bitwise_xor(block // 2, me)
    place = (other & 1) + ((other >> 2) & 3) * 2 + ((other >> 1) & 1) * 8
    return place * 2 + block % 2


def activate(kept_ref, got_ref, steps, part, head, history_ref, taps_ref, twist, row_step):
    fresh = received(kept_ref, got_ref, steps, head)
    column = part * HEADS_WIDTH + head * DK
    carried = history_ref[:, column : column + DK]
    taps = taps_ref[tap_block(column // TAP_WIDTH, twist)]
    inner = column % TAP_WIDTH
    total = taps[TAPS - 1 :, inner : inner + DK] * fresh
    for lag in range(1, TAPS):
        source = jnp.where(row_step >= STEPS - lag, carried, fresh)
        tap = taps[TAPS - 1 - lag : TAPS - lag, inner : inner + DK]
        total = total + tap * pltpu.roll(source, lag, 0)
    return total / (1.0 + jnp.exp(-total))


def keys_kernel(
    twist_ref, query_ref, query_got_ref, key_ref, key_got_ref, history_ref, near_ref, far_ref,
    state_hbm, beta_ref, key_seen_ref, query_seen_ref, pulls_ref, weights_ref, taps_ref,
    state_ref, sems,
):
    per_copy = H // STATE_COPIES
    copies = []
    for at in range(STATE_COPIES):
        some = pl.ds(at * per_copy, per_copy)
        copies.append(
            pltpu.make_async_copy(state_hbm.at[:, some], state_ref.at[:, some], sems.at[at])
        )
        copies[-1].start()
    twist = twist_ref[0]
    half = TAP_BLOCKS // 2
    for at in range(TAP_BLOCKS):
        source = near_ref if at < half else far_ref
        if at % 4 == 0:
            some = source[at % half * TAPS : (at % half + 4) * TAPS, :].astype(jnp.float32)
        taps_ref[at] = some[at % 4 * TAPS : (at % 4 + 1) * TAPS]
    row = lax.broadcasted_iota(jnp.int32, (ROWS, DK), 0)
    row_step = row % STEPS
    query_steps, key_steps = steps_of(query_got_ref), steps_of(key_got_ref)
    gates = received(key_ref, key_got_ref, key_steps, H)
    for head in range(H):
        key = unit_length(
            activate(
                key_ref, key_got_ref, key_steps, 1, head, history_ref, taps_ref, twist, row_step
            )
        )
        query = unit_length(
            activate(
                query_ref, query_got_ref, query_steps, 0, head, history_ref, taps_ref, twist,
                row_step,
            )
        )
        beta_logit = jnp.broadcast_to(gates[:, head : head + 1], (ROWS, DK))
        decay_logit = jnp.broadcast_to(gates[:, H + head : H + head + 1], (ROWS, DK))
        beta = 1.0 / (1.0 + jnp.exp(-beta_logit))
        decay = 1.0 / (1.0 + jnp.exp(decay_logit))
        fades = [jnp.ones_like(decay), decay]
        for lag in range(2, STEPS + 1):
            earlier = pltpu.roll(decay, lag - 1, 0)
            fades.append(jnp.where(row_step >= lag - 1, fades[-1] * earlier, fades[-1]))
        both = jnp.concatenate([key, query], axis=0)
        if head % per_copy == 0:
            copies[head // per_copy].wait()
        both_high = both.astype(jnp.bfloat16)
        both_low = (both - both_high.astype(jnp.float32)).astype(jnp.bfloat16)
        stacked = jnp.concatenate([both_high, both_low], axis=0)
        seen = []
        for r in range(LOCAL):
            state = state_ref[r, head]
            high = state.astype(jnp.bfloat16)
            low = (state - high.astype(jnp.float32)).astype(jnp.bfloat16)
            main = jnp.dot(stacked, high, preferred_element_type=jnp.float32)
            rest = jnp.dot(both_high, low, preferred_element_type=jnp.float32)
            seen.append(main[: 2 * ROWS] + main[2 * ROWS :] + rest)
        beta_ref[head] = beta
        key_seen_ref[head] = beta * fades[STEPS] * jnp.where(
            row < STEPS, seen[0][:ROWS], seen[1][:ROWS]
        )
        query_seen_ref[head] = fades[STEPS] * jnp.where(
            row < STEPS, seen[0][ROWS:], seen[1][ROWS:]
        )
        for lag in range(STEPS):
            moved_key = shift_rows(key, lag, row_step)
            if lag:
                pulls_ref[lag - 1, head] = beta * fades[lag] * lane_sum(key * moved_key)
            weights_ref[lag, head] = fades[lag] * lane_sum(query * moved_key)


def values_kernel(
    slots_ref, halves_ref, lengths_ref, twist_ref, value_ref, value_got_ref, history_ref,
    beta_ref, key_seen_ref, query_seen_ref, pulls_ref, weights_ref, taps_ref, out_ref, heads_ref,
):
    twist = twist_ref[0]
    row = lax.broadcasted_iota(jnp.int32, (ROWS, DK), 0)
    row_step = row % STEPS
    lane = lax.broadcasted_iota(jnp.int32, (ROWS, DK), 1)
    row_length = jnp.where(row < STEPS, lengths_ref[0], lengths_ref[1])
    live = row_step < row_length
    value_steps = steps_of(value_got_ref)
    for head in range(H):
        value = activate(
            value_ref, value_got_ref, value_steps, 2, head, history_ref, taps_ref, twist, row_step
        )
        base = beta_ref[head] * value - key_seen_ref[head]
        solved = base
        for _ in range(STEPS - 1):
            following = base
            for lag in range(1, STEPS):
                following = following - pulls_ref[lag - 1, head] * shift_rows(
                    solved, lag, row_step
                )
            solved = following
        out = query_seen_ref[head]
        for lag in range(STEPS):
            out = out + weights_ref[lag, head] * shift_rows(solved, lag, row_step)
        heads_ref[head] = jnp.where(live, out, 0.0)
    for quad in range(UNITS // 4):
        joined = []
        for pair in (2 * quad, 2 * quad + 1):
            first = heads_ref[slots_ref[2 * pair]]
            second = heads_ref[slots_ref[2 * pair + 1]]
            first = jnp.where(halves_ref[2 * pair] == 0, first, pltpu.roll(first, HALF, 1))
            second = jnp.where(halves_ref[2 * pair + 1] == 0, pltpu.roll(second, HALF, 1), second)
            joined.append(jnp.where(lane < HALF, first, second))
        out_ref[quad] = jnp.concatenate(joined, axis=0).astype(jnp.bfloat16)


def run_delta(slots, halves, lengths, queries, keys, values, history, twist, taps, state):
    smem = pl.BlockSpec(memory_space=pltpu.SMEM)
    vmem = pl.BlockSpec(memory_space=pltpu.VMEM)
    params = pltpu.CompilerParams(vmem_limit_bytes=32 * 1024 * 1024)
    per_head = jax.ShapeDtypeStruct((H, ROWS, DK), jnp.float32)
    lags = [
        jax.ShapeDtypeStruct((count, H, ROWS, DK), jnp.float32) for count in (STEPS - 1, STEPS)
    ]
    tap_blocks = jax.ShapeDtypeStruct((TAP_BLOCKS, TAPS, TAP_WIDTH), jnp.float32)
    prepared = pl.pallas_call(
        keys_kernel,
        out_shape=[per_head] * 3 + lags + [tap_blocks],
        in_specs=[smem] + [vmem] * 7 + [pl.BlockSpec(memory_space=pl.ANY)],
        out_specs=[vmem] * 6,
        scratch_shapes=[
            pltpu.VMEM(state.shape, jnp.float32),
            pltpu.SemaphoreType.DMA((STATE_COPIES,)),
        ],
        compiler_params=params,
        cost_estimate=pl.CostEstimate(flops=40_000_000, bytes_accessed=9_000_000, transcendentals=0),
        name="keys_part",
    )(twist, *queries, *keys, history, *taps, state)
    return pl.pallas_call(
        values_kernel,
        out_shape=jax.ShapeDtypeStruct((UNITS // 4, 2 * ROWS, DK), jnp.bfloat16),
        in_specs=[smem] * 4 + [vmem] * 9,
        out_specs=vmem,
        scratch_shapes=[pltpu.VMEM((H, ROWS, DK), jnp.float32)],
        compiler_params=params,
        cost_estimate=pl.CostEstimate(flops=4_000_000, bytes_accessed=2_000_000, transcendentals=0),
        name="values_part",
    )(slots, halves, lengths, twist, *values, history, *prepared)


def rows_kernel(
    depth, me_ref, slot_of_ref, tokens_hbm, mine_ref, theirs_ref, window_ref, sem
):
    me = me_ref[0]
    width = window_ref.shape[2]
    offset = me // 2 * (2 * depth)
    start = jnp.minimum(offset // DK * DK, D - width)
    columns = pl.ds(pl.multiple_of(start, DK), width)
    copy = pltpu.make_async_copy(tokens_hbm.at[:, :, columns], window_ref, sem)
    copy.start()
    shape = (mine_ref.shape[0], slot_of_ref.shape[1])
    row = lax.broadcasted_iota(jnp.int32, shape, 0)
    place = row // ROWS
    count = (shape[0] // ROWS).bit_length() - 1
    holder = jnp.zeros(shape, jnp.int32)
    for at in range(count):
        holder = holder + ((place >> (count - 1 - at)) & 1) * (2 << at)
    holder = jnp.bitwise_xor(holder, me)
    match = holder * LOCAL + row % ROWS // STEPS == slot_of_ref[...]
    copy.wait()
    window = window_ref[...].astype(jnp.float32)
    total = jnp.zeros((shape[0], width), jnp.float32)
    for step in range(STEPS):
        picker = jnp.where(match & (row % STEPS == step), 1.0, 0.0).astype(jnp.bfloat16)
        here = window[:, step, :].astype(jnp.bfloat16)
        total = total + jnp.dot(picker, here, preferred_element_type=jnp.float32)
    total = pltpu.roll(total, lax.rem(width - (offset - start), width), 1)
    low, high = total[:, :depth], total[:, depth : 2 * depth]
    first_core = me % 2 == 0
    mine_ref[...] = jnp.where(first_core, low, high).astype(jnp.bfloat16)
    theirs_ref[...] = jnp.where(first_core, high, low).astype(jnp.bfloat16)


def run_rows(me, slot_of, tokens, depth, chips):
    width = -(-(2 * depth + DK - 1) // DK) * DK
    out = jax.ShapeDtypeStruct((chips * ROWS, depth), jnp.bfloat16)
    vmem = pl.BlockSpec(memory_space=pltpu.VMEM)
    return pl.pallas_call(
        functools.partial(rows_kernel, depth),
        out_shape=[out, out],
        in_specs=[
            pl.BlockSpec(memory_space=pltpu.SMEM), vmem, pl.BlockSpec(memory_space=pltpu.HBM)
        ],
        out_specs=[vmem, vmem],
        scratch_shapes=[
            pltpu.VMEM((tokens.shape[0], STEPS, width), jnp.bfloat16),
            pltpu.SemaphoreType.DMA,
        ],
        compiler_params=pltpu.CompilerParams(vmem_limit_bytes=32 * 1024 * 1024),
        cost_estimate=pl.CostEstimate(flops=0, bytes_accessed=0, transcendentals=0),
        name="token_rows",
    )(me.reshape(1), slot_of.reshape(1, -1), tokens)


def product_kernel(first, count, mine_ref, theirs_ref, own_hbm, other_hbm, *refs):
    scratch, refs = refs[-3:], refs[:-3]
    (own_ref, other_ref, sems), gate_refs, out_refs = scratch, refs[: -2 * count], refs[-2 * count :]
    half = mine_ref.shape[0] // 2
    step = HEADS_WIDTH // WEIGHT_COPIES
    copies = []
    for at in range(count * WEIGHT_COPIES):
        source, target = pl.ds(first * HEADS_WIDTH + at * step, step), pl.ds(at * step, step)
        pair = [
            pltpu.make_async_copy(hbm.at[:, source], ref.at[:, target], sems.at[side, at])
            for side, (hbm, ref) in enumerate(((own_hbm, own_ref), (other_hbm, other_ref)))
        ]
        for copy in pair:
            copy.start()
        copies.append(pair)

    def product(own, other, dims):
        total = lax.dot_general(mine_ref[...], own, dims, preferred_element_type=jnp.float32)
        return total + lax.dot_general(
            theirs_ref[...], other, dims, preferred_element_type=jnp.float32
        )

    for part in range(count):
        totals = []
        for at in range(part * WEIGHT_COPIES, (part + 1) * WEIGHT_COPIES):
            for copy in copies[at]:
                copy.wait()
            columns = pl.ds(at * step, step)
            totals.append(
                product(own_ref[:, columns], other_ref[:, columns], (((1,), (0,)), ((), ())))
            )
        if gate_refs and part == 0:
            gates = product(gate_refs[0][...], gate_refs[1][...], (((1,), (1,)), ((), ())))
            totals += [gates, jnp.zeros((gates.shape[0], 2 * DK - gates.shape[1]), jnp.float32)]
        total = jnp.concatenate(totals, axis=1)
        out_refs[2 * part][...] = total[:half]
        pack_rows(total[half:], out_refs[2 * part + 1])


def run_product(mine, theirs, weights, first, count, gates=()):
    vmem, hbm = pl.BlockSpec(memory_space=pltpu.VMEM), pl.BlockSpec(memory_space=pl.ANY)
    half = mine.shape[0] // 2
    outs = []
    for part in range(count):
        width = HEADS_WIDTH + (len(gates) * DK if part == 0 else 0)
        outs.append(jax.ShapeDtypeStruct((half, width), jnp.float32))
        outs.append(jax.ShapeDtypeStruct((half, width + scale_lanes(width // DK)), jnp.int16))
    outs = pl.pallas_call(
        functools.partial(product_kernel, first, count),
        out_shape=outs,
        in_specs=[vmem, vmem, hbm, hbm] + [vmem] * len(gates),
        out_specs=[vmem] * len(outs),
        scratch_shapes=[pltpu.VMEM((mine.shape[1], count * HEADS_WIDTH), jnp.bfloat16)] * 2
        + [pltpu.SemaphoreType.DMA((2, count * WEIGHT_COPIES))],
        compiler_params=pltpu.CompilerParams(vmem_limit_bytes=56 * 1024 * 1024),
        cost_estimate=pl.CostEstimate(flops=0, bytes_accessed=0, transcendentals=0),
        name="partial_product",
    )(mine, theirs, *weights, *gates)
    return [outs[2 * part : 2 * part + 2] for part in range(count)]


def combine_kernel(kept_ref, got_ref, still_ref, packed_ref):
    half = still_ref.shape[0]
    steps = steps_of(got_ref)
    sent = []
    for block in range(kept_ref.shape[1] // DK):
        columns = pl.ds(block * DK, DK)
        total = kept_ref[:, columns] + unpack_block(got_ref, steps, block)
        still_ref[:, columns] = total[:half]
        sent.append(total[half:])
    sent = jnp.concatenate(sent, axis=1)
    pack_rows(fold_rows(sent) if half == ROWS else sent, packed_ref)


def run_combine(kept, got):
    vmem = pl.BlockSpec(memory_space=pltpu.VMEM)
    half, width = kept.shape[0] // 2, kept.shape[1]
    rows, packed = (2 * ROWS, width // 2) if half == ROWS else (half, width)
    packed = (rows, packed + scale_lanes(packed // DK))
    return pl.pallas_call(
        combine_kernel,
        out_shape=[
            jax.ShapeDtypeStruct((half, width), jnp.float32),
            jax.ShapeDtypeStruct(packed, jnp.int16),
        ],
        in_specs=[vmem] * 2,
        out_specs=[vmem] * 2,
        compiler_params=pltpu.CompilerParams(vmem_limit_bytes=32 * 1024 * 1024),
        cost_estimate=pl.CostEstimate(flops=0, bytes_accessed=0, transcendentals=0),
        name="combine",
    )(kept, got)


def swap(value, bit, devices):
    return lax.ppermute(value, "heads", [(i, i ^ bit) for i in range(devices)])


def on_device(
    tokens,
    qkv_weight,
    gate_weight,
    conv_weight,
    delta_state,
    conv_state,
    old_heads,
    new_units,
    slot_of,
    lengths,
):
    devices = lax.axis_size("heads")
    me = lax.axis_index("heads")
    per_device = UNITS // devices
    depth = qkv_weight.shape[0]
    row_count = tokens.shape[0]
    chips = devices // 2

    bits = [1 << b for b in range(1, devices.bit_length() - 1)]
    steps = jnp.arange(STEPS, dtype=jnp.int32)
    offered = (slot_of[:, None] * STEPS + steps[None, :]).reshape(-1)

    mine, theirs = run_rows(me, slot_of, tokens, depth, chips)

    weights = (qkv_weight, swap(qkv_weight, 1, devices))
    gate_columns = gate_weight.T
    gates = (gate_columns, swap(gate_columns, 1, devices))

    tie = lambda *values: lax.optimization_barrier(values)

    ride = conv_weight.shape[1] == 2 * TAP_WIDTH and len(bits) == 3
    if ride:
        taps = jnp.concatenate([conv_weight[:, :TAP_WIDTH], conv_weight[:, TAP_WIDTH:]], axis=0)
        taps = jnp.concatenate([taps, swap(taps, 1, devices)], axis=0)
    else:
        taps = lax.all_gather(conv_weight, "heads", axis=1, tiled=True)
        blocks = [block for bit in (0, 4) for block in range(TAP_BLOCKS) if block & 4 == bit]
        taps = [taps[:, block * TAP_WIDTH : (block + 1) * TAP_WIDTH] for block in blocks]
        taps = jnp.concatenate(taps, axis=0)
    (queries,) = run_product(mine, theirs, weights, 0, 1)
    mine, *queries = tie(mine, *queries)
    keys, values = run_product(mine, theirs, weights, 1, 2, gates)

    lengths, old_heads, new_units, carried, *values = tie(
        lengths, old_heads, new_units, conv_state, *values
    )
    old_slots, halves = unit_tables(old_heads, new_units)
    my_rows = me * LOCAL + jnp.arange(LOCAL, dtype=jnp.int32)
    my_lengths = jnp.sum(
        jnp.where(slot_of[None, :] == my_rows[:, None], lengths[None, :], 0), axis=1
    )
    blank = jnp.zeros((1, carried.shape[2]), jnp.float32)
    history = jnp.concatenate([blank, carried[1], blank, carried[0]], axis=0)
    got = [swap(queries[1], bits[0], devices), swap(keys[1], bits[0], devices)]
    got[0], history, my_lengths, old_slots, halves = tie(
        got[0], history, my_lengths, old_slots, halves
    )
    if ride:
        taps, *values = tie(taps, *values)
        taps = jnp.concatenate([taps, swap(taps, 4, devices)], axis=0)
        got[0], values[1], taps = tie(got[0], values[1], taps)
        taps = jnp.concatenate([taps, swap(taps, 8, devices)], axis=0)
        got[1], taps = tie(got[1], taps)
        twist, taps = me.reshape(1), (taps, swap(taps, 2, devices))
    else:
        half = TAP_BLOCKS // 2 * TAPS
        twist, taps = jnp.zeros(1, jnp.int32), (taps[:half], taps[half:])
    got.append(swap(values[1], bits[0], devices))
    kept = [queries[0], keys[0], values[0]]
    for bit in bits[1:]:
        for at in range(3):
            if at:
                got[at], kept[at - 1] = tie(got[at], kept[at - 1])
            kept[at], packed = run_combine(kept[at], got[at])
            got[at] = swap(packed, bit, devices)
    queries, keys, values = zip(kept, got)

    local_out = run_delta(
        old_slots, halves, my_lengths, queries, keys, values, history, twist, taps, delta_state
    )

    placer = (offered[:, None] == jnp.arange(row_count * STEPS, dtype=jnp.int32)[None, :]).astype(
        jnp.bfloat16
    )
    if per_device % 2 == 0:
        pairs = per_device // 2
        sending = local_out.reshape(devices, pairs * ROWS, DK)
        got = lax.all_to_all(sending, "heads", split_axis=0, concat_axis=0, tiled=True)
        got = got.reshape(devices, pairs, ROWS, DK)
        got = jnp.concatenate([got[:, pair] for pair in range(pairs)], axis=-1)
        got = got.reshape(devices * ROWS, pairs * DK)
    else:
        units = local_out.reshape(UNITS // 2, ROWS, 2, HALF).transpose(0, 2, 1, 3)
        sending = units.reshape(devices, per_device * ROWS, HALF)
        got = lax.all_to_all(sending, "heads", split_axis=0, concat_axis=0, tiled=True)
        got = got.reshape(devices, per_device, ROWS, HALF).transpose(0, 2, 1, 3)
        got = got.reshape(devices * ROWS, per_device * HALF)
    outputs = jnp.dot(placer, got, preferred_element_type=jnp.float32).astype(jnp.bfloat16)
    return outputs.reshape(row_count, STEPS, per_device * HALF)


def solution(mesh):
    in_specs = (
        P("groups", None, None),
        P(("groups", "heads"), None),
        P(("groups", "heads"), None),
        P("groups", "heads"),
        P(("groups", "heads"), None, None, None),
        P(("groups", "heads"), None, None),
        P(),
        P(),
        P("groups"),
        P("groups"),
    )
    out_specs = P("groups", None, "heads")
    return jax.shard_map(
        on_device, mesh=mesh, in_specs=in_specs, out_specs=out_specs, check_vma=False
    )
```

```python
import functools

import jax
import jax.numpy as jnp
from jax import lax
from jax.experimental import pallas as pl
from jax.experimental.pallas import tpu as pltpu
from jax.sharding import PartitionSpec as P

D = 2304
H = 32
DK = 128
TAPS = 4
STEPS = 4
HALF = 64
UNITS = 64
LOCAL = 2
ROWS = LOCAL * STEPS
HEADS_WIDTH = H * DK
LEVELS = 32767.0
STATE_COPIES = 4
TAP_WIDTH = 384
TAP_BLOCKS = 3 * HEADS_WIDTH // TAP_WIDTH


norm_eps = 1e-06


def unit_tables(old_heads, new_units):
    positions = jnp.arange(H, dtype=jnp.int32)
    inverse = jnp.sum(
        jnp.where(old_heads[None, :] == positions[:, None], positions[None, :], 0), axis=1
    )
    heads_of = new_units // 2
    halves = new_units % 2
    old_slots = jnp.sum(
        jnp.where(heads_of[:, None] == positions[None, :], inverse[None, :], 0), axis=1
    )
    return (old_slots, halves)


def shift_rows(value, lag, row_step):
    if lag == 0:
        return value
    moved = pltpu.roll(value, lag, 0)
    return jnp.where(row_step >= lag, moved, 0.0)


def lane_sum(value):
    return jnp.sum(value, axis=-1, keepdims=True)


def unit_length(value):
    return value * lax.rsqrt(lane_sum(value * value) + norm_eps)


def scale_lanes(blocks):
    return -(-blocks // HALF) * DK


def pack_rows(total, packed_ref):
    rows, width = total.shape
    blocks = width // DK
    lanes = scale_lanes(blocks)
    lane = lax.broadcasted_iota(jnp.int32, (rows, lanes), 1)
    scales = jnp.zeros((rows, lanes), jnp.float32)
    for block in range(blocks):
        part = total[:, block * DK : (block + 1) * DK]
        top = jnp.max(jnp.abs(part), axis=-1, keepdims=True) + 1e-30
        exponent = jnp.ceil(jnp.log2(top))
        mantissa = jnp.ceil(jnp.minimum(top * jnp.exp2(-exponent) * LEVELS, LEVELS))
        factor = LEVELS * LEVELS * jnp.exp2(-exponent) / mantissa
        coded = jnp.clip(jnp.floor(part * factor + 0.5), -LEVELS, LEVELS)
        packed_ref[:, block * DK : (block + 1) * DK] = coded.astype(jnp.int32).astype(jnp.int16)
        scales = jnp.where(lane == block, mantissa, scales)
        scales = jnp.where(lane == lanes // 2 + block, exponent, scales)
    packed_ref[:, width:] = scales.astype(jnp.int32).astype(jnp.int16)


def to_float(coded):
    return coded.astype(jnp.int32).astype(jnp.float32)


def steps_of(packed_ref):
    lanes = DK if packed_ref.shape[1] <= (HALF + 1) * DK else 2 * DK
    scales = to_float(packed_ref[:, packed_ref.shape[1] - lanes :])
    exponents = pltpu.roll(scales, lanes // 2, 1)
    return scales * jnp.exp2(exponents) * (1.0 / (LEVELS * LEVELS))


def unpack_block(packed_ref, steps, block):
    return to_float(packed_ref[:, block * DK : (block + 1) * DK]) * steps[:, block : block + 1]


def fold_rows(value):
    half = value.shape[1] // 2
    return jnp.concatenate([value[:, :half], value[:, half:]], axis=0)


def received(kept_ref, got_ref, steps, block):
    half = kept_ref.shape[1] // DK // 2
    rows = unpack_block(got_ref, steps, block % half)
    rows = rows[:ROWS] if block < half else rows[ROWS:]
    return kept_ref[:, block * DK : (block + 1) * DK] + rows


def tap_block(block, me):
    other = jnp.bitwise_xor(block // 2, me)
    place = (other & 1) + ((other >> 2) & 3) * 2 + ((other >> 1) & 1) * 8
    return place * 2 + block % 2


def activate(kept_ref, got_ref, steps, part, head, history_ref, taps_ref, twist, row_step):
    fresh = received(kept_ref, got_ref, steps, head)
    column = part * HEADS_WIDTH + head * DK
    carried = history_ref[:, column : column + DK]
    taps = taps_ref[tap_block(column // TAP_WIDTH, twist)]
    inner = column % TAP_WIDTH
    total = taps[TAPS - 1 :, inner : inner + DK] * fresh
    for lag in range(1, TAPS):
        source = jnp.where(row_step >= STEPS - lag, carried, fresh)
        tap = taps[TAPS - 1 - lag : TAPS - lag, inner : inner + DK]
        total = total + tap * pltpu.roll(source, lag, 0)
    return total / (1.0 + jnp.exp(-total))


def keys_kernel(
    twist_ref, query_ref, query_got_ref, key_ref, key_got_ref, history_ref, near_ref, far_ref,
    state_hbm, key_seen_ref, query_seen_ref, pulls_ref, weights_ref, taps_ref, state_ref, sems,
):
    per_copy = H // STATE_COPIES
    copies = []
    for at in range(STATE_COPIES):
        some = pl.ds(at * per_copy, per_copy)
        copies.append(
            pltpu.make_async_copy(state_hbm.at[:, some], state_ref.at[:, some], sems.at[at])
        )
        copies[-1].start()
    twist = twist_ref[0]
    half = TAP_BLOCKS // 2
    for at in range(TAP_BLOCKS):
        source = near_ref if at < half else far_ref
        if at % 4 == 0:
            some = source[at % half * TAPS : (at % half + 4) * TAPS, :].astype(jnp.float32)
        taps_ref[at] = some[at % 4 * TAPS : (at % 4 + 1) * TAPS]
    row = lax.broadcasted_iota(jnp.int32, (ROWS, DK), 0)
    row_step = row % STEPS
    query_steps, key_steps = steps_of(query_got_ref), steps_of(key_got_ref)
    for head in range(H):
        key = unit_length(
            activate(
                key_ref, key_got_ref, key_steps, 1, head, history_ref, taps_ref, twist, row_step
            )
        )
        query = unit_length(
            activate(
                query_ref, query_got_ref, query_steps, 0, head, history_ref, taps_ref, twist,
                row_step,
            )
        )
        both = jnp.concatenate([key, query], axis=0)
        if head % per_copy == 0:
            copies[head // per_copy].wait()
        both_high = both.astype(jnp.bfloat16)
        both_low = (both - both_high.astype(jnp.float32)).astype(jnp.bfloat16)
        stacked = jnp.concatenate([both_high, both_low], axis=0)
        seen = []
        for r in range(LOCAL):
            state = state_ref[r, head]
            high = state.astype(jnp.bfloat16)
            low = (state - high.astype(jnp.float32)).astype(jnp.bfloat16)
            main = jnp.dot(stacked, high, preferred_element_type=jnp.float32)
            rest = jnp.dot(both_high, low, preferred_element_type=jnp.float32)
            seen.append(main[: 2 * ROWS] + main[2 * ROWS :] + rest)
        key_seen_ref[head] = jnp.where(row < STEPS, seen[0][:ROWS], seen[1][:ROWS])
        query_seen_ref[head] = jnp.where(row < STEPS, seen[0][ROWS:], seen[1][ROWS:])
        for lag in range(STEPS):
            moved_key = shift_rows(key, lag, row_step)
            if lag:
                pulls_ref[lag - 1, head] = jnp.broadcast_to(lane_sum(key * moved_key), (ROWS, DK))
            weights_ref[lag, head] = jnp.broadcast_to(lane_sum(query * moved_key), (ROWS, DK))


def values_kernel(
    slots_ref, halves_ref, lengths_ref, twist_ref, value_ref, value_got_ref, history_ref,
    key_seen_ref, query_seen_ref, pulls_ref, weights_ref, taps_ref, out_ref, heads_ref,
):
    twist = twist_ref[0]
    row = lax.broadcasted_iota(jnp.int32, (ROWS, DK), 0)
    row_step = row % STEPS
    lane = lax.broadcasted_iota(jnp.int32, (ROWS, DK), 1)
    row_length = jnp.where(row < STEPS, lengths_ref[0], lengths_ref[1])
    live = row_step < row_length
    value_steps = steps_of(value_got_ref)
    gates = received(value_ref, value_got_ref, value_steps, H)
    for head in range(H):
        value = activate(
            value_ref, value_got_ref, value_steps, 2, head, history_ref, taps_ref, twist, row_step
        )
        beta_logit = jnp.broadcast_to(gates[:, head : head + 1], (ROWS, DK))
        decay_logit = jnp.broadcast_to(gates[:, H + head : H + head + 1], (ROWS, DK))
        beta = 1.0 / (1.0 + jnp.exp(-beta_logit))
        decay = 1.0 / (1.0 + jnp.exp(decay_logit))
        fades = [jnp.ones_like(decay), decay]
        for lag in range(2, STEPS + 1):
            earlier = pltpu.roll(decay, lag - 1, 0)
            fades.append(jnp.where(row_step >= lag - 1, fades[-1] * earlier, fades[-1]))
        base = beta * (value - fades[STEPS] * key_seen_ref[head])
        pulls = [
            beta * fades[lag] * pulls_ref[lag - 1, head] if lag else None for lag in range(STEPS)
        ]
        solved = base
        for _ in range(STEPS - 1):
            following = base
            for lag in range(1, STEPS):
                following = following - pulls[lag] * shift_rows(solved, lag, row_step)
            solved = following
        out = fades[STEPS] * query_seen_ref[head]
        for lag in range(STEPS):
            weight = fades[lag] * weights_ref[lag, head]
            out = out + weight * shift_rows(solved, lag, row_step)
        heads_ref[head] = jnp.where(live, out, 0.0)
    for quad in range(UNITS // 4):
        joined = []
        for pair in (2 * quad, 2 * quad + 1):
            first = heads_ref[slots_ref[2 * pair]]
            second = heads_ref[slots_ref[2 * pair + 1]]
            first = jnp.where(halves_ref[2 * pair] == 0, first, pltpu.roll(first, HALF, 1))
            second = jnp.where(halves_ref[2 * pair + 1] == 0, pltpu.roll(second, HALF, 1), second)
            joined.append(jnp.where(lane < HALF, first, second))
        out_ref[quad] = jnp.concatenate(joined, axis=0).astype(jnp.bfloat16)


def run_delta(slots, halves, lengths, queries, keys, values, history, twist, taps, state):
    smem = pl.BlockSpec(memory_space=pltpu.SMEM)
    vmem = pl.BlockSpec(memory_space=pltpu.VMEM)
    params = pltpu.CompilerParams(vmem_limit_bytes=32 * 1024 * 1024)
    per_head = jax.ShapeDtypeStruct((H, ROWS, DK), jnp.float32)
    lags = [
        jax.ShapeDtypeStruct((count, H, ROWS, DK), jnp.float32) for count in (STEPS - 1, STEPS)
    ]
    tap_blocks = jax.ShapeDtypeStruct((TAP_BLOCKS, TAPS, TAP_WIDTH), jnp.float32)
    prepared = pl.pallas_call(
        keys_kernel,
        out_shape=[per_head] * 2 + lags + [tap_blocks],
        in_specs=[smem] + [vmem] * 7 + [pl.BlockSpec(memory_space=pl.ANY)],
        out_specs=[vmem] * 5,
        scratch_shapes=[
            pltpu.VMEM(state.shape, jnp.float32),
            pltpu.SemaphoreType.DMA((STATE_COPIES,)),
        ],
        compiler_params=params,
        cost_estimate=pl.CostEstimate(flops=40_000_000, bytes_accessed=9_000_000, transcendentals=0),
        name="keys_part",
    )(twist, *queries, *keys, history, *taps, state)
    return pl.pallas_call(
        values_kernel,
        out_shape=jax.ShapeDtypeStruct((UNITS // 4, 2 * ROWS, DK), jnp.bfloat16),
        in_specs=[smem] * 4 + [vmem] * 8,
        out_specs=vmem,
        scratch_shapes=[pltpu.VMEM((H, ROWS, DK), jnp.float32)],
        compiler_params=params,
        cost_estimate=pl.CostEstimate(flops=4_000_000, bytes_accessed=2_000_000, transcendentals=0),
        name="values_part",
    )(slots, halves, lengths, twist, *values, history, *prepared)


def rows_kernel(
    depth, me_ref, slot_of_ref, tokens_hbm, weight_hbm, mine_ref, theirs_ref, weight_ref,
    window_ref, sem, weight_sem,
):
    me = me_ref[0]
    width = window_ref.shape[2]
    offset = me // 2 * (2 * depth)
    start = jnp.minimum(offset // DK * DK, D - width)
    columns = pl.ds(pl.multiple_of(start, DK), width)
    copy = pltpu.make_async_copy(tokens_hbm.at[:, :, columns], window_ref, sem)
    copy.start()
    weight_copy = pltpu.make_async_copy(weight_hbm, weight_ref, weight_sem)
    weight_copy.start()
    shape = (mine_ref.shape[0], slot_of_ref.shape[1])
    row = lax.broadcasted_iota(jnp.int32, shape, 0)
    place = row // ROWS
    count = (shape[0] // ROWS).bit_length() - 1
    holder = jnp.zeros(shape, jnp.int32)
    for at in range(count):
        holder = holder + ((place >> (count - 1 - at)) & 1) * (2 << at)
    holder = jnp.bitwise_xor(holder, me)
    match = holder * LOCAL + row % ROWS // STEPS == slot_of_ref[...]
    copy.wait()
    window = window_ref[...].astype(jnp.float32)
    total = jnp.zeros((shape[0], width), jnp.float32)
    for step in range(STEPS):
        picker = jnp.where(match & (row % STEPS == step), 1.0, 0.0).astype(jnp.bfloat16)
        here = window[:, step, :].astype(jnp.bfloat16)
        total = total + jnp.dot(picker, here, preferred_element_type=jnp.float32)
    total = pltpu.roll(total, lax.rem(width - (offset - start), width), 1)
    low, high = total[:, :depth], total[:, depth : 2 * depth]
    first_core = me % 2 == 0
    mine_ref[...] = jnp.where(first_core, low, high).astype(jnp.bfloat16)
    theirs_ref[...] = jnp.where(first_core, high, low).astype(jnp.bfloat16)
    weight_copy.wait()


def run_rows(me, slot_of, tokens, weight, chips):
    depth = weight.shape[0]
    width = -(-(2 * depth + DK - 1) // DK) * DK
    out = jax.ShapeDtypeStruct((chips * ROWS, depth), jnp.bfloat16)
    vmem = pl.BlockSpec(memory_space=pltpu.VMEM)
    return pl.pallas_call(
        functools.partial(rows_kernel, depth),
        out_shape=[out, out, jax.ShapeDtypeStruct(weight.shape, weight.dtype)],
        in_specs=[
            pl.BlockSpec(memory_space=pltpu.SMEM), vmem, pl.BlockSpec(memory_space=pl.ANY),
            pl.BlockSpec(memory_space=pl.ANY),
        ],
        out_specs=[vmem] * 3,
        scratch_shapes=[
            pltpu.VMEM((tokens.shape[0], STEPS, width), jnp.bfloat16),
            pltpu.SemaphoreType.DMA,
            pltpu.SemaphoreType.DMA,
        ],
        compiler_params=pltpu.CompilerParams(vmem_limit_bytes=32 * 1024 * 1024),
        cost_estimate=pl.CostEstimate(flops=0, bytes_accessed=0, transcendentals=0),
        name="token_rows",
    )(me.reshape(1), slot_of.reshape(1, -1), tokens, weight)


def product_kernel(skipped, *refs):
    mine_ref, theirs_ref, block_ref, other_ref, *refs = refs[skipped:]
    gate_refs, (kept_ref, packed_ref) = refs[:-2], refs[-2:]
    half = mine_ref.shape[0] // 2

    def product(own, other, dims):
        total = lax.dot_general(mine_ref[...], own, dims, preferred_element_type=jnp.float32)
        return total + lax.dot_general(
            theirs_ref[...], other, dims, preferred_element_type=jnp.float32
        )

    total = product(block_ref[...], other_ref[...], (((1,), (0,)), ((), ())))
    if gate_refs:
        gates = product(gate_refs[0][...], gate_refs[1][...], (((1,), (1,)), ((), ())))
        zeros = jnp.zeros((gates.shape[0], 2 * DK - gates.shape[1]), jnp.float32)
        total = jnp.concatenate([total, gates, zeros], axis=1)
    kept_ref[...] = total[:half]
    pack_rows(total[half:], packed_ref)


def run_product(mine, theirs, weights, part, gates=(), earlier=()):
    vmem = pl.BlockSpec(memory_space=pltpu.VMEM)
    block = pl.BlockSpec((mine.shape[1], HEADS_WIDTH), lambda i: (0, part))
    half = mine.shape[0] // 2
    width = HEADS_WIDTH + len(gates) * DK
    return pl.pallas_call(
        functools.partial(product_kernel, len(earlier)),
        grid=(1,),
        out_shape=[
            jax.ShapeDtypeStruct((half, width), jnp.float32),
            jax.ShapeDtypeStruct((half, width + scale_lanes(width // DK)), jnp.int16),
        ],
        in_specs=[pl.BlockSpec(memory_space=pl.ANY)] * len(earlier)
        + [vmem, vmem, block, block]
        + [vmem] * len(gates),
        out_specs=[vmem] * 2,
        compiler_params=pltpu.CompilerParams(vmem_limit_bytes=32 * 1024 * 1024),
        cost_estimate=pl.CostEstimate(flops=0, bytes_accessed=0, transcendentals=0),
        name="partial_product",
    )(*earlier, mine, theirs, *weights, *gates)


def combine_kernel(kept_ref, got_ref, still_ref, packed_ref):
    half = still_ref.shape[0]
    steps = steps_of(got_ref)
    sent = []
    for block in range(kept_ref.shape[1] // DK):
        columns = pl.ds(block * DK, DK)
        total = kept_ref[:, columns] + unpack_block(got_ref, steps, block)
        still_ref[:, columns] = total[:half]
        sent.append(total[half:])
    sent = jnp.concatenate(sent, axis=1)
    pack_rows(fold_rows(sent) if half == ROWS else sent, packed_ref)


def run_combine(kept, got):
    vmem = pl.BlockSpec(memory_space=pltpu.VMEM)
    half, width = kept.shape[0] // 2, kept.shape[1]
    rows, packed = (2 * ROWS, width // 2) if half == ROWS else (half, width)
    packed = (rows, packed + scale_lanes(packed // DK))
    return pl.pallas_call(
        combine_kernel,
        out_shape=[
            jax.ShapeDtypeStruct((half, width), jnp.float32),
            jax.ShapeDtypeStruct(packed, jnp.int16),
        ],
        in_specs=[vmem] * 2,
        out_specs=[vmem] * 2,
        compiler_params=pltpu.CompilerParams(vmem_limit_bytes=32 * 1024 * 1024),
        cost_estimate=pl.CostEstimate(flops=0, bytes_accessed=0, transcendentals=0),
        name="combine",
    )(kept, got)


def swap(value, bit, devices):
    return lax.ppermute(value, "heads", [(i, i ^ bit) for i in range(devices)])


def on_device(
    tokens,
    qkv_weight,
    gate_weight,
    conv_weight,
    delta_state,
    conv_state,
    old_heads,
    new_units,
    slot_of,
    lengths,
):
    devices = lax.axis_size("heads")
    me = lax.axis_index("heads")
    per_device = UNITS // devices
    row_count = tokens.shape[0]
    chips = devices // 2

    bits = [1 << b for b in range(1, devices.bit_length() - 1)]
    steps = jnp.arange(STEPS, dtype=jnp.int32)
    offered = (slot_of[:, None] * STEPS + steps[None, :]).reshape(-1)

    mine, theirs, near_weight = run_rows(me, slot_of, tokens, qkv_weight, chips)

    weights = (near_weight, swap(qkv_weight, 1, devices))
    gate_columns = gate_weight.T
    gates = (gate_columns, swap(gate_columns, 1, devices))

    tie = lambda *values: lax.optimization_barrier(values)

    ride = conv_weight.shape[1] == 2 * TAP_WIDTH and len(bits) == 3
    if ride:
        taps = jnp.concatenate([conv_weight[:, :TAP_WIDTH], conv_weight[:, TAP_WIDTH:]], axis=0)
        far = swap(taps, 1, devices)
    else:
        taps = lax.all_gather(conv_weight, "heads", axis=1, tiled=True)
        blocks = [block for bit in (0, 4) for block in range(TAP_BLOCKS) if block & 4 == bit]
        taps = [taps[:, block * TAP_WIDTH : (block + 1) * TAP_WIDTH] for block in blocks]
        taps = jnp.concatenate(taps, axis=0)
    queries = run_product(mine, theirs, weights, 0)
    keys = run_product(mine, theirs, weights, 1, earlier=queries[:1])
    values = run_product(mine, theirs, weights, 2, gates, earlier=keys[:1])

    lengths, old_heads, new_units, carried, *values = tie(
        lengths, old_heads, new_units, conv_state, *values
    )
    old_slots, halves = unit_tables(old_heads, new_units)
    my_rows = me * LOCAL + jnp.arange(LOCAL, dtype=jnp.int32)
    my_lengths = jnp.sum(
        jnp.where(slot_of[None, :] == my_rows[:, None], lengths[None, :], 0), axis=1
    )
    blank = jnp.zeros((1, carried.shape[2]), jnp.float32)
    history = jnp.concatenate([blank, carried[1], blank, carried[0]], axis=0)
    kept = [chunk[0] for chunk in (queries, keys, values)]
    got = [swap(chunk[1], bits[0], devices) for chunk in (queries, keys, values)]
    for level, bit in enumerate(bits[1:]):
        for at in range(3):
            kept[at], packed = run_combine(kept[at], got[at])
            got[at] = swap(packed, bit, devices)
            if ride and level == 0 and at == 0:
                kept[0], taps, far = tie(kept[0], taps, far)
                taps = jnp.concatenate([taps, far], axis=0)
                taps = jnp.concatenate([taps, swap(taps, 4, devices)], axis=0)
    if ride:
        taps = jnp.concatenate([taps, swap(taps, 8, devices)], axis=0)
        twist, taps = me.reshape(1), (taps, swap(taps, 2, devices))
    else:
        half = TAP_BLOCKS // 2 * TAPS
        twist, taps = jnp.zeros(1, jnp.int32), (taps[:half], taps[half:])
    queries, keys, values = zip(kept, got)

    local_out = run_delta(
        old_slots, halves, my_lengths, queries, keys, values, history, twist, taps, delta_state
    )

    placer = (offered[:, None] == jnp.arange(row_count * STEPS, dtype=jnp.int32)[None, :]).astype(
        jnp.bfloat16
    )
    if per_device % 2 == 0:
        pairs = per_device // 2
        sending = local_out.reshape(devices, pairs * ROWS, DK)
        got = lax.all_to_all(sending, "heads", split_axis=0, concat_axis=0, tiled=True)
        got = got.reshape(devices, pairs, ROWS, DK)
        got = jnp.concatenate([got[:, pair] for pair in range(pairs)], axis=-1)
        got = got.reshape(devices * ROWS, pairs * DK)
    else:
        units = local_out.reshape(UNITS // 2, ROWS, 2, HALF).transpose(0, 2, 1, 3)
        sending = units.reshape(devices, per_device * ROWS, HALF)
        got = lax.all_to_all(sending, "heads", split_axis=0, concat_axis=0, tiled=True)
        got = got.reshape(devices, per_device, ROWS, HALF).transpose(0, 2, 1, 3)
        got = got.reshape(devices * ROWS, per_device * HALF)
    outputs = jnp.dot(placer, got, preferred_element_type=jnp.float32).astype(jnp.bfloat16)
    return outputs.reshape(row_count, STEPS, per_device * HALF)


def solution(mesh):
    in_specs = (
        P("groups", None, None),
        P(("groups", "heads"), None),
        P(("groups", "heads"), None),
        P("groups", "heads"),
        P(("groups", "heads"), None, None, None),
        P(("groups", "heads"), None, None),
        P(),
        P(),
        P("groups"),
        P("groups"),
    )
    out_specs = P("groups", None, "heads")
    return jax.shard_map(
        on_device, mesh=mesh, in_specs=in_specs, out_specs=out_specs, check_vma=False
    )
```

```python
import functools

import jax
import jax.numpy as jnp
from jax import lax
from jax.experimental import pallas as pl
from jax.experimental.pallas import tpu as pltpu
from jax.sharding import PartitionSpec as P

D = 2304
H = 32
DK = 128
TAPS = 4
STEPS = 4
HALF = 64
UNITS = 64
LOCAL = 2
ROWS = LOCAL * STEPS
HEADS_WIDTH = H * DK
LEVELS = 32767.0
STATE_COPIES = 4
TAP_WIDTH = 384
TAP_BLOCKS = 3 * HEADS_WIDTH // TAP_WIDTH


norm_eps = 1e-06


def unit_tables(old_heads, new_units):
    positions = jnp.arange(H, dtype=jnp.int32)
    inverse = jnp.sum(
        jnp.where(old_heads[None, :] == positions[:, None], positions[None, :], 0), axis=1
    )
    heads_of = new_units // 2
    halves = new_units % 2
    old_slots = jnp.sum(
        jnp.where(heads_of[:, None] == positions[None, :], inverse[None, :], 0), axis=1
    )
    return (old_slots, halves)


def shift_rows(value, lag, row_step):
    if lag == 0:
        return value
    moved = pltpu.roll(value, lag, 0)
    return jnp.where(row_step >= lag, moved, 0.0)


def lane_sum(value):
    return jnp.sum(value, axis=-1, keepdims=True)


def unit_length(value):
    return value * lax.rsqrt(lane_sum(value * value) + norm_eps)


def scale_lanes(blocks):
    return -(-blocks // HALF) * DK


def pack_rows(total, packed_ref):
    rows, width = total.shape
    blocks = width // DK
    lanes = scale_lanes(blocks)
    lane = lax.broadcasted_iota(jnp.int32, (rows, lanes), 1)
    scales = jnp.zeros((rows, lanes), jnp.float32)
    for block in range(blocks):
        part = total[:, block * DK : (block + 1) * DK]
        top = jnp.max(jnp.abs(part), axis=-1, keepdims=True) + 1e-30
        exponent = jnp.ceil(jnp.log2(top))
        mantissa = jnp.ceil(jnp.minimum(top * jnp.exp2(-exponent) * LEVELS, LEVELS))
        factor = LEVELS * LEVELS * jnp.exp2(-exponent) / mantissa
        coded = jnp.clip(jnp.floor(part * factor + 0.5), -LEVELS, LEVELS)
        packed_ref[:, block * DK : (block + 1) * DK] = coded.astype(jnp.int32).astype(jnp.int16)
        scales = jnp.where(lane == block, mantissa, scales)
        scales = jnp.where(lane == lanes // 2 + block, exponent, scales)
    packed_ref[:, width:] = scales.astype(jnp.int32).astype(jnp.int16)


def to_float(coded):
    return coded.astype(jnp.int32).astype(jnp.float32)


def steps_of(packed_ref):
    lanes = DK if packed_ref.shape[1] <= (HALF + 1) * DK else 2 * DK
    scales = to_float(packed_ref[:, packed_ref.shape[1] - lanes :])
    exponents = pltpu.roll(scales, lanes // 2, 1)
    return scales * jnp.exp2(exponents) * (1.0 / (LEVELS * LEVELS))


def unpack_block(packed_ref, steps, block):
    return to_float(packed_ref[:, block * DK : (block + 1) * DK]) * steps[:, block : block + 1]


def fold_rows(value):
    half = value.shape[1] // 2
    return jnp.concatenate([value[:, :half], value[:, half:]], axis=0)


def received(kept_ref, got_ref, steps, block):
    half = kept_ref.shape[1] // DK // 2
    rows = unpack_block(got_ref, steps, block % half)
    rows = rows[:ROWS] if block < half else rows[ROWS:]
    return kept_ref[:, block * DK : (block + 1) * DK] + rows


def tap_block(block, me):
    other = jnp.bitwise_xor(block // 2, me)
    place = (other & 1) + ((other >> 2) & 3) * 2 + ((other >> 1) & 1) * 8
    return place * 2 + block % 2


def activate(kept_ref, got_ref, steps, part, head, history_ref, taps_ref, twist, row_step):
    fresh = received(kept_ref, got_ref, steps, head)
    column = part * HEADS_WIDTH + head * DK
    carried = history_ref[:, column : column + DK]
    taps = taps_ref[tap_block(column // TAP_WIDTH, twist)]
    inner = column % TAP_WIDTH
    total = taps[TAPS - 1 :, inner : inner + DK] * fresh
    for lag in range(1, TAPS):
        source = jnp.where(row_step >= STEPS - lag, carried, fresh)
        tap = taps[TAPS - 1 - lag : TAPS - lag, inner : inner + DK]
        total = total + tap * pltpu.roll(source, lag, 0)
    return total / (1.0 + jnp.exp(-total))


def keys_kernel(
    twist_ref, query_ref, query_got_ref, key_ref, key_got_ref, history_ref, near_ref, far_ref,
    state_hbm, key_seen_ref, query_seen_ref, pulls_ref, weights_ref, taps_ref, state_ref, sems,
):
    per_copy = H // STATE_COPIES
    copies = []
    for at in range(STATE_COPIES):
        some = pl.ds(at * per_copy, per_copy)
        copies.append(
            pltpu.make_async_copy(state_hbm.at[:, some], state_ref.at[:, some], sems.at[at])
        )
        copies[-1].start()
    twist = twist_ref[0]
    half = TAP_BLOCKS // 2
    for at in range(TAP_BLOCKS):
        source = near_ref if at < half else far_ref
        if at % 4 == 0:
            some = source[at % half * TAPS : (at % half + 4) * TAPS, :].astype(jnp.float32)
        taps_ref[at] = some[at % 4 * TAPS : (at % 4 + 1) * TAPS]
    row = lax.broadcasted_iota(jnp.int32, (ROWS, DK), 0)
    row_step = row % STEPS
    query_steps, key_steps = steps_of(query_got_ref), steps_of(key_got_ref)
    for head in range(H):
        key = unit_length(
            activate(
                key_ref, key_got_ref, key_steps, 1, head, history_ref, taps_ref, twist, row_step
            )
        )
        query = unit_length(
            activate(
                query_ref, query_got_ref, query_steps, 0, head, history_ref, taps_ref, twist,
                row_step,
            )
        )
        both = jnp.concatenate([key, query], axis=0)
        if head % per_copy == 0:
            copies[head // per_copy].wait()
        both_high = both.astype(jnp.bfloat16)
        both_low = (both - both_high.astype(jnp.float32)).astype(jnp.bfloat16)
        stacked = jnp.concatenate([both_high, both_low], axis=0)
        seen = []
        for r in range(LOCAL):
            state = state_ref[r, head]
            high = state.astype(jnp.bfloat16)
            low = (state - high.astype(jnp.float32)).astype(jnp.bfloat16)
            main = jnp.dot(stacked, high, preferred_element_type=jnp.float32)
            rest = jnp.dot(both_high, low, preferred_element_type=jnp.float32)
            seen.append(main[: 2 * ROWS] + main[2 * ROWS :] + rest)
        key_seen_ref[head] = jnp.where(row < STEPS, seen[0][:ROWS], seen[1][:ROWS])
        query_seen_ref[head] = jnp.where(row < STEPS, seen[0][ROWS:], seen[1][ROWS:])
        for lag in range(STEPS):
            moved_key = shift_rows(key, lag, row_step)
            if lag:
                pulls_ref[lag - 1, head] = jnp.broadcast_to(lane_sum(key * moved_key), (ROWS, DK))
            weights_ref[lag, head] = jnp.broadcast_to(lane_sum(query * moved_key), (ROWS, DK))


def values_kernel(
    slots_ref, halves_ref, lengths_ref, twist_ref, value_ref, value_got_ref, history_ref,
    key_seen_ref, query_seen_ref, pulls_ref, weights_ref, taps_ref, out_ref, heads_ref,
):
    twist = twist_ref[0]
    row = lax.broadcasted_iota(jnp.int32, (ROWS, DK), 0)
    row_step = row % STEPS
    lane = lax.broadcasted_iota(jnp.int32, (ROWS, DK), 1)
    row_length = jnp.where(row < STEPS, lengths_ref[0], lengths_ref[1])
    live = row_step < row_length
    value_steps = steps_of(value_got_ref)
    gates = received(value_ref, value_got_ref, value_steps, H)
    for head in range(H):
        value = activate(
            value_ref, value_got_ref, value_steps, 2, head, history_ref, taps_ref, twist, row_step
        )
        beta_logit = jnp.broadcast_to(gates[:, head : head + 1], (ROWS, DK))
        decay_logit = jnp.broadcast_to(gates[:, H + head : H + head + 1], (ROWS, DK))
        beta = 1.0 / (1.0 + jnp.exp(-beta_logit))
        decay = 1.0 / (1.0 + jnp.exp(decay_logit))
        fades = [jnp.ones_like(decay), decay]
        for lag in range(2, STEPS + 1):
            earlier = pltpu.roll(decay, lag - 1, 0)
            fades.append(jnp.where(row_step >= lag - 1, fades[-1] * earlier, fades[-1]))
        base = beta * (value - fades[STEPS] * key_seen_ref[head])
        pulls = [
            beta * fades[lag] * pulls_ref[lag - 1, head] if lag else None for lag in range(STEPS)
        ]
        solved = base
        for _ in range(STEPS - 1):
            following = base
            for lag in range(1, STEPS):
                following = following - pulls[lag] * shift_rows(solved, lag, row_step)
            solved = following
        out = fades[STEPS] * query_seen_ref[head]
        for lag in range(STEPS):
            weight = fades[lag] * weights_ref[lag, head]
            out = out + weight * shift_rows(solved, lag, row_step)
        heads_ref[head] = jnp.where(live, out, 0.0)
    for quad in range(UNITS // 4):
        joined = []
        for pair in (2 * quad, 2 * quad + 1):
            first = heads_ref[slots_ref[2 * pair]]
            second = heads_ref[slots_ref[2 * pair + 1]]
            first = jnp.where(halves_ref[2 * pair] == 0, first, pltpu.roll(first, HALF, 1))
            second = jnp.where(halves_ref[2 * pair + 1] == 0, pltpu.roll(second, HALF, 1), second)
            joined.append(jnp.where(lane < HALF, first, second))
        out_ref[quad] = jnp.concatenate(joined, axis=0).astype(jnp.bfloat16)


def run_delta(slots, halves, lengths, queries, keys, values, history, twist, taps, state):
    smem = pl.BlockSpec(memory_space=pltpu.SMEM)
    vmem = pl.BlockSpec(memory_space=pltpu.VMEM)
    params = pltpu.CompilerParams(vmem_limit_bytes=32 * 1024 * 1024)
    per_head = jax.ShapeDtypeStruct((H, ROWS, DK), jnp.float32)
    lags = [
        jax.ShapeDtypeStruct((count, H, ROWS, DK), jnp.float32) for count in (STEPS - 1, STEPS)
    ]
    tap_blocks = jax.ShapeDtypeStruct((TAP_BLOCKS, TAPS, TAP_WIDTH), jnp.float32)
    prepared = pl.pallas_call(
        keys_kernel,
        out_shape=[per_head] * 2 + lags + [tap_blocks],
        in_specs=[smem] + [vmem] * 7 + [pl.BlockSpec(memory_space=pl.ANY)],
        out_specs=[vmem] * 5,
        scratch_shapes=[
            pltpu.VMEM(state.shape, jnp.float32),
            pltpu.SemaphoreType.DMA((STATE_COPIES,)),
        ],
        compiler_params=params,
        cost_estimate=pl.CostEstimate(flops=40_000_000, bytes_accessed=9_000_000, transcendentals=0),
        name="keys_part",
    )(twist, *queries, *keys, history, *taps, state)
    return pl.pallas_call(
        values_kernel,
        out_shape=jax.ShapeDtypeStruct((UNITS // 4, 2 * ROWS, DK), jnp.bfloat16),
        in_specs=[smem] * 4 + [vmem] * 8,
        out_specs=vmem,
        scratch_shapes=[pltpu.VMEM((H, ROWS, DK), jnp.float32)],
        compiler_params=params,
        cost_estimate=pl.CostEstimate(flops=4_000_000, bytes_accessed=2_000_000, transcendentals=0),
        name="values_part",
    )(slots, halves, lengths, twist, *values, history, *prepared)


def rows_kernel(
    depth, me_ref, slot_of_ref, tokens_hbm, weight_hbm, mine_ref, theirs_ref, weight_ref,
    window_ref, sem, weight_sem,
):
    me = me_ref[0]
    width = window_ref.shape[2]
    offset = me // 2 * (2 * depth)
    start = jnp.minimum(offset // DK * DK, D - width)
    columns = pl.ds(pl.multiple_of(start, DK), width)
    copy = pltpu.make_async_copy(tokens_hbm.at[:, :, columns], window_ref, sem)
    copy.start()
    weight_copy = pltpu.make_async_copy(weight_hbm, weight_ref, weight_sem)
    weight_copy.start()
    shape = (mine_ref.shape[0], slot_of_ref.shape[1])
    row = lax.broadcasted_iota(jnp.int32, shape, 0)
    place = row // ROWS
    count = (shape[0] // ROWS).bit_length() - 1
    holder = jnp.zeros(shape, jnp.int32)
    for at in range(count):
        holder = holder + ((place >> (count - 1 - at)) & 1) * (2 << at)
    holder = jnp.bitwise_xor(holder, me)
    match = holder * LOCAL + row % ROWS // STEPS == slot_of_ref[...]
    copy.wait()
    window = window_ref[...].astype(jnp.float32)
    total = jnp.zeros((shape[0], width), jnp.float32)
    for step in range(STEPS):
        picker = jnp.where(match & (row % STEPS == step), 1.0, 0.0).astype(jnp.bfloat16)
        here = window[:, step, :].astype(jnp.bfloat16)
        total = total + jnp.dot(picker, here, preferred_element_type=jnp.float32)
    total = pltpu.roll(total, lax.rem(width - (offset - start), width), 1)
    low, high = total[:, :depth], total[:, depth : 2 * depth]
    first_core = me % 2 == 0
    mine_ref[...] = jnp.where(first_core, low, high).astype(jnp.bfloat16)
    theirs_ref[...] = jnp.where(first_core, high, low).astype(jnp.bfloat16)
    weight_copy.wait()


def run_rows(me, slot_of, tokens, weight, chips):
    depth = weight.shape[0]
    width = -(-(2 * depth + DK - 1) // DK) * DK
    out = jax.ShapeDtypeStruct((chips * ROWS, depth), jnp.bfloat16)
    vmem = pl.BlockSpec(memory_space=pltpu.VMEM)
    return pl.pallas_call(
        functools.partial(rows_kernel, depth),
        out_shape=[out, out, jax.ShapeDtypeStruct(weight.shape, weight.dtype)],
        in_specs=[
            pl.BlockSpec(memory_space=pltpu.SMEM), vmem, pl.BlockSpec(memory_space=pl.ANY),
            pl.BlockSpec(memory_space=pl.ANY),
        ],
        out_specs=[vmem] * 3,
        scratch_shapes=[
            pltpu.VMEM((tokens.shape[0], STEPS, width), jnp.bfloat16),
            pltpu.SemaphoreType.DMA,
            pltpu.SemaphoreType.DMA,
        ],
        compiler_params=pltpu.CompilerParams(vmem_limit_bytes=32 * 1024 * 1024),
        cost_estimate=pl.CostEstimate(flops=0, bytes_accessed=0, transcendentals=0),
        name="token_rows",
    )(me.reshape(1), slot_of.reshape(1, -1), tokens, weight)


def product_kernel(skipped, crossed, *refs):
    mine_ref, theirs_ref, block_ref, other_ref, *refs = refs[skipped:]
    gate_refs, (kept_ref, packed_ref) = refs[:-2], refs[-2:]
    half = mine_ref.shape[0] // 2

    def product(own, other, dims):
        total = lax.dot_general(mine_ref[...], own, dims, preferred_element_type=jnp.float32)
        return total + lax.dot_general(
            theirs_ref[...], other, dims, preferred_element_type=jnp.float32
        )

    total = product(block_ref[...], other_ref[...], (((1,), (0,)), ((), ())))
    if gate_refs:
        gates = product(gate_refs[0][...], gate_refs[1][...], (((1,), (1,)), ((), ())))
        zeros = jnp.zeros((gates.shape[0], 2 * DK - gates.shape[1]), jnp.float32)
        total = jnp.concatenate([total, gates, zeros], axis=1)
    kept, sent = total[:half], total[half:]
    if crossed:
        quarter = half // 2
        kept, sent = (
            jnp.concatenate([kept[:quarter], sent[:quarter]], axis=0),
            jnp.concatenate([kept[quarter:], sent[quarter:]], axis=0),
        )
    kept_ref[...] = kept
    pack_rows(sent, packed_ref)


def run_product(mine, theirs, weights, part, gates=(), earlier=(), crossed=False):
    vmem = pl.BlockSpec(memory_space=pltpu.VMEM)
    block = pl.BlockSpec((mine.shape[1], HEADS_WIDTH), lambda i: (0, part))
    half = mine.shape[0] // 2
    width = HEADS_WIDTH + len(gates) * DK
    return pl.pallas_call(
        functools.partial(product_kernel, len(earlier), crossed),
        grid=(1,),
        out_shape=[
            jax.ShapeDtypeStruct((half, width), jnp.float32),
            jax.ShapeDtypeStruct((half, width + scale_lanes(width // DK)), jnp.int16),
        ],
        in_specs=[pl.BlockSpec(memory_space=pl.ANY)] * len(earlier)
        + [vmem, vmem, block, block]
        + [vmem] * len(gates),
        out_specs=[vmem] * 2,
        compiler_params=pltpu.CompilerParams(vmem_limit_bytes=32 * 1024 * 1024),
        cost_estimate=pl.CostEstimate(flops=0, bytes_accessed=0, transcendentals=0),
        name="partial_product",
    )(*earlier, mine, theirs, *weights, *gates)


def combine_kernel(kept_ref, got_ref, still_ref, packed_ref):
    half = still_ref.shape[0]
    steps = steps_of(got_ref)
    sent = []
    for block in range(kept_ref.shape[1] // DK):
        columns = pl.ds(block * DK, DK)
        total = kept_ref[:, columns] + unpack_block(got_ref, steps, block)
        still_ref[:, columns] = total[:half]
        sent.append(total[half:])
    sent = jnp.concatenate(sent, axis=1)
    pack_rows(fold_rows(sent) if half == ROWS else sent, packed_ref)


def run_combine(kept, got):
    vmem = pl.BlockSpec(memory_space=pltpu.VMEM)
    half, width = kept.shape[0] // 2, kept.shape[1]
    rows, packed = (2 * ROWS, width // 2) if half == ROWS else (half, width)
    packed = (rows, packed + scale_lanes(packed // DK))
    return pl.pallas_call(
        combine_kernel,
        out_shape=[
            jax.ShapeDtypeStruct((half, width), jnp.float32),
            jax.ShapeDtypeStruct(packed, jnp.int16),
        ],
        in_specs=[vmem] * 2,
        out_specs=[vmem] * 2,
        compiler_params=pltpu.CompilerParams(vmem_limit_bytes=32 * 1024 * 1024),
        cost_estimate=pl.CostEstimate(flops=0, bytes_accessed=0, transcendentals=0),
        name="combine",
    )(kept, got)


def swap(value, bit, devices):
    return lax.ppermute(value, "heads", [(i, i ^ bit) for i in range(devices)])


def on_device(
    tokens,
    qkv_weight,
    gate_weight,
    conv_weight,
    delta_state,
    conv_state,
    old_heads,
    new_units,
    slot_of,
    lengths,
):
    devices = lax.axis_size("heads")
    me = lax.axis_index("heads")
    per_device = UNITS // devices
    row_count = tokens.shape[0]
    chips = devices // 2

    bits = [1 << b for b in range(1, devices.bit_length() - 1)]
    steps = jnp.arange(STEPS, dtype=jnp.int32)
    offered = (slot_of[:, None] * STEPS + steps[None, :]).reshape(-1)

    mine, theirs, near_weight = run_rows(me, slot_of, tokens, qkv_weight, chips)

    weights = (near_weight, swap(qkv_weight, 1, devices))
    gate_columns = gate_weight.T
    gates = (gate_columns, swap(gate_columns, 1, devices))

    tie = lambda *values: lax.optimization_barrier(values)

    ride = conv_weight.shape[1] == 2 * TAP_WIDTH and len(bits) == 3
    if ride:
        taps = jnp.concatenate([conv_weight[:, :TAP_WIDTH], conv_weight[:, TAP_WIDTH:]], axis=0)
        far = swap(taps, 1, devices)
    else:
        taps = lax.all_gather(conv_weight, "heads", axis=1, tiled=True)
        blocks = [block for bit in (0, 4) for block in range(TAP_BLOCKS) if block & 4 == bit]
        taps = [taps[:, block * TAP_WIDTH : (block + 1) * TAP_WIDTH] for block in blocks]
        taps = jnp.concatenate(taps, axis=0)
    queries = run_product(mine, theirs, weights, 0, crossed=True)
    keys = run_product(mine, theirs, weights, 1, earlier=queries[:1])
    values = run_product(mine, theirs, weights, 2, gates, earlier=keys[:1])

    lengths, old_heads, new_units, carried, *values = tie(
        lengths, old_heads, new_units, conv_state, *values
    )
    old_slots, halves = unit_tables(old_heads, new_units)
    my_rows = me * LOCAL + jnp.arange(LOCAL, dtype=jnp.int32)
    my_lengths = jnp.sum(
        jnp.where(slot_of[None, :] == my_rows[:, None], lengths[None, :], 0), axis=1
    )
    blank = jnp.zeros((1, carried.shape[2]), jnp.float32)
    history = jnp.concatenate([blank, carried[1], blank, carried[0]], axis=0)
    routes = [[bits[1], bits[0]] + bits[2:], bits, bits]
    kept = [chunk[0] for chunk in (queries, keys, values)]
    got = [
        swap(chunk[1], route[0], devices)
        for chunk, route in zip((queries, keys, values), routes)
    ]
    for level in range(1, len(bits)):
        for at in range(3):
            kept[at], packed = run_combine(kept[at], got[at])
            got[at] = swap(packed, routes[at][level], devices)
            if ride and level == 1 and at == 0:
                kept[0], taps, far = tie(kept[0], taps, far)
                taps = jnp.concatenate([taps, far], axis=0)
                taps = jnp.concatenate([taps, swap(taps, 4, devices)], axis=0)
    if ride:
        taps = jnp.concatenate([taps, swap(taps, 8, devices)], axis=0)
        twist, taps = me.reshape(1), (taps, swap(taps, 2, devices))
    else:
        half = TAP_BLOCKS // 2 * TAPS
        twist, taps = jnp.zeros(1, jnp.int32), (taps[:half], taps[half:])
    queries, keys, values = zip(kept, got)

    local_out = run_delta(
        old_slots, halves, my_lengths, queries, keys, values, history, twist, taps, delta_state
    )

    placer = (offered[:, None] == jnp.arange(row_count * STEPS, dtype=jnp.int32)[None, :]).astype(
        jnp.bfloat16
    )
    if per_device % 2 == 0:
        pairs = per_device // 2
        sending = local_out.reshape(devices, pairs * ROWS, DK)
        got = lax.all_to_all(sending, "heads", split_axis=0, concat_axis=0, tiled=True)
        got = got.reshape(devices, pairs, ROWS, DK)
        got = jnp.concatenate([got[:, pair] for pair in range(pairs)], axis=-1)
        got = got.reshape(devices * ROWS, pairs * DK)
    else:
        units = local_out.reshape(UNITS // 2, ROWS, 2, HALF).transpose(0, 2, 1, 3)
        sending = units.reshape(devices, per_device * ROWS, HALF)
        got = lax.all_to_all(sending, "heads", split_axis=0, concat_axis=0, tiled=True)
        got = got.reshape(devices, per_device, ROWS, HALF).transpose(0, 2, 1, 3)
        got = got.reshape(devices * ROWS, per_device * HALF)
    outputs = jnp.dot(placer, got, preferred_element_type=jnp.float32).astype(jnp.bfloat16)
    return outputs.reshape(row_count, STEPS, per_device * HALF)


def solution(mesh):
    in_specs = (
        P("groups", None, None),
        P(("groups", "heads"), None),
        P(("groups", "heads"), None),
        P("groups", "heads"),
        P(("groups", "heads"), None, None, None),
        P(("groups", "heads"), None, None),
        P(),
        P(),
        P("groups"),
        P("groups"),
    )
    out_specs = P("groups", None, "heads")
    return jax.shard_map(
        on_device, mesh=mesh, in_specs=in_specs, out_specs=out_specs, check_vma=False
    )
```

```python
import functools

import jax
import jax.numpy as jnp
from jax import lax
from jax.experimental import pallas as pl
from jax.experimental.pallas import tpu as pltpu
from jax.sharding import PartitionSpec as P

D = 2304
H = 32
DK = 128
TAPS = 4
STEPS = 4
HALF = 64
UNITS = 64
LOCAL = 2
ROWS = LOCAL * STEPS
HEADS_WIDTH = H * DK
LEVELS = 32767.0
STATE_COPIES = 4
TAP_WIDTH = 384
TAP_BLOCKS = 3 * HEADS_WIDTH // TAP_WIDTH


norm_eps = 1e-06


def unit_tables(old_heads, new_units):
    positions = jnp.arange(H, dtype=jnp.int32)
    inverse = jnp.sum(
        jnp.where(old_heads[None, :] == positions[:, None], positions[None, :], 0), axis=1
    )
    heads_of = new_units // 2
    halves = new_units % 2
    old_slots = jnp.sum(
        jnp.where(heads_of[:, None] == positions[None, :], inverse[None, :], 0), axis=1
    )
    return (old_slots, halves)


def shift_rows(value, lag, row_step):
    if lag == 0:
        return value
    moved = pltpu.roll(value, lag, 0)
    return jnp.where(row_step >= lag, moved, 0.0)


def lane_sum(value):
    return jnp.sum(value, axis=-1, keepdims=True)


def unit_length(value):
    return value * lax.rsqrt(lane_sum(value * value) + norm_eps)


def scale_lanes(blocks):
    return -(-blocks // HALF) * DK


def pack_rows(total, packed_ref):
    rows, width = total.shape
    blocks = width // DK
    lanes = scale_lanes(blocks)
    lane = lax.broadcasted_iota(jnp.int32, (rows, lanes), 1)
    scales = jnp.zeros((rows, lanes), jnp.float32)
    for block in range(blocks):
        part = total[:, block * DK : (block + 1) * DK]
        top = jnp.max(jnp.abs(part), axis=-1, keepdims=True) + 1e-30
        exponent = jnp.ceil(jnp.log2(top))
        mantissa = jnp.ceil(jnp.minimum(top * jnp.exp2(-exponent) * LEVELS, LEVELS))
        factor = LEVELS * LEVELS * jnp.exp2(-exponent) / mantissa
        coded = jnp.clip(jnp.floor(part * factor + 0.5), -LEVELS, LEVELS)
        packed_ref[:, block * DK : (block + 1) * DK] = coded.astype(jnp.int32).astype(jnp.int16)
        scales = jnp.where(lane == block, mantissa, scales)
        scales = jnp.where(lane == lanes // 2 + block, exponent, scales)
    packed_ref[:, width:] = scales.astype(jnp.int32).astype(jnp.int16)


def to_float(coded):
    return coded.astype(jnp.int32).astype(jnp.float32)


def steps_of(packed_ref):
    lanes = DK if packed_ref.shape[1] <= (HALF + 1) * DK else 2 * DK
    scales = to_float(packed_ref[:, packed_ref.shape[1] - lanes :])
    exponents = pltpu.roll(scales, lanes // 2, 1)
    return scales * jnp.exp2(exponents) * (1.0 / (LEVELS * LEVELS))


def unpack_block(packed_ref, steps, block):
    return to_float(packed_ref[:, block * DK : (block + 1) * DK]) * steps[:, block : block + 1]


def fold_rows(value):
    half = value.shape[1] // 2
    return jnp.concatenate([value[:, :half], value[:, half:]], axis=0)


def received(kept_ref, got_ref, steps, block):
    half = kept_ref.shape[1] // DK // 2
    rows = unpack_block(got_ref, steps, block % half)
    rows = rows[:ROWS] if block < half else rows[ROWS:]
    return kept_ref[:, block * DK : (block + 1) * DK] + rows


def tap_block(block, me):
    other = jnp.bitwise_xor(block // 2, me)
    place = (other & 1) + ((other >> 2) & 3) * 2 + ((other >> 1) & 1) * 8
    return place * 2 + block % 2


def activate(kept_ref, got_ref, steps, part, head, history_ref, taps_ref, twist, row_step):
    fresh = received(kept_ref, got_ref, steps, head)
    column = part * HEADS_WIDTH + head * DK
    carried = history_ref[:, column : column + DK]
    taps = taps_ref[tap_block(column // TAP_WIDTH, twist)]
    inner = column % TAP_WIDTH
    total = taps[TAPS - 1 :, inner : inner + DK] * fresh
    for lag in range(1, TAPS):
        source = jnp.where(row_step >= STEPS - lag, carried, fresh)
        tap = taps[TAPS - 1 - lag : TAPS - lag, inner : inner + DK]
        total = total + tap * pltpu.roll(source, lag, 0)
    return total / (1.0 + jnp.exp(-total))


def keys_kernel(
    twist_ref, query_ref, query_got_ref, key_ref, key_got_ref, history_ref, near_ref, far_ref,
    state_hbm, key_seen_ref, query_seen_ref, pulls_ref, weights_ref, taps_ref, state_ref, sems,
):
    per_copy = H // STATE_COPIES
    copies = []
    for at in range(STATE_COPIES):
        some = pl.ds(at * per_copy, per_copy)
        copies.append(
            pltpu.make_async_copy(state_hbm.at[:, some], state_ref.at[:, some], sems.at[at])
        )
        copies[-1].start()
    twist = twist_ref[0]
    half = TAP_BLOCKS // 2
    for at in range(TAP_BLOCKS):
        source = near_ref if at < half else far_ref
        if at % 4 == 0:
            some = source[at % half * TAPS : (at % half + 4) * TAPS, :].astype(jnp.float32)
        taps_ref[at] = some[at % 4 * TAPS : (at % 4 + 1) * TAPS]
    row = lax.broadcasted_iota(jnp.int32, (ROWS, DK), 0)
    row_step = row % STEPS
    query_steps, key_steps = steps_of(query_got_ref), steps_of(key_got_ref)
    for head in range(H):
        key = unit_length(
            activate(
                key_ref, key_got_ref, key_steps, 1, head, history_ref, taps_ref, twist, row_step
            )
        )
        query = unit_length(
            activate(
                query_ref, query_got_ref, query_steps, 0, head, history_ref, taps_ref, twist,
                row_step,
            )
        )
        both = jnp.concatenate([key, query], axis=0)
        if head % per_copy == 0:
            copies[head // per_copy].wait()
        both_high = both.astype(jnp.bfloat16)
        both_low = (both - both_high.astype(jnp.float32)).astype(jnp.bfloat16)
        stacked = jnp.concatenate([both_high, both_low], axis=0)
        seen = []
        for r in range(LOCAL):
            state = state_ref[r, head]
            high = state.astype(jnp.bfloat16)
            low = (state - high.astype(jnp.float32)).astype(jnp.bfloat16)
            main = jnp.dot(stacked, high, preferred_element_type=jnp.float32)
            rest = jnp.dot(both_high, low, preferred_element_type=jnp.float32)
            seen.append(main[: 2 * ROWS] + main[2 * ROWS :] + rest)
        key_seen_ref[head] = jnp.where(row < STEPS, seen[0][:ROWS], seen[1][:ROWS])
        query_seen_ref[head] = jnp.where(row < STEPS, seen[0][ROWS:], seen[1][ROWS:])
        for lag in range(STEPS):
            moved_key = shift_rows(key, lag, row_step)
            if lag:
                pulls_ref[lag - 1, head] = jnp.broadcast_to(lane_sum(key * moved_key), (ROWS, DK))
            weights_ref[lag, head] = jnp.broadcast_to(lane_sum(query * moved_key), (ROWS, DK))


def values_kernel(
    slots_ref, halves_ref, lengths_ref, twist_ref, value_ref, value_got_ref, history_ref,
    key_seen_ref, query_seen_ref, pulls_ref, weights_ref, taps_ref, out_ref, heads_ref,
):
    twist = twist_ref[0]
    row = lax.broadcasted_iota(jnp.int32, (ROWS, DK), 0)
    row_step = row % STEPS
    lane = lax.broadcasted_iota(jnp.int32, (ROWS, DK), 1)
    row_length = jnp.where(row < STEPS, lengths_ref[0], lengths_ref[1])
    live = row_step < row_length
    value_steps = steps_of(value_got_ref)
    gates = received(value_ref, value_got_ref, value_steps, H)
    for head in range(H):
        value = activate(
            value_ref, value_got_ref, value_steps, 2, head, history_ref, taps_ref, twist, row_step
        )
        beta_logit = jnp.broadcast_to(gates[:, head : head + 1], (ROWS, DK))
        decay_logit = jnp.broadcast_to(gates[:, H + head : H + head + 1], (ROWS, DK))
        beta = 1.0 / (1.0 + jnp.exp(-beta_logit))
        decay = 1.0 / (1.0 + jnp.exp(decay_logit))
        fades = [jnp.ones_like(decay), decay]
        for lag in range(2, STEPS + 1):
            earlier = pltpu.roll(decay, lag - 1, 0)
            fades.append(jnp.where(row_step >= lag - 1, fades[-1] * earlier, fades[-1]))
        base = beta * (value - fades[STEPS] * key_seen_ref[head])
        pulls = [
            beta * fades[lag] * pulls_ref[lag - 1, head] if lag else None for lag in range(STEPS)
        ]
        solved = base
        for _ in range(STEPS - 1):
            following = base
            for lag in range(1, STEPS):
                following = following - pulls[lag] * shift_rows(solved, lag, row_step)
            solved = following
        out = fades[STEPS] * query_seen_ref[head]
        for lag in range(STEPS):
            weight = fades[lag] * weights_ref[lag, head]
            out = out + weight * shift_rows(solved, lag, row_step)
        heads_ref[head] = jnp.where(live, out, 0.0)
    for quad in range(UNITS // 4):
        joined = []
        for pair in (2 * quad, 2 * quad + 1):
            first = heads_ref[slots_ref[2 * pair]]
            second = heads_ref[slots_ref[2 * pair + 1]]
            first = jnp.where(halves_ref[2 * pair] == 0, first, pltpu.roll(first, HALF, 1))
            second = jnp.where(halves_ref[2 * pair + 1] == 0, pltpu.roll(second, HALF, 1), second)
            joined.append(jnp.where(lane < HALF, first, second))
        out_ref[quad] = jnp.concatenate(joined, axis=0).astype(jnp.bfloat16)


def run_delta(slots, halves, lengths, queries, keys, values, history, twist, taps, state):
    smem = pl.BlockSpec(memory_space=pltpu.SMEM)
    vmem = pl.BlockSpec(memory_space=pltpu.VMEM)
    params = pltpu.CompilerParams(vmem_limit_bytes=32 * 1024 * 1024)
    per_head = jax.ShapeDtypeStruct((H, ROWS, DK), jnp.float32)
    lags = [
        jax.ShapeDtypeStruct((count, H, ROWS, DK), jnp.float32) for count in (STEPS - 1, STEPS)
    ]
    tap_blocks = jax.ShapeDtypeStruct((TAP_BLOCKS, TAPS, TAP_WIDTH), jnp.float32)
    prepared = pl.pallas_call(
        keys_kernel,
        out_shape=[per_head] * 2 + lags + [tap_blocks],
        in_specs=[smem] + [vmem] * 7 + [pl.BlockSpec(memory_space=pl.ANY)],
        out_specs=[vmem] * 5,
        scratch_shapes=[
            pltpu.VMEM(state.shape, jnp.float32),
            pltpu.SemaphoreType.DMA((STATE_COPIES,)),
        ],
        compiler_params=params,
        cost_estimate=pl.CostEstimate(flops=40_000_000, bytes_accessed=9_000_000, transcendentals=0),
        name="keys_part",
    )(twist, *queries, *keys, history, *taps, state)
    return pl.pallas_call(
        values_kernel,
        out_shape=jax.ShapeDtypeStruct((UNITS // 4, 2 * ROWS, DK), jnp.bfloat16),
        in_specs=[smem] * 4 + [vmem] * 8,
        out_specs=vmem,
        scratch_shapes=[pltpu.VMEM((H, ROWS, DK), jnp.float32)],
        compiler_params=params,
        cost_estimate=pl.CostEstimate(flops=4_000_000, bytes_accessed=2_000_000, transcendentals=0),
        name="values_part",
    )(slots, halves, lengths, twist, *values, history, *prepared)


def rows_kernel(
    depth, me_ref, slot_of_ref, tokens_hbm, weight_hbm, mine_ref, theirs_ref, weight_ref,
    window_ref, sem, weight_sem,
):
    me = me_ref[0]
    width = window_ref.shape[2]
    offset = me // 2 * (2 * depth)
    start = jnp.minimum(offset // DK * DK, D - width)
    columns = pl.ds(pl.multiple_of(start, DK), width)
    copy = pltpu.make_async_copy(tokens_hbm.at[:, :, columns], window_ref, sem)
    copy.start()
    weight_copy = pltpu.make_async_copy(weight_hbm, weight_ref, weight_sem)
    weight_copy.start()
    shape = (mine_ref.shape[0], slot_of_ref.shape[1])
    row = lax.broadcasted_iota(jnp.int32, shape, 0)
    place = row // ROWS
    count = (shape[0] // ROWS).bit_length() - 1
    holder = jnp.zeros(shape, jnp.int32)
    for at in range(count):
        holder = holder + ((place >> (count - 1 - at)) & 1) * (2 << at)
    holder = jnp.bitwise_xor(holder, me)
    match = holder * LOCAL + row % ROWS // STEPS == slot_of_ref[...]
    copy.wait()
    window = window_ref[...].astype(jnp.float32)
    total = jnp.zeros((shape[0], width), jnp.float32)
    for step in range(STEPS):
        picker = jnp.where(match & (row % STEPS == step), 1.0, 0.0).astype(jnp.bfloat16)
        here = window[:, step, :].astype(jnp.bfloat16)
        total = total + jnp.dot(picker, here, preferred_element_type=jnp.float32)
    total = pltpu.roll(total, lax.rem(width - (offset - start), width), 1)
    low, high = total[:, :depth], total[:, depth : 2 * depth]
    first_core = me % 2 == 0
    mine_ref[...] = jnp.where(first_core, low, high).astype(jnp.bfloat16)
    theirs_ref[...] = jnp.where(first_core, high, low).astype(jnp.bfloat16)
    weight_copy.wait()


def run_rows(me, slot_of, tokens, weight, chips):
    depth = weight.shape[0]
    width = -(-(2 * depth + DK - 1) // DK) * DK
    out = jax.ShapeDtypeStruct((chips * ROWS, depth), jnp.bfloat16)
    vmem = pl.BlockSpec(memory_space=pltpu.VMEM)
    return pl.pallas_call(
        functools.partial(rows_kernel, depth),
        out_shape=[out, out, jax.ShapeDtypeStruct(weight.shape, weight.dtype)],
        in_specs=[
            pl.BlockSpec(memory_space=pltpu.SMEM), vmem, pl.BlockSpec(memory_space=pl.ANY),
            pl.BlockSpec(memory_space=pl.ANY),
        ],
        out_specs=[vmem] * 3,
        scratch_shapes=[
            pltpu.VMEM((tokens.shape[0], STEPS, width), jnp.bfloat16),
            pltpu.SemaphoreType.DMA,
            pltpu.SemaphoreType.DMA,
        ],
        compiler_params=pltpu.CompilerParams(vmem_limit_bytes=32 * 1024 * 1024),
        cost_estimate=pl.CostEstimate(flops=0, bytes_accessed=0, transcendentals=0),
        name="token_rows",
    )(me.reshape(1), slot_of.reshape(1, -1), tokens, weight)


def product_kernel(skipped, crossed, *refs):
    mine_ref, theirs_ref, block_ref, other_ref, *refs = refs[skipped:]
    gate_refs, (kept_ref, packed_ref) = refs[:-2], refs[-2:]
    half = mine_ref.shape[0] // 2

    def product(own, other, dims):
        total = lax.dot_general(mine_ref[...], own, dims, preferred_element_type=jnp.float32)
        return total + lax.dot_general(
            theirs_ref[...], other, dims, preferred_element_type=jnp.float32
        )

    total = product(block_ref[...], other_ref[...], (((1,), (0,)), ((), ())))
    if gate_refs:
        gates = product(gate_refs[0][...], gate_refs[1][...], (((1,), (1,)), ((), ())))
        zeros = jnp.zeros((gates.shape[0], 2 * DK - gates.shape[1]), jnp.float32)
        total = jnp.concatenate([total, gates, zeros], axis=1)
    kept, sent = total[:half], total[half:]
    if crossed:
        quarter = half // 2
        kept, sent = (
            jnp.concatenate([kept[:quarter], sent[:quarter]], axis=0),
            jnp.concatenate([kept[quarter:], sent[quarter:]], axis=0),
        )
    kept_ref[...] = kept
    pack_rows(sent, packed_ref)


def run_product(mine, theirs, weights, part, gates=(), earlier=(), crossed=False):
    vmem = pl.BlockSpec(memory_space=pltpu.VMEM)
    block = pl.BlockSpec((mine.shape[1], HEADS_WIDTH), lambda i: (0, part))
    half = mine.shape[0] // 2
    width = HEADS_WIDTH + len(gates) * DK
    return pl.pallas_call(
        functools.partial(product_kernel, len(earlier), crossed),
        grid=(1,),
        out_shape=[
            jax.ShapeDtypeStruct((half, width), jnp.float32),
            jax.ShapeDtypeStruct((half, width + scale_lanes(width // DK)), jnp.int16),
        ],
        in_specs=[pl.BlockSpec(memory_space=pl.ANY)] * len(earlier)
        + [vmem, vmem, block, block]
        + [vmem] * len(gates),
        out_specs=[vmem] * 2,
        compiler_params=pltpu.CompilerParams(vmem_limit_bytes=32 * 1024 * 1024),
        cost_estimate=pl.CostEstimate(flops=0, bytes_accessed=0, transcendentals=0),
        name="partial_product",
    )(*earlier, mine, theirs, *weights, *gates)


def combine_kernel(kept_ref, got_ref, still_ref, packed_ref):
    half = still_ref.shape[0]
    steps = steps_of(got_ref)
    sent = []
    for block in range(kept_ref.shape[1] // DK):
        columns = pl.ds(block * DK, DK)
        total = kept_ref[:, columns] + unpack_block(got_ref, steps, block)
        still_ref[:, columns] = total[:half]
        sent.append(total[half:])
    sent = jnp.concatenate(sent, axis=1)
    pack_rows(fold_rows(sent) if half == ROWS else sent, packed_ref)


def run_combine(kept, got):
    vmem = pl.BlockSpec(memory_space=pltpu.VMEM)
    half, width = kept.shape[0] // 2, kept.shape[1]
    rows, packed = (2 * ROWS, width // 2) if half == ROWS else (half, width)
    packed = (rows, packed + scale_lanes(packed // DK))
    return pl.pallas_call(
        combine_kernel,
        out_shape=[
            jax.ShapeDtypeStruct((half, width), jnp.float32),
            jax.ShapeDtypeStruct(packed, jnp.int16),
        ],
        in_specs=[vmem] * 2,
        out_specs=[vmem] * 2,
        compiler_params=pltpu.CompilerParams(vmem_limit_bytes=32 * 1024 * 1024),
        cost_estimate=pl.CostEstimate(flops=0, bytes_accessed=0, transcendentals=0),
        name="combine",
    )(kept, got)


def swap(value, bit, devices):
    return lax.ppermute(value, "heads", [(i, i ^ bit) for i in range(devices)])


def on_device(
    tokens,
    qkv_weight,
    gate_weight,
    conv_weight,
    delta_state,
    conv_state,
    old_heads,
    new_units,
    slot_of,
    lengths,
):
    devices = lax.axis_size("heads")
    me = lax.axis_index("heads")
    per_device = UNITS // devices
    row_count = tokens.shape[0]
    chips = devices // 2

    bits = [1 << b for b in range(1, devices.bit_length() - 1)]
    steps = jnp.arange(STEPS, dtype=jnp.int32)
    offered = (slot_of[:, None] * STEPS + steps[None, :]).reshape(-1)

    mine, theirs, near_weight = run_rows(me, slot_of, tokens, qkv_weight, chips)

    weights = (near_weight, swap(qkv_weight, 1, devices))
    gate_columns = gate_weight.T
    gates = (gate_columns, swap(gate_columns, 1, devices))

    tie = lambda *values: lax.optimization_barrier(values)

    ride = conv_weight.shape[1] == 2 * TAP_WIDTH and len(bits) == 3
    if ride:
        taps = jnp.concatenate([conv_weight[:, :TAP_WIDTH], conv_weight[:, TAP_WIDTH:]], axis=0)
        far = swap(taps, 1, devices)
    else:
        taps = lax.all_gather(conv_weight, "heads", axis=1, tiled=True)
        blocks = [block for bit in (0, 4) for block in range(TAP_BLOCKS) if block & 4 == bit]
        taps = [taps[:, block * TAP_WIDTH : (block + 1) * TAP_WIDTH] for block in blocks]
        taps = jnp.concatenate(taps, axis=0)
    keys = run_product(mine, theirs, weights, 1)
    values = run_product(mine, theirs, weights, 2, gates, earlier=keys[:1])
    queries = run_product(mine, theirs, weights, 0, earlier=values[:1], crossed=True)

    lengths, old_heads, new_units, carried, *values = tie(
        lengths, old_heads, new_units, conv_state, *values
    )
    old_slots, halves = unit_tables(old_heads, new_units)
    my_rows = me * LOCAL + jnp.arange(LOCAL, dtype=jnp.int32)
    my_lengths = jnp.sum(
        jnp.where(slot_of[None, :] == my_rows[:, None], lengths[None, :], 0), axis=1
    )
    blank = jnp.zeros((1, carried.shape[2]), jnp.float32)
    history = jnp.concatenate([blank, carried[1], blank, carried[0]], axis=0)
    routes = [[bits[1], bits[0]] + bits[2:], bits, bits]
    kept = [chunk[0] for chunk in (queries, keys, values)]
    got = [
        swap(chunk[1], route[0], devices)
        for chunk, route in zip((queries, keys, values), routes)
    ]
    for level in range(1, len(bits)):
        for at in range(3):
            kept[at], packed = run_combine(kept[at], got[at])
            got[at] = swap(packed, routes[at][level], devices)
            if ride and level == 1 and at == 0:
                kept[0], taps, far = tie(kept[0], taps, far)
                taps = jnp.concatenate([taps, far], axis=0)
                taps = jnp.concatenate([taps, swap(taps, 4, devices)], axis=0)
    if ride:
        taps = jnp.concatenate([taps, swap(taps, 8, devices)], axis=0)
        twist, taps = me.reshape(1), (taps, swap(taps, 2, devices))
    else:
        half = TAP_BLOCKS // 2 * TAPS
        twist, taps = jnp.zeros(1, jnp.int32), (taps[:half], taps[half:])
    queries, keys, values = zip(kept, got)

    local_out = run_delta(
        old_slots, halves, my_lengths, queries, keys, values, history, twist, taps, delta_state
    )

    placer = (offered[:, None] == jnp.arange(row_count * STEPS, dtype=jnp.int32)[None, :]).astype(
        jnp.bfloat16
    )
    if per_device % 2 == 0:
        pairs = per_device // 2
        sending = local_out.reshape(devices, pairs * ROWS, DK)
        got = lax.all_to_all(sending, "heads", split_axis=0, concat_axis=0, tiled=True)
        got = got.reshape(devices, pairs, ROWS, DK)
        got = jnp.concatenate([got[:, pair] for pair in range(pairs)], axis=-1)
        got = got.reshape(devices * ROWS, pairs * DK)
    else:
        units = local_out.reshape(UNITS // 2, ROWS, 2, HALF).transpose(0, 2, 1, 3)
        sending = units.reshape(devices, per_device * ROWS, HALF)
        got = lax.all_to_all(sending, "heads", split_axis=0, concat_axis=0, tiled=True)
        got = got.reshape(devices, per_device, ROWS, HALF).transpose(0, 2, 1, 3)
        got = got.reshape(devices * ROWS, per_device * HALF)
    outputs = jnp.dot(placer, got, preferred_element_type=jnp.float32).astype(jnp.bfloat16)
    return outputs.reshape(row_count, STEPS, per_device * HALF)


def solution(mesh):
    in_specs = (
        P("groups", None, None),
        P(("groups", "heads"), None),
        P(("groups", "heads"), None),
        P("groups", "heads"),
        P(("groups", "heads"), None, None, None),
        P(("groups", "heads"), None, None),
        P(),
        P(),
        P("groups"),
        P("groups"),
    )
    out_specs = P("groups", None, "heads")
    return jax.shard_map(
        on_device, mesh=mesh, in_specs=in_specs, out_specs=out_specs, check_vma=False
    )
```

```python
import functools

import jax
import jax.numpy as jnp
from jax import lax
from jax.experimental import pallas as pl
from jax.experimental.pallas import tpu as pltpu
from jax.sharding import PartitionSpec as P

D = 2304
H = 32
DK = 128
TAPS = 4
STEPS = 4
HALF = 64
UNITS = 64
LOCAL = 2
ROWS = LOCAL * STEPS
HEADS_WIDTH = H * DK
LEVELS = 32767.0
STATE_COPIES = 4
TAP_WIDTH = 384
TAP_BLOCKS = 3 * HEADS_WIDTH // TAP_WIDTH


norm_eps = 1e-06


def unit_tables(old_heads, new_units):
    positions = jnp.arange(H, dtype=jnp.int32)
    inverse = jnp.sum(
        jnp.where(old_heads[None, :] == positions[:, None], positions[None, :], 0), axis=1
    )
    heads_of = new_units // 2
    halves = new_units % 2
    old_slots = jnp.sum(
        jnp.where(heads_of[:, None] == positions[None, :], inverse[None, :], 0), axis=1
    )
    return (old_slots, halves)


def shift_rows(value, lag, row_step):
    if lag == 0:
        return value
    moved = pltpu.roll(value, lag, 0)
    return jnp.where(row_step >= lag, moved, 0.0)


def lane_sum(value):
    return jnp.sum(value, axis=-1, keepdims=True)


def unit_length(value):
    return value * lax.rsqrt(lane_sum(value * value) + norm_eps)


def scale_lanes(blocks):
    return -(-blocks // HALF) * DK


def pack_rows(total, packed_ref):
    rows, width = total.shape
    blocks = width // DK
    lanes = scale_lanes(blocks)
    lane = lax.broadcasted_iota(jnp.int32, (rows, lanes), 1)
    scales = jnp.zeros((rows, lanes), jnp.float32)
    for block in range(blocks):
        part = total[:, block * DK : (block + 1) * DK]
        top = jnp.max(jnp.abs(part), axis=-1, keepdims=True) + 1e-30
        exponent = jnp.ceil(jnp.log2(top))
        mantissa = jnp.ceil(jnp.minimum(top * jnp.exp2(-exponent) * LEVELS, LEVELS))
        factor = LEVELS * LEVELS * jnp.exp2(-exponent) / mantissa
        coded = jnp.clip(jnp.floor(part * factor + 0.5), -LEVELS, LEVELS)
        packed_ref[:, block * DK : (block + 1) * DK] = coded.astype(jnp.int32).astype(jnp.int16)
        scales = jnp.where(lane == block, mantissa, scales)
        scales = jnp.where(lane == lanes // 2 + block, exponent, scales)
    packed_ref[:, width:] = scales.astype(jnp.int32).astype(jnp.int16)


def to_float(coded):
    return coded.astype(jnp.int32).astype(jnp.float32)


def steps_of(packed_ref):
    lanes = DK if packed_ref.shape[1] <= (HALF + 1) * DK else 2 * DK
    scales = to_float(packed_ref[:, packed_ref.shape[1] - lanes :])
    exponents = pltpu.roll(scales, lanes // 2, 1)
    return scales * jnp.exp2(exponents) * (1.0 / (LEVELS * LEVELS))


def unpack_block(packed_ref, steps, block):
    return to_float(packed_ref[:, block * DK : (block + 1) * DK]) * steps[:, block : block + 1]


def fold_rows(value):
    half = value.shape[1] // 2
    return jnp.concatenate([value[:, :half], value[:, half:]], axis=0)


def received(kept_ref, got_ref, steps, block):
    half = kept_ref.shape[1] // DK // 2
    rows = unpack_block(got_ref, steps, block % half)
    rows = rows[:ROWS] if block < half else rows[ROWS:]
    return kept_ref[:, block * DK : (block + 1) * DK] + rows


def tap_block(block, me):
    other = jnp.bitwise_xor(block // 2, me)
    place = (other & 1) + ((other >> 2) & 3) * 2 + ((other >> 1) & 1) * 8
    return place * 2 + block % 2


def activate(kept_ref, got_ref, steps, part, head, history_ref, taps_ref, twist, row_step):
    fresh = received(kept_ref, got_ref, steps, head)
    column = part * HEADS_WIDTH + head * DK
    carried = history_ref[:, column : column + DK]
    taps = taps_ref[tap_block(column // TAP_WIDTH, twist)]
    inner = column % TAP_WIDTH
    total = taps[TAPS - 1 :, inner : inner + DK] * fresh
    for lag in range(1, TAPS):
        source = jnp.where(row_step >= STEPS - lag, carried, fresh)
        tap = taps[TAPS - 1 - lag : TAPS - lag, inner : inner + DK]
        total = total + tap * pltpu.roll(source, lag, 0)
    return total / (1.0 + jnp.exp(-total))


def keys_kernel(
    twist_ref, query_ref, query_got_ref, key_ref, key_got_ref, history_ref, near_ref, far_ref,
    state_hbm, key_seen_ref, query_seen_ref, pulls_ref, weights_ref, taps_ref, state_ref, sems,
):
    per_copy = H // STATE_COPIES
    copies = []
    for at in range(STATE_COPIES):
        some = pl.ds(at * per_copy, per_copy)
        copies.append(
            pltpu.make_async_copy(state_hbm.at[:, some], state_ref.at[:, some], sems.at[at])
        )
        copies[-1].start()
    twist = twist_ref[0]
    half = TAP_BLOCKS // 2
    for at in range(TAP_BLOCKS):
        source = near_ref if at < half else far_ref
        if at % 4 == 0:
            some = source[at % half * TAPS : (at % half + 4) * TAPS, :].astype(jnp.float32)
        taps_ref[at] = some[at % 4 * TAPS : (at % 4 + 1) * TAPS]
    row = lax.broadcasted_iota(jnp.int32, (ROWS, DK), 0)
    row_step = row % STEPS
    query_steps, key_steps = steps_of(query_got_ref), steps_of(key_got_ref)
    for head in range(H):
        key = unit_length(
            activate(
                key_ref, key_got_ref, key_steps, 1, head, history_ref, taps_ref, twist, row_step
            )
        )
        query = unit_length(
            activate(
                query_ref, query_got_ref, query_steps, 0, head, history_ref, taps_ref, twist,
                row_step,
            )
        )
        both = jnp.concatenate([key, query], axis=0)
        if head % per_copy == 0:
            copies[head // per_copy].wait()
        both_high = both.astype(jnp.bfloat16)
        both_low = (both - both_high.astype(jnp.float32)).astype(jnp.bfloat16)
        stacked = jnp.concatenate([both_high, both_low], axis=0)
        seen = []
        for r in range(LOCAL):
            state = state_ref[r, head]
            high = state.astype(jnp.bfloat16)
            low = (state - high.astype(jnp.float32)).astype(jnp.bfloat16)
            main = jnp.dot(stacked, high, preferred_element_type=jnp.float32)
            rest = jnp.dot(both_high, low, preferred_element_type=jnp.float32)
            seen.append(main[: 2 * ROWS] + main[2 * ROWS :] + rest)
        key_seen_ref[head] = jnp.where(row < STEPS, seen[0][:ROWS], seen[1][:ROWS])
        query_seen_ref[head] = jnp.where(row < STEPS, seen[0][ROWS:], seen[1][ROWS:])
        for lag in range(STEPS):
            moved_key = shift_rows(key, lag, row_step)
            if lag:
                pulls_ref[lag - 1, head] = jnp.broadcast_to(lane_sum(key * moved_key), (ROWS, DK))
            weights_ref[lag, head] = jnp.broadcast_to(lane_sum(query * moved_key), (ROWS, DK))


def values_kernel(
    slots_ref, halves_ref, lengths_ref, twist_ref, value_ref, value_got_ref, history_ref,
    key_seen_ref, query_seen_ref, pulls_ref, weights_ref, taps_ref, out_ref, heads_ref,
):
    twist = twist_ref[0]
    row = lax.broadcasted_iota(jnp.int32, (ROWS, DK), 0)
    row_step = row % STEPS
    lane = lax.broadcasted_iota(jnp.int32, (ROWS, DK), 1)
    row_length = jnp.where(row < STEPS, lengths_ref[0], lengths_ref[1])
    live = row_step < row_length
    value_steps = steps_of(value_got_ref)
    gates = received(value_ref, value_got_ref, value_steps, H)
    for head in range(H):
        value = activate(
            value_ref, value_got_ref, value_steps, 2, head, history_ref, taps_ref, twist, row_step
        )
        beta_logit = jnp.broadcast_to(gates[:, head : head + 1], (ROWS, DK))
        decay_logit = jnp.broadcast_to(gates[:, H + head : H + head + 1], (ROWS, DK))
        beta = 1.0 / (1.0 + jnp.exp(-beta_logit))
        decay = 1.0 / (1.0 + jnp.exp(decay_logit))
        fades = [jnp.ones_like(decay), decay]
        for lag in range(2, STEPS + 1):
            earlier = pltpu.roll(decay, lag - 1, 0)
            fades.append(jnp.where(row_step >= lag - 1, fades[-1] * earlier, fades[-1]))
        base = beta * (value - fades[STEPS] * key_seen_ref[head])
        pulls = [
            beta * fades[lag] * pulls_ref[lag - 1, head] if lag else None for lag in range(STEPS)
        ]
        solved = base
        for _ in range(STEPS - 1):
            following = base
            for lag in range(1, STEPS):
                following = following - pulls[lag] * shift_rows(solved, lag, row_step)
            solved = following
        out = fades[STEPS] * query_seen_ref[head]
        for lag in range(STEPS):
            weight = fades[lag] * weights_ref[lag, head]
            out = out + weight * shift_rows(solved, lag, row_step)
        heads_ref[head] = jnp.where(live, out, 0.0)
    for quad in range(UNITS // 4):
        joined = []
        for pair in (2 * quad, 2 * quad + 1):
            first = heads_ref[slots_ref[2 * pair]]
            second = heads_ref[slots_ref[2 * pair + 1]]
            first = jnp.where(halves_ref[2 * pair] == 0, first, pltpu.roll(first, HALF, 1))
            second = jnp.where(halves_ref[2 * pair + 1] == 0, pltpu.roll(second, HALF, 1), second)
            joined.append(jnp.where(lane < HALF, first, second))
        out_ref[quad] = jnp.concatenate(joined, axis=0).astype(jnp.bfloat16)


def run_delta(slots, halves, lengths, queries, keys, values, history, twist, taps, state):
    smem = pl.BlockSpec(memory_space=pltpu.SMEM)
    vmem = pl.BlockSpec(memory_space=pltpu.VMEM)
    params = pltpu.CompilerParams(vmem_limit_bytes=32 * 1024 * 1024)
    per_head = jax.ShapeDtypeStruct((H, ROWS, DK), jnp.float32)
    lags = [
        jax.ShapeDtypeStruct((count, H, ROWS, DK), jnp.float32) for count in (STEPS - 1, STEPS)
    ]
    tap_blocks = jax.ShapeDtypeStruct((TAP_BLOCKS, TAPS, TAP_WIDTH), jnp.float32)
    prepared = pl.pallas_call(
        keys_kernel,
        out_shape=[per_head] * 2 + lags + [tap_blocks],
        in_specs=[smem] + [vmem] * 7 + [pl.BlockSpec(memory_space=pl.ANY)],
        out_specs=[vmem] * 5,
        scratch_shapes=[
            pltpu.VMEM(state.shape, jnp.float32),
            pltpu.SemaphoreType.DMA((STATE_COPIES,)),
        ],
        compiler_params=params,
        cost_estimate=pl.CostEstimate(flops=40_000_000, bytes_accessed=9_000_000, transcendentals=0),
        name="keys_part",
    )(twist, *queries, *keys, history, *taps, state)
    return pl.pallas_call(
        values_kernel,
        out_shape=jax.ShapeDtypeStruct((UNITS // 4, 2 * ROWS, DK), jnp.bfloat16),
        in_specs=[smem] * 4 + [vmem] * 8,
        out_specs=vmem,
        scratch_shapes=[pltpu.VMEM((H, ROWS, DK), jnp.float32)],
        compiler_params=params,
        cost_estimate=pl.CostEstimate(flops=4_000_000, bytes_accessed=2_000_000, transcendentals=0),
        name="values_part",
    )(slots, halves, lengths, twist, *values, history, *prepared)


def rows_kernel(
    depth, me_ref, slot_of_ref, tokens_hbm, weight_hbm, mine_ref, theirs_ref, weight_ref,
    window_ref, sem, weight_sem,
):
    me = me_ref[0]
    width = window_ref.shape[2]
    offset = me // 2 * (2 * depth)
    start = jnp.minimum(offset // DK * DK, D - width)
    columns = pl.ds(pl.multiple_of(start, DK), width)
    copy = pltpu.make_async_copy(tokens_hbm.at[:, :, columns], window_ref, sem)
    copy.start()
    weight_copy = pltpu.make_async_copy(weight_hbm, weight_ref, weight_sem)
    weight_copy.start()
    shape = (mine_ref.shape[0], slot_of_ref.shape[1])
    row = lax.broadcasted_iota(jnp.int32, shape, 0)
    place = row // ROWS
    count = (shape[0] // ROWS).bit_length() - 1
    holder = jnp.zeros(shape, jnp.int32)
    for at in range(count):
        holder = holder + ((place >> (count - 1 - at)) & 1) * (2 << at)
    holder = jnp.bitwise_xor(holder, me)
    match = holder * LOCAL + row % ROWS // STEPS == slot_of_ref[...]
    copy.wait()
    window = window_ref[...].astype(jnp.float32)
    total = jnp.zeros((shape[0], width), jnp.float32)
    for step in range(STEPS):
        picker = jnp.where(match & (row % STEPS == step), 1.0, 0.0).astype(jnp.bfloat16)
        here = window[:, step, :].astype(jnp.bfloat16)
        total = total + jnp.dot(picker, here, preferred_element_type=jnp.float32)
    total = pltpu.roll(total, lax.rem(width - (offset - start), width), 1)
    low, high = total[:, :depth], total[:, depth : 2 * depth]
    first_core = me % 2 == 0
    mine_ref[...] = jnp.where(first_core, low, high).astype(jnp.bfloat16)
    theirs_ref[...] = jnp.where(first_core, high, low).astype(jnp.bfloat16)
    weight_copy.wait()


def run_rows(me, slot_of, tokens, weight, chips):
    depth = weight.shape[0]
    width = -(-(2 * depth + DK - 1) // DK) * DK
    out = jax.ShapeDtypeStruct((chips * ROWS, depth), jnp.bfloat16)
    vmem = pl.BlockSpec(memory_space=pltpu.VMEM)
    return pl.pallas_call(
        functools.partial(rows_kernel, depth),
        out_shape=[out, out, jax.ShapeDtypeStruct(weight.shape, weight.dtype)],
        in_specs=[
            pl.BlockSpec(memory_space=pltpu.SMEM), vmem, pl.BlockSpec(memory_space=pl.ANY),
            pl.BlockSpec(memory_space=pl.ANY),
        ],
        out_specs=[vmem] * 3,
        scratch_shapes=[
            pltpu.VMEM((tokens.shape[0], STEPS, width), jnp.bfloat16),
            pltpu.SemaphoreType.DMA,
            pltpu.SemaphoreType.DMA,
        ],
        compiler_params=pltpu.CompilerParams(vmem_limit_bytes=32 * 1024 * 1024),
        cost_estimate=pl.CostEstimate(flops=0, bytes_accessed=0, transcendentals=0),
        name="token_rows",
    )(me.reshape(1), slot_of.reshape(1, -1), tokens, weight)


def product_kernel(skipped, crossed, *refs):
    mine_ref, theirs_ref, block_ref, other_ref, *refs = refs[skipped:]
    gate_refs, (kept_ref, packed_ref) = refs[:-2], refs[-2:]
    half = mine_ref.shape[0] // 2

    def product(own, other, dims):
        total = lax.dot_general(mine_ref[...], own, dims, preferred_element_type=jnp.float32)
        return total + lax.dot_general(
            theirs_ref[...], other, dims, preferred_element_type=jnp.float32
        )

    total = product(block_ref[...], other_ref[...], (((1,), (0,)), ((), ())))
    if gate_refs:
        gates = product(gate_refs[0][...], gate_refs[1][...], (((1,), (1,)), ((), ())))
        zeros = jnp.zeros((gates.shape[0], 2 * DK - gates.shape[1]), jnp.float32)
        total = jnp.concatenate([total, gates, zeros], axis=1)
    kept, sent = total[:half], total[half:]
    if crossed:
        quarter = half // 2
        kept, sent = (
            jnp.concatenate([kept[:quarter], sent[:quarter]], axis=0),
            jnp.concatenate([kept[quarter:], sent[quarter:]], axis=0),
        )
    kept_ref[...] = kept
    pack_rows(sent, packed_ref)


def run_product(mine, theirs, weights, part, gates=(), earlier=(), crossed=False):
    vmem = pl.BlockSpec(memory_space=pltpu.VMEM)
    block = pl.BlockSpec((mine.shape[1], HEADS_WIDTH), lambda i: (0, part))
    half = mine.shape[0] // 2
    width = HEADS_WIDTH + len(gates) * DK
    return pl.pallas_call(
        functools.partial(product_kernel, len(earlier), crossed),
        grid=(1,),
        out_shape=[
            jax.ShapeDtypeStruct((half, width), jnp.float32),
            jax.ShapeDtypeStruct((half, width + scale_lanes(width // DK)), jnp.int16),
        ],
        in_specs=[pl.BlockSpec(memory_space=pl.ANY)] * len(earlier)
        + [vmem, vmem, block, block]
        + [vmem] * len(gates),
        out_specs=[vmem] * 2,
        compiler_params=pltpu.CompilerParams(vmem_limit_bytes=32 * 1024 * 1024),
        cost_estimate=pl.CostEstimate(flops=0, bytes_accessed=0, transcendentals=0),
        name="partial_product",
    )(*earlier, mine, theirs, *weights, *gates)


def combine_kernel(kept_ref, got_ref, *refs):
    still_ref, packed_ref = refs[-2:]
    half = still_ref.shape[0]
    steps = steps_of(got_ref)
    sent = []
    for block in range(kept_ref.shape[1] // DK):
        columns = pl.ds(block * DK, DK)
        total = kept_ref[:, columns] + unpack_block(got_ref, steps, block)
        still_ref[:, columns] = total[:half]
        sent.append(total[half:])
    sent = jnp.concatenate(sent, axis=1)
    pack_rows(fold_rows(sent) if half == ROWS else sent, packed_ref)


def run_combine(kept, got, earlier):
    vmem = pl.BlockSpec(memory_space=pltpu.VMEM)
    half, width = kept.shape[0] // 2, kept.shape[1]
    rows, packed = (2 * ROWS, width // 2) if half == ROWS else (half, width)
    packed = (rows, packed + scale_lanes(packed // DK))
    return pl.pallas_call(
        combine_kernel,
        out_shape=[
            jax.ShapeDtypeStruct((half, width), jnp.float32),
            jax.ShapeDtypeStruct(packed, jnp.int16),
        ],
        in_specs=[vmem] * 2 + [pl.BlockSpec(memory_space=pl.ANY)] * len(earlier),
        out_specs=[vmem] * 2,
        compiler_params=pltpu.CompilerParams(vmem_limit_bytes=32 * 1024 * 1024),
        cost_estimate=pl.CostEstimate(flops=0, bytes_accessed=0, transcendentals=0),
        name="combine",
    )(kept, got, *earlier)


def swap(value, bit, devices):
    return lax.ppermute(value, "heads", [(i, i ^ bit) for i in range(devices)])


def on_device(
    tokens,
    qkv_weight,
    gate_weight,
    conv_weight,
    delta_state,
    conv_state,
    old_heads,
    new_units,
    slot_of,
    lengths,
):
    devices = lax.axis_size("heads")
    me = lax.axis_index("heads")
    per_device = UNITS // devices
    row_count = tokens.shape[0]
    chips = devices // 2

    bits = [1 << b for b in range(1, devices.bit_length() - 1)]

    mine, theirs, near_weight = run_rows(me, slot_of, tokens, qkv_weight, chips)

    weights = (near_weight, swap(qkv_weight, 1, devices))
    gate_columns = gate_weight.T
    gates = (gate_columns, swap(gate_columns, 1, devices))

    tie = lambda *values: lax.optimization_barrier(values)

    ride = conv_weight.shape[1] == 2 * TAP_WIDTH and len(bits) == 3
    if ride:
        taps = jnp.concatenate([conv_weight, swap(conv_weight, 1, devices)], axis=1)
        blocks = range(0, taps.shape[1], TAP_WIDTH)
        taps = jnp.concatenate([taps[:, at : at + TAP_WIDTH] for at in blocks], axis=0)
        taps = jnp.concatenate([taps, swap(taps, 4, devices)], axis=0)
    else:
        taps = lax.all_gather(conv_weight, "heads", axis=1, tiled=True)
        blocks = [block for bit in (0, 4) for block in range(TAP_BLOCKS) if block & 4 == bit]
        taps = [taps[:, block * TAP_WIDTH : (block + 1) * TAP_WIDTH] for block in blocks]
        taps = jnp.concatenate(taps, axis=0)
    keys = run_product(mine, theirs, weights, 1)
    values = run_product(mine, theirs, weights, 2, gates, earlier=keys[:1])
    queries = run_product(mine, theirs, weights, 0, earlier=(values[0], taps), crossed=True)

    slot_of, lengths, old_heads, new_units, carried, *values = tie(
        slot_of, lengths, old_heads, new_units, conv_state, *values
    )
    steps = jnp.arange(STEPS, dtype=jnp.int32)
    offered = (slot_of[:, None] * STEPS + steps[None, :]).reshape(-1)
    old_slots, halves = unit_tables(old_heads, new_units)
    my_rows = me * LOCAL + jnp.arange(LOCAL, dtype=jnp.int32)
    my_lengths = jnp.sum(
        jnp.where(slot_of[None, :] == my_rows[:, None], lengths[None, :], 0), axis=1
    )
    blank = jnp.zeros((1, carried.shape[2]), jnp.float32)
    history = jnp.concatenate([blank, carried[1], blank, carried[0]], axis=0)
    routes = [[bits[1], bits[0]] + bits[2:], bits, bits]
    kept = [chunk[0] for chunk in (queries, keys, values)]
    got = [
        swap(chunk[1], route[0], devices)
        for chunk, route in zip((queries, keys, values), routes)
    ]
    for level in range(1, len(bits)):
        for at in range(3):
            if ride and level == 1 and at == 0:
                taps = jnp.concatenate([taps, swap(taps, 8, devices)], axis=0)
            earlier = (taps,) if level == 1 and at == 0 else ()
            kept[at], packed = run_combine(kept[at], got[at], earlier)
            got[at] = swap(packed, routes[at][level], devices)
    if ride:
        twist, taps = me.reshape(1), (taps, swap(taps, 2, devices))
    else:
        half = TAP_BLOCKS // 2 * TAPS
        twist, taps = jnp.zeros(1, jnp.int32), (taps[:half], taps[half:])
    queries, keys, values = zip(kept, got)

    local_out = run_delta(
        old_slots, halves, my_lengths, queries, keys, values, history, twist, taps, delta_state
    )

    placer = (offered[:, None] == jnp.arange(row_count * STEPS, dtype=jnp.int32)[None, :]).astype(
        jnp.bfloat16
    )
    if per_device % 2 == 0:
        pairs = per_device // 2
        sending = local_out.reshape(devices, pairs * ROWS, DK)
        got = lax.all_to_all(sending, "heads", split_axis=0, concat_axis=0, tiled=True)
        got = got.reshape(devices, pairs, ROWS, DK)
        got = jnp.concatenate([got[:, pair] for pair in range(pairs)], axis=-1)
        got = got.reshape(devices * ROWS, pairs * DK)
    else:
        units = local_out.reshape(UNITS // 2, ROWS, 2, HALF).transpose(0, 2, 1, 3)
        sending = units.reshape(devices, per_device * ROWS, HALF)
        got = lax.all_to_all(sending, "heads", split_axis=0, concat_axis=0, tiled=True)
        got = got.reshape(devices, per_device, ROWS, HALF).transpose(0, 2, 1, 3)
        got = got.reshape(devices * ROWS, per_device * HALF)
    outputs = jnp.dot(placer, got, preferred_element_type=jnp.float32).astype(jnp.bfloat16)
    return outputs.reshape(row_count, STEPS, per_device * HALF)


def solution(mesh):
    in_specs = (
        P("groups", None, None),
        P(("groups", "heads"), None),
        P(("groups", "heads"), None),
        P("groups", "heads"),
        P(("groups", "heads"), None, None, None),
        P(("groups", "heads"), None, None),
        P(),
        P(),
        P("groups"),
        P("groups"),
    )
    out_specs = P("groups", None, "heads")
    return jax.shard_map(
        on_device, mesh=mesh, in_specs=in_specs, out_specs=out_specs, check_vma=False
    )
```

```python
import functools

import jax
import jax.numpy as jnp
from jax import lax
from jax.experimental import pallas as pl
from jax.experimental.pallas import tpu as pltpu
from jax.sharding import PartitionSpec as P

D = 2304
H = 32
DK = 128
TAPS = 4
STEPS = 4
HALF = 64
UNITS = 64
LOCAL = 2
ROWS = LOCAL * STEPS
HEADS_WIDTH = H * DK
LEVELS = 32767.0
STATE_COPIES = 4
TAP_WIDTH = 384
TAP_BLOCKS = 3 * HEADS_WIDTH // TAP_WIDTH


norm_eps = 1e-06


def unit_tables(old_heads, new_units):
    positions = jnp.arange(H, dtype=jnp.int32)
    inverse = jnp.sum(
        jnp.where(old_heads[None, :] == positions[:, None], positions[None, :], 0), axis=1
    )
    heads_of = new_units // 2
    halves = new_units % 2
    old_slots = jnp.sum(
        jnp.where(heads_of[:, None] == positions[None, :], inverse[None, :], 0), axis=1
    )
    return (old_slots, halves)


def shift_rows(value, lag, row_step):
    if lag == 0:
        return value
    moved = pltpu.roll(value, lag, 0)
    return jnp.where(row_step >= lag, moved, 0.0)


def lane_sum(value):
    return jnp.sum(value, axis=-1, keepdims=True)


def unit_length(value):
    return value * lax.rsqrt(lane_sum(value * value) + norm_eps)


def scale_lanes(blocks):
    return -(-blocks // HALF) * DK


def pack_rows(total, packed_ref):
    rows, width = total.shape
    blocks = width // DK
    lanes = scale_lanes(blocks)
    lane = lax.broadcasted_iota(jnp.int32, (rows, lanes), 1)
    scales = jnp.zeros((rows, lanes), jnp.float32)
    for block in range(blocks):
        part = total[:, block * DK : (block + 1) * DK]
        top = jnp.max(jnp.abs(part), axis=-1, keepdims=True) + 1e-30
        exponent = jnp.ceil(jnp.log2(top))
        mantissa = jnp.ceil(jnp.minimum(top * jnp.exp2(-exponent) * LEVELS, LEVELS))
        factor = LEVELS * LEVELS * jnp.exp2(-exponent) / mantissa
        coded = jnp.clip(jnp.floor(part * factor + 0.5), -LEVELS, LEVELS)
        packed_ref[:, block * DK : (block + 1) * DK] = coded.astype(jnp.int32).astype(jnp.int16)
        scales = jnp.where(lane == block, mantissa, scales)
        scales = jnp.where(lane == lanes // 2 + block, exponent, scales)
    packed_ref[:, width:] = scales.astype(jnp.int32).astype(jnp.int16)


def to_float(coded):
    return coded.astype(jnp.int32).astype(jnp.float32)


def steps_of(packed_ref):
    lanes = DK if packed_ref.shape[1] <= (HALF + 1) * DK else 2 * DK
    scales = to_float(packed_ref[:, packed_ref.shape[1] - lanes :])
    exponents = pltpu.roll(scales, lanes // 2, 1)
    return scales * jnp.exp2(exponents) * (1.0 / (LEVELS * LEVELS))


def unpack_block(packed_ref, steps, block):
    return to_float(packed_ref[:, block * DK : (block + 1) * DK]) * steps[:, block : block + 1]


def fold_rows(value):
    half = value.shape[1] // 2
    return jnp.concatenate([value[:, :half], value[:, half:]], axis=0)


def received(kept_ref, got_ref, steps, block):
    half = kept_ref.shape[1] // DK // 2
    rows = unpack_block(got_ref, steps, block % half)
    rows = rows[:ROWS] if block < half else rows[ROWS:]
    return kept_ref[:, block * DK : (block + 1) * DK] + rows


def tap_block(block, me):
    other = jnp.bitwise_xor(block // 2, me)
    place = ((other >> 2) & 3) + ((other >> 1) & 1) * 4 + (other & 1) * 8
    return place * 2 + block % 2


def activate(kept_ref, got_ref, steps, part, head, history_ref, taps_ref, twist, row_step):
    fresh = received(kept_ref, got_ref, steps, head)
    column = part * HEADS_WIDTH + head * DK
    carried = history_ref[:, column : column + DK]
    taps = taps_ref[tap_block(column // TAP_WIDTH, twist)]
    inner = column % TAP_WIDTH
    total = taps[TAPS - 1 :, inner : inner + DK] * fresh
    for lag in range(1, TAPS):
        source = jnp.where(row_step >= STEPS - lag, carried, fresh)
        tap = taps[TAPS - 1 - lag : TAPS - lag, inner : inner + DK]
        total = total + tap * pltpu.roll(source, lag, 0)
    return total / (1.0 + jnp.exp(-total))


def keys_kernel(
    twist_ref, query_ref, query_got_ref, key_ref, key_got_ref, history_ref, near_ref, far_ref,
    state_hbm, key_seen_ref, query_seen_ref, pulls_ref, weights_ref, taps_ref, state_ref, sems,
):
    per_copy = H // STATE_COPIES
    copies = []
    for at in range(STATE_COPIES):
        some = pl.ds(at * per_copy, per_copy)
        copies.append(
            pltpu.make_async_copy(state_hbm.at[:, some], state_ref.at[:, some], sems.at[at])
        )
        copies[-1].start()
    twist = twist_ref[0]
    half = TAP_BLOCKS // 2
    for at in range(TAP_BLOCKS):
        source = near_ref if at < half else far_ref
        if at % 4 == 0:
            some = source[at % half * TAPS : (at % half + 4) * TAPS, :].astype(jnp.float32)
        taps_ref[at] = some[at % 4 * TAPS : (at % 4 + 1) * TAPS]
    row = lax.broadcasted_iota(jnp.int32, (ROWS, DK), 0)
    row_step = row % STEPS
    query_steps, key_steps = steps_of(query_got_ref), steps_of(key_got_ref)
    for head in range(H):
        key = unit_length(
            activate(
                key_ref, key_got_ref, key_steps, 1, head, history_ref, taps_ref, twist, row_step
            )
        )
        query = unit_length(
            activate(
                query_ref, query_got_ref, query_steps, 0, head, history_ref, taps_ref, twist,
                row_step,
            )
        )
        both = jnp.concatenate([key, query], axis=0)
        if head % per_copy == 0:
            copies[head // per_copy].wait()
        both_high = both.astype(jnp.bfloat16)
        both_low = (both - both_high.astype(jnp.float32)).astype(jnp.bfloat16)
        stacked = jnp.concatenate([both_high, both_low], axis=0)
        seen = []
        for r in range(LOCAL):
            state = state_ref[r, head]
            high = state.astype(jnp.bfloat16)
            low = (state - high.astype(jnp.float32)).astype(jnp.bfloat16)
            main = jnp.dot(stacked, high, preferred_element_type=jnp.float32)
            rest = jnp.dot(both_high, low, preferred_element_type=jnp.float32)
            seen.append(main[: 2 * ROWS] + main[2 * ROWS :] + rest)
        key_seen_ref[head] = jnp.where(row < STEPS, seen[0][:ROWS], seen[1][:ROWS])
        query_seen_ref[head] = jnp.where(row < STEPS, seen[0][ROWS:], seen[1][ROWS:])
        for lag in range(STEPS):
            moved_key = shift_rows(key, lag, row_step)
            if lag:
                pulls_ref[lag - 1, head] = jnp.broadcast_to(lane_sum(key * moved_key), (ROWS, DK))
            weights_ref[lag, head] = jnp.broadcast_to(lane_sum(query * moved_key), (ROWS, DK))


def values_kernel(
    slots_ref, halves_ref, lengths_ref, twist_ref, value_ref, value_got_ref, history_ref,
    key_seen_ref, query_seen_ref, pulls_ref, weights_ref, taps_ref, out_ref, heads_ref,
):
    twist = twist_ref[0]
    row = lax.broadcasted_iota(jnp.int32, (ROWS, DK), 0)
    row_step = row % STEPS
    lane = lax.broadcasted_iota(jnp.int32, (ROWS, DK), 1)
    row_length = jnp.where(row < STEPS, lengths_ref[0], lengths_ref[1])
    live = row_step < row_length
    value_steps = steps_of(value_got_ref)
    gates = received(value_ref, value_got_ref, value_steps, H)
    for head in range(H):
        value = activate(
            value_ref, value_got_ref, value_steps, 2, head, history_ref, taps_ref, twist, row_step
        )
        beta_logit = jnp.broadcast_to(gates[:, head : head + 1], (ROWS, DK))
        decay_logit = jnp.broadcast_to(gates[:, H + head : H + head + 1], (ROWS, DK))
        beta = 1.0 / (1.0 + jnp.exp(-beta_logit))
        decay = 1.0 / (1.0 + jnp.exp(decay_logit))
        fades = [jnp.ones_like(decay), decay]
        for lag in range(2, STEPS + 1):
            earlier = pltpu.roll(decay, lag - 1, 0)
            fades.append(jnp.where(row_step >= lag - 1, fades[-1] * earlier, fades[-1]))
        base = beta * (value - fades[STEPS] * key_seen_ref[head])
        pulls = [
            beta * fades[lag] * pulls_ref[lag - 1, head] if lag else None for lag in range(STEPS)
        ]
        solved = base
        for _ in range(STEPS - 1):
            following = base
            for lag in range(1, STEPS):
                following = following - pulls[lag] * shift_rows(solved, lag, row_step)
            solved = following
        out = fades[STEPS] * query_seen_ref[head]
        for lag in range(STEPS):
            weight = fades[lag] * weights_ref[lag, head]
            out = out + weight * shift_rows(solved, lag, row_step)
        heads_ref[head] = jnp.where(live, out, 0.0)
    for quad in range(UNITS // 4):
        joined = []
        for pair in (2 * quad, 2 * quad + 1):
            first = heads_ref[slots_ref[2 * pair]]
            second = heads_ref[slots_ref[2 * pair + 1]]
            first = jnp.where(halves_ref[2 * pair] == 0, first, pltpu.roll(first, HALF, 1))
            second = jnp.where(halves_ref[2 * pair + 1] == 0, pltpu.roll(second, HALF, 1), second)
            joined.append(jnp.where(lane < HALF, first, second))
        out_ref[quad] = jnp.concatenate(joined, axis=0).astype(jnp.bfloat16)


def run_delta(slots, halves, lengths, queries, keys, values, history, twist, taps, state):
    smem = pl.BlockSpec(memory_space=pltpu.SMEM)
    vmem = pl.BlockSpec(memory_space=pltpu.VMEM)
    params = pltpu.CompilerParams(vmem_limit_bytes=32 * 1024 * 1024)
    per_head = jax.ShapeDtypeStruct((H, ROWS, DK), jnp.float32)
    lags = [
        jax.ShapeDtypeStruct((count, H, ROWS, DK), jnp.float32) for count in (STEPS - 1, STEPS)
    ]
    tap_blocks = jax.ShapeDtypeStruct((TAP_BLOCKS, TAPS, TAP_WIDTH), jnp.float32)
    prepared = pl.pallas_call(
        keys_kernel,
        out_shape=[per_head] * 2 + lags + [tap_blocks],
        in_specs=[smem] + [vmem] * 7 + [pl.BlockSpec(memory_space=pl.ANY)],
        out_specs=[vmem] * 5,
        scratch_shapes=[
            pltpu.VMEM(state.shape, jnp.float32),
            pltpu.SemaphoreType.DMA((STATE_COPIES,)),
        ],
        compiler_params=params,
        cost_estimate=pl.CostEstimate(flops=40_000_000, bytes_accessed=9_000_000, transcendentals=0),
        name="keys_part",
    )(twist, *queries, *keys, history, *taps, state)
    return pl.pallas_call(
        values_kernel,
        out_shape=jax.ShapeDtypeStruct((UNITS // 4, 2 * ROWS, DK), jnp.bfloat16),
        in_specs=[smem] * 4 + [vmem] * 8,
        out_specs=vmem,
        scratch_shapes=[pltpu.VMEM((H, ROWS, DK), jnp.float32)],
        compiler_params=params,
        cost_estimate=pl.CostEstimate(flops=4_000_000, bytes_accessed=2_000_000, transcendentals=0),
        name="values_part",
    )(slots, halves, lengths, twist, *values, history, *prepared)


def rows_kernel(
    depth, me_ref, slot_of_ref, tokens_hbm, weight_hbm, mine_ref, theirs_ref,
    weight_ref, window_ref, sem, weight_sem,
):
    me = me_ref[0]
    width = window_ref.shape[2]
    offset = me // 2 * (2 * depth)
    start = jnp.minimum(offset // DK * DK, D - width)
    columns = pl.ds(pl.multiple_of(start, DK), width)
    copy = pltpu.make_async_copy(tokens_hbm.at[:, :, columns], window_ref, sem)
    copy.start()
    weight_copy = pltpu.make_async_copy(weight_hbm, weight_ref, weight_sem)
    weight_copy.start()
    shape = (mine_ref.shape[0], slot_of_ref.shape[1])
    row = lax.broadcasted_iota(jnp.int32, shape, 0)
    place = row // ROWS
    count = (shape[0] // ROWS).bit_length() - 1
    holder = jnp.zeros(shape, jnp.int32)
    for at in range(count):
        holder = holder + ((place >> (count - 1 - at)) & 1) * (2 << at)
    holder = jnp.bitwise_xor(holder, me)
    match = holder * LOCAL + row % ROWS // STEPS == slot_of_ref[...]
    copy.wait()
    window = window_ref[...].astype(jnp.float32)
    total = jnp.zeros((shape[0], width), jnp.float32)
    for step in range(STEPS):
        picker = jnp.where(match & (row % STEPS == step), 1.0, 0.0).astype(jnp.bfloat16)
        here = window[:, step, :].astype(jnp.bfloat16)
        total = total + jnp.dot(picker, here, preferred_element_type=jnp.float32)
    total = pltpu.roll(total, lax.rem(width - (offset - start), width), 1)
    low, high = total[:, :depth], total[:, depth : 2 * depth]
    first_core = me % 2 == 0
    mine_ref[...] = jnp.where(first_core, low, high).astype(jnp.bfloat16)
    theirs_ref[...] = jnp.where(first_core, high, low).astype(jnp.bfloat16)
    weight_copy.wait()


def run_rows(me, slot_of, tokens, weight, chips):
    depth = weight.shape[0]
    width = -(-(2 * depth + DK - 1) // DK) * DK
    out = jax.ShapeDtypeStruct((chips * ROWS, depth), jnp.bfloat16)
    vmem = pl.BlockSpec(memory_space=pltpu.VMEM)
    return pl.pallas_call(
        functools.partial(rows_kernel, depth),
        out_shape=[out, out, jax.ShapeDtypeStruct(weight.shape, weight.dtype)],
        in_specs=[
            pl.BlockSpec(memory_space=pltpu.SMEM), vmem, pl.BlockSpec(memory_space=pl.ANY),
            pl.BlockSpec(memory_space=pl.ANY),
        ],
        out_specs=[vmem] * 3,
        scratch_shapes=[
            pltpu.VMEM((tokens.shape[0], STEPS, width), jnp.bfloat16),
            pltpu.SemaphoreType.DMA,
            pltpu.SemaphoreType.DMA,
        ],
        compiler_params=pltpu.CompilerParams(vmem_limit_bytes=32 * 1024 * 1024),
        cost_estimate=pl.CostEstimate(flops=0, bytes_accessed=0, transcendentals=0),
        name="token_rows",
    )(me.reshape(1), slot_of.reshape(1, -1), tokens, weight)


def product_kernel(skipped, crossed, *refs):
    mine_ref, theirs_ref, block_ref, other_ref, *refs = refs[skipped:]
    gate_refs, (kept_ref, packed_ref) = refs[:-2], refs[-2:]
    half = mine_ref.shape[0] // 2

    def product(own, other, dims):
        total = lax.dot_general(mine_ref[...], own, dims, preferred_element_type=jnp.float32)
        return total + lax.dot_general(
            theirs_ref[...], other, dims, preferred_element_type=jnp.float32
        )

    total = product(block_ref[...], other_ref[...], (((1,), (0,)), ((), ())))
    if gate_refs:
        gates = product(gate_refs[0][...], gate_refs[1][...], (((1,), (1,)), ((), ())))
        zeros = jnp.zeros((gates.shape[0], 2 * DK - gates.shape[1]), jnp.float32)
        total = jnp.concatenate([total, gates, zeros], axis=1)
    kept, sent = total[:half], total[half:]
    if crossed:
        quarter = half // 2
        kept, sent = (
            jnp.concatenate([kept[:quarter], sent[:quarter]], axis=0),
            jnp.concatenate([kept[quarter:], sent[quarter:]], axis=0),
        )
    kept_ref[...] = kept
    pack_rows(sent, packed_ref)


def run_product(mine, theirs, weights, part, gates=(), earlier=(), crossed=False):
    vmem = pl.BlockSpec(memory_space=pltpu.VMEM)
    block = pl.BlockSpec((mine.shape[1], HEADS_WIDTH), lambda i: (0, part))
    half = mine.shape[0] // 2
    width = HEADS_WIDTH + len(gates) * DK
    return pl.pallas_call(
        functools.partial(product_kernel, len(earlier), crossed),
        grid=(1,),
        out_shape=[
            jax.ShapeDtypeStruct((half, width), jnp.float32),
            jax.ShapeDtypeStruct((half, width + scale_lanes(width // DK)), jnp.int16),
        ],
        in_specs=[pl.BlockSpec(memory_space=pl.ANY)] * len(earlier)
        + [vmem, vmem, block, block]
        + [vmem] * len(gates),
        out_specs=[vmem] * 2,
        compiler_params=pltpu.CompilerParams(vmem_limit_bytes=32 * 1024 * 1024),
        cost_estimate=pl.CostEstimate(flops=0, bytes_accessed=0, transcendentals=0),
        name="partial_product",
    )(*earlier, mine, theirs, *weights, *gates)


def combine_kernel(kept_ref, got_ref, still_ref, packed_ref):
    half = still_ref.shape[0]
    steps = steps_of(got_ref)
    sent = []
    for block in range(kept_ref.shape[1] // DK):
        columns = pl.ds(block * DK, DK)
        total = kept_ref[:, columns] + unpack_block(got_ref, steps, block)
        still_ref[:, columns] = total[:half]
        sent.append(total[half:])
    sent = jnp.concatenate(sent, axis=1)
    pack_rows(fold_rows(sent) if half == ROWS else sent, packed_ref)


def run_combine(kept, got):
    vmem = pl.BlockSpec(memory_space=pltpu.VMEM)
    half, width = kept.shape[0] // 2, kept.shape[1]
    rows, packed = (2 * ROWS, width // 2) if half == ROWS else (half, width)
    packed = (rows, packed + scale_lanes(packed // DK))
    return pl.pallas_call(
        combine_kernel,
        out_shape=[
            jax.ShapeDtypeStruct((half, width), jnp.float32),
            jax.ShapeDtypeStruct(packed, jnp.int16),
        ],
        in_specs=[vmem] * 2,
        out_specs=[vmem] * 2,
        compiler_params=pltpu.CompilerParams(vmem_limit_bytes=32 * 1024 * 1024),
        cost_estimate=pl.CostEstimate(flops=0, bytes_accessed=0, transcendentals=0),
        name="combine",
    )(kept, got)


def join_kernel(first_ref, second_ref, earlier_ref, out_ref):
    both = [ref[...].astype(jnp.float32) for ref in (first_ref, second_ref)]
    out_ref[...] = jnp.concatenate(both, axis=0).astype(out_ref.dtype)


def join(first, second, earlier):
    vmem = pl.BlockSpec(memory_space=pltpu.VMEM)
    rows, width = first.shape
    return pl.pallas_call(
        join_kernel,
        out_shape=jax.ShapeDtypeStruct((2 * rows, width), first.dtype),
        in_specs=[vmem, vmem, pl.BlockSpec(memory_space=pl.ANY)],
        out_specs=vmem,
        compiler_params=pltpu.CompilerParams(vmem_limit_bytes=32 * 1024 * 1024),
        cost_estimate=pl.CostEstimate(flops=0, bytes_accessed=0, transcendentals=0),
        name="join_taps",
    )(first, second, earlier)


def swap(value, bit, devices):
    return lax.ppermute(value, "heads", [(i, i ^ bit) for i in range(devices)])


def on_device(
    tokens,
    qkv_weight,
    gate_weight,
    conv_weight,
    delta_state,
    conv_state,
    old_heads,
    new_units,
    slot_of,
    lengths,
):
    devices = lax.axis_size("heads")
    me = lax.axis_index("heads")
    per_device = UNITS // devices
    row_count = tokens.shape[0]
    chips = devices // 2

    bits = [1 << b for b in range(1, devices.bit_length() - 1)]

    ride = conv_weight.shape[1] == 2 * TAP_WIDTH and len(bits) == 3
    if ride:
        taps = jnp.concatenate([conv_weight[:, :TAP_WIDTH], conv_weight[:, TAP_WIDTH:]], axis=0)
        far = swap(taps, 4, devices)
    else:
        taps = lax.all_gather(conv_weight, "heads", axis=1, tiled=True)
        order = [
            2 * (at >> 4 & 1) + 4 * (at >> 3 & 1) + 8 * (at >> 1 & 1) + 16 * (at >> 2 & 1) + (at & 1)
            for at in range(TAP_BLOCKS)
        ]
        taps = [taps[:, block * TAP_WIDTH : (block + 1) * TAP_WIDTH] for block in order]
        taps = jnp.concatenate(taps, axis=0)

    mine, theirs, near_weight = run_rows(me, slot_of, tokens, qkv_weight, chips)

    weights = (near_weight, swap(qkv_weight, 1, devices))
    gate_columns = gate_weight.T
    gates = (gate_columns, swap(gate_columns, 1, devices))

    tie = lambda *values: lax.optimization_barrier(values)

    if ride:
        taps = join(taps, far, mine)
        far = swap(taps, 8, devices)
    keys = run_product(mine, theirs, weights, 1)
    values = run_product(mine, theirs, weights, 2, gates, earlier=keys[:1])
    if ride:
        taps = join(taps, far, values[0])
        far = swap(taps, 2, devices)
    queries = run_product(mine, theirs, weights, 0, earlier=(values[0], taps), crossed=True)

    slot_of, lengths, old_heads, new_units, carried, *values = tie(
        slot_of, lengths, old_heads, new_units, conv_state, *values
    )
    steps = jnp.arange(STEPS, dtype=jnp.int32)
    offered = (slot_of[:, None] * STEPS + steps[None, :]).reshape(-1)
    old_slots, halves = unit_tables(old_heads, new_units)
    my_rows = me * LOCAL + jnp.arange(LOCAL, dtype=jnp.int32)
    my_lengths = jnp.sum(
        jnp.where(slot_of[None, :] == my_rows[:, None], lengths[None, :], 0), axis=1
    )
    blank = jnp.zeros((1, carried.shape[2]), jnp.float32)
    history = jnp.concatenate([blank, carried[1], blank, carried[0]], axis=0)
    routes = [[bits[1], bits[0]] + bits[2:], bits, bits]
    kept = [chunk[0] for chunk in (queries, keys, values)]
    got = [
        swap(chunk[1], route[0], devices)
        for chunk, route in zip((queries, keys, values), routes)
    ]
    for level in range(1, len(bits)):
        for at in range(3):
            kept[at], packed = run_combine(kept[at], got[at])
            got[at] = swap(packed, routes[at][level], devices)
        if ride and level == 1:
            taps = join(taps, far, kept[2])
            far = swap(taps, 1, devices)
    if ride:
        twist, taps = me.reshape(1), (taps, far)
    else:
        half = TAP_BLOCKS // 2 * TAPS
        twist, taps = jnp.zeros(1, jnp.int32), (taps[:half], taps[half:])
    queries, keys, values = zip(kept, got)

    local_out = run_delta(
        old_slots, halves, my_lengths, queries, keys, values, history, twist, taps, delta_state
    )

    placer = (offered[:, None] == jnp.arange(row_count * STEPS, dtype=jnp.int32)[None, :]).astype(
        jnp.bfloat16
    )
    if per_device % 2 == 0:
        pairs = per_device // 2
        sending = local_out.reshape(devices, pairs * ROWS, DK)
        got = lax.all_to_all(sending, "heads", split_axis=0, concat_axis=0, tiled=True)
        got = got.reshape(devices, pairs, ROWS, DK)
        got = jnp.concatenate([got[:, pair] for pair in range(pairs)], axis=-1)
        got = got.reshape(devices * ROWS, pairs * DK)
    else:
        units = local_out.reshape(UNITS // 2, ROWS, 2, HALF).transpose(0, 2, 1, 3)
        sending = units.reshape(devices, per_device * ROWS, HALF)
        got = lax.all_to_all(sending, "heads", split_axis=0, concat_axis=0, tiled=True)
        got = got.reshape(devices, per_device, ROWS, HALF).transpose(0, 2, 1, 3)
        got = got.reshape(devices * ROWS, per_device * HALF)
    outputs = jnp.dot(placer, got, preferred_element_type=jnp.float32).astype(jnp.bfloat16)
    return outputs.reshape(row_count, STEPS, per_device * HALF)


def solution(mesh):
    in_specs = (
        P("groups", None, None),
        P(("groups", "heads"), None),
        P(("groups", "heads"), None),
        P("groups", "heads"),
        P(("groups", "heads"), None, None, None),
        P(("groups", "heads"), None, None),
        P(),
        P(),
        P("groups"),
        P("groups"),
    )
    out_specs = P("groups", None, "heads")
    return jax.shard_map(
        on_device, mesh=mesh, in_specs=in_specs, out_specs=out_specs, check_vma=False
    )
```

```python
import functools

import jax
import jax.numpy as jnp
from jax import lax
from jax.experimental import pallas as pl
from jax.experimental.pallas import tpu as pltpu
from jax.sharding import PartitionSpec as P

D = 2304
H = 32
DK = 128
TAPS = 4
STEPS = 4
HALF = 64
UNITS = 64
LOCAL = 2
ROWS = LOCAL * STEPS
HEADS_WIDTH = H * DK
LEVELS = 32767.0
STATE_COPIES = 4
TAP_WIDTH = 384
TAP_BLOCKS = 3 * HEADS_WIDTH // TAP_WIDTH


norm_eps = 1e-06


def unit_tables(old_heads, new_units):
    positions = jnp.arange(H, dtype=jnp.int32)
    inverse = jnp.sum(
        jnp.where(old_heads[None, :] == positions[:, None], positions[None, :], 0), axis=1
    )
    heads_of = new_units // 2
    halves = new_units % 2
    old_slots = jnp.sum(
        jnp.where(heads_of[:, None] == positions[None, :], inverse[None, :], 0), axis=1
    )
    return (old_slots, halves)


def shift_rows(value, lag, row_step):
    if lag == 0:
        return value
    moved = pltpu.roll(value, lag, 0)
    return jnp.where(row_step >= lag, moved, 0.0)


def lane_sum(value):
    return jnp.sum(value, axis=-1, keepdims=True)


def unit_length(value):
    return value * lax.rsqrt(lane_sum(value * value) + norm_eps)


def scale_lanes(blocks):
    return -(-blocks // HALF) * DK


def pack_rows(total, packed_ref):
    rows, width = total.shape
    blocks = width // DK
    lanes = scale_lanes(blocks)
    lane = lax.broadcasted_iota(jnp.int32, (rows, lanes), 1)
    scales = jnp.zeros((rows, lanes), jnp.float32)
    for block in range(blocks):
        part = total[:, block * DK : (block + 1) * DK]
        top = jnp.max(jnp.abs(part), axis=-1, keepdims=True) + 1e-30
        exponent = jnp.ceil(jnp.log2(top))
        mantissa = jnp.ceil(jnp.minimum(top * jnp.exp2(-exponent) * LEVELS, LEVELS))
        factor = LEVELS * LEVELS * jnp.exp2(-exponent) / mantissa
        coded = jnp.clip(jnp.floor(part * factor + 0.5), -LEVELS, LEVELS)
        packed_ref[:, block * DK : (block + 1) * DK] = coded.astype(jnp.int32).astype(jnp.int16)
        scales = jnp.where(lane == block, mantissa, scales)
        scales = jnp.where(lane == lanes // 2 + block, exponent, scales)
    packed_ref[:, width:] = scales.astype(jnp.int32).astype(jnp.int16)


def to_float(coded):
    return coded.astype(jnp.int32).astype(jnp.float32)


def steps_of(packed_ref):
    lanes = DK if packed_ref.shape[1] <= (HALF + 1) * DK else 2 * DK
    scales = to_float(packed_ref[:, packed_ref.shape[1] - lanes :])
    exponents = pltpu.roll(scales, lanes // 2, 1)
    return scales * jnp.exp2(exponents) * (1.0 / (LEVELS * LEVELS))


def unpack_block(packed_ref, steps, block):
    return to_float(packed_ref[:, block * DK : (block + 1) * DK]) * steps[:, block : block + 1]


def fold_rows(value):
    half = value.shape[1] // 2
    return jnp.concatenate([value[:, :half], value[:, half:]], axis=0)


def received(kept_ref, got_ref, steps, block):
    half = kept_ref.shape[1] // DK // 2
    rows = unpack_block(got_ref, steps, block % half)
    rows = rows[:ROWS] if block < half else rows[ROWS:]
    return kept_ref[:, block * DK : (block + 1) * DK] + rows


def tap_block(block, me):
    other = jnp.bitwise_xor(block // 2, me)
    place = ((other >> 2) & 3) + ((other >> 1) & 1) * 4 + (other & 1) * 8
    return place * 2 + block % 2


def activate(kept_ref, got_ref, steps, part, head, history_ref, taps_ref, twist, row_step):
    fresh = received(kept_ref, got_ref, steps, head)
    column = part * HEADS_WIDTH + head * DK
    carried = history_ref[:, column : column + DK]
    taps = taps_ref[tap_block(column // TAP_WIDTH, twist)]
    inner = column % TAP_WIDTH
    total = taps[TAPS - 1 :, inner : inner + DK] * fresh
    for lag in range(1, TAPS):
        source = jnp.where(row_step >= STEPS - lag, carried, fresh)
        tap = taps[TAPS - 1 - lag : TAPS - lag, inner : inner + DK]
        total = total + tap * pltpu.roll(source, lag, 0)
    return total / (1.0 + jnp.exp(-total))


def keys_kernel(
    twist_ref, query_ref, query_got_ref, key_ref, key_got_ref, history_ref, near_ref, far_ref,
    state_hbm, key_seen_ref, query_seen_ref, pulls_ref, weights_ref, taps_ref, state_ref, sems,
):
    per_copy = H // STATE_COPIES
    copies = []
    for at in range(STATE_COPIES):
        some = pl.ds(at * per_copy, per_copy)
        copies.append(
            pltpu.make_async_copy(state_hbm.at[:, some], state_ref.at[:, some], sems.at[at])
        )
        copies[-1].start()
    twist = twist_ref[0]
    half = TAP_BLOCKS // 2
    for at in range(TAP_BLOCKS):
        source = near_ref if at < half else far_ref
        if at % 4 == 0:
            some = source[at % half * TAPS : (at % half + 4) * TAPS, :].astype(jnp.float32)
        taps_ref[at] = some[at % 4 * TAPS : (at % 4 + 1) * TAPS]
    row = lax.broadcasted_iota(jnp.int32, (ROWS, DK), 0)
    row_step = row % STEPS
    query_steps, key_steps = steps_of(query_got_ref), steps_of(key_got_ref)
    for head in range(H):
        key = unit_length(
            activate(
                key_ref, key_got_ref, key_steps, 1, head, history_ref, taps_ref, twist, row_step
            )
        )
        query = unit_length(
            activate(
                query_ref, query_got_ref, query_steps, 0, head, history_ref, taps_ref, twist,
                row_step,
            )
        )
        both = jnp.concatenate([key, query], axis=0)
        if head % per_copy == 0:
            copies[head // per_copy].wait()
        both_high = both.astype(jnp.bfloat16)
        both_low = (both - both_high.astype(jnp.float32)).astype(jnp.bfloat16)
        stacked = jnp.concatenate([both_high, both_low], axis=0)
        seen = []
        for r in range(LOCAL):
            state = state_ref[r, head]
            high = state.astype(jnp.bfloat16)
            low = (state - high.astype(jnp.float32)).astype(jnp.bfloat16)
            main = jnp.dot(stacked, high, preferred_element_type=jnp.float32)
            rest = jnp.dot(both_high, low, preferred_element_type=jnp.float32)
            seen.append(main[: 2 * ROWS] + main[2 * ROWS :] + rest)
        key_seen_ref[head] = jnp.where(row < STEPS, seen[0][:ROWS], seen[1][:ROWS])
        query_seen_ref[head] = jnp.where(row < STEPS, seen[0][ROWS:], seen[1][ROWS:])
        for lag in range(STEPS):
            moved_key = shift_rows(key, lag, row_step)
            if lag:
                pulls_ref[lag - 1, head] = jnp.broadcast_to(lane_sum(key * moved_key), (ROWS, DK))
            weights_ref[lag, head] = jnp.broadcast_to(lane_sum(query * moved_key), (ROWS, DK))


def values_kernel(
    slots_ref, halves_ref, lengths_ref, twist_ref, value_ref, value_got_ref, history_ref,
    key_seen_ref, query_seen_ref, pulls_ref, weights_ref, taps_ref, out_ref, heads_ref,
):
    twist = twist_ref[0]
    row = lax.broadcasted_iota(jnp.int32, (ROWS, DK), 0)
    row_step = row % STEPS
    lane = lax.broadcasted_iota(jnp.int32, (ROWS, DK), 1)
    row_length = jnp.where(row < STEPS, lengths_ref[0], lengths_ref[1])
    live = row_step < row_length
    value_steps = steps_of(value_got_ref)
    gates = received(value_ref, value_got_ref, value_steps, H)
    for head in range(H):
        value = activate(
            value_ref, value_got_ref, value_steps, 2, head, history_ref, taps_ref, twist, row_step
        )
        beta_logit = jnp.broadcast_to(gates[:, head : head + 1], (ROWS, DK))
        decay_logit = jnp.broadcast_to(gates[:, H + head : H + head + 1], (ROWS, DK))
        beta = 1.0 / (1.0 + jnp.exp(-beta_logit))
        decay = 1.0 / (1.0 + jnp.exp(decay_logit))
        fades = [jnp.ones_like(decay), decay]
        for lag in range(2, STEPS + 1):
            earlier = pltpu.roll(decay, lag - 1, 0)
            fades.append(jnp.where(row_step >= lag - 1, fades[-1] * earlier, fades[-1]))
        base = beta * (value - fades[STEPS] * key_seen_ref[head])
        pulls = [
            beta * fades[lag] * pulls_ref[lag - 1, head] if lag else None for lag in range(STEPS)
        ]
        solved = base
        for _ in range(STEPS - 1):
            following = base
            for lag in range(1, STEPS):
                following = following - pulls[lag] * shift_rows(solved, lag, row_step)
            solved = following
        out = fades[STEPS] * query_seen_ref[head]
        for lag in range(STEPS):
            weight = fades[lag] * weights_ref[lag, head]
            out = out + weight * shift_rows(solved, lag, row_step)
        heads_ref[head] = jnp.where(live, out, 0.0)
    for quad in range(UNITS // 4):
        joined = []
        for pair in (2 * quad, 2 * quad + 1):
            first = heads_ref[slots_ref[2 * pair]]
            second = heads_ref[slots_ref[2 * pair + 1]]
            first = jnp.where(halves_ref[2 * pair] == 0, first, pltpu.roll(first, HALF, 1))
            second = jnp.where(halves_ref[2 * pair + 1] == 0, pltpu.roll(second, HALF, 1), second)
            joined.append(jnp.where(lane < HALF, first, second))
        out_ref[quad] = jnp.concatenate(joined, axis=0).astype(jnp.bfloat16)


def run_delta(slots, halves, lengths, queries, keys, values, history, twist, taps, state):
    smem = pl.BlockSpec(memory_space=pltpu.SMEM)
    vmem = pl.BlockSpec(memory_space=pltpu.VMEM)
    params = pltpu.CompilerParams(vmem_limit_bytes=32 * 1024 * 1024)
    per_head = jax.ShapeDtypeStruct((H, ROWS, DK), jnp.float32)
    lags = [
        jax.ShapeDtypeStruct((count, H, ROWS, DK), jnp.float32) for count in (STEPS - 1, STEPS)
    ]
    tap_blocks = jax.ShapeDtypeStruct((TAP_BLOCKS, TAPS, TAP_WIDTH), jnp.float32)
    prepared = pl.pallas_call(
        keys_kernel,
        out_shape=[per_head] * 2 + lags + [tap_blocks],
        in_specs=[smem] + [vmem] * 7 + [pl.BlockSpec(memory_space=pl.ANY)],
        out_specs=[vmem] * 5,
        scratch_shapes=[
            pltpu.VMEM(state.shape, jnp.float32),
            pltpu.SemaphoreType.DMA((STATE_COPIES,)),
        ],
        compiler_params=params,
        cost_estimate=pl.CostEstimate(flops=40_000_000, bytes_accessed=9_000_000, transcendentals=0),
        name="keys_part",
    )(twist, *queries, *keys, history, *taps, state)
    return pl.pallas_call(
        values_kernel,
        out_shape=jax.ShapeDtypeStruct((UNITS // 4, 2 * ROWS, DK), jnp.bfloat16),
        in_specs=[smem] * 4 + [vmem] * 8,
        out_specs=vmem,
        scratch_shapes=[pltpu.VMEM((H, ROWS, DK), jnp.float32)],
        compiler_params=params,
        cost_estimate=pl.CostEstimate(flops=4_000_000, bytes_accessed=2_000_000, transcendentals=0),
        name="values_part",
    )(slots, halves, lengths, twist, *values, history, *prepared)


def rows_kernel(
    depth, me_ref, slot_of_ref, tokens_hbm, weight_hbm, mine_ref, theirs_ref,
    weight_ref, window_ref, sem, weight_sem,
):
    me = me_ref[0]
    width = window_ref.shape[2]
    offset = me // 2 * (2 * depth)
    start = jnp.minimum(offset // DK * DK, D - width)
    columns = pl.ds(pl.multiple_of(start, DK), width)
    copy = pltpu.make_async_copy(tokens_hbm.at[:, :, columns], window_ref, sem)
    copy.start()
    weight_copy = pltpu.make_async_copy(weight_hbm, weight_ref, weight_sem)
    weight_copy.start()
    shape = (mine_ref.shape[0], slot_of_ref.shape[1])
    row = lax.broadcasted_iota(jnp.int32, shape, 0)
    place = row // ROWS
    count = (shape[0] // ROWS).bit_length() - 1
    holder = jnp.zeros(shape, jnp.int32)
    for at in range(count):
        holder = holder + ((place >> (count - 1 - at)) & 1) * (2 << at)
    holder = jnp.bitwise_xor(holder, me)
    match = holder * LOCAL + row % ROWS // STEPS == slot_of_ref[...]
    copy.wait()
    window = window_ref[...].astype(jnp.float32)
    total = jnp.zeros((shape[0], width), jnp.float32)
    for step in range(STEPS):
        picker = jnp.where(match & (row % STEPS == step), 1.0, 0.0).astype(jnp.bfloat16)
        here = window[:, step, :].astype(jnp.bfloat16)
        total = total + jnp.dot(picker, here, preferred_element_type=jnp.float32)
    total = pltpu.roll(total, lax.rem(width - (offset - start), width), 1)
    low, high = total[:, :depth], total[:, depth : 2 * depth]
    first_core = me % 2 == 0
    mine_ref[...] = jnp.where(first_core, low, high).astype(jnp.bfloat16)
    theirs_ref[...] = jnp.where(first_core, high, low).astype(jnp.bfloat16)
    weight_copy.wait()


def run_rows(me, slot_of, tokens, weight, chips):
    depth = weight.shape[0]
    width = -(-(2 * depth + DK - 1) // DK) * DK
    out = jax.ShapeDtypeStruct((chips * ROWS, depth), jnp.bfloat16)
    vmem = pl.BlockSpec(memory_space=pltpu.VMEM)
    return pl.pallas_call(
        functools.partial(rows_kernel, depth),
        out_shape=[out, out, jax.ShapeDtypeStruct(weight.shape, weight.dtype)],
        in_specs=[
            pl.BlockSpec(memory_space=pltpu.SMEM), vmem, pl.BlockSpec(memory_space=pl.ANY),
            pl.BlockSpec(memory_space=pl.ANY),
        ],
        out_specs=[vmem] * 3,
        scratch_shapes=[
            pltpu.VMEM((tokens.shape[0], STEPS, width), jnp.bfloat16),
            pltpu.SemaphoreType.DMA,
            pltpu.SemaphoreType.DMA,
        ],
        compiler_params=pltpu.CompilerParams(vmem_limit_bytes=32 * 1024 * 1024),
        cost_estimate=pl.CostEstimate(flops=0, bytes_accessed=0, transcendentals=0),
        name="token_rows",
    )(me.reshape(1), slot_of.reshape(1, -1), tokens, weight)


def product_kernel(skipped, crossed, *refs):
    mine_ref, theirs_ref, block_ref, other_ref, *refs = refs[skipped:]
    gate_refs, (kept_ref, packed_ref) = refs[:-2], refs[-2:]
    half = mine_ref.shape[0] // 2

    def product(own, other, dims):
        total = lax.dot_general(mine_ref[...], own, dims, preferred_element_type=jnp.float32)
        return total + lax.dot_general(
            theirs_ref[...], other, dims, preferred_element_type=jnp.float32
        )

    total = product(block_ref[...], other_ref[...], (((1,), (0,)), ((), ())))
    if gate_refs:
        gates = product(gate_refs[0][...], gate_refs[1][...], (((1,), (1,)), ((), ())))
        zeros = jnp.zeros((gates.shape[0], 2 * DK - gates.shape[1]), jnp.float32)
        total = jnp.concatenate([total, gates, zeros], axis=1)
    if crossed:
        starts = [start for at in range(0, half, ROWS) for start in (at, half + at)]
        total = jnp.concatenate([total[start : start + ROWS] for start in starts], axis=0)
    kept, sent = total[:half], total[half:]
    kept_ref[...] = kept
    pack_rows(sent, packed_ref)


def run_product(mine, theirs, weights, part, gates=(), earlier=(), crossed=False):
    vmem = pl.BlockSpec(memory_space=pltpu.VMEM)
    block = pl.BlockSpec((mine.shape[1], HEADS_WIDTH), lambda i: (0, part))
    half = mine.shape[0] // 2
    width = HEADS_WIDTH + len(gates) * DK
    return pl.pallas_call(
        functools.partial(product_kernel, len(earlier), crossed),
        grid=(1,),
        out_shape=[
            jax.ShapeDtypeStruct((half, width), jnp.float32),
            jax.ShapeDtypeStruct((half, width + scale_lanes(width // DK)), jnp.int16),
        ],
        in_specs=[pl.BlockSpec(memory_space=pl.ANY)] * len(earlier)
        + [vmem, vmem, block, block]
        + [vmem] * len(gates),
        out_specs=[vmem] * 2,
        compiler_params=pltpu.CompilerParams(vmem_limit_bytes=32 * 1024 * 1024),
        cost_estimate=pl.CostEstimate(flops=0, bytes_accessed=0, transcendentals=0),
        name="partial_product",
    )(*earlier, mine, theirs, *weights, *gates)


def combine_kernel(kept_ref, got_ref, still_ref, packed_ref):
    half = still_ref.shape[0]
    steps = steps_of(got_ref)
    sent = []
    for block in range(kept_ref.shape[1] // DK):
        columns = pl.ds(block * DK, DK)
        total = kept_ref[:, columns] + unpack_block(got_ref, steps, block)
        still_ref[:, columns] = total[:half]
        sent.append(total[half:])
    sent = jnp.concatenate(sent, axis=1)
    pack_rows(fold_rows(sent) if half == ROWS else sent, packed_ref)


def run_combine(kept, got):
    vmem = pl.BlockSpec(memory_space=pltpu.VMEM)
    half, width = kept.shape[0] // 2, kept.shape[1]
    rows, packed = (2 * ROWS, width // 2) if half == ROWS else (half, width)
    packed = (rows, packed + scale_lanes(packed // DK))
    return pl.pallas_call(
        combine_kernel,
        out_shape=[
            jax.ShapeDtypeStruct((half, width), jnp.float32),
            jax.ShapeDtypeStruct(packed, jnp.int16),
        ],
        in_specs=[vmem] * 2,
        out_specs=[vmem] * 2,
        compiler_params=pltpu.CompilerParams(vmem_limit_bytes=32 * 1024 * 1024),
        cost_estimate=pl.CostEstimate(flops=0, bytes_accessed=0, transcendentals=0),
        name="combine",
    )(kept, got)


def join_kernel(first_ref, second_ref, earlier_ref, out_ref):
    both = [ref[...].astype(jnp.float32) for ref in (first_ref, second_ref)]
    out_ref[...] = jnp.concatenate(both, axis=0).astype(out_ref.dtype)


def join(first, second, earlier):
    vmem = pl.BlockSpec(memory_space=pltpu.VMEM)
    rows, width = first.shape
    return pl.pallas_call(
        join_kernel,
        out_shape=jax.ShapeDtypeStruct((2 * rows, width), first.dtype),
        in_specs=[vmem, vmem, pl.BlockSpec(memory_space=pl.ANY)],
        out_specs=vmem,
        compiler_params=pltpu.CompilerParams(vmem_limit_bytes=32 * 1024 * 1024),
        cost_estimate=pl.CostEstimate(flops=0, bytes_accessed=0, transcendentals=0),
        name="join_taps",
    )(first, second, earlier)


def swap(value, bit, devices):
    return lax.ppermute(value, "heads", [(i, i ^ bit) for i in range(devices)])


def on_device(
    tokens,
    qkv_weight,
    gate_weight,
    conv_weight,
    delta_state,
    conv_state,
    old_heads,
    new_units,
    slot_of,
    lengths,
):
    devices = lax.axis_size("heads")
    me = lax.axis_index("heads")
    per_device = UNITS // devices
    row_count = tokens.shape[0]
    chips = devices // 2

    bits = [1 << b for b in range(1, devices.bit_length() - 1)]

    ride = conv_weight.shape[1] == 2 * TAP_WIDTH and len(bits) == 3
    if ride:
        taps = jnp.concatenate([conv_weight[:, :TAP_WIDTH], conv_weight[:, TAP_WIDTH:]], axis=0)
        far = swap(taps, 4, devices)
    else:
        taps = lax.all_gather(conv_weight, "heads", axis=1, tiled=True)
        order = [
            2 * (at >> 4 & 1) + 4 * (at >> 3 & 1) + 8 * (at >> 1 & 1) + 16 * (at >> 2 & 1) + (at & 1)
            for at in range(TAP_BLOCKS)
        ]
        taps = [taps[:, block * TAP_WIDTH : (block + 1) * TAP_WIDTH] for block in order]
        taps = jnp.concatenate(taps, axis=0)

    mine, theirs, near_weight = run_rows(me, slot_of, tokens, qkv_weight, chips)

    weights = (near_weight, swap(qkv_weight, 1, devices))
    gate_columns = gate_weight.T
    gates = (gate_columns, swap(gate_columns, 1, devices))

    tie = lambda *values: lax.optimization_barrier(values)

    if ride:
        taps = join(taps, far, mine)
        far = swap(taps, 8, devices)
    keys = run_product(mine, theirs, weights, 1)
    values = run_product(mine, theirs, weights, 2, gates, earlier=keys[:1])
    if ride:
        taps = join(taps, far, values[0])
        far = swap(taps, 2, devices)
    queries = run_product(mine, theirs, weights, 0, earlier=(values[0], taps), crossed=True)

    slot_of, lengths, old_heads, new_units, carried, *values = tie(
        slot_of, lengths, old_heads, new_units, conv_state, *values
    )
    steps = jnp.arange(STEPS, dtype=jnp.int32)
    offered = (slot_of[:, None] * STEPS + steps[None, :]).reshape(-1)
    old_slots, halves = unit_tables(old_heads, new_units)
    my_rows = me * LOCAL + jnp.arange(LOCAL, dtype=jnp.int32)
    my_lengths = jnp.sum(
        jnp.where(slot_of[None, :] == my_rows[:, None], lengths[None, :], 0), axis=1
    )
    blank = jnp.zeros((1, carried.shape[2]), jnp.float32)
    history = jnp.concatenate([blank, carried[1], blank, carried[0]], axis=0)
    routes = [bits[1:] + bits[:1], bits, bits]
    kept = [chunk[0] for chunk in (queries, keys, values)]
    got = [
        swap(chunk[1], route[0], devices)
        for chunk, route in zip((queries, keys, values), routes)
    ]
    for level in range(1, len(bits)):
        for at in range(3):
            kept[at], packed = run_combine(kept[at], got[at])
            got[at] = swap(packed, routes[at][level], devices)
        if ride and level == 1:
            taps = join(taps, far, kept[2])
            far = swap(taps, 1, devices)
    if ride:
        twist, taps = me.reshape(1), (taps, far)
    else:
        half = TAP_BLOCKS // 2 * TAPS
        twist, taps = jnp.zeros(1, jnp.int32), (taps[:half], taps[half:])
    queries, keys, values = zip(kept, got)

    local_out = run_delta(
        old_slots, halves, my_lengths, queries, keys, values, history, twist, taps, delta_state
    )

    placer = (offered[:, None] == jnp.arange(row_count * STEPS, dtype=jnp.int32)[None, :]).astype(
        jnp.bfloat16
    )
    if per_device % 2 == 0:
        pairs = per_device // 2
        sending = local_out.reshape(devices, pairs * ROWS, DK)
        got = lax.all_to_all(sending, "heads", split_axis=0, concat_axis=0, tiled=True)
        got = got.reshape(devices, pairs, ROWS, DK)
        got = jnp.concatenate([got[:, pair] for pair in range(pairs)], axis=-1)
        got = got.reshape(devices * ROWS, pairs * DK)
    else:
        units = local_out.reshape(UNITS // 2, ROWS, 2, HALF).transpose(0, 2, 1, 3)
        sending = units.reshape(devices, per_device * ROWS, HALF)
        got = lax.all_to_all(sending, "heads", split_axis=0, concat_axis=0, tiled=True)
        got = got.reshape(devices, per_device, ROWS, HALF).transpose(0, 2, 1, 3)
        got = got.reshape(devices * ROWS, per_device * HALF)
    outputs = jnp.dot(placer, got, preferred_element_type=jnp.float32).astype(jnp.bfloat16)
    return outputs.reshape(row_count, STEPS, per_device * HALF)


def solution(mesh):
    in_specs = (
        P("groups", None, None),
        P(("groups", "heads"), None),
        P(("groups", "heads"), None),
        P("groups", "heads"),
        P(("groups", "heads"), None, None, None),
        P(("groups", "heads"), None, None),
        P(),
        P(),
        P("groups"),
        P("groups"),
    )
    out_specs = P("groups", None, "heads")
    return jax.shard_map(
        on_device, mesh=mesh, in_specs=in_specs, out_specs=out_specs, check_vma=False
    )
```

```python
import functools

import jax
import jax.numpy as jnp
from jax import lax
from jax.experimental import pallas as pl
from jax.experimental.pallas import tpu as pltpu
from jax.sharding import PartitionSpec as P

D = 2304
H = 32
DK = 128
TAPS = 4
STEPS = 4
HALF = 64
UNITS = 64
LOCAL = 2
ROWS = LOCAL * STEPS
HEADS_WIDTH = H * DK
LEVELS = 32767.0
STATE_COPIES = 4
TAP_WIDTH = 384
TAP_BLOCKS = 3 * HEADS_WIDTH // TAP_WIDTH


norm_eps = 1e-06


def unit_tables(old_heads, new_units):
    positions = jnp.arange(H, dtype=jnp.int32)
    inverse = jnp.sum(
        jnp.where(old_heads[None, :] == positions[:, None], positions[None, :], 0), axis=1
    )
    heads_of = new_units // 2
    halves = new_units % 2
    old_slots = jnp.sum(
        jnp.where(heads_of[:, None] == positions[None, :], inverse[None, :], 0), axis=1
    )
    return (old_slots, halves)


def shift_rows(value, lag, row_step):
    if lag == 0:
        return value
    moved = pltpu.roll(value, lag, 0)
    return jnp.where(row_step >= lag, moved, 0.0)


def lane_sum(value):
    return jnp.sum(value, axis=-1, keepdims=True)


def unit_length(value):
    return value * lax.rsqrt(lane_sum(value * value) + norm_eps)


def scale_lanes(blocks):
    return -(-blocks // HALF) * DK


def pack_rows(total, packed_ref):
    rows, width = total.shape
    blocks = width // DK
    lanes = scale_lanes(blocks)
    lane = lax.broadcasted_iota(jnp.int32, (rows, lanes), 1)
    scales = jnp.zeros((rows, lanes), jnp.float32)
    for block in range(blocks):
        part = total[:, block * DK : (block + 1) * DK]
        top = jnp.max(jnp.abs(part), axis=-1, keepdims=True) + 1e-30
        exponent = jnp.ceil(jnp.log2(top))
        mantissa = jnp.ceil(jnp.minimum(top * jnp.exp2(-exponent) * LEVELS, LEVELS))
        factor = LEVELS * LEVELS * jnp.exp2(-exponent) / mantissa
        coded = jnp.clip(jnp.floor(part * factor + 0.5), -LEVELS, LEVELS)
        packed_ref[:, block * DK : (block + 1) * DK] = coded.astype(jnp.int32).astype(jnp.int16)
        scales = jnp.where(lane == block, mantissa, scales)
        scales = jnp.where(lane == lanes // 2 + block, exponent, scales)
    packed_ref[:, width:] = scales.astype(jnp.int32).astype(jnp.int16)


def to_float(coded):
    return coded.astype(jnp.int32).astype(jnp.float32)


def steps_of(packed_ref):
    lanes = DK if packed_ref.shape[1] <= (HALF + 1) * DK else 2 * DK
    scales = to_float(packed_ref[:, packed_ref.shape[1] - lanes :])
    exponents = pltpu.roll(scales, lanes // 2, 1)
    return scales * jnp.exp2(exponents) * (1.0 / (LEVELS * LEVELS))


def unpack_block(packed_ref, steps, block):
    return to_float(packed_ref[:, block * DK : (block + 1) * DK]) * steps[:, block : block + 1]


def fold_rows(value):
    half = value.shape[1] // 2
    return jnp.concatenate([value[:, :half], value[:, half:]], axis=0)


def received(kept_ref, got_ref, steps, block):
    half = kept_ref.shape[1] // DK // 2
    rows = unpack_block(got_ref, steps, block % half)
    rows = rows[:ROWS] if block < half else rows[ROWS:]
    return kept_ref[:, block * DK : (block + 1) * DK] + rows


def tap_block(block, me):
    other = jnp.bitwise_xor(block // 2, me)
    place = ((other >> 2) & 3) + ((other >> 1) & 1) * 4 + (other & 1) * 8
    return place * 2 + block % 2


def activate(kept_ref, got_ref, steps, part, head, history_ref, taps_ref, twist, row_step):
    fresh = received(kept_ref, got_ref, steps, head)
    column = part * HEADS_WIDTH + head * DK
    carried = history_ref[:, column : column + DK]
    taps = taps_ref[tap_block(column // TAP_WIDTH, twist)]
    inner = column % TAP_WIDTH
    total = taps[TAPS - 1 :, inner : inner + DK] * fresh
    for lag in range(1, TAPS):
        source = jnp.where(row_step >= STEPS - lag, carried, fresh)
        tap = taps[TAPS - 1 - lag : TAPS - lag, inner : inner + DK]
        total = total + tap * pltpu.roll(source, lag, 0)
    return total / (1.0 + jnp.exp(-total))


def keys_kernel(
    twist_ref, query_ref, query_got_ref, key_ref, key_got_ref, history_ref, near_ref, far_ref,
    state_hbm, key_seen_ref, query_seen_ref, pulls_ref, weights_ref, taps_ref, state_ref, sems,
):
    per_copy = H // STATE_COPIES
    copies = []
    for at in range(STATE_COPIES):
        some = pl.ds(at * per_copy, per_copy)
        copies.append(
            pltpu.make_async_copy(state_hbm.at[:, some], state_ref.at[:, some], sems.at[at])
        )
        copies[-1].start()
    twist = twist_ref[0]
    half = TAP_BLOCKS // 2
    for at in range(TAP_BLOCKS):
        source = near_ref if at < half else far_ref
        if at % 4 == 0:
            some = source[at % half * TAPS : (at % half + 4) * TAPS, :].astype(jnp.float32)
        taps_ref[at] = some[at % 4 * TAPS : (at % 4 + 1) * TAPS]
    row = lax.broadcasted_iota(jnp.int32, (ROWS, DK), 0)
    row_step = row % STEPS
    query_steps, key_steps = steps_of(query_got_ref), steps_of(key_got_ref)
    for head in range(H):
        key = unit_length(
            activate(
                key_ref, key_got_ref, key_steps, 1, head, history_ref, taps_ref, twist, row_step
            )
        )
        query = unit_length(
            activate(
                query_ref, query_got_ref, query_steps, 0, head, history_ref, taps_ref, twist,
                row_step,
            )
        )
        both = jnp.concatenate([key, query], axis=0)
        if head % per_copy == 0:
            copies[head // per_copy].wait()
        both_high = both.astype(jnp.bfloat16)
        both_low = (both - both_high.astype(jnp.float32)).astype(jnp.bfloat16)
        stacked = jnp.concatenate([both_high, both_low], axis=0)
        seen = []
        for r in range(LOCAL):
            state = state_ref[r, head]
            high = state.astype(jnp.bfloat16)
            low = (state - high.astype(jnp.float32)).astype(jnp.bfloat16)
            main = jnp.dot(stacked, high, preferred_element_type=jnp.float32)
            rest = jnp.dot(both_high, low, preferred_element_type=jnp.float32)
            seen.append(main[: 2 * ROWS] + main[2 * ROWS :] + rest)
        key_seen_ref[head] = jnp.where(row < STEPS, seen[0][:ROWS], seen[1][:ROWS])
        query_seen_ref[head] = jnp.where(row < STEPS, seen[0][ROWS:], seen[1][ROWS:])
        for lag in range(STEPS):
            moved_key = shift_rows(key, lag, row_step)
            if lag:
                pulls_ref[lag - 1, head] = jnp.broadcast_to(lane_sum(key * moved_key), (ROWS, DK))
            weights_ref[lag, head] = jnp.broadcast_to(lane_sum(query * moved_key), (ROWS, DK))


def values_kernel(
    slots_ref, halves_ref, lengths_ref, twist_ref, value_ref, value_got_ref, history_ref,
    key_seen_ref, query_seen_ref, pulls_ref, weights_ref, taps_ref, out_ref, heads_ref,
):
    twist = twist_ref[0]
    row = lax.broadcasted_iota(jnp.int32, (ROWS, DK), 0)
    row_step = row % STEPS
    lane = lax.broadcasted_iota(jnp.int32, (ROWS, DK), 1)
    row_length = jnp.where(row < STEPS, lengths_ref[0], lengths_ref[1])
    live = row_step < row_length
    value_steps = steps_of(value_got_ref)
    gates = received(value_ref, value_got_ref, value_steps, H)
    for head in range(H):
        value = activate(
            value_ref, value_got_ref, value_steps, 2, head, history_ref, taps_ref, twist, row_step
        )
        beta_logit = jnp.broadcast_to(gates[:, head : head + 1], (ROWS, DK))
        decay_logit = jnp.broadcast_to(gates[:, H + head : H + head + 1], (ROWS, DK))
        beta = 1.0 / (1.0 + jnp.exp(-beta_logit))
        decay = 1.0 / (1.0 + jnp.exp(decay_logit))
        fades = [jnp.ones_like(decay), decay]
        for lag in range(2, STEPS + 1):
            earlier = pltpu.roll(decay, lag - 1, 0)
            fades.append(jnp.where(row_step >= lag - 1, fades[-1] * earlier, fades[-1]))
        base = beta * (value - fades[STEPS] * key_seen_ref[head])
        pulls = [
            beta * fades[lag] * pulls_ref[lag - 1, head] if lag else None for lag in range(STEPS)
        ]
        solved = base
        for _ in range(STEPS - 1):
            following = base
            for lag in range(1, STEPS):
                following = following - pulls[lag] * shift_rows(solved, lag, row_step)
            solved = following
        out = fades[STEPS] * query_seen_ref[head]
        for lag in range(STEPS):
            weight = fades[lag] * weights_ref[lag, head]
            out = out + weight * shift_rows(solved, lag, row_step)
        heads_ref[head] = jnp.where(live, out, 0.0)
    for quad in range(UNITS // 4):
        joined = []
        for pair in (2 * quad, 2 * quad + 1):
            first = heads_ref[slots_ref[2 * pair]]
            second = heads_ref[slots_ref[2 * pair + 1]]
            first = jnp.where(halves_ref[2 * pair] == 0, first, pltpu.roll(first, HALF, 1))
            second = jnp.where(halves_ref[2 * pair + 1] == 0, pltpu.roll(second, HALF, 1), second)
            joined.append(jnp.where(lane < HALF, first, second))
        out_ref[quad] = jnp.concatenate(joined, axis=0).astype(jnp.bfloat16)


def run_delta(slots, halves, lengths, queries, keys, values, history, twist, taps, state):
    smem = pl.BlockSpec(memory_space=pltpu.SMEM)
    vmem = pl.BlockSpec(memory_space=pltpu.VMEM)
    params = pltpu.CompilerParams(vmem_limit_bytes=32 * 1024 * 1024)
    per_head = jax.ShapeDtypeStruct((H, ROWS, DK), jnp.float32)
    lags = [
        jax.ShapeDtypeStruct((count, H, ROWS, DK), jnp.float32) for count in (STEPS - 1, STEPS)
    ]
    tap_blocks = jax.ShapeDtypeStruct((TAP_BLOCKS, TAPS, TAP_WIDTH), jnp.float32)
    prepared = pl.pallas_call(
        keys_kernel,
        out_shape=[per_head] * 2 + lags + [tap_blocks],
        in_specs=[smem] + [vmem] * 7 + [pl.BlockSpec(memory_space=pl.ANY)],
        out_specs=[vmem] * 5,
        scratch_shapes=[
            pltpu.VMEM(state.shape, jnp.float32),
            pltpu.SemaphoreType.DMA((STATE_COPIES,)),
        ],
        compiler_params=params,
        cost_estimate=pl.CostEstimate(flops=40_000_000, bytes_accessed=9_000_000, transcendentals=0),
        name="keys_part",
    )(twist, *queries, *keys, history, *taps, state)
    return pl.pallas_call(
        values_kernel,
        out_shape=jax.ShapeDtypeStruct((UNITS // 4, 2 * ROWS, DK), jnp.bfloat16),
        in_specs=[smem] * 4 + [vmem] * 8,
        out_specs=vmem,
        scratch_shapes=[pltpu.VMEM((H, ROWS, DK), jnp.float32)],
        compiler_params=params,
        cost_estimate=pl.CostEstimate(flops=4_000_000, bytes_accessed=2_000_000, transcendentals=0),
        name="values_part",
    )(slots, halves, lengths, twist, *values, history, *prepared)


def rows_kernel(
    depth, me_ref, slot_of_ref, tokens_hbm, weight_hbm, mine_ref, theirs_ref,
    weight_ref, window_ref, sem, weight_sem,
):
    me = me_ref[0]
    width = window_ref.shape[2]
    offset = me // 2 * (2 * depth)
    start = jnp.minimum(offset // DK * DK, D - width)
    columns = pl.ds(pl.multiple_of(start, DK), width)
    copy = pltpu.make_async_copy(tokens_hbm.at[:, :, columns], window_ref, sem)
    copy.start()
    weight_copy = pltpu.make_async_copy(weight_hbm, weight_ref, weight_sem)
    weight_copy.start()
    shape = (mine_ref.shape[0], slot_of_ref.shape[1])
    row = lax.broadcasted_iota(jnp.int32, shape, 0)
    place = row // ROWS
    count = (shape[0] // ROWS).bit_length() - 1
    holder = jnp.zeros(shape, jnp.int32)
    for at in range(count):
        holder = holder + ((place >> (count - 1 - at)) & 1) * (2 << at)
    holder = jnp.bitwise_xor(holder, me)
    match = holder * LOCAL + row % ROWS // STEPS == slot_of_ref[...]
    copy.wait()
    window = window_ref[...].astype(jnp.float32)
    total = jnp.zeros((shape[0], width), jnp.float32)
    for step in range(STEPS):
        picker = jnp.where(match & (row % STEPS == step), 1.0, 0.0).astype(jnp.bfloat16)
        here = window[:, step, :].astype(jnp.bfloat16)
        total = total + jnp.dot(picker, here, preferred_element_type=jnp.float32)
    total = pltpu.roll(total, lax.rem(width - (offset - start), width), 1)
    low, high = total[:, :depth], total[:, depth : 2 * depth]
    first_core = me % 2 == 0
    mine_ref[...] = jnp.where(first_core, low, high).astype(jnp.bfloat16)
    theirs_ref[...] = jnp.where(first_core, high, low).astype(jnp.bfloat16)
    weight_copy.wait()


def run_rows(me, slot_of, tokens, weight, chips):
    depth = weight.shape[0]
    width = -(-(2 * depth + DK - 1) // DK) * DK
    out = jax.ShapeDtypeStruct((chips * ROWS, depth), jnp.bfloat16)
    vmem = pl.BlockSpec(memory_space=pltpu.VMEM)
    return pl.pallas_call(
        functools.partial(rows_kernel, depth),
        out_shape=[out, out, jax.ShapeDtypeStruct(weight.shape, weight.dtype)],
        in_specs=[
            pl.BlockSpec(memory_space=pltpu.SMEM), vmem, pl.BlockSpec(memory_space=pl.ANY),
            pl.BlockSpec(memory_space=pl.ANY),
        ],
        out_specs=[vmem] * 3,
        scratch_shapes=[
            pltpu.VMEM((tokens.shape[0], STEPS, width), jnp.bfloat16),
            pltpu.SemaphoreType.DMA,
            pltpu.SemaphoreType.DMA,
        ],
        compiler_params=pltpu.CompilerParams(vmem_limit_bytes=32 * 1024 * 1024),
        cost_estimate=pl.CostEstimate(flops=0, bytes_accessed=0, transcendentals=0),
        name="token_rows",
    )(me.reshape(1), slot_of.reshape(1, -1), tokens, weight)


def product_kernel(skipped, crossed, *refs):
    mine_ref, theirs_ref, block_ref, other_ref, *refs = refs[skipped:]
    gate_refs, (kept_ref, packed_ref) = refs[:-2], refs[-2:]
    half = mine_ref.shape[0] // 2

    def product(own, other, dims):
        total = lax.dot_general(mine_ref[...], own, dims, preferred_element_type=jnp.float32)
        return total + lax.dot_general(
            theirs_ref[...], other, dims, preferred_element_type=jnp.float32
        )

    total = product(block_ref[...], other_ref[...], (((1,), (0,)), ((), ())))
    if gate_refs:
        gates = product(gate_refs[0][...], gate_refs[1][...], (((1,), (1,)), ((), ())))
        zeros = jnp.zeros((gates.shape[0], 2 * DK - gates.shape[1]), jnp.float32)
        total = jnp.concatenate([total, gates, zeros], axis=1)
    if crossed:
        starts = [start for at in range(0, half, ROWS) for start in (at, half + at)]
        total = jnp.concatenate([total[start : start + ROWS] for start in starts], axis=0)
    kept, sent = total[:half], total[half:]
    kept_ref[...] = kept
    pack_rows(sent, packed_ref)


def run_product(mine, theirs, weights, part, gates=(), earlier=(), crossed=False):
    vmem = pl.BlockSpec(memory_space=pltpu.VMEM)
    block = pl.BlockSpec((mine.shape[1], HEADS_WIDTH), lambda i: (0, part))
    half = mine.shape[0] // 2
    width = HEADS_WIDTH + len(gates) * DK
    return pl.pallas_call(
        functools.partial(product_kernel, len(earlier), crossed),
        grid=(1,),
        out_shape=[
            jax.ShapeDtypeStruct((half, width), jnp.float32),
            jax.ShapeDtypeStruct((half, width + scale_lanes(width // DK)), jnp.int16),
        ],
        in_specs=[pl.BlockSpec(memory_space=pl.ANY)] * len(earlier)
        + [vmem, vmem, block, block]
        + [vmem] * len(gates),
        out_specs=[vmem] * 2,
        compiler_params=pltpu.CompilerParams(vmem_limit_bytes=32 * 1024 * 1024),
        cost_estimate=pl.CostEstimate(flops=0, bytes_accessed=0, transcendentals=0),
        name="partial_product",
    )(*earlier, mine, theirs, *weights, *gates)


def combine_kernel(kept_ref, got_ref, still_ref, packed_ref):
    half = still_ref.shape[0]
    steps = steps_of(got_ref)
    sent = []
    for block in range(kept_ref.shape[1] // DK):
        columns = pl.ds(block * DK, DK)
        total = kept_ref[:, columns] + unpack_block(got_ref, steps, block)
        still_ref[:, columns] = total[:half]
        sent.append(total[half:])
    sent = jnp.concatenate(sent, axis=1)
    pack_rows(fold_rows(sent) if half == ROWS else sent, packed_ref)


def run_combine(kept, got):
    vmem = pl.BlockSpec(memory_space=pltpu.VMEM)
    half, width = kept.shape[0] // 2, kept.shape[1]
    rows, packed = (2 * ROWS, width // 2) if half == ROWS else (half, width)
    packed = (rows, packed + scale_lanes(packed // DK))
    return pl.pallas_call(
        combine_kernel,
        out_shape=[
            jax.ShapeDtypeStruct((half, width), jnp.float32),
            jax.ShapeDtypeStruct(packed, jnp.int16),
        ],
        in_specs=[vmem] * 2,
        out_specs=[vmem] * 2,
        compiler_params=pltpu.CompilerParams(vmem_limit_bytes=32 * 1024 * 1024),
        cost_estimate=pl.CostEstimate(flops=0, bytes_accessed=0, transcendentals=0),
        name="combine",
    )(kept, got)


def join_kernel(first_ref, second_ref, earlier_ref, out_ref):
    both = [ref[...].astype(jnp.float32) for ref in (first_ref, second_ref)]
    out_ref[...] = jnp.concatenate(both, axis=0).astype(out_ref.dtype)


def join(first, second, earlier):
    vmem = pl.BlockSpec(memory_space=pltpu.VMEM)
    rows, width = first.shape
    return pl.pallas_call(
        join_kernel,
        out_shape=jax.ShapeDtypeStruct((2 * rows, width), first.dtype),
        in_specs=[vmem, vmem, pl.BlockSpec(memory_space=pl.ANY)],
        out_specs=vmem,
        compiler_params=pltpu.CompilerParams(vmem_limit_bytes=32 * 1024 * 1024),
        cost_estimate=pl.CostEstimate(flops=0, bytes_accessed=0, transcendentals=0),
        name="join_taps",
    )(first, second, earlier)


def swap(value, bit, devices):
    return lax.ppermute(value, "heads", [(i, i ^ bit) for i in range(devices)])


def on_device(
    tokens,
    qkv_weight,
    gate_weight,
    conv_weight,
    delta_state,
    conv_state,
    old_heads,
    new_units,
    slot_of,
    lengths,
):
    devices = lax.axis_size("heads")
    me = lax.axis_index("heads")
    per_device = UNITS // devices
    row_count = tokens.shape[0]
    chips = devices // 2

    bits = [1 << b for b in range(1, devices.bit_length() - 1)]

    ride = conv_weight.shape[1] == 2 * TAP_WIDTH and len(bits) == 3
    if ride:
        taps = jnp.concatenate([conv_weight[:, :TAP_WIDTH], conv_weight[:, TAP_WIDTH:]], axis=0)
        far = swap(taps, 4, devices)
    else:
        taps = lax.all_gather(conv_weight, "heads", axis=1, tiled=True)
        order = [
            2 * (at >> 4 & 1) + 4 * (at >> 3 & 1) + 8 * (at >> 1 & 1) + 16 * (at >> 2 & 1) + (at & 1)
            for at in range(TAP_BLOCKS)
        ]
        taps = [taps[:, block * TAP_WIDTH : (block + 1) * TAP_WIDTH] for block in order]
        taps = jnp.concatenate(taps, axis=0)

    mine, theirs, near_weight = run_rows(me, slot_of, tokens, qkv_weight, chips)

    weights = (near_weight, swap(qkv_weight, 1, devices))
    gate_columns = gate_weight.T
    gates = (gate_columns, swap(gate_columns, 1, devices))

    tie = lambda *values: lax.optimization_barrier(values)

    if ride:
        taps = join(taps, far, mine)
        far = swap(taps, 8, devices)
    keys = run_product(mine, theirs, weights, 1)
    values = run_product(mine, theirs, weights, 2, gates, earlier=keys[:1])
    queries = run_product(mine, theirs, weights, 0, earlier=values[:1], crossed=True)

    slot_of, lengths, old_heads, new_units, carried, *values = tie(
        slot_of, lengths, old_heads, new_units, conv_state, *values
    )
    steps = jnp.arange(STEPS, dtype=jnp.int32)
    offered = (slot_of[:, None] * STEPS + steps[None, :]).reshape(-1)
    old_slots, halves = unit_tables(old_heads, new_units)
    my_rows = me * LOCAL + jnp.arange(LOCAL, dtype=jnp.int32)
    my_lengths = jnp.sum(
        jnp.where(slot_of[None, :] == my_rows[:, None], lengths[None, :], 0), axis=1
    )
    blank = jnp.zeros((1, carried.shape[2]), jnp.float32)
    history = jnp.concatenate([blank, carried[1], blank, carried[0]], axis=0)
    routes = [bits[1:] + bits[:1], bits, bits]
    kept = [chunk[0] for chunk in (queries, keys, values)]
    got = [
        swap(chunk[1], route[0], devices)
        for chunk, route in zip((queries, keys, values), routes)
    ]
    for level in range(1, len(bits)):
        for at in range(3):
            kept[at], packed = run_combine(kept[at], got[at])
            got[at] = swap(packed, routes[at][level], devices)
            if ride and at == 2 - level:
                taps = join(taps, far, kept[at])
                far = swap(taps, 3 - level, devices)
    if ride:
        twist, taps = me.reshape(1), (taps, far)
    else:
        half = TAP_BLOCKS // 2 * TAPS
        twist, taps = jnp.zeros(1, jnp.int32), (taps[:half], taps[half:])
    queries, keys, values = zip(kept, got)

    local_out = run_delta(
        old_slots, halves, my_lengths, queries, keys, values, history, twist, taps, delta_state
    )

    placer = (offered[:, None] == jnp.arange(row_count * STEPS, dtype=jnp.int32)[None, :]).astype(
        jnp.bfloat16
    )
    if per_device % 2 == 0:
        pairs = per_device // 2
        sending = local_out.reshape(devices, pairs * ROWS, DK)
        got = lax.all_to_all(sending, "heads", split_axis=0, concat_axis=0, tiled=True)
        got = got.reshape(devices, pairs, ROWS, DK)
        got = jnp.concatenate([got[:, pair] for pair in range(pairs)], axis=-1)
        got = got.reshape(devices * ROWS, pairs * DK)
    else:
        units = local_out.reshape(UNITS // 2, ROWS, 2, HALF).transpose(0, 2, 1, 3)
        sending = units.reshape(devices, per_device * ROWS, HALF)
        got = lax.all_to_all(sending, "heads", split_axis=0, concat_axis=0, tiled=True)
        got = got.reshape(devices, per_device, ROWS, HALF).transpose(0, 2, 1, 3)
        got = got.reshape(devices * ROWS, per_device * HALF)
    outputs = jnp.dot(placer, got, preferred_element_type=jnp.float32).astype(jnp.bfloat16)
    return outputs.reshape(row_count, STEPS, per_device * HALF)


def solution(mesh):
    in_specs = (
        P("groups", None, None),
        P(("groups", "heads"), None),
        P(("groups", "heads"), None),
        P("groups", "heads"),
        P(("groups", "heads"), None, None, None),
        P(("groups", "heads"), None, None),
        P(),
        P(),
        P("groups"),
        P("groups"),
    )
    out_specs = P("groups", None, "heads")
    return jax.shard_map(
        on_device, mesh=mesh, in_specs=in_specs, out_specs=out_specs, check_vma=False
    )
```

```python
import functools

import jax
import jax.numpy as jnp
from jax import lax
from jax.experimental import pallas as pl
from jax.experimental.pallas import tpu as pltpu
from jax.sharding import PartitionSpec as P

D = 2304
H = 32
DK = 128
TAPS = 4
STEPS = 4
HALF = 64
UNITS = 64
LOCAL = 2
ROWS = LOCAL * STEPS
HEADS_WIDTH = H * DK
LEVELS = 32767.0
STATE_COPIES = 4
TAP_WIDTH = 384
TAP_BLOCKS = 3 * HEADS_WIDTH // TAP_WIDTH


norm_eps = 1e-06


def unit_tables(old_heads, new_units):
    positions = jnp.arange(H, dtype=jnp.int32)
    inverse = jnp.sum(
        jnp.where(old_heads[None, :] == positions[:, None], positions[None, :], 0), axis=1
    )
    heads_of = new_units // 2
    halves = new_units % 2
    old_slots = jnp.sum(
        jnp.where(heads_of[:, None] == positions[None, :], inverse[None, :], 0), axis=1
    )
    return (old_slots, halves)


def shift_rows(value, lag, row_step):
    if lag == 0:
        return value
    moved = pltpu.roll(value, lag, 0)
    return jnp.where(row_step >= lag, moved, 0.0)


def lane_sum(value):
    return jnp.sum(value, axis=-1, keepdims=True)


def unit_length(value):
    return value * lax.rsqrt(lane_sum(value * value) + norm_eps)


def scale_lanes(blocks):
    return -(-blocks // HALF) * DK


def pack_rows(total, packed_ref):
    rows, width = total.shape
    blocks = width // DK
    lanes = scale_lanes(blocks)
    lane = lax.broadcasted_iota(jnp.int32, (rows, lanes), 1)
    scales = jnp.zeros((rows, lanes), jnp.float32)
    for block in range(blocks):
        part = total[:, block * DK : (block + 1) * DK]
        top = jnp.max(jnp.abs(part), axis=-1, keepdims=True) + 1e-30
        exponent = jnp.ceil(jnp.log2(top))
        mantissa = jnp.ceil(jnp.minimum(top * jnp.exp2(-exponent) * LEVELS, LEVELS))
        factor = LEVELS * LEVELS * jnp.exp2(-exponent) / mantissa
        coded = jnp.clip(jnp.floor(part * factor + 0.5), -LEVELS, LEVELS)
        packed_ref[:, block * DK : (block + 1) * DK] = coded.astype(jnp.int32).astype(jnp.int16)
        scales = jnp.where(lane == block, mantissa, scales)
        scales = jnp.where(lane == lanes // 2 + block, exponent, scales)
    packed_ref[:, width:] = scales.astype(jnp.int32).astype(jnp.int16)


def to_float(coded):
    return coded.astype(jnp.int32).astype(jnp.float32)


def steps_of(packed_ref):
    lanes = DK if packed_ref.shape[1] <= (HALF + 1) * DK else 2 * DK
    scales = to_float(packed_ref[:, packed_ref.shape[1] - lanes :])
    exponents = pltpu.roll(scales, lanes // 2, 1)
    return scales * jnp.exp2(exponents) * (1.0 / (LEVELS * LEVELS))


def unpack_block(packed_ref, steps, block):
    return to_float(packed_ref[:, block * DK : (block + 1) * DK]) * steps[:, block : block + 1]


def fold_rows(value):
    half = value.shape[1] // 2
    return jnp.concatenate([value[:, :half], value[:, half:]], axis=0)


def received(kept_ref, got_ref, steps, block):
    half = kept_ref.shape[1] // DK // 2
    rows = unpack_block(got_ref, steps, block % half)
    rows = rows[:ROWS] if block < half else rows[ROWS:]
    return kept_ref[:, block * DK : (block + 1) * DK] + rows


def tap_block(block, me):
    other = jnp.bitwise_xor(block // 2, me)
    place = ((other >> 2) & 3) + ((other >> 1) & 1) * 4 + (other & 1) * 8
    return place * 2 + block % 2


def activate(kept_ref, got_ref, steps, part, head, history_ref, taps_ref, twist, row_step):
    fresh = received(kept_ref, got_ref, steps, head)
    column = part * HEADS_WIDTH + head * DK
    carried = history_ref[:, column : column + DK]
    taps = taps_ref[tap_block(column // TAP_WIDTH, twist)]
    inner = column % TAP_WIDTH
    total = taps[TAPS - 1 :, inner : inner + DK] * fresh
    for lag in range(1, TAPS):
        source = jnp.where(row_step >= STEPS - lag, carried, fresh)
        tap = taps[TAPS - 1 - lag : TAPS - lag, inner : inner + DK]
        total = total + tap * pltpu.roll(source, lag, 0)
    return total / (1.0 + jnp.exp(-total))


def keys_kernel(
    twist_ref, query_ref, query_got_ref, key_ref, key_got_ref, history_ref, near_ref, far_ref,
    state_hbm, key_seen_ref, query_seen_ref, pulls_ref, weights_ref, taps_ref, state_ref, sems,
):
    per_copy = H // STATE_COPIES
    copies = []
    for at in range(STATE_COPIES):
        some = pl.ds(at * per_copy, per_copy)
        copies.append(
            pltpu.make_async_copy(state_hbm.at[:, some], state_ref.at[:, some], sems.at[at])
        )
        copies[-1].start()
    twist = twist_ref[0]
    half = TAP_BLOCKS // 2
    for at in range(TAP_BLOCKS):
        source = near_ref if at < half else far_ref
        if at % 4 == 0:
            some = source[at % half * TAPS : (at % half + 4) * TAPS, :].astype(jnp.float32)
        taps_ref[at] = some[at % 4 * TAPS : (at % 4 + 1) * TAPS]
    row = lax.broadcasted_iota(jnp.int32, (ROWS, DK), 0)
    row_step = row % STEPS
    query_steps, key_steps = steps_of(query_got_ref), steps_of(key_got_ref)
    for head in range(H):
        key = unit_length(
            activate(
                key_ref, key_got_ref, key_steps, 1, head, history_ref, taps_ref, twist, row_step
            )
        )
        query = unit_length(
            activate(
                query_ref, query_got_ref, query_steps, 0, head, history_ref, taps_ref, twist,
                row_step,
            )
        )
        both = jnp.concatenate([key, query], axis=0)
        if head % per_copy == 0:
            copies[head // per_copy].wait()
        both_high = both.astype(jnp.bfloat16)
        both_low = (both - both_high.astype(jnp.float32)).astype(jnp.bfloat16)
        stacked = jnp.concatenate([both_high, both_low], axis=0)
        seen = []
        for r in range(LOCAL):
            state = state_ref[r, head]
            high = state.astype(jnp.bfloat16)
            low = (state - high.astype(jnp.float32)).astype(jnp.bfloat16)
            main = jnp.dot(stacked, high, preferred_element_type=jnp.float32)
            rest = jnp.dot(both_high, low, preferred_element_type=jnp.float32)
            seen.append(main[: 2 * ROWS] + main[2 * ROWS :] + rest)
        key_seen_ref[head] = jnp.where(row < STEPS, seen[0][:ROWS], seen[1][:ROWS])
        query_seen_ref[head] = jnp.where(row < STEPS, seen[0][ROWS:], seen[1][ROWS:])
        for lag in range(STEPS):
            moved_key = shift_rows(key, lag, row_step)
            if lag:
                pulls_ref[lag - 1, head] = jnp.broadcast_to(lane_sum(key * moved_key), (ROWS, DK))
            weights_ref[lag, head] = jnp.broadcast_to(lane_sum(query * moved_key), (ROWS, DK))


def values_kernel(
    slots_ref, halves_ref, lengths_ref, twist_ref, value_ref, value_got_ref, history_ref,
    key_seen_ref, query_seen_ref, pulls_ref, weights_ref, taps_ref, out_ref, heads_ref,
):
    twist = twist_ref[0]
    row = lax.broadcasted_iota(jnp.int32, (ROWS, DK), 0)
    row_step = row % STEPS
    lane = lax.broadcasted_iota(jnp.int32, (ROWS, DK), 1)
    row_length = jnp.where(row < STEPS, lengths_ref[0], lengths_ref[1])
    live = row_step < row_length
    value_steps = steps_of(value_got_ref)
    gates = received(value_ref, value_got_ref, value_steps, H)
    for head in range(H):
        value = activate(
            value_ref, value_got_ref, value_steps, 2, head, history_ref, taps_ref, twist, row_step
        )
        beta_logit = jnp.broadcast_to(gates[:, head : head + 1], (ROWS, DK))
        decay_logit = jnp.broadcast_to(gates[:, H + head : H + head + 1], (ROWS, DK))
        beta = 1.0 / (1.0 + jnp.exp(-beta_logit))
        decay = 1.0 / (1.0 + jnp.exp(decay_logit))
        fades = [jnp.ones_like(decay), decay]
        for lag in range(2, STEPS + 1):
            earlier = pltpu.roll(decay, lag - 1, 0)
            fades.append(jnp.where(row_step >= lag - 1, fades[-1] * earlier, fades[-1]))
        base = beta * (value - fades[STEPS] * key_seen_ref[head])
        pulls = [
            beta * fades[lag] * pulls_ref[lag - 1, head] if lag else None for lag in range(STEPS)
        ]
        solved = base
        for _ in range(STEPS - 1):
            following = base
            for lag in range(1, STEPS):
                following = following - pulls[lag] * shift_rows(solved, lag, row_step)
            solved = following
        out = fades[STEPS] * query_seen_ref[head]
        for lag in range(STEPS):
            weight = fades[lag] * weights_ref[lag, head]
            out = out + weight * shift_rows(solved, lag, row_step)
        heads_ref[head] = jnp.where(live, out, 0.0)
    for quad in range(UNITS // 4):
        joined = []
        for pair in (2 * quad, 2 * quad + 1):
            first = heads_ref[slots_ref[2 * pair]]
            second = heads_ref[slots_ref[2 * pair + 1]]
            first = jnp.where(halves_ref[2 * pair] == 0, first, pltpu.roll(first, HALF, 1))
            second = jnp.where(halves_ref[2 * pair + 1] == 0, pltpu.roll(second, HALF, 1), second)
            joined.append(jnp.where(lane < HALF, first, second))
        out_ref[quad] = jnp.concatenate(joined, axis=0).astype(jnp.bfloat16)


def run_delta(slots, halves, lengths, queries, keys, values, history, twist, taps, state):
    smem = pl.BlockSpec(memory_space=pltpu.SMEM)
    vmem = pl.BlockSpec(memory_space=pltpu.VMEM)
    params = pltpu.CompilerParams(vmem_limit_bytes=32 * 1024 * 1024)
    per_head = jax.ShapeDtypeStruct((H, ROWS, DK), jnp.float32)
    lags = [
        jax.ShapeDtypeStruct((count, H, ROWS, DK), jnp.float32) for count in (STEPS - 1, STEPS)
    ]
    tap_blocks = jax.ShapeDtypeStruct((TAP_BLOCKS, TAPS, TAP_WIDTH), jnp.float32)
    prepared = pl.pallas_call(
        keys_kernel,
        out_shape=[per_head] * 2 + lags + [tap_blocks],
        in_specs=[smem] + [vmem] * 7 + [pl.BlockSpec(memory_space=pl.ANY)],
        out_specs=[vmem] * 5,
        scratch_shapes=[
            pltpu.VMEM(state.shape, jnp.float32),
            pltpu.SemaphoreType.DMA((STATE_COPIES,)),
        ],
        compiler_params=params,
        cost_estimate=pl.CostEstimate(flops=40_000_000, bytes_accessed=9_000_000, transcendentals=0),
        name="keys_part",
    )(twist, *queries, *keys, history, *taps, state)
    return pl.pallas_call(
        values_kernel,
        out_shape=jax.ShapeDtypeStruct((UNITS // 4, 2 * ROWS, DK), jnp.bfloat16),
        in_specs=[smem] * 4 + [vmem] * 8,
        out_specs=vmem,
        scratch_shapes=[pltpu.VMEM((H, ROWS, DK), jnp.float32)],
        compiler_params=params,
        cost_estimate=pl.CostEstimate(flops=4_000_000, bytes_accessed=2_000_000, transcendentals=0),
        name="values_part",
    )(slots, halves, lengths, twist, *values, history, *prepared)


def rows_kernel(
    depth, me_ref, slot_of_ref, tokens_hbm, weight_hbm, mine_ref, theirs_ref,
    weight_ref, window_ref, sem, weight_sem,
):
    me = me_ref[0]
    width = window_ref.shape[2]
    offset = me // 2 * (2 * depth)
    start = jnp.minimum(offset // DK * DK, D - width)
    columns = pl.ds(pl.multiple_of(start, DK), width)
    copy = pltpu.make_async_copy(tokens_hbm.at[:, :, columns], window_ref, sem)
    copy.start()
    weight_copy = pltpu.make_async_copy(weight_hbm, weight_ref, weight_sem)
    weight_copy.start()
    shape = (mine_ref.shape[0], slot_of_ref.shape[1])
    row = lax.broadcasted_iota(jnp.int32, shape, 0)
    place = row // ROWS
    count = (shape[0] // ROWS).bit_length() - 1
    holder = jnp.zeros(shape, jnp.int32)
    for at in range(count):
        holder = holder + ((place >> (count - 1 - at)) & 1) * (2 << at)
    holder = jnp.bitwise_xor(holder, me)
    match = holder * LOCAL + row % ROWS // STEPS == slot_of_ref[...]
    copy.wait()
    window = window_ref[...].astype(jnp.float32)
    total = jnp.zeros((shape[0], width), jnp.float32)
    for step in range(STEPS):
        picker = jnp.where(match & (row % STEPS == step), 1.0, 0.0).astype(jnp.bfloat16)
        here = window[:, step, :].astype(jnp.bfloat16)
        total = total + jnp.dot(picker, here, preferred_element_type=jnp.float32)
    total = pltpu.roll(total, lax.rem(width - (offset - start), width), 1)
    low, high = total[:, :depth], total[:, depth : 2 * depth]
    first_core = me % 2 == 0
    mine_ref[...] = jnp.where(first_core, low, high).astype(jnp.bfloat16)
    theirs_ref[...] = jnp.where(first_core, high, low).astype(jnp.bfloat16)
    weight_copy.wait()


def run_rows(me, slot_of, tokens, weight, chips):
    depth = weight.shape[0]
    width = -(-(2 * depth + DK - 1) // DK) * DK
    out = jax.ShapeDtypeStruct((chips * ROWS, depth), jnp.bfloat16)
    vmem = pl.BlockSpec(memory_space=pltpu.VMEM)
    return pl.pallas_call(
        functools.partial(rows_kernel, depth),
        out_shape=[out, out, jax.ShapeDtypeStruct(weight.shape, weight.dtype)],
        in_specs=[
            pl.BlockSpec(memory_space=pltpu.SMEM), vmem, pl.BlockSpec(memory_space=pl.ANY),
            pl.BlockSpec(memory_space=pl.ANY),
        ],
        out_specs=[vmem] * 3,
        scratch_shapes=[
            pltpu.VMEM((tokens.shape[0], STEPS, width), jnp.bfloat16),
            pltpu.SemaphoreType.DMA,
            pltpu.SemaphoreType.DMA,
        ],
        compiler_params=pltpu.CompilerParams(vmem_limit_bytes=32 * 1024 * 1024),
        cost_estimate=pl.CostEstimate(flops=0, bytes_accessed=0, transcendentals=0),
        name="token_rows",
    )(me.reshape(1), slot_of.reshape(1, -1), tokens, weight)


def product_kernel(skipped, crossed, *refs):
    mine_ref, theirs_ref, block_ref, other_ref, *refs = refs[skipped:]
    gate_refs, (kept_ref, packed_ref) = refs[:-2], refs[-2:]
    half = mine_ref.shape[0] // 2

    def product(own, other, dims):
        total = lax.dot_general(mine_ref[...], own, dims, preferred_element_type=jnp.float32)
        return total + lax.dot_general(
            theirs_ref[...], other, dims, preferred_element_type=jnp.float32
        )

    total = product(block_ref[...], other_ref[...], (((1,), (0,)), ((), ())))
    if gate_refs:
        gates = product(gate_refs[0][...], gate_refs[1][...], (((1,), (1,)), ((), ())))
        zeros = jnp.zeros((gates.shape[0], 2 * DK - gates.shape[1]), jnp.float32)
        total = jnp.concatenate([total, gates, zeros], axis=1)
    if crossed:
        starts = [start for at in range(0, half, ROWS) for start in (at, half + at)]
        total = jnp.concatenate([total[start : start + ROWS] for start in starts], axis=0)
    kept, sent = total[:half], total[half:]
    kept_ref[...] = kept
    pack_rows(sent, packed_ref)


def run_product(mine, theirs, weights, part, gates=(), earlier=(), crossed=False):
    vmem = pl.BlockSpec(memory_space=pltpu.VMEM)
    block = pl.BlockSpec((mine.shape[1], HEADS_WIDTH), lambda i: (0, part))
    half = mine.shape[0] // 2
    width = HEADS_WIDTH + len(gates) * DK
    return pl.pallas_call(
        functools.partial(product_kernel, len(earlier), crossed),
        grid=(1,),
        out_shape=[
            jax.ShapeDtypeStruct((half, width), jnp.float32),
            jax.ShapeDtypeStruct((half, width + scale_lanes(width // DK)), jnp.int16),
        ],
        in_specs=[pl.BlockSpec(memory_space=pl.ANY)] * len(earlier)
        + [vmem, vmem, block, block]
        + [vmem] * len(gates),
        out_specs=[vmem] * 2,
        compiler_params=pltpu.CompilerParams(vmem_limit_bytes=32 * 1024 * 1024),
        cost_estimate=pl.CostEstimate(flops=0, bytes_accessed=0, transcendentals=0),
        name="partial_product",
    )(*earlier, mine, theirs, *weights, *gates)


def combine_kernel(kept_ref, got_ref, still_ref, packed_ref):
    half = still_ref.shape[0]
    steps = steps_of(got_ref)
    sent = []
    for block in range(kept_ref.shape[1] // DK):
        columns = pl.ds(block * DK, DK)
        total = kept_ref[:, columns] + unpack_block(got_ref, steps, block)
        still_ref[:, columns] = total[:half]
        sent.append(total[half:])
    sent = jnp.concatenate(sent, axis=1)
    pack_rows(fold_rows(sent) if half == ROWS else sent, packed_ref)


def run_combine(kept, got):
    vmem = pl.BlockSpec(memory_space=pltpu.VMEM)
    half, width = kept.shape[0] // 2, kept.shape[1]
    rows, packed = (2 * ROWS, width // 2) if half == ROWS else (half, width)
    packed = (rows, packed + scale_lanes(packed // DK))
    return pl.pallas_call(
        combine_kernel,
        out_shape=[
            jax.ShapeDtypeStruct((half, width), jnp.float32),
            jax.ShapeDtypeStruct(packed, jnp.int16),
        ],
        in_specs=[vmem] * 2,
        out_specs=[vmem] * 2,
        compiler_params=pltpu.CompilerParams(vmem_limit_bytes=32 * 1024 * 1024),
        cost_estimate=pl.CostEstimate(flops=0, bytes_accessed=0, transcendentals=0),
        name="combine",
    )(kept, got)


def join_kernel(first_ref, second_ref, earlier_ref, out_ref):
    both = [ref[...].astype(jnp.float32) for ref in (first_ref, second_ref)]
    out_ref[...] = jnp.concatenate(both, axis=0).astype(out_ref.dtype)


def join(first, second, earlier):
    vmem = pl.BlockSpec(memory_space=pltpu.VMEM)
    rows, width = first.shape
    return pl.pallas_call(
        join_kernel,
        out_shape=jax.ShapeDtypeStruct((2 * rows, width), first.dtype),
        in_specs=[vmem, vmem, pl.BlockSpec(memory_space=pl.ANY)],
        out_specs=vmem,
        compiler_params=pltpu.CompilerParams(vmem_limit_bytes=32 * 1024 * 1024),
        cost_estimate=pl.CostEstimate(flops=0, bytes_accessed=0, transcendentals=0),
        name="join_taps",
    )(first, second, earlier)


def swap(value, bit, devices):
    return lax.ppermute(value, "heads", [(i, i ^ bit) for i in range(devices)])


def on_device(
    tokens,
    qkv_weight,
    gate_weight,
    conv_weight,
    delta_state,
    conv_state,
    old_heads,
    new_units,
    slot_of,
    lengths,
):
    devices = lax.axis_size("heads")
    me = lax.axis_index("heads")
    per_device = UNITS // devices
    row_count = tokens.shape[0]
    chips = devices // 2

    bits = [1 << b for b in range(1, devices.bit_length() - 1)]

    ride = conv_weight.shape[1] == 2 * TAP_WIDTH and len(bits) == 3
    if ride:
        taps = jnp.concatenate([conv_weight[:, :TAP_WIDTH], conv_weight[:, TAP_WIDTH:]], axis=0)
        far = swap(taps, 4, devices)
    else:
        taps = lax.all_gather(conv_weight, "heads", axis=1, tiled=True)
        order = [
            2 * (at >> 4 & 1) + 4 * (at >> 3 & 1) + 8 * (at >> 1 & 1) + 16 * (at >> 2 & 1) + (at & 1)
            for at in range(TAP_BLOCKS)
        ]
        taps = [taps[:, block * TAP_WIDTH : (block + 1) * TAP_WIDTH] for block in order]
        taps = jnp.concatenate(taps, axis=0)

    mine, theirs, near_weight = run_rows(me, slot_of, tokens, qkv_weight, chips)

    weights = (near_weight, swap(qkv_weight, 1, devices))
    gate_columns = gate_weight.T
    gates = (gate_columns, swap(gate_columns, 1, devices))

    tie = lambda *values: lax.optimization_barrier(values)

    if ride:
        taps = join(taps, far, mine)
        far = swap(taps, 8, devices)
    queries = run_product(mine, theirs, weights, 0, crossed=True)
    keys = run_product(mine, theirs, weights, 1, earlier=queries[:1])
    values = run_product(mine, theirs, weights, 2, gates, earlier=keys[:1])

    slot_of, lengths, old_heads, new_units, carried, *values = tie(
        slot_of, lengths, old_heads, new_units, conv_state, *values
    )
    steps = jnp.arange(STEPS, dtype=jnp.int32)
    offered = (slot_of[:, None] * STEPS + steps[None, :]).reshape(-1)
    old_slots, halves = unit_tables(old_heads, new_units)
    my_rows = me * LOCAL + jnp.arange(LOCAL, dtype=jnp.int32)
    my_lengths = jnp.sum(
        jnp.where(slot_of[None, :] == my_rows[:, None], lengths[None, :], 0), axis=1
    )
    blank = jnp.zeros((1, carried.shape[2]), jnp.float32)
    history = jnp.concatenate([blank, carried[1], blank, carried[0]], axis=0)
    routes = [bits[1:] + bits[:1], bits, bits]
    kept = [chunk[0] for chunk in (queries, keys, values)]
    got = [
        swap(chunk[1], route[0], devices)
        for chunk, route in zip((queries, keys, values), routes)
    ]
    for level in range(1, len(bits)):
        for at in range(3):
            kept[at], packed = run_combine(kept[at], got[at])
            got[at] = swap(packed, routes[at][level], devices)
            if ride and at == 2 - level:
                taps = join(taps, far, kept[at])
                far = swap(taps, 3 - level, devices)
    if ride:
        twist, taps = me.reshape(1), (taps, far)
    else:
        half = TAP_BLOCKS // 2 * TAPS
        twist, taps = jnp.zeros(1, jnp.int32), (taps[:half], taps[half:])
    queries, keys, values = zip(kept, got)

    local_out = run_delta(
        old_slots, halves, my_lengths, queries, keys, values, history, twist, taps, delta_state
    )

    placer = (offered[:, None] == jnp.arange(row_count * STEPS, dtype=jnp.int32)[None, :]).astype(
        jnp.bfloat16
    )
    if per_device % 2 == 0:
        pairs = per_device // 2
        sending = local_out.reshape(devices, pairs * ROWS, DK)
        got = lax.all_to_all(sending, "heads", split_axis=0, concat_axis=0, tiled=True)
        got = got.reshape(devices, pairs, ROWS, DK)
        got = jnp.concatenate([got[:, pair] for pair in range(pairs)], axis=-1)
        got = got.reshape(devices * ROWS, pairs * DK)
    else:
        units = local_out.reshape(UNITS // 2, ROWS, 2, HALF).transpose(0, 2, 1, 3)
        sending = units.reshape(devices, per_device * ROWS, HALF)
        got = lax.all_to_all(sending, "heads", split_axis=0, concat_axis=0, tiled=True)
        got = got.reshape(devices, per_device, ROWS, HALF).transpose(0, 2, 1, 3)
        got = got.reshape(devices * ROWS, per_device * HALF)
    outputs = jnp.dot(placer, got, preferred_element_type=jnp.float32).astype(jnp.bfloat16)
    return outputs.reshape(row_count, STEPS, per_device * HALF)


def solution(mesh):
    in_specs = (
        P("groups", None, None),
        P(("groups", "heads"), None),
        P(("groups", "heads"), None),
        P("groups", "heads"),
        P(("groups", "heads"), None, None, None),
        P(("groups", "heads"), None, None),
        P(),
        P(),
        P("groups"),
        P("groups"),
    )
    out_specs = P("groups", None, "heads")
    return jax.shard_map(
        on_device, mesh=mesh, in_specs=in_specs, out_specs=out_specs, check_vma=False
    )
```

```python
import functools

import jax
import jax.numpy as jnp
from jax import lax
from jax.experimental import pallas as pl
from jax.experimental.pallas import tpu as pltpu
from jax.sharding import PartitionSpec as P

D = 2304
H = 32
DK = 128
TAPS = 4
STEPS = 4
HALF = 64
UNITS = 64
LOCAL = 2
ROWS = LOCAL * STEPS
HEADS_WIDTH = H * DK
LEVELS = 32767.0
STATE_COPIES = 4
TAP_WIDTH = 384
TAP_BLOCKS = 3 * HEADS_WIDTH // TAP_WIDTH


norm_eps = 1e-06


def unit_tables(old_heads, new_units):
    positions = jnp.arange(H, dtype=jnp.int32)
    inverse = jnp.sum(
        jnp.where(old_heads[None, :] == positions[:, None], positions[None, :], 0), axis=1
    )
    heads_of = new_units // 2
    halves = new_units % 2
    old_slots = jnp.sum(
        jnp.where(heads_of[:, None] == positions[None, :], inverse[None, :], 0), axis=1
    )
    return (old_slots, halves)


def shift_rows(value, lag, row_step):
    if lag == 0:
        return value
    moved = pltpu.roll(value, lag, 0)
    return jnp.where(row_step >= lag, moved, 0.0)


def lane_sum(value):
    return jnp.sum(value, axis=-1, keepdims=True)


def unit_length(value):
    return value * lax.rsqrt(lane_sum(value * value) + norm_eps)


def scale_lanes(blocks):
    return -(-blocks // HALF) * DK


def pack_rows(total, packed_ref):
    rows, width = total.shape
    blocks = width // DK
    lanes = scale_lanes(blocks)
    lane = lax.broadcasted_iota(jnp.int32, (rows, lanes), 1)
    scales = jnp.zeros((rows, lanes), jnp.float32)
    for block in range(blocks):
        part = total[:, block * DK : (block + 1) * DK]
        top = jnp.max(jnp.abs(part), axis=-1, keepdims=True) + 1e-30
        exponent = jnp.ceil(jnp.log2(top))
        mantissa = jnp.ceil(jnp.minimum(top * jnp.exp2(-exponent) * LEVELS, LEVELS))
        factor = LEVELS * LEVELS * jnp.exp2(-exponent) / mantissa
        coded = jnp.clip(jnp.floor(part * factor + 0.5), -LEVELS, LEVELS)
        packed_ref[:, block * DK : (block + 1) * DK] = coded.astype(jnp.int32).astype(jnp.int16)
        scales = jnp.where(lane == block, mantissa, scales)
        scales = jnp.where(lane == lanes // 2 + block, exponent, scales)
    packed_ref[:, width:] = scales.astype(jnp.int32).astype(jnp.int16)


def to_float(coded):
    return coded.astype(jnp.int32).astype(jnp.float32)


def steps_of(packed_ref):
    lanes = DK if packed_ref.shape[1] <= (HALF + 1) * DK else 2 * DK
    scales = to_float(packed_ref[:, packed_ref.shape[1] - lanes :])
    exponents = pltpu.roll(scales, lanes // 2, 1)
    return scales * jnp.exp2(exponents) * (1.0 / (LEVELS * LEVELS))


def unpack_block(packed_ref, steps, block):
    return to_float(packed_ref[:, block * DK : (block + 1) * DK]) * steps[:, block : block + 1]


def fold_rows(value):
    half = value.shape[1] // 2
    return jnp.concatenate([value[:, :half], value[:, half:]], axis=0)


def received(kept_ref, got_ref, steps, block):
    half = kept_ref.shape[1] // DK // 2
    rows = unpack_block(got_ref, steps, block % half)
    rows = rows[:ROWS] if block < half else rows[ROWS:]
    return kept_ref[:, block * DK : (block + 1) * DK] + rows


def tap_block(block, me):
    other = jnp.bitwise_xor(block // 2, me)
    place = ((other >> 2) & 3) + ((other >> 1) & 1) * 4 + (other & 1) * 8
    return place * 2 + block % 2


def activate(kept_ref, got_ref, steps, part, head, history_ref, taps_ref, twist, row_step):
    fresh = received(kept_ref, got_ref, steps, head)
    column = part * HEADS_WIDTH + head * DK
    carried = history_ref[:, column : column + DK]
    taps = taps_ref[tap_block(column // TAP_WIDTH, twist)]
    inner = column % TAP_WIDTH
    total = taps[TAPS - 1 :, inner : inner + DK] * fresh
    for lag in range(1, TAPS):
        source = jnp.where(row_step >= STEPS - lag, carried, fresh)
        tap = taps[TAPS - 1 - lag : TAPS - lag, inner : inner + DK]
        total = total + tap * pltpu.roll(source, lag, 0)
    return total / (1.0 + jnp.exp(-total))


def start_states(state_hbm, state_ref, sems):
    per_copy = H // STATE_COPIES
    copies = []
    for at in range(STATE_COPIES):
        some = pl.ds(at * per_copy, per_copy)
        copies.append(
            pltpu.make_async_copy(state_hbm.at[:, some], state_ref.at[:, some], sems.at[at])
        )
        copies[-1].start()
    return copies


def seen_by(vectors, state_ref, head, row, copies):
    per_copy = H // STATE_COPIES
    if head % per_copy == 0:
        copies[head // per_copy].wait()
    rows_high = vectors.astype(jnp.bfloat16)
    rows_low = (vectors - rows_high.astype(jnp.float32)).astype(jnp.bfloat16)
    stacked = jnp.concatenate([rows_high, rows_low], axis=0)
    seen = []
    for r in range(LOCAL):
        state = state_ref[r, head]
        high = state.astype(jnp.bfloat16)
        low = (state - high.astype(jnp.float32)).astype(jnp.bfloat16)
        main = jnp.dot(stacked, high, preferred_element_type=jnp.float32)
        rest = jnp.dot(rows_high, low, preferred_element_type=jnp.float32)
        seen.append(main[:ROWS] + main[ROWS:] + rest)
    return jnp.where(row < STEPS, seen[0], seen[1])


def keys_kernel(
    twist_ref, kept_ref, got_ref, history_ref, near_ref, far_ref, state_hbm,
    keys_ref, key_seen_ref, pulls_ref, taps_ref, state_ref, sems,
):
    copies = start_states(state_hbm, state_ref, sems)
    twist = twist_ref[0]
    half = TAP_BLOCKS // 2
    for at in range(TAP_BLOCKS):
        source = near_ref if at < half else far_ref
        if at % 4 == 0:
            some = source[at % half * TAPS : (at % half + 4) * TAPS, :].astype(jnp.float32)
        taps_ref[at] = some[at % 4 * TAPS : (at % 4 + 1) * TAPS]
    row = lax.broadcasted_iota(jnp.int32, (ROWS, DK), 0)
    row_step = row % STEPS
    steps = steps_of(got_ref)
    for head in range(H):
        key = unit_length(
            activate(kept_ref, got_ref, steps, 1, head, history_ref, taps_ref, twist, row_step)
        )
        keys_ref[head] = key
        key_seen_ref[head] = seen_by(key, state_ref, head, row, copies)
        for lag in range(1, STEPS):
            moved_key = shift_rows(key, lag, row_step)
            pulls_ref[lag - 1, head] = jnp.broadcast_to(lane_sum(key * moved_key), (ROWS, DK))


def queries_kernel(
    twist_ref, kept_ref, got_ref, history_ref, keys_ref, taps_ref, state_hbm,
    query_seen_ref, weights_ref, state_ref, sems,
):
    copies = start_states(state_hbm, state_ref, sems)
    twist = twist_ref[0]
    row = lax.broadcasted_iota(jnp.int32, (ROWS, DK), 0)
    row_step = row % STEPS
    steps = steps_of(got_ref)
    for head in range(H):
        query = unit_length(
            activate(kept_ref, got_ref, steps, 0, head, history_ref, taps_ref, twist, row_step)
        )
        query_seen_ref[head] = seen_by(query, state_ref, head, row, copies)
        for lag in range(STEPS):
            moved_key = shift_rows(keys_ref[head], lag, row_step)
            weights_ref[lag, head] = jnp.broadcast_to(lane_sum(query * moved_key), (ROWS, DK))


def values_kernel(
    slots_ref, halves_ref, lengths_ref, twist_ref, value_ref, value_got_ref, history_ref,
    key_seen_ref, query_seen_ref, pulls_ref, weights_ref, taps_ref, out_ref, heads_ref,
):
    twist = twist_ref[0]
    row = lax.broadcasted_iota(jnp.int32, (ROWS, DK), 0)
    row_step = row % STEPS
    lane = lax.broadcasted_iota(jnp.int32, (ROWS, DK), 1)
    row_length = jnp.where(row < STEPS, lengths_ref[0], lengths_ref[1])
    live = row_step < row_length
    value_steps = steps_of(value_got_ref)
    gates = received(value_ref, value_got_ref, value_steps, H)
    for head in range(H):
        value = activate(
            value_ref, value_got_ref, value_steps, 2, head, history_ref, taps_ref, twist, row_step
        )
        beta_logit = jnp.broadcast_to(gates[:, head : head + 1], (ROWS, DK))
        decay_logit = jnp.broadcast_to(gates[:, H + head : H + head + 1], (ROWS, DK))
        beta = 1.0 / (1.0 + jnp.exp(-beta_logit))
        decay = 1.0 / (1.0 + jnp.exp(decay_logit))
        fades = [jnp.ones_like(decay), decay]
        for lag in range(2, STEPS + 1):
            earlier = pltpu.roll(decay, lag - 1, 0)
            fades.append(jnp.where(row_step >= lag - 1, fades[-1] * earlier, fades[-1]))
        base = beta * (value - fades[STEPS] * key_seen_ref[head])
        pulls = [
            beta * fades[lag] * pulls_ref[lag - 1, head] if lag else None for lag in range(STEPS)
        ]
        solved = base
        for _ in range(STEPS - 1):
            following = base
            for lag in range(1, STEPS):
                following = following - pulls[lag] * shift_rows(solved, lag, row_step)
            solved = following
        out = fades[STEPS] * query_seen_ref[head]
        for lag in range(STEPS):
            weight = fades[lag] * weights_ref[lag, head]
            out = out + weight * shift_rows(solved, lag, row_step)
        heads_ref[head] = jnp.where(live, out, 0.0)
    for quad in range(UNITS // 4):
        joined = []
        for pair in (2 * quad, 2 * quad + 1):
            first = heads_ref[slots_ref[2 * pair]]
            second = heads_ref[slots_ref[2 * pair + 1]]
            first = jnp.where(halves_ref[2 * pair] == 0, first, pltpu.roll(first, HALF, 1))
            second = jnp.where(halves_ref[2 * pair + 1] == 0, pltpu.roll(second, HALF, 1), second)
            joined.append(jnp.where(lane < HALF, first, second))
        out_ref[quad] = jnp.concatenate(joined, axis=0).astype(jnp.bfloat16)


def run_delta(slots, halves, lengths, queries, keys, values, history, twist, taps, state):
    smem = pl.BlockSpec(memory_space=pltpu.SMEM)
    vmem = pl.BlockSpec(memory_space=pltpu.VMEM)
    params = pltpu.CompilerParams(vmem_limit_bytes=32 * 1024 * 1024)
    per_head = jax.ShapeDtypeStruct((H, ROWS, DK), jnp.float32)
    lags = [
        jax.ShapeDtypeStruct((count, H, ROWS, DK), jnp.float32) for count in (STEPS - 1, STEPS)
    ]
    tap_blocks = jax.ShapeDtypeStruct((TAP_BLOCKS, TAPS, TAP_WIDTH), jnp.float32)
    states = dict(
        scratch_shapes=[
            pltpu.VMEM(state.shape, jnp.float32),
            pltpu.SemaphoreType.DMA((STATE_COPIES,)),
        ],
        compiler_params=params,
        cost_estimate=pl.CostEstimate(flops=20_000_000, bytes_accessed=5_000_000, transcendentals=0),
    )
    key_rows, key_seen, pulls, tap_rows = pl.pallas_call(
        keys_kernel,
        out_shape=[per_head, per_head, lags[0], tap_blocks],
        in_specs=[smem] + [vmem] * 5 + [pl.BlockSpec(memory_space=pl.ANY)],
        out_specs=[vmem] * 4,
        name="keys_part",
        **states,
    )(twist, *keys, history, *taps, state)
    query_seen, weights = pl.pallas_call(
        queries_kernel,
        out_shape=[per_head, lags[1]],
        in_specs=[smem] + [vmem] * 5 + [pl.BlockSpec(memory_space=pl.ANY)],
        out_specs=[vmem] * 2,
        name="queries_part",
        **states,
    )(twist, *queries, history, key_rows, tap_rows, state)
    prepared = (key_seen, query_seen, pulls, weights, tap_rows)
    return pl.pallas_call(
        values_kernel,
        out_shape=jax.ShapeDtypeStruct((UNITS // 4, 2 * ROWS, DK), jnp.bfloat16),
        in_specs=[smem] * 4 + [vmem] * 8,
        out_specs=vmem,
        scratch_shapes=[pltpu.VMEM((H, ROWS, DK), jnp.float32)],
        compiler_params=params,
        cost_estimate=pl.CostEstimate(flops=4_000_000, bytes_accessed=2_000_000, transcendentals=0),
        name="values_part",
    )(slots, halves, lengths, twist, *values, history, *prepared)


def rows_kernel(
    depth, me_ref, slot_of_ref, tokens_hbm, weight_hbm, mine_ref, theirs_ref,
    weight_ref, window_ref, sem, weight_sem,
):
    me = me_ref[0]
    width = window_ref.shape[2]
    offset = me // 2 * (2 * depth)
    start = jnp.minimum(offset // DK * DK, D - width)
    columns = pl.ds(pl.multiple_of(start, DK), width)
    copy = pltpu.make_async_copy(tokens_hbm.at[:, :, columns], window_ref, sem)
    copy.start()
    weight_copy = pltpu.make_async_copy(weight_hbm, weight_ref, weight_sem)
    weight_copy.start()
    shape = (mine_ref.shape[0], slot_of_ref.shape[1])
    row = lax.broadcasted_iota(jnp.int32, shape, 0)
    place = row // ROWS
    count = (shape[0] // ROWS).bit_length() - 1
    holder = jnp.zeros(shape, jnp.int32)
    for at in range(count):
        holder = holder + ((place >> (count - 1 - at)) & 1) * (2 << at)
    holder = jnp.bitwise_xor(holder, me)
    match = holder * LOCAL + row % ROWS // STEPS == slot_of_ref[...]
    copy.wait()
    window = window_ref[...].astype(jnp.float32)
    total = jnp.zeros((shape[0], width), jnp.float32)
    for step in range(STEPS):
        picker = jnp.where(match & (row % STEPS == step), 1.0, 0.0).astype(jnp.bfloat16)
        here = window[:, step, :].astype(jnp.bfloat16)
        total = total + jnp.dot(picker, here, preferred_element_type=jnp.float32)
    total = pltpu.roll(total, lax.rem(width - (offset - start), width), 1)
    low, high = total[:, :depth], total[:, depth : 2 * depth]
    first_core = me % 2 == 0
    mine_ref[...] = jnp.where(first_core, low, high).astype(jnp.bfloat16)
    theirs_ref[...] = jnp.where(first_core, high, low).astype(jnp.bfloat16)
    weight_copy.wait()


def run_rows(me, slot_of, tokens, weight, chips):
    depth = weight.shape[0]
    width = -(-(2 * depth + DK - 1) // DK) * DK
    out = jax.ShapeDtypeStruct((chips * ROWS, depth), jnp.bfloat16)
    vmem = pl.BlockSpec(memory_space=pltpu.VMEM)
    return pl.pallas_call(
        functools.partial(rows_kernel, depth),
        out_shape=[out, out, jax.ShapeDtypeStruct(weight.shape, weight.dtype)],
        in_specs=[
            pl.BlockSpec(memory_space=pltpu.SMEM), vmem, pl.BlockSpec(memory_space=pl.ANY),
            pl.BlockSpec(memory_space=pl.ANY),
        ],
        out_specs=[vmem] * 3,
        scratch_shapes=[
            pltpu.VMEM((tokens.shape[0], STEPS, width), jnp.bfloat16),
            pltpu.SemaphoreType.DMA,
            pltpu.SemaphoreType.DMA,
        ],
        compiler_params=pltpu.CompilerParams(vmem_limit_bytes=32 * 1024 * 1024),
        cost_estimate=pl.CostEstimate(flops=0, bytes_accessed=0, transcendentals=0),
        name="token_rows",
    )(me.reshape(1), slot_of.reshape(1, -1), tokens, weight)


def product_kernel(skipped, crossed, *refs):
    mine_ref, theirs_ref, block_ref, other_ref, *refs = refs[skipped:]
    gate_refs, (kept_ref, packed_ref) = refs[:-2], refs[-2:]
    half = mine_ref.shape[0] // 2

    def product(own, other, dims):
        total = lax.dot_general(mine_ref[...], own, dims, preferred_element_type=jnp.float32)
        return total + lax.dot_general(
            theirs_ref[...], other, dims, preferred_element_type=jnp.float32
        )

    total = product(block_ref[...], other_ref[...], (((1,), (0,)), ((), ())))
    if gate_refs:
        gates = product(gate_refs[0][...], gate_refs[1][...], (((1,), (1,)), ((), ())))
        zeros = jnp.zeros((gates.shape[0], 2 * DK - gates.shape[1]), jnp.float32)
        total = jnp.concatenate([total, gates, zeros], axis=1)
    if crossed:
        starts = [start for at in range(0, half, ROWS) for start in (at, half + at)]
        total = jnp.concatenate([total[start : start + ROWS] for start in starts], axis=0)
    kept, sent = total[:half], total[half:]
    kept_ref[...] = kept
    pack_rows(sent, packed_ref)


def run_product(mine, theirs, weights, part, gates=(), earlier=(), crossed=False):
    vmem = pl.BlockSpec(memory_space=pltpu.VMEM)
    block = pl.BlockSpec((mine.shape[1], HEADS_WIDTH), lambda i: (0, part))
    half = mine.shape[0] // 2
    width = HEADS_WIDTH + len(gates) * DK
    return pl.pallas_call(
        functools.partial(product_kernel, len(earlier), crossed),
        grid=(1,),
        out_shape=[
            jax.ShapeDtypeStruct((half, width), jnp.float32),
            jax.ShapeDtypeStruct((half, width + scale_lanes(width // DK)), jnp.int16),
        ],
        in_specs=[pl.BlockSpec(memory_space=pl.ANY)] * len(earlier)
        + [vmem, vmem, block, block]
        + [vmem] * len(gates),
        out_specs=[vmem] * 2,
        compiler_params=pltpu.CompilerParams(vmem_limit_bytes=32 * 1024 * 1024),
        cost_estimate=pl.CostEstimate(flops=0, bytes_accessed=0, transcendentals=0),
        name="partial_product",
    )(*earlier, mine, theirs, *weights, *gates)


def combine_kernel(kept_ref, got_ref, still_ref, packed_ref):
    half = still_ref.shape[0]
    steps = steps_of(got_ref)
    sent = []
    for block in range(kept_ref.shape[1] // DK):
        columns = pl.ds(block * DK, DK)
        total = kept_ref[:, columns] + unpack_block(got_ref, steps, block)
        still_ref[:, columns] = total[:half]
        sent.append(total[half:])
    sent = jnp.concatenate(sent, axis=1)
    pack_rows(fold_rows(sent) if half == ROWS else sent, packed_ref)


def run_combine(kept, got):
    vmem = pl.BlockSpec(memory_space=pltpu.VMEM)
    half, width = kept.shape[0] // 2, kept.shape[1]
    rows, packed = (2 * ROWS, width // 2) if half == ROWS else (half, width)
    packed = (rows, packed + scale_lanes(packed // DK))
    return pl.pallas_call(
        combine_kernel,
        out_shape=[
            jax.ShapeDtypeStruct((half, width), jnp.float32),
            jax.ShapeDtypeStruct(packed, jnp.int16),
        ],
        in_specs=[vmem] * 2,
        out_specs=[vmem] * 2,
        compiler_params=pltpu.CompilerParams(vmem_limit_bytes=32 * 1024 * 1024),
        cost_estimate=pl.CostEstimate(flops=0, bytes_accessed=0, transcendentals=0),
        name="combine",
    )(kept, got)


def join_kernel(first_ref, second_ref, earlier_ref, out_ref):
    both = [ref[...].astype(jnp.float32) for ref in (first_ref, second_ref)]
    out_ref[...] = jnp.concatenate(both, axis=0).astype(out_ref.dtype)


def join(first, second, earlier):
    vmem = pl.BlockSpec(memory_space=pltpu.VMEM)
    rows, width = first.shape
    return pl.pallas_call(
        join_kernel,
        out_shape=jax.ShapeDtypeStruct((2 * rows, width), first.dtype),
        in_specs=[vmem, vmem, pl.BlockSpec(memory_space=pl.ANY)],
        out_specs=vmem,
        compiler_params=pltpu.CompilerParams(vmem_limit_bytes=32 * 1024 * 1024),
        cost_estimate=pl.CostEstimate(flops=0, bytes_accessed=0, transcendentals=0),
        name="join_taps",
    )(first, second, earlier)


def swap(value, bit, devices):
    return lax.ppermute(value, "heads", [(i, i ^ bit) for i in range(devices)])


def on_device(
    tokens,
    qkv_weight,
    gate_weight,
    conv_weight,
    delta_state,
    conv_state,
    old_heads,
    new_units,
    slot_of,
    lengths,
):
    devices = lax.axis_size("heads")
    me = lax.axis_index("heads")
    per_device = UNITS // devices
    row_count = tokens.shape[0]
    chips = devices // 2

    bits = [1 << b for b in range(1, devices.bit_length() - 1)]

    ride = conv_weight.shape[1] == 2 * TAP_WIDTH and len(bits) == 3
    if ride:
        taps = jnp.concatenate([conv_weight[:, :TAP_WIDTH], conv_weight[:, TAP_WIDTH:]], axis=0)
        far = swap(taps, 4, devices)
    else:
        taps = lax.all_gather(conv_weight, "heads", axis=1, tiled=True)
        order = [
            2 * (at >> 4 & 1) + 4 * (at >> 3 & 1) + 8 * (at >> 1 & 1) + 16 * (at >> 2 & 1) + (at & 1)
            for at in range(TAP_BLOCKS)
        ]
        taps = [taps[:, block * TAP_WIDTH : (block + 1) * TAP_WIDTH] for block in order]
        taps = jnp.concatenate(taps, axis=0)

    mine, theirs, near_weight = run_rows(me, slot_of, tokens, qkv_weight, chips)

    weights = (near_weight, swap(qkv_weight, 1, devices))
    gate_columns = gate_weight.T
    gates = (gate_columns, swap(gate_columns, 1, devices))

    tie = lambda *values: lax.optimization_barrier(values)

    if ride:
        taps = join(taps, far, mine)
        far = swap(taps, 8, devices)
    keys = run_product(mine, theirs, weights, 1)
    values = run_product(mine, theirs, weights, 2, gates, earlier=keys[:1])
    queries = run_product(mine, theirs, weights, 0, earlier=values[:1], crossed=True)

    slot_of, lengths, old_heads, new_units, carried, *values = tie(
        slot_of, lengths, old_heads, new_units, conv_state, *values
    )
    steps = jnp.arange(STEPS, dtype=jnp.int32)
    offered = (slot_of[:, None] * STEPS + steps[None, :]).reshape(-1)
    old_slots, halves = unit_tables(old_heads, new_units)
    my_rows = me * LOCAL + jnp.arange(LOCAL, dtype=jnp.int32)
    my_lengths = jnp.sum(
        jnp.where(slot_of[None, :] == my_rows[:, None], lengths[None, :], 0), axis=1
    )
    blank = jnp.zeros((1, carried.shape[2]), jnp.float32)
    history = jnp.concatenate([blank, carried[1], blank, carried[0]], axis=0)
    routes = [bits[1:] + bits[:1], bits, bits]
    kept = [chunk[0] for chunk in (queries, keys, values)]
    got = [
        swap(chunk[1], route[0], devices)
        for chunk, route in zip((queries, keys, values), routes)
    ]
    for level in range(1, len(bits)):
        for at in range(3):
            kept[at], packed = run_combine(kept[at], got[at])
            got[at] = swap(packed, routes[at][level], devices)
            if ride and at == 2 - level:
                taps = join(taps, far, kept[at])
                far = swap(taps, 3 - level, devices)
    if ride:
        twist, taps = me.reshape(1), (taps, far)
    else:
        half = TAP_BLOCKS // 2 * TAPS
        twist, taps = jnp.zeros(1, jnp.int32), (taps[:half], taps[half:])
    queries, keys, values = zip(kept, got)

    local_out = run_delta(
        old_slots, halves, my_lengths, queries, keys, values, history, twist, taps, delta_state
    )

    placer = (offered[:, None] == jnp.arange(row_count * STEPS, dtype=jnp.int32)[None, :]).astype(
        jnp.bfloat16
    )
    if per_device % 2 == 0:
        pairs = per_device // 2
        sending = local_out.reshape(devices, pairs * ROWS, DK)
        got = lax.all_to_all(sending, "heads", split_axis=0, concat_axis=0, tiled=True)
        got = got.reshape(devices, pairs, ROWS, DK)
        got = jnp.concatenate([got[:, pair] for pair in range(pairs)], axis=-1)
        got = got.reshape(devices * ROWS, pairs * DK)
    else:
        units = local_out.reshape(UNITS // 2, ROWS, 2, HALF).transpose(0, 2, 1, 3)
        sending = units.reshape(devices, per_device * ROWS, HALF)
        got = lax.all_to_all(sending, "heads", split_axis=0, concat_axis=0, tiled=True)
        got = got.reshape(devices, per_device, ROWS, HALF).transpose(0, 2, 1, 3)
        got = got.reshape(devices * ROWS, per_device * HALF)
    outputs = jnp.dot(placer, got, preferred_element_type=jnp.float32).astype(jnp.bfloat16)
    return outputs.reshape(row_count, STEPS, per_device * HALF)


def solution(mesh):
    in_specs = (
        P("groups", None, None),
        P(("groups", "heads"), None),
        P(("groups", "heads"), None),
        P("groups", "heads"),
        P(("groups", "heads"), None, None, None),
        P(("groups", "heads"), None, None),
        P(),
        P(),
        P("groups"),
        P("groups"),
    )
    out_specs = P("groups", None, "heads")
    return jax.shard_map(
        on_device, mesh=mesh, in_specs=in_specs, out_specs=out_specs, check_vma=False
    )
```

```python
import functools

import jax
import jax.numpy as jnp
from jax import lax
from jax.experimental import pallas as pl
from jax.experimental.pallas import tpu as pltpu
from jax.sharding import PartitionSpec as P

D = 2304
H = 32
DK = 128
TAPS = 4
STEPS = 4
HALF = 64
UNITS = 64
LOCAL = 2
ROWS = LOCAL * STEPS
HEADS_WIDTH = H * DK
LEVELS = 32767.0
STATE_COPIES = 4
TAP_WIDTH = 384
TAP_BLOCKS = 3 * HEADS_WIDTH // TAP_WIDTH


norm_eps = 1e-06


def unit_tables(old_heads, new_units):
    positions = jnp.arange(H, dtype=jnp.int32)
    inverse = jnp.sum(
        jnp.where(old_heads[None, :] == positions[:, None], positions[None, :], 0), axis=1
    )
    heads_of = new_units // 2
    halves = new_units % 2
    old_slots = jnp.sum(
        jnp.where(heads_of[:, None] == positions[None, :], inverse[None, :], 0), axis=1
    )
    return (old_slots, halves)


def shift_rows(value, lag, row_step):
    if lag == 0:
        return value
    moved = pltpu.roll(value, lag, 0)
    return jnp.where(row_step >= lag, moved, 0.0)


def lane_sum(value):
    return jnp.sum(value, axis=-1, keepdims=True)


def unit_length(value):
    return value * lax.rsqrt(lane_sum(value * value) + norm_eps)


def scale_lanes(blocks):
    return -(-blocks // HALF) * DK


def pack_rows(total, packed_ref):
    rows, width = total.shape
    blocks = width // DK
    lanes = scale_lanes(blocks)
    lane = lax.broadcasted_iota(jnp.int32, (rows, lanes), 1)
    scales = jnp.zeros((rows, lanes), jnp.float32)
    for block in range(blocks):
        part = total[:, block * DK : (block + 1) * DK]
        top = jnp.max(jnp.abs(part), axis=-1, keepdims=True) + 1e-30
        exponent = jnp.ceil(jnp.log2(top))
        mantissa = jnp.ceil(jnp.minimum(top * jnp.exp2(-exponent) * LEVELS, LEVELS))
        factor = LEVELS * LEVELS * jnp.exp2(-exponent) / mantissa
        coded = jnp.clip(jnp.floor(part * factor + 0.5), -LEVELS, LEVELS)
        packed_ref[:, block * DK : (block + 1) * DK] = coded.astype(jnp.int32).astype(jnp.int16)
        scales = jnp.where(lane == block, mantissa, scales)
        scales = jnp.where(lane == lanes // 2 + block, exponent, scales)
    packed_ref[:, width:] = scales.astype(jnp.int32).astype(jnp.int16)


def to_float(coded):
    return coded.astype(jnp.int32).astype(jnp.float32)


def steps_of(packed_ref):
    lanes = DK if packed_ref.shape[1] <= (HALF + 1) * DK else 2 * DK
    scales = to_float(packed_ref[:, packed_ref.shape[1] - lanes :])
    exponents = pltpu.roll(scales, lanes // 2, 1)
    return scales * jnp.exp2(exponents) * (1.0 / (LEVELS * LEVELS))


def unpack_block(packed_ref, steps, block):
    return to_float(packed_ref[:, block * DK : (block + 1) * DK]) * steps[:, block : block + 1]


def fold_rows(value):
    half = value.shape[1] // 2
    return jnp.concatenate([value[:, :half], value[:, half:]], axis=0)


def received(kept_ref, got_ref, steps, block):
    half = kept_ref.shape[1] // DK // 2
    rows = unpack_block(got_ref, steps, block % half)
    rows = rows[:ROWS] if block < half else rows[ROWS:]
    return kept_ref[:, block * DK : (block + 1) * DK] + rows


def tap_block(block, me):
    other = jnp.bitwise_xor(block // 2, me)
    place = ((other >> 2) & 3) + ((other >> 1) & 1) * 4 + (other & 1) * 8
    return place * 2 + block % 2


def activate(kept_ref, got_ref, steps, part, head, history_ref, taps_ref, twist, row_step):
    fresh = received(kept_ref, got_ref, steps, head)
    column = part * HEADS_WIDTH + head * DK
    carried = history_ref[:, column : column + DK]
    taps = taps_ref[tap_block(column // TAP_WIDTH, twist)]
    inner = column % TAP_WIDTH
    total = taps[TAPS - 1 :, inner : inner + DK] * fresh
    for lag in range(1, TAPS):
        source = jnp.where(row_step >= STEPS - lag, carried, fresh)
        tap = taps[TAPS - 1 - lag : TAPS - lag, inner : inner + DK]
        total = total + tap * pltpu.roll(source, lag, 0)
    return total / (1.0 + jnp.exp(-total))


def keys_kernel(
    twist_ref, query_ref, query_got_ref, key_ref, key_got_ref, history_ref, near_ref, far_ref,
    state_hbm, key_seen_ref, query_seen_ref, pulls_ref, weights_ref, taps_ref, state_ref, sems,
):
    per_copy = H // STATE_COPIES
    copies = []
    for at in range(STATE_COPIES):
        some = pl.ds(at * per_copy, per_copy)
        copies.append(
            pltpu.make_async_copy(state_hbm.at[:, some], state_ref.at[:, some], sems.at[at])
        )
        copies[-1].start()
    twist = twist_ref[0]
    half = TAP_BLOCKS // 2
    for at in range(TAP_BLOCKS):
        source = near_ref if at < half else far_ref
        if at % 4 == 0:
            some = source[at % half * TAPS : (at % half + 4) * TAPS, :].astype(jnp.float32)
        taps_ref[at] = some[at % 4 * TAPS : (at % 4 + 1) * TAPS]
    row = lax.broadcasted_iota(jnp.int32, (ROWS, DK), 0)
    row_step = row % STEPS
    query_steps, key_steps = steps_of(query_got_ref), steps_of(key_got_ref)
    for head in range(H):
        key = unit_length(
            activate(
                key_ref, key_got_ref, key_steps, 1, head, history_ref, taps_ref, twist, row_step
            )
        )
        query = unit_length(
            activate(
                query_ref, query_got_ref, query_steps, 0, head, history_ref, taps_ref, twist,
                row_step,
            )
        )
        both = jnp.concatenate([key, query], axis=0)
        if head % per_copy == 0:
            copies[head // per_copy].wait()
        both_high = both.astype(jnp.bfloat16)
        both_low = (both - both_high.astype(jnp.float32)).astype(jnp.bfloat16)
        stacked = jnp.concatenate([both_high, both_low], axis=0)
        seen = []
        for r in range(LOCAL):
            state = state_ref[r, head]
            high = state.astype(jnp.bfloat16)
            low = (state - high.astype(jnp.float32)).astype(jnp.bfloat16)
            main = jnp.dot(stacked, high, preferred_element_type=jnp.float32)
            rest = jnp.dot(both_high, low, preferred_element_type=jnp.float32)
            seen.append(main[: 2 * ROWS] + main[2 * ROWS :] + rest)
        key_seen_ref[head] = jnp.where(row < STEPS, seen[0][:ROWS], seen[1][:ROWS])
        query_seen_ref[head] = jnp.where(row < STEPS, seen[0][ROWS:], seen[1][ROWS:])
        for lag in range(STEPS):
            moved_key = shift_rows(key, lag, row_step)
            if lag:
                pulls_ref[lag - 1, head] = jnp.broadcast_to(lane_sum(key * moved_key), (ROWS, DK))
            weights_ref[lag, head] = jnp.broadcast_to(lane_sum(query * moved_key), (ROWS, DK))


def values_kernel(
    slots_ref, halves_ref, lengths_ref, twist_ref, value_ref, value_got_ref, history_ref,
    key_seen_ref, query_seen_ref, pulls_ref, weights_ref, taps_ref, out_ref, heads_ref,
):
    twist = twist_ref[0]
    row = lax.broadcasted_iota(jnp.int32, (ROWS, DK), 0)
    row_step = row % STEPS
    lane = lax.broadcasted_iota(jnp.int32, (ROWS, DK), 1)
    row_length = jnp.where(row < STEPS, lengths_ref[0], lengths_ref[1])
    live = row_step < row_length
    value_steps = steps_of(value_got_ref)
    gates = received(value_ref, value_got_ref, value_steps, H)
    for head in range(H):
        value = activate(
            value_ref, value_got_ref, value_steps, 2, head, history_ref, taps_ref, twist, row_step
        )
        beta_logit = jnp.broadcast_to(gates[:, head : head + 1], (ROWS, DK))
        decay_logit = jnp.broadcast_to(gates[:, H + head : H + head + 1], (ROWS, DK))
        beta = 1.0 / (1.0 + jnp.exp(-beta_logit))
        decay = 1.0 / (1.0 + jnp.exp(decay_logit))
        fades = [jnp.ones_like(decay), decay]
        for lag in range(2, STEPS + 1):
            earlier = pltpu.roll(decay, lag - 1, 0)
            fades.append(jnp.where(row_step >= lag - 1, fades[-1] * earlier, fades[-1]))
        base = beta * (value - fades[STEPS] * key_seen_ref[head])
        pulls = [
            beta * fades[lag] * pulls_ref[lag - 1, head] if lag else None for lag in range(STEPS)
        ]
        solved = base
        for _ in range(STEPS - 1):
            following = base
            for lag in range(1, STEPS):
                following = following - pulls[lag] * shift_rows(solved, lag, row_step)
            solved = following
        out = fades[STEPS] * query_seen_ref[head]
        for lag in range(STEPS):
            weight = fades[lag] * weights_ref[lag, head]
            out = out + weight * shift_rows(solved, lag, row_step)
        heads_ref[head] = jnp.where(live, out, 0.0)
    for quad in range(UNITS // 4):
        joined = []
        for pair in (2 * quad, 2 * quad + 1):
            first = heads_ref[slots_ref[2 * pair]]
            second = heads_ref[slots_ref[2 * pair + 1]]
            first = jnp.where(halves_ref[2 * pair] == 0, first, pltpu.roll(first, HALF, 1))
            second = jnp.where(halves_ref[2 * pair + 1] == 0, pltpu.roll(second, HALF, 1), second)
            joined.append(jnp.where(lane < HALF, first, second))
        out_ref[quad] = jnp.concatenate(joined, axis=0).astype(jnp.bfloat16)


def run_delta(slots, halves, lengths, queries, keys, values, history, twist, taps, state):
    smem = pl.BlockSpec(memory_space=pltpu.SMEM)
    vmem = pl.BlockSpec(memory_space=pltpu.VMEM)
    params = pltpu.CompilerParams(vmem_limit_bytes=32 * 1024 * 1024)
    per_head = jax.ShapeDtypeStruct((H, ROWS, DK), jnp.float32)
    lags = [
        jax.ShapeDtypeStruct((count, H, ROWS, DK), jnp.float32) for count in (STEPS - 1, STEPS)
    ]
    tap_blocks = jax.ShapeDtypeStruct((TAP_BLOCKS, TAPS, TAP_WIDTH), jnp.float32)
    prepared = pl.pallas_call(
        keys_kernel,
        out_shape=[per_head] * 2 + lags + [tap_blocks],
        in_specs=[smem] + [vmem] * 7 + [pl.BlockSpec(memory_space=pl.ANY)],
        out_specs=[vmem] * 5,
        scratch_shapes=[
            pltpu.VMEM(state.shape, jnp.float32),
            pltpu.SemaphoreType.DMA((STATE_COPIES,)),
        ],
        compiler_params=params,
        cost_estimate=pl.CostEstimate(flops=40_000_000, bytes_accessed=9_000_000, transcendentals=0),
        name="keys_part",
    )(twist, *queries, *keys, history, *taps, state)
    return pl.pallas_call(
        values_kernel,
        out_shape=jax.ShapeDtypeStruct((UNITS // 4, 2 * ROWS, DK), jnp.bfloat16),
        in_specs=[smem] * 4 + [vmem] * 8,
        out_specs=vmem,
        scratch_shapes=[pltpu.VMEM((H, ROWS, DK), jnp.float32)],
        compiler_params=params,
        cost_estimate=pl.CostEstimate(flops=4_000_000, bytes_accessed=2_000_000, transcendentals=0),
        name="values_part",
    )(slots, halves, lengths, twist, *values, history, *prepared)


def rows_kernel(
    depth, me_ref, slot_of_ref, tokens_hbm, weight_hbm, mine_ref, theirs_ref,
    weight_ref, window_ref, sem, weight_sem,
):
    me = me_ref[0]
    width = window_ref.shape[2]
    offset = me // 2 * (2 * depth)
    start = jnp.minimum(offset // DK * DK, D - width)
    columns = pl.ds(pl.multiple_of(start, DK), width)
    copy = pltpu.make_async_copy(tokens_hbm.at[:, :, columns], window_ref, sem)
    copy.start()
    weight_copy = pltpu.make_async_copy(weight_hbm, weight_ref, weight_sem)
    weight_copy.start()
    shape = (mine_ref.shape[0], slot_of_ref.shape[1])
    row = lax.broadcasted_iota(jnp.int32, shape, 0)
    place = row // ROWS
    count = (shape[0] // ROWS).bit_length() - 1
    holder = jnp.zeros(shape, jnp.int32)
    for at in range(count):
        holder = holder + ((place >> (count - 1 - at)) & 1) * (2 << at)
    holder = jnp.bitwise_xor(holder, me)
    match = holder * LOCAL + row % ROWS // STEPS == slot_of_ref[...]
    copy.wait()
    window = window_ref[...].astype(jnp.float32)
    total = jnp.zeros((shape[0], width), jnp.float32)
    for step in range(STEPS):
        picker = jnp.where(match & (row % STEPS == step), 1.0, 0.0).astype(jnp.bfloat16)
        here = window[:, step, :].astype(jnp.bfloat16)
        total = total + jnp.dot(picker, here, preferred_element_type=jnp.float32)
    total = pltpu.roll(total, lax.rem(width - (offset - start), width), 1)
    low, high = total[:, :depth], total[:, depth : 2 * depth]
    first_core = me % 2 == 0
    mine_ref[...] = jnp.where(first_core, low, high).astype(jnp.bfloat16)
    theirs_ref[...] = jnp.where(first_core, high, low).astype(jnp.bfloat16)
    weight_copy.wait()


def run_rows(me, slot_of, tokens, weight, chips):
    depth = weight.shape[0]
    width = -(-(2 * depth + DK - 1) // DK) * DK
    out = jax.ShapeDtypeStruct((chips * ROWS, depth), jnp.bfloat16)
    vmem = pl.BlockSpec(memory_space=pltpu.VMEM)
    return pl.pallas_call(
        functools.partial(rows_kernel, depth),
        out_shape=[out, out, jax.ShapeDtypeStruct(weight.shape, weight.dtype)],
        in_specs=[
            pl.BlockSpec(memory_space=pltpu.SMEM), vmem, pl.BlockSpec(memory_space=pl.ANY),
            pl.BlockSpec(memory_space=pl.ANY),
        ],
        out_specs=[vmem] * 3,
        scratch_shapes=[
            pltpu.VMEM((tokens.shape[0], STEPS, width), jnp.bfloat16),
            pltpu.SemaphoreType.DMA,
            pltpu.SemaphoreType.DMA,
        ],
        compiler_params=pltpu.CompilerParams(vmem_limit_bytes=32 * 1024 * 1024),
        cost_estimate=pl.CostEstimate(flops=0, bytes_accessed=0, transcendentals=0),
        name="token_rows",
    )(me.reshape(1), slot_of.reshape(1, -1), tokens, weight)


def product_kernel(skipped, crossed, *refs):
    mine_ref, theirs_ref, block_ref, other_ref, *refs = refs[skipped:]
    gate_refs, (kept_ref, packed_ref) = refs[:-2], refs[-2:]
    half = mine_ref.shape[0] // 2

    def product(own, other, dims):
        total = lax.dot_general(mine_ref[...], own, dims, preferred_element_type=jnp.float32)
        return total + lax.dot_general(
            theirs_ref[...], other, dims, preferred_element_type=jnp.float32
        )

    total = product(block_ref[...], other_ref[...], (((1,), (0,)), ((), ())))
    if gate_refs:
        gates = product(gate_refs[0][...], gate_refs[1][...], (((1,), (1,)), ((), ())))
        zeros = jnp.zeros((gates.shape[0], 2 * DK - gates.shape[1]), jnp.float32)
        total = jnp.concatenate([total, gates, zeros], axis=1)
    if crossed:
        starts = [start for at in range(0, half, ROWS) for start in (at, half + at)]
        total = jnp.concatenate([total[start : start + ROWS] for start in starts], axis=0)
    kept, sent = total[:half], total[half:]
    kept_ref[...] = kept
    pack_rows(sent, packed_ref)


def run_product(mine, theirs, weights, part, gates=(), earlier=(), crossed=False):
    vmem = pl.BlockSpec(memory_space=pltpu.VMEM)
    block = pl.BlockSpec((mine.shape[1], HEADS_WIDTH), lambda i: (0, part))
    half = mine.shape[0] // 2
    width = HEADS_WIDTH + len(gates) * DK
    return pl.pallas_call(
        functools.partial(product_kernel, len(earlier), crossed),
        grid=(1,),
        out_shape=[
            jax.ShapeDtypeStruct((half, width), jnp.float32),
            jax.ShapeDtypeStruct((half, width + scale_lanes(width // DK)), jnp.int16),
        ],
        in_specs=[pl.BlockSpec(memory_space=pl.ANY)] * len(earlier)
        + [vmem, vmem, block, block]
        + [vmem] * len(gates),
        out_specs=[vmem] * 2,
        compiler_params=pltpu.CompilerParams(vmem_limit_bytes=32 * 1024 * 1024),
        cost_estimate=pl.CostEstimate(flops=0, bytes_accessed=0, transcendentals=0),
        name="partial_product",
    )(*earlier, mine, theirs, *weights, *gates)


def combine_kernel(kept_ref, got_ref, still_ref, packed_ref):
    half = still_ref.shape[0]
    steps = steps_of(got_ref)
    sent = []
    for block in range(kept_ref.shape[1] // DK):
        columns = pl.ds(block * DK, DK)
        total = kept_ref[:, columns] + unpack_block(got_ref, steps, block)
        still_ref[:, columns] = total[:half]
        sent.append(total[half:])
    sent = jnp.concatenate(sent, axis=1)
    pack_rows(fold_rows(sent) if half == ROWS else sent, packed_ref)


def run_combine(kept, got):
    vmem = pl.BlockSpec(memory_space=pltpu.VMEM)
    half, width = kept.shape[0] // 2, kept.shape[1]
    rows, packed = (2 * ROWS, width // 2) if half == ROWS else (half, width)
    packed = (rows, packed + scale_lanes(packed // DK))
    return pl.pallas_call(
        combine_kernel,
        out_shape=[
            jax.ShapeDtypeStruct((half, width), jnp.float32),
            jax.ShapeDtypeStruct(packed, jnp.int16),
        ],
        in_specs=[vmem] * 2,
        out_specs=[vmem] * 2,
        compiler_params=pltpu.CompilerParams(vmem_limit_bytes=32 * 1024 * 1024),
        cost_estimate=pl.CostEstimate(flops=0, bytes_accessed=0, transcendentals=0),
        name="combine",
    )(kept, got)


def join_kernel(first_ref, second_ref, earlier_ref, out_ref):
    both = [ref[...].astype(jnp.float32) for ref in (first_ref, second_ref)]
    out_ref[...] = jnp.concatenate(both, axis=0).astype(out_ref.dtype)


def join(first, second, earlier):
    vmem = pl.BlockSpec(memory_space=pltpu.VMEM)
    rows, width = first.shape
    return pl.pallas_call(
        join_kernel,
        out_shape=jax.ShapeDtypeStruct((2 * rows, width), first.dtype),
        in_specs=[vmem, vmem, pl.BlockSpec(memory_space=pl.ANY)],
        out_specs=vmem,
        compiler_params=pltpu.CompilerParams(vmem_limit_bytes=32 * 1024 * 1024),
        cost_estimate=pl.CostEstimate(flops=0, bytes_accessed=0, transcendentals=0),
        name="join_taps",
    )(first, second, earlier)


def swap(value, bit, devices):
    return lax.ppermute(value, "heads", [(i, i ^ bit) for i in range(devices)])


def on_device(
    tokens,
    qkv_weight,
    gate_weight,
    conv_weight,
    delta_state,
    conv_state,
    old_heads,
    new_units,
    slot_of,
    lengths,
):
    devices = lax.axis_size("heads")
    me = lax.axis_index("heads")
    per_device = UNITS // devices
    row_count = tokens.shape[0]
    chips = devices // 2

    bits = [1 << b for b in range(1, devices.bit_length() - 1)]

    ride = conv_weight.shape[1] == 2 * TAP_WIDTH and len(bits) == 3
    if ride:
        taps = jnp.concatenate([conv_weight[:, :TAP_WIDTH], conv_weight[:, TAP_WIDTH:]], axis=0)
        far = swap(taps, 4, devices)
    else:
        taps = lax.all_gather(conv_weight, "heads", axis=1, tiled=True)
        order = [
            2 * (at >> 4 & 1) + 4 * (at >> 3 & 1) + 8 * (at >> 1 & 1) + 16 * (at >> 2 & 1) + (at & 1)
            for at in range(TAP_BLOCKS)
        ]
        taps = [taps[:, block * TAP_WIDTH : (block + 1) * TAP_WIDTH] for block in order]
        taps = jnp.concatenate(taps, axis=0)

    mine, theirs, near_weight = run_rows(me, slot_of, tokens, qkv_weight, chips)

    weights = (near_weight, swap(qkv_weight, 1, devices))
    gate_columns = gate_weight.T
    gates = (gate_columns, swap(gate_columns, 1, devices))

    tie = lambda *values: lax.optimization_barrier(values)

    if ride:
        taps = join(taps, far, mine)
        far = swap(taps, 8, devices)
    keys = run_product(mine, theirs, weights, 1)
    values = run_product(mine, theirs, weights, 2, gates, earlier=keys[:1])
    queries = run_product(mine, theirs, weights, 0, earlier=values[:1], crossed=True)

    slot_of, lengths, old_heads, new_units, carried, *values = tie(
        slot_of, lengths, old_heads, new_units, conv_state, *values
    )
    steps = jnp.arange(STEPS, dtype=jnp.int32)
    offered = (slot_of[:, None] * STEPS + steps[None, :]).reshape(-1)
    old_slots, halves = unit_tables(old_heads, new_units)
    my_rows = me * LOCAL + jnp.arange(LOCAL, dtype=jnp.int32)
    my_lengths = jnp.sum(
        jnp.where(slot_of[None, :] == my_rows[:, None], lengths[None, :], 0), axis=1
    )
    blank = jnp.zeros((1, carried.shape[2]), jnp.float32)
    history = jnp.concatenate([blank, carried[1], blank, carried[0]], axis=0)
    routes = [bits[1:] + bits[:1], bits, bits]
    kept = [chunk[0] for chunk in (queries, keys, values)]
    got = [
        swap(chunk[1], route[0], devices)
        for chunk, route in zip((queries, keys, values), routes)
    ]
    for level in range(1, len(bits)):
        for at in range(3):
            kept[at], packed = run_combine(kept[at], got[at])
            got[at] = swap(packed, routes[at][level], devices)
            if ride and at == level:
                taps = join(taps, far, kept[at])
                far = swap(taps, 3 - level, devices)
    if ride:
        twist, taps = me.reshape(1), (taps, far)
    else:
        half = TAP_BLOCKS // 2 * TAPS
        twist, taps = jnp.zeros(1, jnp.int32), (taps[:half], taps[half:])
    queries, keys, values = zip(kept, got)

    local_out = run_delta(
        old_slots, halves, my_lengths, queries, keys, values, history, twist, taps, delta_state
    )

    placer = (offered[:, None] == jnp.arange(row_count * STEPS, dtype=jnp.int32)[None, :]).astype(
        jnp.bfloat16
    )
    if per_device % 2 == 0:
        pairs = per_device // 2
        sending = local_out.reshape(devices, pairs * ROWS, DK)
        got = lax.all_to_all(sending, "heads", split_axis=0, concat_axis=0, tiled=True)
        got = got.reshape(devices, pairs, ROWS, DK)
        got = jnp.concatenate([got[:, pair] for pair in range(pairs)], axis=-1)
        got = got.reshape(devices * ROWS, pairs * DK)
    else:
        units = local_out.reshape(UNITS // 2, ROWS, 2, HALF).transpose(0, 2, 1, 3)
        sending = units.reshape(devices, per_device * ROWS, HALF)
        got = lax.all_to_all(sending, "heads", split_axis=0, concat_axis=0, tiled=True)
        got = got.reshape(devices, per_device, ROWS, HALF).transpose(0, 2, 1, 3)
        got = got.reshape(devices * ROWS, per_device * HALF)
    outputs = jnp.dot(placer, got, preferred_element_type=jnp.float32).astype(jnp.bfloat16)
    return outputs.reshape(row_count, STEPS, per_device * HALF)


def solution(mesh):
    in_specs = (
        P("groups", None, None),
        P(("groups", "heads"), None),
        P(("groups", "heads"), None),
        P("groups", "heads"),
        P(("groups", "heads"), None, None, None),
        P(("groups", "heads"), None, None),
        P(),
        P(),
        P("groups"),
        P("groups"),
    )
    out_specs = P("groups", None, "heads")
    return jax.shard_map(
        on_device, mesh=mesh, in_specs=in_specs, out_specs=out_specs, check_vma=False
    )
```
